32 devices in a mesh: fsdp: 4 (over y, x), ctx: 4 (over z), tp: 2 (over core).
Axes of the slice: x: 2, y: 2, z: 4, core: 2. Of those that a mesh axis runs over, the one named last changes fastest.
Arguments:
- inputs: bfloat16 [8, 1024, 2048], P('fsdp', 'ctx'), may hold values from -6 to 6
- lengths: int32 [8], P('fsdp'), may hold values from 256 to 1024, as said below
- cotangent: bfloat16 [8, 1024, 2048], P('fsdp', 'ctx'), may hold values from -6 to 6
- norm1_gain: bfloat16 [2048], P(('fsdp', 'ctx')), may hold values from 0.5 to 1.5
- w_query: bfloat16 [2048, 2048], P(('fsdp', 'ctx'), 'tp'), may hold values from -0.5 to 0.5
- w_key: bfloat16 [2048, 512], P(('fsdp', 'ctx'), 'tp'), may hold values from -0.5 to 0.5
- w_value: bfloat16 [2048, 512], P(('fsdp', 'ctx'), 'tp'), may hold values from -0.125 to 0.125
- w_out: bfloat16 [2048, 2048], P(('fsdp', 'ctx'), 'tp'), may hold values from -1 to 1
- norm2_gain: bfloat16 [2048], P(('fsdp', 'ctx')), may hold values from 0.5 to 1.5
- w_gate: bfloat16 [2048, 8192], P(('fsdp', 'ctx'), 'tp'), may hold values from -0.125 to 0.125
- w_up: bfloat16 [2048, 8192], P(('fsdp', 'ctx'), 'tp'), may hold values from -0.125 to 0.125
- w_down: bfloat16 [2048, 8192], P(('fsdp', 'ctx'), 'tp'), may hold values from -0.25 to 0.25
Outputs:
- output: bfloat16 [8, 1024, 2048], P('fsdp', 'ctx')
- input_grad: bfloat16 [8, 1024, 2048], P('fsdp', 'ctx')
- norm1_gain_grad: float32 [2048], P(('fsdp', 'ctx'))
- w_query_grad: float32 [2048, 2048], P(('fsdp', 'ctx'), 'tp')
- w_key_grad: float32 [2048, 512], P(('fsdp', 'ctx'), 'tp')
- w_value_grad: float32 [2048, 512], P(('fsdp', 'ctx'), 'tp')
- w_out_grad: float32 [2048, 2048], P(('fsdp', 'ctx'), 'tp')
- norm2_gain_grad: float32 [2048], P(('fsdp', 'ctx'))
- w_gate_grad: float32 [2048, 8192], P(('fsdp', 'ctx'), 'tp')
- w_up_grad: float32 [2048, 8192], P(('fsdp', 'ctx'), 'tp')
- w_down_grad: float32 [2048, 8192], P(('fsdp', 'ctx'), 'tp')
The draws below stay inside these ranges and needn't reach their ends.
Inputs may be any that keep to these rules, and one draw needn't show every extreme that they name: `lengths`: in each aligned group of 2 sequences at least one has length 1024.
All inputs are finite; a program needn't handle non-finite values.
Results may differ from the reference program's by a relative error of at most 0.015.
Values may be sent and summed in bfloat16 or wider, within the bound.
A program may use at most 256 MiB of HBM per device.

```python
import math
from functools import partial
import jax
import jax.numpy as jnp
from jax import lax

D = 2048
HEADS = 32
KV_HEADS = 8
HD = 64
FF = 8192
LEN = 1024
SEQ_DEV = 2
SEQS = 8


def draw_lengths(key, part):
    key = jax.random.fold_in(key, 11)
    first_key, second_key = jax.random.split(key)
    drawn_lengths = jax.random.randint(first_key, (SEQS,), LEN // 4, LEN + 1)
    chosen = jax.random.randint(second_key, (SEQS // SEQ_DEV,), 0, SEQ_DEV)
    slot_index = jnp.arange(SEQS) % SEQ_DEV
    full_length = slot_index == jnp.repeat(chosen, SEQ_DEV, total_repeat_length=SEQS)
    return jnp.where(full_length, LEN, drawn_lengths).astype(jnp.int32)


def steps_of(stream_key, dims, cuts, least, high):
    factor_of = 1.0
    for position, parts in cuts:
        heights = jax.random.uniform(jax.random.fold_in(jax.random.fold_in(stream_key, 6), position), (parts,), jnp.float32, least / len(cuts), high / len(cuts))
        factor_of = factor_of * jnp.repeat(jnp.exp(heights), dims[position] // parts).reshape((-1,) + (1,) * (len(dims) - 1 - position))
    return factor_of


def normal_values(rng, shape, spread, reach, cuts=(), kind=jnp.bfloat16):
    entries = jax.random.normal(rng, shape, jnp.float32) * spread
    if len(cuts) > 0:
        entries = steps_of(rng, shape, cuts, -0.22, 0.18) * entries
    return jnp.clip(entries, min=-reach, max=reach).astype(kind)


def setup_inputs(seed: int = 0) -> dict:
    arg_keys = jax.random.split(jax.random.key(seed), 13)
    return {
        "inputs": normal_values(arg_keys[0], (SEQS, LEN, D), 1.0, 6.0, ((0, 4), (1, 4))),
        "lengths": draw_lengths(jax.random.fold_in(arg_keys[12], 71), 0),
        "cotangent": normal_values(arg_keys[2], (SEQS, LEN, D), 1.0, 6.0, ((0, 4), (1, 4))),
        "norm1_gain": jnp.clip(1.0 + 0.1 * jax.random.normal(arg_keys[3], (D,), jnp.float32), 0.5, 1.5).astype(jnp.bfloat16),
        "w_query": normal_values(arg_keys[4], (D, HEADS * HD), (D // 16) ** -0.5, 0.5, ((0, 16), (1, 2))),
        "w_key": normal_values(arg_keys[5], (D, KV_HEADS * HD), (D // 16) ** -0.5, 0.5, ((0, 16), (1, 2))),
        "w_value": normal_values(arg_keys[6], (D, KV_HEADS * HD), D ** -0.5, 0.125, ((0, 16), (1, 2))),
        "w_out": normal_values(arg_keys[7], (D, HEADS * HD), (max(HEADS * HD // 64, 1)) ** -0.5, 1.0, ((0, 16), (1, 2))),
        "norm2_gain": jnp.clip(1.0 + 0.1 * jax.random.normal(arg_keys[8], (D,), jnp.float32), 0.5, 1.5).astype(jnp.bfloat16),
        "w_gate": normal_values(arg_keys[9], (D, FF), D ** -0.5, 0.125, ((0, 16), (1, 2))),
        "w_up": normal_values(arg_keys[10], (D, FF), D ** -0.5, 0.125, ((0, 16), (1, 2))),
        "w_down": normal_values(arg_keys[11], (D, FF), (FF // 16) ** -0.5, 0.25, ((0, 16), (1, 2))),
    }


@jax.custom_vjp
def reduced_precision_forward(v):
    return lax.optimization_barrier(v.astype(jnp.bfloat16)).astype(jnp.float32)

@jax.custom_vjp
def reduced_precision_backward(v):
    return v

def low_keep(v):
    return (reduced_precision_forward(v), None)

def low_pass(kept, grad):
    return (grad,)

def back_keep(v):
    return (v, None)

def back_low(kept, grad):
    return (reduced_precision_forward(grad),)
reduced_precision_forward.defvjp(low_keep, low_pass)
reduced_precision_backward.defvjp(back_keep, back_low)
norm_eps = 1e-05
residual_scale = 0.22
score_scale = 1.0 / 64.0
rope_base = 10000000.0
masked_score = -1e+30

def rope_tables(positions, head_dim):
    half_dim = head_dim // 2
    frequency = rope_base ** (-(jnp.arange(half_dim, dtype=jnp.float32) * 2.0) / head_dim)
    angles = positions.astype(jnp.float32)[:, None] * frequency[None, :]
    return (jnp.concatenate([jnp.cos(angles), jnp.cos(angles)], -1), jnp.concatenate([jnp.sin(angles), jnp.sin(angles)], -1))

def rotate(values_in, cosines, sines):
    half_dim = values_in.shape[-1] // 2
    turned = jnp.concatenate([-values_in[..., half_dim:], values_in[..., :half_dim]], -1)
    return values_in * cosines + turned * sines

def matmul(left, right):
    return jnp.dot(left, right, precision=lax.Precision.HIGHEST)

def head_group(block_item, key_mask):
    grouped_query_rows, key_row_block, value_row_block = block_item
    unmasked_scores = jnp.einsum('luay,lpy->laup', grouped_query_rows, key_row_block, precision=lax.Precision.HIGHEST)
    scores = reduced_precision_backward(unmasked_scores * score_scale)
    scores = jnp.where(key_mask[:, None], scores, masked_score)
    attention_probabilities = jax.nn.softmax(scores, axis=-1)
    head_output = reduced_precision_backward(jnp.einsum('ayoh,ahz->aoyz', reduced_precision_forward(attention_probabilities), value_row_block, precision=lax.Precision.HIGHEST))
    return reduced_precision_forward(head_output)

def layer(layer_in, valid_rows, key_mask, cosines, sines, gain_one, w_query, w_key, w_value, w_out, gain_two, w_gate, w_up, w_down):
    seq_count, length, model_width = layer_in.shape
    group_size = HEADS // KV_HEADS
    first_rms = lax.rsqrt(lax.optimization_barrier(jnp.mean(layer_in * layer_in, -1, keepdims=True)) + norm_eps)
    first_normed = reduced_precision_forward(layer_in * first_rms * gain_one)
    query_heads = reduced_precision_backward(matmul(first_normed, w_query)).reshape(seq_count, length, HEADS, HD)
    key_heads = reduced_precision_backward(matmul(first_normed, w_key)).reshape(seq_count, length, KV_HEADS, HD)
    value_heads = reduced_precision_forward(reduced_precision_backward(matmul(first_normed, w_value))).reshape(seq_count, length, KV_HEADS, HD)
    query_heads = reduced_precision_forward(rotate(query_heads, cosines[:, None, :], sines[:, None, :]))
    key_heads = reduced_precision_forward(rotate(key_heads, cosines[:, None, :], sines[:, None, :]))
    query_split = jnp.moveaxis(query_heads.reshape(seq_count, length, KV_HEADS, group_size, HD), 2, 0)
    key_split = jnp.moveaxis(key_heads, 2, 0)
    value_split = jnp.moveaxis(value_heads, 2, 0)
    attended = lax.map(jax.checkpoint(partial(head_group, key_mask=key_mask)), (query_split, key_split, value_split))
    attended = jnp.moveaxis(attended, 0, 2).reshape(seq_count, length, HEADS * HD)
    attn_branch = reduced_precision_backward(matmul(attended, w_out.T))
    middle = layer_in + residual_scale * attn_branch
    second_rms = lax.rsqrt(lax.optimization_barrier(jnp.mean(middle * middle, -1, keepdims=True)) + norm_eps)
    second_normed = reduced_precision_forward(middle * second_rms * gain_two)
    gate_lin = reduced_precision_backward(matmul(second_normed, w_gate))
    up_lin = reduced_precision_backward(matmul(second_normed, w_up))
    hidden = reduced_precision_forward(jax.nn.silu(gate_lin) * up_lin)
    ff_branch = reduced_precision_backward(matmul(hidden, w_down.T))
    return valid_rows[..., None] * (middle + residual_scale * ff_branch)

def reference(inputs, lengths, cotangent, norm1_gain, w_query, w_key, w_value, w_out, norm2_gain, w_gate, w_up, w_down):
    weights = tuple((w.astype(jnp.float32) for w in (norm1_gain, w_query, w_key, w_value, w_out, norm2_gain, w_gate, w_up, w_down)))
    group_size = math.gcd(SEQS, max(1, 4096 // LEN))
    blocks = SEQS // group_size
    places = jnp.arange(LEN, dtype=jnp.int32)
    cosines, sines = rope_tables(places, HD)
    causal = places[None, :] <= places[:, None]

    def block_step(totals, block_item):
        block_in, block_len, block_cot = block_item
        valid_rows = (places[None, :] < block_len[:, None]).astype(jnp.float32)
        key_mask = causal[None] & (places[None, None, :] < block_len[:, None, None])

        def forward(layer_in, *params):
            return layer(layer_in, valid_rows, key_mask, cosines, sines, *params)
        result, pullback = jax.vjp(forward, block_in.astype(jnp.float32), *weights)
        gradients = pullback(block_cot.astype(jnp.float32))
        totals = tuple(jax.tree.map(jnp.add, totals, tuple(gradients[1:])))
        return (totals, (result.astype(jnp.bfloat16), gradients[0].astype(jnp.bfloat16)))
    zero_grads = tuple((jnp.zeros_like(w) for w in weights))
    totals, (outputs, input_grads) = lax.scan(block_step, zero_grads, (inputs.reshape(blocks, group_size, LEN, D), lengths.reshape(blocks, group_size), cotangent.reshape(blocks, group_size, LEN, D)))
    return (outputs.reshape(SEQS, LEN, D), input_grads.reshape(SEQS, LEN, D), totals[0], totals[1], totals[2], totals[3], totals[4], totals[5], totals[6], totals[7], totals[8])
```

```python
from functools import partial

import jax
import jax.numpy as jnp
from jax import lax
from jax.sharding import PartitionSpec as P

HD = 64


norm_eps = 1e-05
residual_scale = 0.22
score_scale = 1.0 / 64.0
rope_base = 10000000.0
masked_score = -1e30


def rope_tables(positions, head_dim):
    half_dim = head_dim // 2
    frequency = rope_base ** (-(jnp.arange(half_dim, dtype=jnp.float32) * 2.0) / head_dim)
    angles = positions.astype(jnp.float32)[:, None] * frequency[None, :]
    return (
        jnp.concatenate([jnp.cos(angles), jnp.cos(angles)], -1),
        jnp.concatenate([jnp.sin(angles), jnp.sin(angles)], -1),
    )


def rotate(values_in, cosines, sines):
    half_dim = values_in.shape[-1] // 2
    turned = jnp.concatenate([-values_in[..., half_dim:], values_in[..., :half_dim]], -1)
    return values_in * cosines + turned * sines


def unrotate(grad_in, cosines, sines):
    half_dim = grad_in.shape[-1] // 2
    scaled = grad_in * sines
    return grad_in * cosines + jnp.concatenate(
        [scaled[..., half_dim:], -scaled[..., :half_dim]], -1
    )


def rms_scale(values_in):
    return lax.rsqrt(jnp.mean(values_in * values_in, -1, keepdims=True) + norm_eps)


def norm_back(grad_normed, values_in, scale, gain):
    scaled_grad = grad_normed * gain
    return scale * scaled_grad - values_in * scale**3 * jnp.mean(
        scaled_grad * values_in, -1, keepdims=True
    )


def masked_scores(grouped_query_rows, key_row_block, key_mask):
    scores = (
        jnp.einsum(
            "sqgd,skd->sgqk", grouped_query_rows, key_row_block, preferred_element_type=jnp.float32
        )
        * score_scale
    )
    return jnp.where(key_mask[:, None], scores, masked_score)


def attend_forward(block_item, key_mask):
    grouped_query_rows, key_row_block, value_row_block = block_item
    scores = masked_scores(grouped_query_rows, key_row_block, key_mask)
    top_score = jnp.max(scores, -1, keepdims=True)
    exp_scores = jnp.exp(scores - top_score)
    total_mass = jnp.sum(exp_scores, -1, keepdims=True)
    probs_low = (exp_scores / total_mass).astype(jnp.bfloat16)
    head_output = jnp.einsum(
        "sgqk,skd->sqgd", probs_low, value_row_block, preferred_element_type=jnp.float32
    )
    return (head_output.astype(jnp.bfloat16), top_score + jnp.log(total_mass))


def attend_backward(block_item, key_mask):
    grouped_query_rows, key_row_block, value_row_block, out_grad, log_mass = block_item
    scores = masked_scores(grouped_query_rows, key_row_block, key_mask)
    attention_probabilities = jnp.exp(scores - log_mass)
    probs_low = attention_probabilities.astype(jnp.bfloat16)
    value_grad = jnp.einsum(
        "sgqk,sqgd->skd", probs_low, out_grad, preferred_element_type=jnp.float32
    )
    probs_grad = jnp.einsum(
        "sqgd,skd->sgqk", out_grad, value_row_block, preferred_element_type=jnp.float32
    )
    score_grad = (
        attention_probabilities
        * (probs_grad - jnp.sum(attention_probabilities * probs_grad, -1, keepdims=True))
    ).astype(jnp.bfloat16)
    query_grad = (
        jnp.einsum("sgqk,skd->sqgd", score_grad, key_row_block, preferred_element_type=jnp.float32)
        * score_scale
    )
    key_grad = (
        jnp.einsum(
            "sgqk,sqgd->skd", score_grad, grouped_query_rows, preferred_element_type=jnp.float32
        )
        * score_scale
    )
    return (query_grad, key_grad, value_grad)


def local(
    inputs,
    lengths,
    cotangent,
    norm1_gain,
    w_query,
    w_key,
    w_value,
    w_out,
    norm2_gain,
    w_gate,
    w_up,
    w_down,
):
    seq_count, local_rows, model_width = inputs.shape
    tokens = seq_count * local_rows
    fsdp = lax.axis_size("fsdp")
    ctx = lax.axis_size("ctx")
    full_rows = local_rows * ctx
    shard = w_query.shape[0]
    positions = lax.axis_index("ctx") * local_rows + jnp.arange(local_rows, dtype=jnp.int32)
    key_places = jnp.arange(full_rows, dtype=jnp.int32)
    valid_rows = (positions[None, :] < lengths[:, None]).astype(jnp.float32)[..., None]
    key_mask = (key_places[None, None, :] <= positions[None, :, None]) & (
        key_places[None, None, :] < lengths[:, None, None]
    )
    cosines, sines = rope_tables(positions, HD)
    head_cos = cosines[None, :, None, :]
    head_sin = sines[None, :, None, :]
    query_width = w_query.shape[1]
    kv_width = w_key.shape[1]

    gains = jnp.pad(jnp.stack([norm1_gain, norm2_gain], 1), ((0, 0), (0, 126)))
    qkv_full = lax.all_gather(
        jnp.concatenate([w_query, w_key, w_value, gains], 1), ("fsdp", "ctx"), axis=0, tiled=True
    )
    out_full = lax.all_gather(w_out, ("fsdp", "ctx"), axis=0, tiled=True)
    query_full = qkv_full[:, :query_width]
    key_full = qkv_full[:, query_width : query_width + kv_width]
    value_full = qkv_full[:, query_width + kv_width : query_width + 2 * kv_width]
    gain_one = qkv_full[:, query_width + 2 * kv_width].astype(jnp.float32)
    gain_two = qkv_full[:, query_width + 2 * kv_width + 1].astype(jnp.float32)
    kv_end = query_width + 2 * kv_width

    def spread_units(weight):
        swapped = lax.all_to_all(weight, "fsdp", 1, 0, tiled=True)
        units = swapped.shape[1]
        whole = lax.all_gather(swapped.reshape(fsdp, shard, units), "ctx", axis=1, tiled=True)
        return whole.reshape(model_width, units)

    gate_full = spread_units(w_gate)
    up_full = spread_units(w_up)
    down_full = spread_units(w_down)
    units = gate_full.shape[1]

    back = cotangent.astype(jnp.float32) * valid_rows
    ff_grad = (residual_scale * back).astype(jnp.bfloat16).reshape(tokens, model_width)
    ff_grad_all = lax.all_gather(ff_grad, "fsdp", axis=0, tiled=True)

    query_heads = query_width // HD
    kv_heads = kv_width // HD
    group_size = query_heads // kv_heads
    layer_in = inputs.astype(jnp.float32)
    first_rms = rms_scale(layer_in)
    first_normed = (layer_in * first_rms * gain_one).astype(jnp.bfloat16)
    qkv_lin = jnp.dot(
        first_normed.reshape(tokens, model_width),
        qkv_full[:, :kv_end],
        preferred_element_type=jnp.float32,
    ).reshape(seq_count, local_rows, kv_end)
    query_rot = rotate(
        qkv_lin[..., :query_width].reshape(seq_count, local_rows, query_heads, HD),
        head_cos,
        head_sin,
    ).astype(jnp.bfloat16)
    key_rot = (
        rotate(
            qkv_lin[..., query_width : query_width + kv_width].reshape(
                seq_count, local_rows, kv_heads, HD
            ),
            head_cos,
            head_sin,
        )
        .astype(jnp.bfloat16)
        .reshape(seq_count, local_rows, kv_width)
    )
    value_low = qkv_lin[..., query_width + kv_width :].astype(jnp.bfloat16)
    kv_all = lax.all_gather(
        jnp.concatenate([key_rot, value_low], -1), "ctx", axis=1, tiled=True
    )
    key_split = jnp.moveaxis(
        kv_all[..., :kv_width].reshape(seq_count, full_rows, kv_heads, HD), 2, 0
    )
    value_split = jnp.moveaxis(
        kv_all[..., kv_width:].reshape(seq_count, full_rows, kv_heads, HD), 2, 0
    )
    query_split = jnp.moveaxis(
        query_rot.reshape(seq_count, local_rows, kv_heads, group_size, HD), 2, 0
    )
    head_output, log_mass = lax.map(
        partial(attend_forward, key_mask=key_mask), (query_split, key_split, value_split)
    )
    attended = jnp.moveaxis(head_output, 0, 2).reshape(tokens, query_width)
    attn_part = jnp.einsum("tj,dj->td", attended, out_full, preferred_element_type=jnp.float32)
    attn_branch = lax.psum(attn_part.astype(jnp.bfloat16), "tp").astype(jnp.float32)
    middle = layer_in + residual_scale * attn_branch.reshape(layer_in.shape)

    second_rms = rms_scale(middle)
    second_normed = (middle * second_rms * gain_two).astype(jnp.bfloat16)
    normed_all = lax.all_gather(
        second_normed.reshape(tokens, model_width), "fsdp", axis=0, tiled=True
    )
    gate_lin = jnp.dot(normed_all, gate_full, preferred_element_type=jnp.float32)
    up_lin = jnp.dot(normed_all, up_full, preferred_element_type=jnp.float32)
    gate_sig = jax.nn.sigmoid(gate_lin)
    gate_act = gate_lin * gate_sig
    hidden = (gate_act * up_lin).astype(jnp.bfloat16)

    hidden_grad = jnp.dot(ff_grad_all, down_full, preferred_element_type=jnp.float32)
    gate_grad = (hidden_grad * up_lin * gate_sig * (1.0 + gate_lin * (1.0 - gate_sig))).astype(
        jnp.bfloat16
    )
    up_grad = (hidden_grad * gate_act).astype(jnp.bfloat16)
    second_part = jnp.einsum(
        "tf,df->td", gate_grad, gate_full, preferred_element_type=jnp.float32
    ) + jnp.einsum("tf,df->td", up_grad, up_full, preferred_element_type=jnp.float32)

    def gather_sum(part):
        own = lax.psum_scatter(
            part.astype(jnp.bfloat16), "fsdp", scatter_dimension=0, tiled=True
        )
        return lax.psum(own, "tp").astype(jnp.float32).reshape(layer_in.shape)

    second_grad = gather_sum(second_part)

    def return_units(left, right):
        term = jnp.einsum("td,tf->df", left, right, preferred_element_type=jnp.float32)
        own = lax.psum_scatter(
            term.astype(jnp.bfloat16).reshape(fsdp, ctx * shard, units),
            "ctx",
            scatter_dimension=1,
            tiled=True,
        )
        return lax.all_to_all(
            own.reshape(fsdp * shard, units), "fsdp", 0, 1, tiled=True
        ).astype(jnp.float32)

    w_down_grad = return_units(ff_grad_all, hidden)
    w_gate_grad = return_units(normed_all, gate_grad)
    w_up_grad = return_units(normed_all, up_grad)

    ff_part = jnp.einsum("tf,df->td", hidden, down_full, preferred_element_type=jnp.float32)
    ff_branch = gather_sum(ff_part)
    output = (valid_rows * (middle + residual_scale * ff_branch)).astype(jnp.bfloat16)

    gain_two_term = jnp.sum(second_grad * middle * second_rms, axis=(0, 1))
    middle_grad = back + norm_back(second_grad, middle, second_rms, gain_two)

    attn_grad = (residual_scale * middle_grad).astype(jnp.bfloat16).reshape(tokens, model_width)
    out_term = jnp.einsum("td,tj->dj", attn_grad, attended, preferred_element_type=jnp.float32)
    w_out_grad = lax.psum_scatter(
        out_term.astype(jnp.bfloat16), ("fsdp", "ctx"), scatter_dimension=0, tiled=True
    ).astype(jnp.float32)
    attended_grad = jnp.dot(attn_grad, out_full, preferred_element_type=jnp.float32).astype(
        jnp.bfloat16
    )
    grad_split = jnp.moveaxis(
        attended_grad.reshape(seq_count, local_rows, kv_heads, group_size, HD), 2, 0
    )
    query_back, key_back, value_back = lax.map(
        partial(attend_backward, key_mask=key_mask),
        (query_split, key_split, value_split, grad_split, log_mass),
    )
    query_back = jnp.moveaxis(query_back, 0, 2).reshape(seq_count, local_rows, query_heads, HD)
    query_grad = (
        unrotate(query_back, head_cos, head_sin).astype(jnp.bfloat16).reshape(tokens, query_width)
    )
    key_spread = jnp.moveaxis(key_back, 0, 2).reshape(seq_count, full_rows, kv_width)
    value_spread = jnp.moveaxis(value_back, 0, 2).reshape(seq_count, full_rows, kv_width)
    kv_own = lax.psum_scatter(
        jnp.concatenate([key_spread, value_spread], -1).astype(jnp.bfloat16),
        "ctx",
        scatter_dimension=1,
        tiled=True,
    ).astype(jnp.float32)
    key_grad = (
        unrotate(
            kv_own[..., :kv_width].reshape(seq_count, local_rows, kv_heads, HD), head_cos, head_sin
        )
        .astype(jnp.bfloat16)
        .reshape(tokens, kv_width)
    )
    value_grad = kv_own[..., kv_width:].astype(jnp.bfloat16).reshape(tokens, kv_width)
    qkv_grad = jnp.concatenate([query_grad, key_grad, value_grad], -1)
    qkv_term = jnp.einsum(
        "td,tj->dj",
        first_normed.reshape(tokens, model_width),
        qkv_grad,
        preferred_element_type=jnp.float32,
    )
    first_part = jnp.einsum(
        "tj,dj->td", qkv_grad, qkv_full[:, :kv_end], preferred_element_type=jnp.float32
    )
    first_grad = (
        lax.psum(first_part.astype(jnp.bfloat16), "tp")
        .astype(jnp.float32)
        .reshape(layer_in.shape)
    )
    gain_one_term = jnp.sum(first_grad * layer_in * first_rms, axis=(0, 1))
    input_grad = (
        middle_grad + norm_back(first_grad, layer_in, first_rms, gain_one)
    ).astype(jnp.bfloat16)
    qkv_own = lax.psum_scatter(
        qkv_term.astype(jnp.bfloat16), ("fsdp", "ctx"), scatter_dimension=0, tiled=True
    ).astype(jnp.float32)
    gain_own = lax.psum_scatter(
        jnp.stack([gain_one_term, gain_two_term], 1), ("fsdp", "ctx"), scatter_dimension=0, tiled=True
    )
    return (
        output,
        input_grad,
        gain_own[:, 0],
        qkv_own[:, :query_width],
        qkv_own[:, query_width : query_width + kv_width],
        qkv_own[:, query_width + kv_width :],
        w_out_grad,
        gain_own[:, 1],
        w_gate_grad,
        w_up_grad,
        w_down_grad,
    )


def solution(mesh):
    placed = (
        P("fsdp", "ctx", None),
        P("fsdp"),
        P("fsdp", "ctx", None),
        P(("fsdp", "ctx")),
        P(("fsdp", "ctx"), "tp"),
        P(("fsdp", "ctx"), "tp"),
        P(("fsdp", "ctx"), "tp"),
        P(("fsdp", "ctx"), "tp"),
        P(("fsdp", "ctx")),
        P(("fsdp", "ctx"), "tp"),
        P(("fsdp", "ctx"), "tp"),
        P(("fsdp", "ctx"), "tp"),
    )
    return jax.shard_map(
        local,
        mesh=mesh,
        in_specs=placed,
        out_specs=(
            P("fsdp", "ctx", None),
            P("fsdp", "ctx", None),
            P(("fsdp", "ctx")),
            P(("fsdp", "ctx"), "tp"),
            P(("fsdp", "ctx"), "tp"),
            P(("fsdp", "ctx"), "tp"),
            P(("fsdp", "ctx"), "tp"),
            P(("fsdp", "ctx")),
            P(("fsdp", "ctx"), "tp"),
            P(("fsdp", "ctx"), "tp"),
            P(("fsdp", "ctx"), "tp"),
        ),
        check_vma=False,
    )
```

```python
from functools import partial

import jax
import jax.numpy as jnp
from jax import lax
from jax.experimental import pallas as pl
from jax.experimental.pallas import tpu as pltpu
from jax.sharding import PartitionSpec as P

HD = 64


norm_eps = 1e-05
residual_scale = 0.22
score_scale = 1.0 / 64.0
rope_base = 10000000.0
masked_score = -1e30


def rope_tables(positions, head_dim):
    half_dim = head_dim // 2
    frequency = rope_base ** (-(jnp.arange(half_dim, dtype=jnp.float32) * 2.0) / head_dim)
    angles = positions.astype(jnp.float32)[:, None] * frequency[None, :]
    return (
        jnp.concatenate([jnp.cos(angles), jnp.cos(angles)], -1),
        jnp.concatenate([jnp.sin(angles), jnp.sin(angles)], -1),
    )


def rotate(values_in, cosines, sines):
    half_dim = values_in.shape[-1] // 2
    turned = jnp.concatenate([-values_in[..., half_dim:], values_in[..., :half_dim]], -1)
    return values_in * cosines + turned * sines


def unrotate(grad_in, cosines, sines):
    half_dim = grad_in.shape[-1] // 2
    scaled = grad_in * sines
    return grad_in * cosines + jnp.concatenate(
        [scaled[..., half_dim:], -scaled[..., :half_dim]], -1
    )


def rms_scale(values_in):
    return lax.rsqrt(jnp.mean(values_in * values_in, -1, keepdims=True) + norm_eps)


def norm_back(grad_normed, values_in, scale, gain):
    scaled_grad = grad_normed * gain
    return scale * scaled_grad - values_in * scale**3 * jnp.mean(
        scaled_grad * values_in, -1, keepdims=True
    )


def masked_scores(grouped_query_rows, key_row_block, key_mask):
    scores = (
        jnp.einsum(
            "sqgd,skd->sgqk", grouped_query_rows, key_row_block, preferred_element_type=jnp.float32
        )
        * score_scale
    )
    return jnp.where(key_mask[:, None], scores, masked_score)


def attend_forward(block_item, key_mask):
    grouped_query_rows, key_row_block, value_row_block = block_item
    scores = masked_scores(grouped_query_rows, key_row_block, key_mask)
    top_score = jnp.max(scores, -1, keepdims=True)
    exp_scores = jnp.exp(scores - top_score)
    total_mass = jnp.sum(exp_scores, -1, keepdims=True)
    probs_low = (exp_scores / total_mass).astype(jnp.bfloat16)
    head_output = jnp.einsum(
        "sgqk,skd->sqgd", probs_low, value_row_block, preferred_element_type=jnp.float32
    )
    return (head_output.astype(jnp.bfloat16), top_score + jnp.log(total_mass))


def attend_backward(block_item, key_mask):
    grouped_query_rows, key_row_block, value_row_block, out_grad, log_mass = block_item
    scores = masked_scores(grouped_query_rows, key_row_block, key_mask)
    attention_probabilities = jnp.exp(scores - log_mass)
    probs_low = attention_probabilities.astype(jnp.bfloat16)
    value_grad = jnp.einsum(
        "sgqk,sqgd->skd", probs_low, out_grad, preferred_element_type=jnp.float32
    )
    probs_grad = jnp.einsum(
        "sqgd,skd->sgqk", out_grad, value_row_block, preferred_element_type=jnp.float32
    )
    score_grad = (
        attention_probabilities
        * (probs_grad - jnp.sum(attention_probabilities * probs_grad, -1, keepdims=True))
    ).astype(jnp.bfloat16)
    query_grad = (
        jnp.einsum("sgqk,skd->sqgd", score_grad, key_row_block, preferred_element_type=jnp.float32)
        * score_scale
    )
    key_grad = (
        jnp.einsum(
            "sgqk,sqgd->skd", score_grad, grouped_query_rows, preferred_element_type=jnp.float32
        )
        * score_scale
    )
    return (query_grad, key_grad, value_grad)


MESH_ID = pl.DeviceIdType.MESH


def low_bit(k):
    return k & -k


def high_bit(k):
    return 1 << (k.bit_length() - 1)


def fsdp_order(fsdp):
    return sorted(range(1, fsdp), key=lambda k: (bin(k).count("1"), k))


def flip_index(me, k, fsdp):
    out = me
    for i in range(fsdp.bit_length() - 1):
        b = 1 << i
        if k & b:
            out = out + b - 2 * b * lax.rem(me // b, 2)
    return out


def line_neighbours(me, count):
    return (me > 0).astype(jnp.int32) + (me < count - 1).astype(jnp.int32)


def line_kernel(fsdp, ctx, group, lines, swaps, spots, *refs):
    line_in = refs[:lines]
    swap_in = refs[lines : lines + swaps]
    line_out = refs[lines + swaps : 2 * lines + swaps]
    swap_out = refs[2 * lines + swaps : -5]
    own_sem, z_send, z_recv, f_send, f_recv = refs[-5:]
    me_f = lax.axis_index("fsdp")
    me_c = lax.axis_index("ctx")
    me_t = lax.axis_index("tp")

    def along(step, act):
        there = me_c + step

        @pl.when((there >= 0) & (there < ctx))
        def _():
            act(there)

    barrier = pltpu.get_barrier_semaphore()
    for k in range(1, group):
        pl.semaphore_signal(
            barrier, inc=1, device_id=(flip_index(me_f, k, fsdp), me_c, me_t), device_id_type=MESH_ID
        )
    for step in (-1, 1):
        along(
            step,
            lambda there: pl.semaphore_signal(
                barrier, inc=1, device_id=(me_f, there, me_t), device_id_type=MESH_ID
            ),
        )
    pl.semaphore_wait(barrier, group - 1 + line_neighbours(me_c, ctx))

    def z_copy(i, shard, step, src=None):
        place = line_out[i].at[shard]
        way = 0 if step > 0 else 1
        return pltpu.make_async_remote_copy(
            src_ref=place if src is None else src,
            dst_ref=place,
            send_sem=z_send.at[i, way, shard],
            recv_sem=z_recv.at[i, way, shard],
            device_id=(me_f, me_c + step, me_t),
            device_id_type=MESH_ID,
        )

    def landing(i, f):
        out, start = spots[i]
        width = swap_in[i].shape[1] // group
        return swap_out[out].at[lax.rem(f, group), :, pl.ds(start, width)]

    def columns(i, f):
        width = swap_in[i].shape[1] // group
        return swap_in[i].at[:, pl.ds(pl.multiple_of(lax.rem(f, group) * width, 128), width)]

    def f_copy(i, k):
        there = flip_index(me_f, k, fsdp)
        return pltpu.make_async_remote_copy(
            src_ref=columns(i, there),
            dst_ref=landing(i, me_f),
            send_sem=f_send.at[i, k],
            recv_sem=f_recv.at[i, k],
            device_id=(there, me_c, me_t),
            device_id_type=MESH_ID,
        )

    def f_arrival(i, k):
        there = flip_index(me_f, k, fsdp)
        return pltpu.make_async_remote_copy(
            src_ref=landing(i, there),
            dst_ref=landing(i, there),
            send_sem=f_send.at[i, k],
            recv_sem=f_recv.at[i, k],
            device_id=(there, me_c, me_t),
            device_id_type=MESH_ID,
        )

    for i in range(lines):
        for step in (1, -1):
            along(step, lambda there: z_copy(i, me_c, step, line_in[i]).start())
    order = fsdp_order(group)
    for i in range(swaps):
        for k in order:
            f_copy(i, k).start()
    own = [
        pltpu.make_async_copy(line_in[i], line_out[i].at[me_c], own_sem.at[i])
        for i in range(lines)
    ] + [
        pltpu.make_async_copy(columns(i, me_f), landing(i, me_f), own_sem.at[lines + i])
        for i in range(swaps)
    ]
    for copy in own:
        copy.start()
    for i in range(lines):
        for distance in range(1, ctx):
            for step in (1, -1):
                shard = me_c - step * distance

                @pl.when((shard >= 0) & (shard < ctx))
                def _():
                    z_copy(i, shard, step).wait_recv()
                    along(step, lambda there: z_copy(i, shard, step).start())

    for i in range(swaps):
        for k in order:
            f_arrival(i, k).wait_recv()
            f_copy(i, k).wait_send()
    for copy in own:
        copy.wait()
    for i in range(lines):
        for step in (1, -1):
            along(step, lambda there: z_copy(i, me_c, step, line_in[i]).wait_send())
            for distance in range(1, ctx - 1):
                shard = me_c - step * distance

                @pl.when((shard >= 0) & (shard < ctx))
                def _():
                    along(step, lambda there: z_copy(i, shard, step).wait_send())


def start_exchange(fsdp, ctx, group, lines, swap_sets):
    sems = pltpu.SemaphoreType.DMA
    out_shape = [jax.ShapeDtypeStruct((ctx,) + v.shape, v.dtype) for v in lines]
    swaps, spots = [], []
    for out, arrays in enumerate(swap_sets):
        start = 0
        for v in arrays:
            spots.append((out, start))
            swaps.append(v)
            start += v.shape[1] // group
        out_shape.append(
            jax.ShapeDtypeStruct((group, arrays[0].shape[0], start), arrays[0].dtype)
        )
    count = len(lines) + len(swaps)
    outs = pl.pallas_call(
        partial(line_kernel, fsdp, ctx, group, len(lines), len(swaps), spots),
        out_shape=out_shape,
        in_specs=[pl.BlockSpec(memory_space=pl.ANY)] * count,
        out_specs=[pl.BlockSpec(memory_space=pl.ANY)] * len(out_shape),
        scratch_shapes=[
            sems((count,)),
            sems((len(lines), 2, ctx)),
            sems((len(lines), 2, ctx)),
            sems((len(swaps), group)),
            sems((len(swaps), group)),
        ],
        compiler_params=pltpu.CompilerParams(collective_id=0, has_side_effects=True),
    )(*lines, *swaps)
    return outs[: len(lines)], outs[len(lines) :]


def spread_kernel(fsdp, ctx, count, *refs):
    ins = refs[:count]
    outs = refs[count : 2 * count]
    own_sem, f_send, f_recv = refs[2 * count :]
    me_f = lax.axis_index("fsdp")
    me_c = lax.axis_index("ctx")
    me_t = lax.axis_index("tp")
    bits = [1 << i for i in range(fsdp.bit_length() - 1)]
    order = fsdp_order(fsdp)

    def peer(k):
        return (flip_index(me_f, k, fsdp), me_c, me_t)

    barrier = pltpu.get_barrier_semaphore()
    for b in bits:
        pl.semaphore_signal(barrier, inc=1, device_id=peer(b), device_id_type=MESH_ID)
    pl.semaphore_wait(barrier, len(bits))

    def place(i, shard, have, k, part):
        block = outs[i].at[flip_index(me_f, have, fsdp), shard]
        half = ins[i].shape[1] // 2
        return block if k == low_bit(k) else block.at[pl.ds(part * half, half)]

    def f_copy(i, shard, have, b):
        k = have | b
        part = 1 if have and b == high_bit(k) else 0
        block = place(i, shard, have, k, part)
        return pltpu.make_async_remote_copy(
            src_ref=block if have else ins[i].at[shard],
            dst_ref=block,
            send_sem=f_send.at[i, shard, k, part],
            recv_sem=f_recv.at[i, shard, k, part],
            device_id=peer(b),
            device_id_type=MESH_ID,
        )

    def ways(have):
        return [
            b
            for b in bits
            if not have & b and (not have or b in (low_bit(have | b), high_bit(have | b)))
        ]

    own = [
        pltpu.make_async_copy(ins[i], outs[i].at[me_f], own_sem.at[i]) for i in range(count)
    ]
    for i in range(count):
        for shard in range(ctx):
            for b in ways(0):
                f_copy(i, shard, 0, b).start()
        own[i].start()
    for i in range(count):
        for k in order:
            parts = [(0, k)] if k == low_bit(k) else [(0, low_bit(k)), (1, high_bit(k))]
            for shard in range(ctx):
                for part, b in parts:
                    block = place(i, shard, k, k, part)
                    pltpu.make_async_remote_copy(
                        src_ref=block,
                        dst_ref=block,
                        send_sem=f_send.at[i, shard, k, part],
                        recv_sem=f_recv.at[i, shard, k, part],
                        device_id=peer(b),
                        device_id_type=MESH_ID,
                    ).wait_recv()
                for b in ways(k):
                    f_copy(i, shard, k, b).start()
    for i in range(count):
        own[i].wait()
        for have in [0] + order:
            for shard in range(ctx):
                for b in ways(have):
                    f_copy(i, shard, have, b).wait_send()


def spread_weights(fsdp, ctx, arrays):
    count = len(arrays)
    sems = pltpu.SemaphoreType.DMA
    outs = pl.pallas_call(
        partial(spread_kernel, fsdp, ctx, count),
        out_shape=[jax.ShapeDtypeStruct((fsdp,) + v.shape, v.dtype) for v in arrays],
        in_specs=[pl.BlockSpec(memory_space=pl.ANY)] * count,
        out_specs=[pl.BlockSpec(memory_space=pl.ANY)] * count,
        scratch_shapes=[
            sems((count,)),
            sems((count, ctx, fsdp, 2)),
            sems((count, ctx, fsdp, 2)),
        ],
        compiler_params=pltpu.CompilerParams(collective_id=1, has_side_effects=True),
    )(*arrays)
    return [o.reshape(-1, v.shape[-1]) for o, v in zip(outs, arrays)]


def sum_kernel(fsdp, ctx, count, *refs):
    ins = refs[:count]
    outs = refs[count : 2 * count]
    held = refs[2 * count : 3 * count]
    got = refs[3 * count : 4 * count]
    line = refs[4 * count : 5 * count]
    in_sem, f_send, f_recv, z_send, z_recv = refs[5 * count :]
    me_f = lax.axis_index("fsdp")
    me_c = lax.axis_index("ctx")
    me_t = lax.axis_index("tp")
    bits = [1 << i for i in range(fsdp.bit_length() - 1)]
    order = fsdp_order(fsdp)

    def peer(k):
        return (flip_index(me_f, k, fsdp), me_c, me_t)

    def along(step, act):
        there = me_c + step

        @pl.when((there >= 0) & (there < ctx))
        def _():
            act(there)

    loads = {}
    for i in range(count):
        for k in reversed([0] + order):
            loads[i, k] = pltpu.make_async_copy(
                ins[i].at[flip_index(me_f, k, fsdp)], held[i].at[k], in_sem.at[i, k]
            )
            loads[i, k].start()

    barrier = pltpu.get_barrier_semaphore()
    for b in bits:
        pl.semaphore_signal(barrier, inc=1, device_id=peer(b), device_id_type=MESH_ID)
    for step in (-1, 1):
        along(
            step,
            lambda there: pl.semaphore_signal(
                barrier, inc=1, device_id=(me_f, there, me_t), device_id_type=MESH_ID
            ),
        )
    pl.semaphore_wait(barrier, len(bits) + line_neighbours(me_c, ctx))

    def ways(k):
        return [(0, k)] if k == low_bit(k) else [(0, low_bit(k)), (1, high_bit(k))]

    def piece(i, k, part):
        rows = ins[i].shape[2]
        return pl.ds(0, rows) if k == low_bit(k) else pl.ds(part * (rows // 2), rows // 2)

    def f_copy(i, shard, k, part, b):
        span = piece(i, k, part)
        return pltpu.make_async_remote_copy(
            src_ref=held[i].at[k, shard, span],
            dst_ref=got[i].at[k, shard, span],
            send_sem=f_send.at[i, shard, k, part],
            recv_sem=f_recv.at[i, shard, k, part],
            device_id=peer(b),
            device_id_type=MESH_ID,
        )

    def add(into, other):
        rows = into.shape[0]

        def body(r, _):
            span = pl.ds(pl.multiple_of(r * 16, 16), 16)
            into[span] = (
                into[span].astype(jnp.float32) + other[span].astype(jnp.float32)
            ).astype(into.dtype)
            return 0

        lax.fori_loop(0, rows // 16, body, 0)

    def collect(i, shard, k):
        for far in order:
            for part, b in ways(far):
                if far ^ b == k:
                    f_copy(i, shard, far, part, b).wait_recv()
                    span = piece(i, far, part)
                    add(held[i].at[k, shard, span], got[i].at[far, shard, span])

    def z_copy(i, shard, step):
        way = 0 if step > 0 else 1
        return pltpu.make_async_remote_copy(
            src_ref=held[i].at[0, shard],
            dst_ref=line[i].at[way, shard],
            send_sem=z_send.at[i, way, shard],
            recv_sem=z_recv.at[i, way, shard],
            device_id=(me_f, me_c + step, me_t),
            device_id_type=MESH_ID,
        )

    def on_line(i, shard):
        for step in (1, -1):
            way = 0 if step > 0 else 1

            @pl.when((step * (shard - me_c) >= 0) & (me_c - step >= 0) & (me_c - step < ctx))
            def _():
                z_copy(i, shard, step).wait_recv()
                add(held[i].at[0, shard], line[i].at[way, shard])

            @pl.when(step * (shard - me_c) > 0)
            def _():
                z_copy(i, shard, step).start()

        @pl.when(shard == me_c)
        def _():
            rows = outs[i].shape[0]

            def body(r, _):
                span = pl.ds(pl.multiple_of(r * 16, 16), 16)
                outs[i][span] = held[i][0, shard, span].astype(outs[i].dtype)
                return 0

            lax.fori_loop(0, rows // 16, body, 0)

    shards = sorted(range(ctx), key=lambda c: -abs(2 * c - ctx + 1))
    work = [(i, shard) for i in range(count) for shard in shards]
    levels = sorted({bin(k).count("1") for k in order}, reverse=True)
    for level in levels:
        ks = [k for k in order if bin(k).count("1") == level]
        for i in range(count):
            for k in ks:
                loads[i, k].wait()
            for shard in shards:
                for k in ks:
                    collect(i, shard, k)
                    for part, b in ways(k):
                        f_copy(i, shard, k, part, b).start()
    for i in range(count):
        loads[i, 0].wait()
    late = None
    for item in work + [None]:
        if item is not None:
            collect(item[0], item[1], 0)
        if late is not None:
            on_line(*late)
        late = item
    for i, shard in work:
        for k in order:
            for part, b in ways(k):
                f_copy(i, shard, k, part, b).wait_send()
        for step in (1, -1):

            @pl.when(step * (shard - me_c) > 0)
            def _():
                z_copy(i, shard, step).wait_send()


def sum_weights(fsdp, ctx, arrays):
    count = len(arrays)
    sems = pltpu.SemaphoreType.DMA
    shards = [v.reshape(fsdp, ctx, -1, v.shape[-1]) for v in arrays]
    vmem = pltpu.VMEM
    return pl.pallas_call(
        partial(sum_kernel, fsdp, ctx, count),
        out_shape=[jax.ShapeDtypeStruct(v.shape[2:], jnp.float32) for v in shards],
        in_specs=[pl.BlockSpec(memory_space=pl.ANY)] * count,
        out_specs=[pl.BlockSpec(memory_space=pltpu.VMEM)] * count,
        scratch_shapes=[vmem(v.shape, v.dtype) for v in shards]
        + [vmem(v.shape, v.dtype) for v in shards]
        + [vmem((2,) + v.shape[1:], v.dtype) for v in shards]
        + [
            sems((count, fsdp)),
            sems((count, ctx, fsdp, 2)),
            sems((count, ctx, fsdp, 2)),
            sems((count, 2, ctx)),
            sems((count, 2, ctx)),
        ],
        compiler_params=pltpu.CompilerParams(
            collective_id=2, has_side_effects=True, vmem_limit_bytes=50 * 1024 * 1024
        ),
    )(*shards)


def local(
    inputs,
    lengths,
    cotangent,
    norm1_gain,
    w_query,
    w_key,
    w_value,
    w_out,
    norm2_gain,
    w_gate,
    w_up,
    w_down,
):
    seq_count, local_rows, model_width = inputs.shape
    tokens = seq_count * local_rows
    half = tokens // 2
    fsdp = lax.axis_size("fsdp")
    ctx = lax.axis_size("ctx")
    shard = w_query.shape[0]
    query_width = w_query.shape[1]
    kv_width = w_key.shape[1]
    kv_end = query_width + 2 * kv_width
    group = min(fsdp, 4)
    far = fsdp // group
    units = w_gate.shape[1] // group
    me_f = lax.axis_index("fsdp")
    me_c = lax.axis_index("ctx")
    me_t = lax.axis_index("tp")
    order = fsdp_order(group)
    low = jnp.bfloat16
    wide = jnp.float32

    def hop(v, k):
        return lax.ppermute(v, "fsdp", [(i, i ^ k) for i in range(fsdp)])

    def swap(v):
        return lax.ppermute(v, "tp", [(0, 1), (1, 0)])

    def up_line(v):
        return lax.ppermute(v, "ctx", [(i, i + 1) for i in range(ctx - 1)])

    def down_line(v):
        return lax.ppermute(v, "ctx", [(i + 1, i) for i in range(ctx - 1)])

    def pair_sum(part):
        part = part.astype(low)
        return part.astype(wide) + swap(part).astype(wide)

    def by_ctx(v):
        rest = v.shape[:-1]
        return v.reshape(*rest, fsdp, ctx, shard).swapaxes(-3, -2).reshape(*rest, model_width)

    def by_fsdp(v):
        rest = v.shape[:-1]
        return v.reshape(*rest, ctx, fsdp, shard).swapaxes(-3, -2).reshape(*rest, model_width)

    def gather_tokens(v):
        mine = lax.dynamic_slice_in_dim(v, me_t * half, half)
        other = lax.dynamic_slice_in_dim(v, (1 - me_t) * half, half)
        got = {0: mine}
        for k in order:
            lo, hi = low_bit(k), high_bit(k)
            if lo == hi:
                got[k] = hop(mine, k)
            else:
                cut = half // 2
                got[k] = jnp.concatenate(
                    [hop(got[k ^ lo][:cut], lo), hop(got[k ^ hi][cut:], hi)]
                )
        return [(mine, other)] + [(got[k], swap(got[k])) for k in range(1, group)]

    def scatter_tokens(blocks):
        total = {}
        for k in reversed([0] + order):
            mine, other = blocks[k]
            total[k] = mine.astype(wide) + swap(other.astype(low)).astype(wide)
        for k in reversed(order):
            lo, hi = low_bit(k), high_bit(k)
            sent = total[k].astype(low)
            if lo == hi:
                total[0] = total[0] + hop(sent, k).astype(wide)
            else:
                cut = half // 2
                for there, first, b in ((k ^ lo, True, lo), (k ^ hi, False, hi)):
                    piece = hop(sent[:cut] if first else sent[cut:], b).astype(wide)
                    base = total[there]
                    total[there] = jnp.concatenate(
                        [base[:cut] + piece, base[cut:]]
                        if first
                        else [base[:cut], base[cut:] + piece]
                    )
        own = total[0].astype(low)
        other = swap(own)
        return jnp.where(
            me_t == 0, jnp.concatenate([own, other]), jnp.concatenate([other, own])
        ).astype(wide)

    positions = me_c * local_rows + jnp.arange(local_rows, dtype=jnp.int32)
    key_places = (
        (me_c - jnp.arange(ctx, dtype=jnp.int32))[:, None] * local_rows
        + jnp.arange(local_rows, dtype=jnp.int32)[None, :]
    ).reshape(-1)
    valid_rows = (positions[None, :] < lengths[:, None]).astype(wide)[..., None]
    key_mask = (
        (key_places[None, None, :] <= positions[None, :, None])
        & (key_places[None, None, :] < lengths[:, None, None])
        & (key_places >= 0)[None, None, :]
    )
    cosines, sines = rope_tables(positions, HD)
    head_cos = cosines[None, :, None, :]
    head_sin = sines[None, :, None, :]

    gains = jnp.pad(jnp.stack([norm1_gain, norm2_gain], 1), ((0, 0), (0, 126)))
    lined, held = start_exchange(
        fsdp,
        ctx,
        group,
        [jnp.concatenate([w_query, w_key, w_value, gains], 1), w_out],
        [[w_gate, w_up], [w_down]],
    )
    far_groups = [[h * group + g for h in range(far)] for g in range(group)]
    near_groups = [[h * group + g for g in range(group)] for h in range(far)]

    def whole_width(v):
        if far > 1:
            v = lax.all_gather(v, "fsdp", axis=0, tiled=False, axis_index_groups=far_groups)
        return lax.all_gather(v, "ctx", axis=0, tiled=False).reshape(model_width, -1)

    both_full, down_full = [whole_width(v) for v in held]
    qkv_full, out_full = spread_weights(fsdp, ctx, lined)
    gain_one = qkv_full[:, kv_end].astype(wide)
    gain_two = qkv_full[:, kv_end + 1].astype(wide)

    back = cotangent.astype(wide) * valid_rows
    ff_grad = by_ctx((residual_scale * back).astype(low).reshape(tokens, model_width))
    ff_grad_blocks = gather_tokens(ff_grad)

    query_heads = query_width // HD
    kv_heads = kv_width // HD
    group_size = query_heads // kv_heads
    layer_in = inputs.astype(wide)
    first_rms = rms_scale(layer_in)
    first_normed = (layer_in * first_rms * gain_one).astype(low)
    qkv_lin = jnp.dot(
        first_normed.reshape(tokens, model_width),
        qkv_full[:, :kv_end],
        preferred_element_type=wide,
    ).reshape(seq_count, local_rows, kv_end)
    query_rot = rotate(
        qkv_lin[..., :query_width].reshape(seq_count, local_rows, query_heads, HD),
        head_cos,
        head_sin,
    ).astype(low)
    key_rot = (
        rotate(
            qkv_lin[..., query_width : query_width + kv_width].reshape(
                seq_count, local_rows, kv_heads, HD
            ),
            head_cos,
            head_sin,
        )
        .astype(low)
        .reshape(seq_count, local_rows, kv_width)
    )
    value_low = qkv_lin[..., query_width + kv_width :].astype(low)
    kv_blocks = [jnp.concatenate([key_rot, value_low], -1)]
    for _ in range(ctx - 1):
        kv_blocks.append(up_line(kv_blocks[-1]))
    kv_all = jnp.concatenate(kv_blocks, 1)
    full_rows = kv_all.shape[1]
    key_split = jnp.moveaxis(
        kv_all[..., :kv_width].reshape(seq_count, full_rows, kv_heads, HD), 2, 0
    )
    value_split = jnp.moveaxis(
        kv_all[..., kv_width:].reshape(seq_count, full_rows, kv_heads, HD), 2, 0
    )
    query_split = jnp.moveaxis(
        query_rot.reshape(seq_count, local_rows, kv_heads, group_size, HD), 2, 0
    )
    head_output, log_mass = lax.map(
        partial(attend_forward, key_mask=key_mask), (query_split, key_split, value_split)
    )
    attended = jnp.moveaxis(head_output, 0, 2).reshape(tokens, query_width)
    attn_part = jnp.einsum("tj,dj->td", attended, out_full, preferred_element_type=wide)
    attn_branch = pair_sum(attn_part)
    middle = layer_in + residual_scale * attn_branch.reshape(layer_in.shape)

    second_rms = rms_scale(middle)
    second_normed = (middle * second_rms * gain_two).astype(low)
    normed_blocks = gather_tokens(by_ctx(second_normed.reshape(tokens, model_width)))
    normed_all = jnp.concatenate([jnp.concatenate(b) for b in normed_blocks])
    ff_grad_all = jnp.concatenate([jnp.concatenate(b) for b in ff_grad_blocks])

    both_lin = jnp.dot(normed_all, both_full, preferred_element_type=wide)
    gate_lin = both_lin[:, :units]
    up_lin = both_lin[:, units:]
    gate_sig = jax.nn.sigmoid(gate_lin)
    gate_act = gate_lin * gate_sig
    hidden = (gate_act * up_lin).astype(low)
    hidden_grad = jnp.dot(ff_grad_all, down_full, preferred_element_type=wide)
    gate_grad = (hidden_grad * up_lin * gate_sig * (1.0 + gate_lin * (1.0 - gate_sig))).astype(low)
    up_grad = (hidden_grad * gate_act).astype(low)

    def sum_blocks(left, right):
        blocks = [None] * group
        for k in reversed([0] + order):
            rows = slice(k * tokens, (k + 1) * tokens)
            part = jnp.einsum(
                "tf,df->td", left[rows], right, preferred_element_type=wide
            ).astype(low)
            blocks[k] = (part[:half], part[half:])
        return by_fsdp(scatter_tokens(blocks)).reshape(layer_in.shape)

    def unit_term(left, right):
        return jnp.einsum("td,tf->df", left, right, preferred_element_type=wide).astype(low)

    def return_units(term):
        own = lax.psum_scatter(
            term.reshape(ctx, fsdp, shard, units), "ctx", scatter_dimension=0, tiled=False
        )
        if far > 1:
            own = lax.psum_scatter(
                own.reshape(far, group, shard, units),
                "fsdp",
                scatter_dimension=0,
                tiled=False,
                axis_index_groups=far_groups,
            )
        return lax.all_to_all(
            own.reshape(group * shard, units),
            "fsdp",
            0,
            1,
            tiled=True,
            axis_index_groups=near_groups if far > 1 else None,
        ).astype(wide)

    second_grad = sum_blocks(jnp.concatenate([gate_grad, up_grad], 1), both_full)
    ff_branch = sum_blocks(hidden, down_full)
    down_term = unit_term(ff_grad_all, hidden)
    gate_term = unit_term(normed_all, gate_grad)
    up_term = unit_term(normed_all, up_grad)
    second_grad, ff_branch, _, _, _ = lax.optimization_barrier(
        (second_grad, ff_branch, down_term, gate_term, up_term)
    )
    w_down_grad = return_units(down_term)
    w_gate_grad = return_units(gate_term)
    w_up_grad = return_units(up_term)
    output = (valid_rows * (middle + residual_scale * ff_branch)).astype(low)

    gain_two_term = jnp.sum(second_grad * middle * second_rms, axis=(0, 1))
    middle_grad = back + norm_back(second_grad, middle, second_rms, gain_two)

    attn_grad = (residual_scale * middle_grad).astype(low).reshape(tokens, model_width)
    out_term = jnp.einsum("td,tj->dj", attn_grad, attended, preferred_element_type=wide)
    attended_grad = jnp.dot(attn_grad, out_full, preferred_element_type=wide).astype(low)
    grad_split = jnp.moveaxis(
        attended_grad.reshape(seq_count, local_rows, kv_heads, group_size, HD), 2, 0
    )
    query_back, key_back, value_back = lax.map(
        partial(attend_backward, key_mask=key_mask),
        (query_split, key_split, value_split, grad_split, log_mass),
    )
    query_back = jnp.moveaxis(query_back, 0, 2).reshape(seq_count, local_rows, query_heads, HD)
    query_grad = (
        unrotate(query_back, head_cos, head_sin).astype(low).reshape(tokens, query_width)
    )
    key_spread = jnp.moveaxis(key_back, 0, 2).reshape(seq_count, full_rows, kv_width)
    value_spread = jnp.moveaxis(value_back, 0, 2).reshape(seq_count, full_rows, kv_width)
    kv_spread = jnp.concatenate([key_spread, value_spread], -1).reshape(
        seq_count, ctx, local_rows, 2 * kv_width
    )
    kv_own = kv_spread[:, ctx - 1]
    for s in reversed(range(ctx - 1)):
        kv_own = kv_spread[:, s] + down_line(kv_own.astype(low)).astype(wide)
    key_grad = (
        unrotate(
            kv_own[..., :kv_width].reshape(seq_count, local_rows, kv_heads, HD), head_cos, head_sin
        )
        .astype(low)
        .reshape(tokens, kv_width)
    )
    value_grad = kv_own[..., kv_width:].astype(low).reshape(tokens, kv_width)
    qkv_grad = jnp.concatenate([query_grad, key_grad, value_grad], -1)
    qkv_term = jnp.einsum(
        "td,tj->dj",
        first_normed.reshape(tokens, model_width),
        qkv_grad,
        preferred_element_type=wide,
    )
    first_part = jnp.einsum(
        "tj,dj->td", qkv_grad, qkv_full[:, :kv_end], preferred_element_type=wide
    )
    first_grad = pair_sum(first_part).reshape(layer_in.shape)
    gain_one_term = jnp.sum(first_grad * layer_in * first_rms, axis=(0, 1))
    input_grad = (middle_grad + norm_back(first_grad, layer_in, first_rms, gain_one)).astype(low)
    gain_terms = jnp.pad(jnp.stack([gain_one_term, gain_two_term], 1), ((0, 0), (0, 126)))
    qkv_term = jnp.concatenate([qkv_term, gain_terms], 1).astype(low)
    qkv_term, w_down_grad, w_gate_grad, w_up_grad = lax.optimization_barrier(
        (qkv_term, w_down_grad, w_gate_grad, w_up_grad)
    )
    w_out_grad, qkv_own = sum_weights(fsdp, ctx, [out_term.astype(low), qkv_term])
    return (
        output,
        input_grad,
        qkv_own[:, kv_end],
        qkv_own[:, :query_width],
        qkv_own[:, query_width : query_width + kv_width],
        qkv_own[:, query_width + kv_width : kv_end],
        w_out_grad,
        qkv_own[:, kv_end + 1],
        w_gate_grad,
        w_up_grad,
        w_down_grad,
    )


def solution(mesh):
    placed = (
        P("fsdp", "ctx", None),
        P("fsdp"),
        P("fsdp", "ctx", None),
        P(("fsdp", "ctx")),
        P(("fsdp", "ctx"), "tp"),
        P(("fsdp", "ctx"), "tp"),
        P(("fsdp", "ctx"), "tp"),
        P(("fsdp", "ctx"), "tp"),
        P(("fsdp", "ctx")),
        P(("fsdp", "ctx"), "tp"),
        P(("fsdp", "ctx"), "tp"),
        P(("fsdp", "ctx"), "tp"),
    )
    return jax.shard_map(
        local,
        mesh=mesh,
        in_specs=placed,
        out_specs=(
            P("fsdp", "ctx", None),
            P("fsdp", "ctx", None),
            P(("fsdp", "ctx")),
            P(("fsdp", "ctx"), "tp"),
            P(("fsdp", "ctx"), "tp"),
            P(("fsdp", "ctx"), "tp"),
            P(("fsdp", "ctx"), "tp"),
            P(("fsdp", "ctx")),
            P(("fsdp", "ctx"), "tp"),
            P(("fsdp", "ctx"), "tp"),
            P(("fsdp", "ctx"), "tp"),
        ),
        check_vma=False,
    )
```

```python
from functools import partial

import jax
import jax.numpy as jnp
from jax import lax
from jax.experimental import pallas as pl
from jax.experimental.pallas import tpu as pltpu
from jax.sharding import PartitionSpec as P

HD = 64


norm_eps = 1e-05
residual_scale = 0.22
score_scale = 1.0 / 64.0
rope_base = 10000000.0
masked_score = -1e30


def rope_tables(positions, head_dim):
    half_dim = head_dim // 2
    frequency = rope_base ** (-(jnp.arange(half_dim, dtype=jnp.float32) * 2.0) / head_dim)
    angles = positions.astype(jnp.float32)[:, None] * frequency[None, :]
    return (
        jnp.concatenate([jnp.cos(angles), jnp.cos(angles)], -1),
        jnp.concatenate([jnp.sin(angles), jnp.sin(angles)], -1),
    )


def rotate(values_in, cosines, sines):
    half_dim = values_in.shape[-1] // 2
    turned = jnp.concatenate([-values_in[..., half_dim:], values_in[..., :half_dim]], -1)
    return values_in * cosines + turned * sines


def unrotate(grad_in, cosines, sines):
    half_dim = grad_in.shape[-1] // 2
    scaled = grad_in * sines
    return grad_in * cosines + jnp.concatenate(
        [scaled[..., half_dim:], -scaled[..., :half_dim]], -1
    )


def rms_scale(values_in):
    return lax.rsqrt(jnp.mean(values_in * values_in, -1, keepdims=True) + norm_eps)


def norm_back(grad_normed, values_in, scale, gain):
    scaled_grad = grad_normed * gain
    return scale * scaled_grad - values_in * scale**3 * jnp.mean(
        scaled_grad * values_in, -1, keepdims=True
    )


MESH_ID = pl.DeviceIdType.MESH
NT = (((1,), (1,)), ((), ()))
TN = (((0,), (0,)), ((), ()))
SMEM = pltpu.SMEM


def mul(left, right, dims=(((1,), (0,)), ((), ()))):
    return lax.dot_general(left, right, dims, preferred_element_type=jnp.float32)


def reorder(v, first, second, width):
    if width % 128:
        return v
    pieces = []
    for b in range(second):
        for a in range(first):
            start = (a * second + b) * width
            pieces.append(v[:, start : start + width])
    return jnp.concatenate(pieces, 1)


def turn(t, sign):
    lane = lax.broadcasted_iota(jnp.int32, t.shape, 1)
    ahead = pltpu.roll(t, 128 - HD // 2, 1)
    behind = pltpu.roll(t, HD // 2, 1)
    return jnp.where(lax.rem(lane, HD) < HD // 2, -sign * ahead, sign * behind)


def row_valid(len_ref, rows, local_rows):
    step = pl.program_id(0)
    start = step * rows
    seq = start // local_rows
    place = (
        lax.axis_index("ctx") * local_rows
        + lax.rem(start, local_rows)
        + lax.broadcasted_iota(jnp.int32, (rows, 1), 0)
    )
    return (place < len_ref[seq]).astype(jnp.float32)


def qkv_kernel(dims, x_ref, w_ref, gain_ref, cos_ref, sin_ref, normed_ref, q_ref, kv_ref):
    x = reorder(x_ref[...].astype(jnp.float32), *dims)
    normed = (x * rms_scale(x) * gain_ref[...]).astype(jnp.bfloat16)
    normed_ref[...] = normed
    lin = mul(normed, w_ref[...])
    cosines, sines = cos_ref[...], sin_ref[...]
    width = q_ref.shape[1]
    half = kv_ref.shape[1] // 2
    for start in range(0, width + half, 128):
        t = lin[:, start : start + 128]
        t = (t * cosines + turn(t, 1.0) * sines).astype(jnp.bfloat16)
        if start < width:
            q_ref[:, start : start + 128] = t
        else:
            kv_ref[:, start - width : start - width + 128] = t
    kv_ref[:, half:] = lin[:, width + half :].astype(jnp.bfloat16)


def key_biases(len_ref, rows, ctx):
    length = len_ref[pl.program_id(0)]
    me = lax.axis_index("ctx")
    row = lax.broadcasted_iota(jnp.int32, (rows, rows), 0)
    col = lax.broadcasted_iota(jnp.int32, (rows, rows), 1)
    first = jnp.where((col <= row) & (me * rows + col < length), 0.0, masked_score)
    out = [first]
    for s in range(1, ctx):
        place = (me - s) * rows + lax.broadcasted_iota(jnp.int32, (1, rows), 1)
        out.append(jnp.where((place >= 0) & (place < length), 0.0, masked_score))
    return out


def attend_kernel(ctx, len_ref, q_ref, *refs):
    keys, values = refs[:ctx], refs[ctx : 2 * ctx]
    o_ref, lse_ref = refs[2 * ctx :]
    rows = q_ref.shape[0]
    biases = key_biases(len_ref, rows, ctx)
    lane = lax.broadcasted_iota(jnp.int32, (rows, 128), 1)
    lse_all = jnp.zeros((rows, 128), jnp.float32)
    for j in range(q_ref.shape[1] // 128):
        q_pair = q_ref[:, j * 128 : (j + 1) * 128] * jnp.bfloat16(score_scale)
        outs = []
        for g in range(2):
            mine = (lane < HD) if g == 0 else (lane >= HD)
            q_head = jnp.where(mine, q_pair, jnp.zeros_like(q_pair))
            scores = [mul(q_head, k[...], NT) + b for k, b in zip(keys, biases)]
            top = scores[0].max(-1, keepdims=True)
            for s in scores[1:]:
                top = jnp.maximum(top, s.max(-1, keepdims=True))
            mass, out = 0.0, 0.0
            for s, v in zip(scores, values):
                p = jnp.exp(s - top)
                mass = mass + p.sum(-1, keepdims=True)
                out = out + mul(p.astype(jnp.bfloat16), v[...])
            outs.append(out / mass)
            lse_all = jnp.where(lane == 2 * j + g, top + jnp.log(mass), lse_all)
        o_ref[:, j * 128 : (j + 1) * 128] = jnp.where(lane < HD, outs[0], outs[1]).astype(
            jnp.bfloat16
        )
    lse_ref[...] = lse_all


def attend_back_kernel(ctx, len_ref, q_ref, do_ref, lse_ref, cos_ref, sin_ref, *refs):
    keys, values = refs[:ctx], refs[ctx : 2 * ctx]
    dq_ref, dkv_ref, dk_sum, dv_sum = refs[2 * ctx :]
    rows = q_ref.shape[0]
    biases = key_biases(len_ref, rows, ctx)
    lane = lax.broadcasted_iota(jnp.int32, (rows, 128), 1)
    dk_sum[...] = jnp.zeros_like(dk_sum)
    dv_sum[...] = jnp.zeros_like(dv_sum)
    lse_all = lse_ref[...]
    for j in range(q_ref.shape[1] // 128):
        q_pair = q_ref[:, j * 128 : (j + 1) * 128] * jnp.bfloat16(score_scale)
        do_pair = do_ref[:, j * 128 : (j + 1) * 128]
        dqs = []
        for g in range(2):
            mine = (lane < HD) if g == 0 else (lane >= HD)
            q_head = jnp.where(mine, q_pair, jnp.zeros_like(q_pair))
            do_head = jnp.where(mine, do_pair, jnp.zeros_like(do_pair))
            h = 2 * j + g
            lse = lse_all[:, h : h + 1]
            probs, grads, total = [], [], 0.0
            for s in range(ctx):
                p = jnp.exp(mul(q_head, keys[s][...], NT) + (biases[s] - lse))
                dp = mul(do_head, values[s][...], NT)
                total = total + (p * dp).sum(-1, keepdims=True)
                probs.append(p)
                grads.append(dp)
            dq = 0.0
            for s in range(ctx):
                ds = (probs[s] * (grads[s] - total)).astype(jnp.bfloat16)
                dv_sum[s] += mul(probs[s].astype(jnp.bfloat16), do_head, TN)
                dk_sum[s] += mul(ds, q_head, TN)
                dq = dq + mul(ds, keys[s][...])
            dqs.append(dq)
        dq = jnp.where(lane < HD, dqs[0], dqs[1]) * score_scale
        dq = dq * cos_ref[...] + turn(dq * sin_ref[...], -1.0)
        dq_ref[:, j * 128 : (j + 1) * 128] = dq.astype(jnp.bfloat16)
    for s in range(ctx):
        dkv_ref[s, 0] = dk_sum[s].astype(dkv_ref.dtype)
        dkv_ref[s, 1] = dv_sum[s].astype(dkv_ref.dtype)


def cot_kernel(dims, local_rows, len_ref, cot_ref, ff_ref):
    rows = cot_ref.shape[0]
    back = cot_ref[...].astype(jnp.float32) * row_valid(len_ref, rows, local_rows)
    ff_ref[...] = reorder((residual_scale * back).astype(jnp.bfloat16), *dims)


def middle_kernel(dims, x_ref, part_ref, other_ref, gain_ref, middle_ref, normed_ref):
    branch = part_ref[...].astype(jnp.float32) + other_ref[...].astype(jnp.float32)
    middle = reorder(x_ref[...].astype(jnp.float32), *dims) + residual_scale * branch
    middle_ref[...] = middle
    normed_ref[...] = (middle * rms_scale(middle) * gain_ref[...]).astype(jnp.bfloat16)


def swiglu_kernel(n_ref, g_ref, both_ref, down_ref, hidden_ref, grads_ref, second_ref, ff_ref):
    units = hidden_ref.shape[1]
    lin = mul(n_ref[...], both_ref[...])
    gate, up = lin[:, :units], lin[:, units:]
    sig = jax.nn.sigmoid(gate)
    act = gate * sig
    hidden = (act * up).astype(jnp.bfloat16)
    hidden_ref[...] = hidden
    hidden_grad = mul(g_ref[...], down_ref[...])
    grads_ref[:, :units] = (hidden_grad * up * sig * (1.0 + gate * (1.0 - sig))).astype(
        jnp.bfloat16
    )
    grads_ref[:, units:] = (hidden_grad * act).astype(jnp.bfloat16)
    second_ref[...] = mul(grads_ref[...], both_ref[...], NT).astype(jnp.bfloat16)
    ff_ref[...] = mul(hidden, down_ref[...], NT).astype(jnp.bfloat16)


def middle_back_kernel(
    dims, local_rows, len_ref, cot_ref, middle_ref, grad_ref, gain_ref, back_ref, attn_ref, gain_sum
):
    rows = cot_ref.shape[0]
    back = cot_ref[...].astype(jnp.float32) * row_valid(len_ref, rows, local_rows)
    middle = middle_ref[...]
    grad = grad_ref[...].astype(jnp.float32)
    scale = rms_scale(middle)
    out = reorder(back, *dims) + norm_back(grad, middle, scale, gain_ref[...])
    back_ref[...] = out
    attn_ref[...] = (residual_scale * out).astype(jnp.bfloat16)

    @pl.when(pl.program_id(0) == 0)
    def _():
        gain_sum[...] = jnp.zeros_like(gain_sum)

    gain_sum[...] += (grad * middle * scale).sum(0, keepdims=True)


def output_kernel(dims, local_rows, len_ref, middle_ref, ff_ref, out_ref):
    rows = middle_ref.shape[0]
    out = middle_ref[...] + residual_scale * ff_ref[...].astype(jnp.float32)
    out = (out * row_valid(len_ref, rows, local_rows)).astype(jnp.bfloat16)
    out_ref[...] = reorder(out, *dims)


def input_back_kernel(
    dims, x_ref, part_ref, other_ref, back_ref, gain_ref, out_ref, gain_sum
):
    first, second, width = dims
    x = reorder(x_ref[...].astype(jnp.float32), *dims)
    grad = (part_ref[...].astype(jnp.float32) + other_ref[...].astype(jnp.float32))
    scale = rms_scale(x)
    out = back_ref[...] + norm_back(grad, x, scale, gain_ref[...])
    out_ref[...] = reorder(out.astype(jnp.bfloat16), second, first, width)

    @pl.when(pl.program_id(0) == 0)
    def _():
        gain_sum[...] = jnp.zeros_like(gain_sum)

    gain_sum[...] += (grad * x * scale).sum(0, keepdims=True)


def by_rows(kernel, rows, ins, outs, flops=0, limit=40):
    total = max(v.shape[0] for v, kind in ins if kind == "rows")
    in_specs = []
    moved = 0
    for v, kind in ins:
        moved += v.size * v.dtype.itemsize
        if kind == "rows":
            in_specs.append(pl.BlockSpec((rows, v.shape[1]), lambda i: (i, 0)))
        elif kind == "cycle":
            period = v.shape[0] // rows
            in_specs.append(
                pl.BlockSpec((rows, v.shape[1]), lambda i, period=period: (lax.rem(i, period), 0))
            )
        elif kind == "smem":
            in_specs.append(pl.BlockSpec(memory_space=SMEM))
        else:
            in_specs.append(
                pl.BlockSpec(v.shape, lambda i: (0, 0), pipeline_mode=pl.Buffered(1))
            )
    out_specs = []
    for shape, dtype in outs:
        moved += shape[0] * shape[1] * jnp.dtype(dtype).itemsize
        if shape[0] == 1:
            out_specs.append(pl.BlockSpec(shape, lambda i: (0, 0)))
        else:
            out_specs.append(pl.BlockSpec((rows, shape[1]), lambda i: (i, 0)))
    return pl.pallas_call(
        kernel,
        grid=(total // rows,),
        in_specs=in_specs,
        out_specs=out_specs,
        out_shape=[jax.ShapeDtypeStruct(shape, dtype) for shape, dtype in outs],
        compiler_params=pltpu.CompilerParams(vmem_limit_bytes=limit * 1024 * 1024),
        cost_estimate=pl.CostEstimate(flops=flops, bytes_accessed=moved, transcendentals=0),
    )(*[v for v, _ in ins])


def kv_specs(ctx, rows, pairs):
    def spec(slot, start):
        return pl.BlockSpec((None, rows, 128), lambda s, p: (slot, s, start + p))

    return [spec(slot, start) for start in (0, pairs) for slot in range(ctx)]


def attend(lengths, query, kv_all):
    ctx = kv_all.shape[0]
    seqs = lengths.shape[0]
    rows = query.shape[0] // seqs
    pairs = kv_all.shape[2] // 256
    wide = query.shape[1] // pairs
    flops = 4 * query.shape[0] * query.shape[1] * rows * ctx
    return pl.pallas_call(
        partial(attend_kernel, ctx),
        grid=(seqs, pairs),
        in_specs=[
            pl.BlockSpec(memory_space=SMEM),
            pl.BlockSpec((rows, wide), lambda s, p: (s, p)),
        ]
        + kv_specs(ctx, rows, pairs),
        out_specs=[
            pl.BlockSpec((rows, wide), lambda s, p: (s, p)),
            pl.BlockSpec((rows, 128), lambda s, p: (s, p)),
        ],
        out_shape=[
            jax.ShapeDtypeStruct(query.shape, jnp.bfloat16),
            jax.ShapeDtypeStruct((query.shape[0], 128 * pairs), jnp.float32),
        ],
        compiler_params=pltpu.CompilerParams(vmem_limit_bytes=40 * 1024 * 1024),
        cost_estimate=pl.CostEstimate(flops=4 * flops, bytes_accessed=6 << 20, transcendentals=0),
    )(lengths, query, *[kv_all] * (2 * ctx))


def attend_back(lengths, query, out_grad, lse, cosines, sines, kv_all):
    ctx = kv_all.shape[0]
    seqs = lengths.shape[0]
    rows = query.shape[0] // seqs
    pairs = kv_all.shape[2] // 256
    wide = query.shape[1] // pairs
    flops = 10 * query.shape[0] * query.shape[1] * rows * ctx
    return pl.pallas_call(
        partial(attend_back_kernel, ctx),
        grid=(seqs, pairs),
        in_specs=[
            pl.BlockSpec(memory_space=SMEM),
            pl.BlockSpec((rows, wide), lambda s, p: (s, p)),
            pl.BlockSpec((rows, wide), lambda s, p: (s, p)),
            pl.BlockSpec((rows, 128), lambda s, p: (s, p)),
            pl.BlockSpec((rows, 128), lambda s, p: (0, 0)),
            pl.BlockSpec((rows, 128), lambda s, p: (0, 0)),
        ]
        + kv_specs(ctx, rows, pairs),
        out_specs=[
            pl.BlockSpec((rows, wide), lambda s, p: (s, p)),
            pl.BlockSpec((ctx, 2, rows, 128), lambda s, p: (0, 0, s, p)),
        ],
        out_shape=[
            jax.ShapeDtypeStruct(query.shape, jnp.bfloat16),
            jax.ShapeDtypeStruct((ctx, 2, query.shape[0], 128 * pairs), jnp.bfloat16),
        ],
        scratch_shapes=[pltpu.VMEM((ctx, rows, 128), jnp.float32)] * 2,
        compiler_params=pltpu.CompilerParams(vmem_limit_bytes=40 * 1024 * 1024),
        cost_estimate=pl.CostEstimate(flops=4 * flops, bytes_accessed=10 << 20, transcendentals=0),
    )(lengths, query, out_grad, lse, cosines, sines, *[kv_all] * (2 * ctx))


def low_bit(k):
    return k & -k


def high_bit(k):
    return 1 << (k.bit_length() - 1)


def fsdp_order(fsdp):
    return sorted(range(1, fsdp), key=lambda k: (bin(k).count("1"), k))


def flip_index(me, k, fsdp):
    out = me
    for i in range(fsdp.bit_length() - 1):
        b = 1 << i
        if k & b:
            out = out + b - 2 * b * lax.rem(me // b, 2)
    return out


def line_neighbours(me, count):
    return (me > 0).astype(jnp.int32) + (me < count - 1).astype(jnp.int32)


def line_kernel(fsdp, ctx, group, lines, swaps, spots, *refs):
    line_in = refs[:lines]
    swap_in = refs[lines : lines + swaps]
    line_out = refs[lines + swaps : 2 * lines + swaps]
    swap_out = refs[2 * lines + swaps : -5]
    own_sem, z_send, z_recv, f_send, f_recv = refs[-5:]
    me_f = lax.axis_index("fsdp")
    me_c = lax.axis_index("ctx")
    me_t = lax.axis_index("tp")

    def along(step, act):
        there = me_c + step

        @pl.when((there >= 0) & (there < ctx))
        def _():
            act(there)

    barrier = pltpu.get_barrier_semaphore()
    for k in range(1, group):
        pl.semaphore_signal(
            barrier, inc=1, device_id=(flip_index(me_f, k, fsdp), me_c, me_t), device_id_type=MESH_ID
        )
    for step in (-1, 1):
        along(
            step,
            lambda there: pl.semaphore_signal(
                barrier, inc=1, device_id=(me_f, there, me_t), device_id_type=MESH_ID
            ),
        )
    pl.semaphore_wait(barrier, group - 1 + line_neighbours(me_c, ctx))

    def z_copy(i, shard, step, src=None):
        place = line_out[i].at[shard]
        way = 0 if step > 0 else 1
        return pltpu.make_async_remote_copy(
            src_ref=place if src is None else src,
            dst_ref=place,
            send_sem=z_send.at[i, way, shard],
            recv_sem=z_recv.at[i, way, shard],
            device_id=(me_f, me_c + step, me_t),
            device_id_type=MESH_ID,
        )

    def landing(i, f):
        out, start = spots[i]
        width = swap_in[i].shape[1] // group
        return swap_out[out].at[lax.rem(f, group), :, pl.ds(start, width)]

    def columns(i, f):
        width = swap_in[i].shape[1] // group
        return swap_in[i].at[:, pl.ds(pl.multiple_of(lax.rem(f, group) * width, 128), width)]

    def f_copy(i, k):
        there = flip_index(me_f, k, fsdp)
        return pltpu.make_async_remote_copy(
            src_ref=columns(i, there),
            dst_ref=landing(i, me_f),
            send_sem=f_send.at[i, k],
            recv_sem=f_recv.at[i, k],
            device_id=(there, me_c, me_t),
            device_id_type=MESH_ID,
        )

    def f_arrival(i, k):
        there = flip_index(me_f, k, fsdp)
        return pltpu.make_async_remote_copy(
            src_ref=landing(i, there),
            dst_ref=landing(i, there),
            send_sem=f_send.at[i, k],
            recv_sem=f_recv.at[i, k],
            device_id=(there, me_c, me_t),
            device_id_type=MESH_ID,
        )

    for i in range(lines):
        for step in (1, -1):
            along(step, lambda there: z_copy(i, me_c, step, line_in[i]).start())
    order = fsdp_order(group)
    for i in range(swaps):
        for k in order:
            f_copy(i, k).start()
    own = [
        pltpu.make_async_copy(line_in[i], line_out[i].at[me_c], own_sem.at[i])
        for i in range(lines)
    ] + [
        pltpu.make_async_copy(columns(i, me_f), landing(i, me_f), own_sem.at[lines + i])
        for i in range(swaps)
    ]
    for copy in own:
        copy.start()
    for i in range(lines):
        for distance in range(1, ctx):
            for step in (1, -1):
                shard = me_c - step * distance

                @pl.when((shard >= 0) & (shard < ctx))
                def _():
                    z_copy(i, shard, step).wait_recv()
                    along(step, lambda there: z_copy(i, shard, step).start())

    for i in range(swaps):
        for k in order:
            f_arrival(i, k).wait_recv()
            f_copy(i, k).wait_send()
    for copy in own:
        copy.wait()
    for i in range(lines):
        for step in (1, -1):
            along(step, lambda there: z_copy(i, me_c, step, line_in[i]).wait_send())
            for distance in range(1, ctx - 1):
                shard = me_c - step * distance

                @pl.when((shard >= 0) & (shard < ctx))
                def _():
                    along(step, lambda there: z_copy(i, shard, step).wait_send())


def start_exchange(fsdp, ctx, group, lines, swap_sets):
    sems = pltpu.SemaphoreType.DMA
    out_shape = [jax.ShapeDtypeStruct((ctx,) + v.shape, v.dtype) for v in lines]
    swaps, spots = [], []
    for out, arrays in enumerate(swap_sets):
        start = 0
        for v in arrays:
            spots.append((out, start))
            swaps.append(v)
            start += v.shape[1] // group
        out_shape.append(
            jax.ShapeDtypeStruct((group, arrays[0].shape[0], start), arrays[0].dtype)
        )
    count = len(lines) + len(swaps)
    outs = pl.pallas_call(
        partial(line_kernel, fsdp, ctx, group, len(lines), len(swaps), spots),
        out_shape=out_shape,
        in_specs=[pl.BlockSpec(memory_space=pl.ANY)] * count,
        out_specs=[pl.BlockSpec(memory_space=pl.ANY)] * len(out_shape),
        scratch_shapes=[
            sems((count,)),
            sems((len(lines), 2, ctx)),
            sems((len(lines), 2, ctx)),
            sems((len(swaps), group)),
            sems((len(swaps), group)),
        ],
        compiler_params=pltpu.CompilerParams(collective_id=0, has_side_effects=True),
    )(*lines, *swaps)
    return outs[: len(lines)], outs[len(lines) :]


def spread_kernel(fsdp, ctx, count, chain, *refs):
    ins = refs[:count]
    outs = refs[count + chain : 2 * count + chain]
    own_sem, f_send, f_recv, c_own, c_send, c_recv = refs[2 * (count + chain) :]
    me_f = lax.axis_index("fsdp")
    me_c = lax.axis_index("ctx")
    me_t = lax.axis_index("tp")
    bits = [1 << i for i in range(fsdp.bit_length() - 1)]
    order = fsdp_order(fsdp)

    def peer(k):
        return (flip_index(me_f, k, fsdp), me_c, me_t)

    barrier = pltpu.get_barrier_semaphore()
    for b in bits:
        pl.semaphore_signal(barrier, inc=1, device_id=peer(b), device_id_type=MESH_ID)
    if chain:
        chain_in, chain_out = refs[count], refs[2 * count + 1]
        for step in (-1, 1):
            there = me_c + step

            @pl.when((there >= 0) & (there < ctx))
            def _():
                pl.semaphore_signal(
                    barrier, inc=1, device_id=(me_f, there, me_t), device_id_type=MESH_ID
                )

        pl.semaphore_wait(barrier, len(bits) + line_neighbours(me_c, ctx))
    else:
        pl.semaphore_wait(barrier, len(bits))

    def climb(s):
        return pltpu.make_async_remote_copy(
            src_ref=chain_out.at[s] if s else chain_in,
            dst_ref=chain_out.at[s + 1],
            send_sem=c_send.at[s],
            recv_sem=c_recv.at[s + 1],
            device_id=(me_f, me_c + 1, me_t),
            device_id_type=MESH_ID,
        )

    def keep(s):
        return pltpu.make_async_copy(chain_in, chain_out.at[s], c_own.at[s])

    def send_up(s):
        @pl.when((me_c >= s) & (me_c < ctx - 1))
        def _():
            climb(s).start()

    def take_up(s):
        @pl.when(me_c >= s)
        def _():
            pltpu.make_async_remote_copy(
                src_ref=chain_out.at[s],
                dst_ref=chain_out.at[s],
                send_sem=c_send.at[s - 1],
                recv_sem=c_recv.at[s],
                device_id=(me_f, me_c - 1, me_t),
                device_id_type=MESH_ID,
            ).wait_recv()

        if s < ctx - 1:
            send_up(s)

    if chain:
        send_up(0)
        keep(0).start()
        for s in range(1, ctx):
            @pl.when(me_c < s)
            def _():
                keep(s).start()

    def place(i, shard, have, k, part):
        block = outs[i].at[shard, flip_index(me_f, have, fsdp)]
        half = ins[i].shape[1] // 2
        return block if k == low_bit(k) else block.at[pl.ds(part * half, half)]

    def f_copy(i, shard, have, b):
        k = have | b
        part = 1 if have and b == high_bit(k) else 0
        block = place(i, shard, have, k, part)
        return pltpu.make_async_remote_copy(
            src_ref=block if have else ins[i].at[shard],
            dst_ref=block,
            send_sem=f_send.at[i, shard, k, part],
            recv_sem=f_recv.at[i, shard, k, part],
            device_id=peer(b),
            device_id_type=MESH_ID,
        )

    def ways(have):
        return [
            b
            for b in bits
            if not have & b and (not have or b in (low_bit(have | b), high_bit(have | b)))
        ]

    own = [
        pltpu.make_async_copy(ins[i], outs[i].at[:, me_f], own_sem.at[i]) for i in range(count)
    ]
    for i in range(count):
        for shard in range(ctx):
            for b in ways(0):
                f_copy(i, shard, 0, b).start()
        own[i].start()
    climbed = 1
    for i in range(count):
        for k in order:
            if chain and climbed < ctx:
                take_up(climbed)
                climbed += 1
            parts = [(0, k)] if k == low_bit(k) else [(0, low_bit(k)), (1, high_bit(k))]
            for shard in range(ctx):
                for part, b in parts:
                    block = place(i, shard, k, k, part)
                    pltpu.make_async_remote_copy(
                        src_ref=block,
                        dst_ref=block,
                        send_sem=f_send.at[i, shard, k, part],
                        recv_sem=f_recv.at[i, shard, k, part],
                        device_id=peer(b),
                        device_id_type=MESH_ID,
                    ).wait_recv()
                for b in ways(k):
                    f_copy(i, shard, k, b).start()
    if chain:
        for s in range(climbed, ctx):
            take_up(s)
        keep(0).wait()
        for s in range(ctx):
            if s:

                @pl.when(me_c < s)
                def _():
                    keep(s).wait()

            if s < ctx - 1:

                @pl.when((me_c >= s) & (me_c < ctx - 1))
                def _():
                    climb(s).wait_send()

    for i in range(count):
        own[i].wait()
        for have in [0] + order:
            for shard in range(ctx):
                for b in ways(have):
                    f_copy(i, shard, have, b).wait_send()


def spread_weights(fsdp, ctx, arrays, chain=None):
    count = len(arrays)
    sems = pltpu.SemaphoreType.DMA
    extra = [] if chain is None else [chain]
    outs = pl.pallas_call(
        partial(spread_kernel, fsdp, ctx, count, len(extra)),
        out_shape=[
            jax.ShapeDtypeStruct((ctx, fsdp) + v.shape[1:], v.dtype) for v in arrays
        ]
        + [jax.ShapeDtypeStruct((ctx,) + v.shape, v.dtype) for v in extra],
        in_specs=[pl.BlockSpec(memory_space=pl.ANY)] * (count + len(extra)),
        out_specs=[pl.BlockSpec(memory_space=pl.ANY)] * (count + len(extra)),
        scratch_shapes=[
            sems((count,)),
            sems((count, ctx, fsdp, 2)),
            sems((count, ctx, fsdp, 2)),
            sems((ctx,)),
            sems((ctx,)),
            sems((ctx,)),
        ],
        compiler_params=pltpu.CompilerParams(
            collective_id=1 if chain is None else 3, has_side_effects=True
        ),
    )(*arrays, *extra)
    return [o.reshape(-1, v.shape[-1]) for o, v in zip(outs, arrays)] + list(outs[count:])


def sum_kernel(fsdp, ctx, count, chain, *refs):
    ins = refs[:count]
    if chain:
        parts_ref, cos_ref, sin_ref = refs[count : count + 3]
        refs = refs[:count] + refs[count + 3 :]
        kv_ref = refs[2 * count]
        refs = refs[: 2 * count] + refs[2 * count + 1 :]
    outs = refs[count : 2 * count]
    held = refs[2 * count : 3 * count]
    got = refs[3 * count : 4 * count]
    line = refs[4 * count : 5 * count]
    in_sem, f_send, f_recv, z_send, z_recv = refs[5 * count : 5 * count + 5]
    if chain:
        kv_parts, kv_got, kv_sem, c_send, c_recv = refs[5 * count + 5 :]
    me_f = lax.axis_index("fsdp")
    me_c = lax.axis_index("ctx")
    me_t = lax.axis_index("tp")
    bits = [1 << i for i in range(fsdp.bit_length() - 1)]
    order = fsdp_order(fsdp)

    def peer(k):
        return (flip_index(me_f, k, fsdp), me_c, me_t)

    def along(step, act):
        there = me_c + step

        @pl.when((there >= 0) & (there < ctx))
        def _():
            act(there)

    loads = {}
    if chain:
        kv_load = pltpu.make_async_copy(parts_ref, kv_parts, kv_sem.at[0])
        kv_load.start()
    for i in range(count):
        for k in reversed([0] + order):
            loads[i, k] = pltpu.make_async_copy(
                ins[i].at[:, flip_index(me_f, k, fsdp)], held[i].at[k], in_sem.at[i, k]
            )
            loads[i, k].start()

    barrier = pltpu.get_barrier_semaphore()
    for b in bits:
        pl.semaphore_signal(barrier, inc=1, device_id=peer(b), device_id_type=MESH_ID)
    for step in (-1, 1):
        along(
            step,
            lambda there: pl.semaphore_signal(
                barrier, inc=1, device_id=(me_f, there, me_t), device_id_type=MESH_ID
            ),
        )
    pl.semaphore_wait(barrier, len(bits) + line_neighbours(me_c, ctx))

    def ways(k):
        return [(0, k)] if k == low_bit(k) else [(0, low_bit(k)), (1, high_bit(k))]

    def piece(i, k, part):
        rows = ins[i].shape[2]
        return pl.ds(0, rows) if k == low_bit(k) else pl.ds(part * (rows // 2), rows // 2)

    def f_copy(i, shard, k, part, b):
        span = piece(i, k, part)
        return pltpu.make_async_remote_copy(
            src_ref=held[i].at[k, shard, span],
            dst_ref=got[i].at[k, shard, span],
            send_sem=f_send.at[i, shard, k, part],
            recv_sem=f_recv.at[i, shard, k, part],
            device_id=peer(b),
            device_id_type=MESH_ID,
        )

    def add(into, other):
        tile = 16 if into.dtype == jnp.bfloat16 else 8

        def body(r, _):
            span = pl.ds(pl.multiple_of(r * tile, tile), tile)
            into[span] = (
                into[span].astype(jnp.float32) + other[span].astype(jnp.float32)
            ).astype(into.dtype)
            return 0

        lax.fori_loop(0, into.shape[0] // tile, body, 0)

    def collect(i, shard, k):
        for far in order:
            for part, b in ways(far):
                if far ^ b == k:
                    f_copy(i, shard, far, part, b).wait_recv()
                    span = piece(i, far, part)
                    add(held[i].at[k, shard, span], got[i].at[far, shard, span])

    def z_copy(i, shard, step):
        way = 0 if step > 0 else 1
        return pltpu.make_async_remote_copy(
            src_ref=held[i].at[0, shard],
            dst_ref=line[i].at[way, shard],
            send_sem=z_send.at[i, way, shard],
            recv_sem=z_recv.at[i, way, shard],
            device_id=(me_f, me_c + step, me_t),
            device_id_type=MESH_ID,
        )

    def on_line(i, shard):
        for step in (1, -1):
            way = 0 if step > 0 else 1

            @pl.when((step * (shard - me_c) >= 0) & (me_c - step >= 0) & (me_c - step < ctx))
            def _():
                z_copy(i, shard, step).wait_recv()
                add(held[i].at[0, shard], line[i].at[way, shard])

            @pl.when(step * (shard - me_c) > 0)
            def _():
                z_copy(i, shard, step).start()

        @pl.when(shard == me_c)
        def _():
            rows = outs[i].shape[0]

            def body(r, _):
                span = pl.ds(pl.multiple_of(r * 16, 16), 16)
                outs[i][span] = held[i][0, shard, span].astype(outs[i].dtype)
                return 0

            lax.fori_loop(0, rows // 16, body, 0)

    def descend(s):
        return pltpu.make_async_remote_copy(
            src_ref=kv_parts.at[s],
            dst_ref=kv_got.at[s - 1],
            send_sem=c_send.at[s],
            recv_sem=c_recv.at[s - 1],
            device_id=(me_f, me_c - 1, me_t),
            device_id_type=MESH_ID,
        )

    def chain_step(s):
        if s < ctx - 1:

            @pl.when((me_c >= s) & (me_c < ctx - 1))
            def _():
                pltpu.make_async_remote_copy(
                    src_ref=kv_got.at[s],
                    dst_ref=kv_got.at[s],
                    send_sem=c_send.at[s + 1],
                    recv_sem=c_recv.at[s],
                    device_id=(me_f, me_c + 1, me_t),
                    device_id_type=MESH_ID,
                ).wait_recv()
                for side in range(2):
                    add(kv_parts.at[s, side], kv_got.at[s, side])

        if s:

            @pl.when(me_c >= s)
            def _():
                descend(s).start()

    def chain_result():
        width = kv_parts.shape[3]
        rows = cos_ref.shape[0]
        for seq in range(kv_parts.shape[2] // rows):
            span = pl.ds(seq * rows, rows)
            for start in range(0, width, 128):
                cols = slice(start, start + 128)
                t = kv_parts[0, 0, span, cols].astype(jnp.float32)
                t = t * cos_ref[...] + turn(t * sin_ref[...], -1.0)
                kv_ref[span, cols] = t.astype(kv_ref.dtype)
            kv_ref[span, width:] = kv_parts[0, 1, span]

    steps = list(reversed(range(ctx))) if chain else []

    def next_step():
        if steps:
            s = steps.pop(0)
            chain_step(s)
            if s == 0:
                chain_result()

    if chain:
        kv_load.wait()
        next_step()
    shards = sorted(range(ctx), key=lambda c: -abs(2 * c - ctx + 1))
    work = [(i, shard) for i in range(count) for shard in shards]
    levels = sorted({bin(k).count("1") for k in order}, reverse=True)
    for level in levels:
        ks = [k for k in order if bin(k).count("1") == level]
        for i in range(count):
            for k in ks:
                loads[i, k].wait()
            for shard in shards:
                for k in ks:
                    collect(i, shard, k)
                    for part, b in ways(k):
                        f_copy(i, shard, k, part, b).start()
        next_step()
    for i in range(count):
        loads[i, 0].wait()
    late = None
    while steps:
        next_step()
    for item in work + [None]:
        if item is not None:
            collect(item[0], item[1], 0)
        if late is not None:
            on_line(*late)
        late = item
    for i, shard in work:
        for k in order:
            for part, b in ways(k):
                f_copy(i, shard, k, part, b).wait_send()
        for step in (1, -1):

            @pl.when(step * (shard - me_c) > 0)
            def _():
                z_copy(i, shard, step).wait_send()

    if chain:
        for s in range(1, ctx):

            @pl.when(me_c >= s)
            def _():
                descend(s).wait_send()


def sum_weights(fsdp, ctx, arrays, chain=()):
    count = len(arrays)
    sems = pltpu.SemaphoreType.DMA
    shards = [v.reshape(ctx, fsdp, -1, v.shape[-1]) for v in arrays]
    vmem = pltpu.VMEM
    blocks = [(fsdp, ctx) + v.shape[2:] for v in shards]
    return pl.pallas_call(
        partial(sum_kernel, fsdp, ctx, count, bool(chain)),
        out_shape=[jax.ShapeDtypeStruct(v.shape[2:], jnp.float32) for v in shards]
        + [jax.ShapeDtypeStruct((v.shape[2], 2 * v.shape[3]), v.dtype) for v in chain[:1]],
        in_specs=[pl.BlockSpec(memory_space=pl.ANY)] * (count + len(chain[:1]))
        + [pl.BlockSpec(memory_space=pltpu.VMEM)] * len(chain[1:]),
        out_specs=[pl.BlockSpec(memory_space=pltpu.VMEM)] * (count + len(chain[:1])),
        scratch_shapes=[vmem(b, v.dtype) for b, v in zip(blocks, shards)]
        + [vmem(b, v.dtype) for b, v in zip(blocks, shards)]
        + [vmem((2,) + b[1:], v.dtype) for b, v in zip(blocks, shards)]
        + [
            sems((count, fsdp)),
            sems((count, ctx, fsdp, 2)),
            sems((count, ctx, fsdp, 2)),
            sems((count, 2, ctx)),
            sems((count, 2, ctx)),
        ]
        + [
            scratch
            for v in chain[:1]
            for scratch in (
                vmem(v.shape, v.dtype),
                vmem((ctx - 1,) + v.shape[1:], v.dtype),
                sems((1,)),
                sems((ctx,)),
                sems((ctx,)),
            )
        ],
        compiler_params=pltpu.CompilerParams(
            collective_id=4 if chain else 2,
            has_side_effects=True,
            vmem_limit_bytes=50 * 1024 * 1024,
        ),
    )(*shards, *chain)


def local(
    inputs,
    lengths,
    cotangent,
    norm1_gain,
    w_query,
    w_key,
    w_value,
    w_out,
    norm2_gain,
    w_gate,
    w_up,
    w_down,
):
    seq_count, local_rows, model_width = inputs.shape
    tokens = seq_count * local_rows
    half = tokens // 2
    fsdp = lax.axis_size("fsdp")
    ctx = lax.axis_size("ctx")
    shard = w_query.shape[0]
    query_width = w_query.shape[1]
    kv_width = w_key.shape[1]
    kv_end = query_width + 2 * kv_width
    pairs = kv_width // (2 * HD)
    group_size = query_width // kv_width
    group = min(fsdp, 4)
    far = fsdp // group
    units = w_gate.shape[1] // group
    me_c = lax.axis_index("ctx")
    me_t = lax.axis_index("tp")
    order = fsdp_order(group)
    low = jnp.bfloat16
    wide = jnp.float32

    def hop(v, k):
        return lax.ppermute(v, "fsdp", [(i, i ^ k) for i in range(fsdp)])

    def swap(v):
        return lax.ppermute(v, "tp", [(0, 1), (1, 0)])

    inside = shard % 128 == 0
    dims = (fsdp, ctx, shard)
    back_dims = (ctx, fsdp, shard)

    def by_ctx(v):
        if inside:
            return v
        rows = v.shape[0]
        return v.reshape(rows, fsdp, ctx, shard).swapaxes(1, 2).reshape(rows, model_width)

    def by_fsdp(v):
        if inside:
            return v
        rows = v.shape[0]
        return v.reshape(rows, ctx, fsdp, shard).swapaxes(1, 2).reshape(rows, model_width)

    def pair_heads(v):
        rows = v.shape[0]
        return (
            v.reshape(rows, pairs, 2, group_size, HD).swapaxes(2, 3).reshape(rows, query_width)
        )

    def plain_heads(v):
        rows = v.shape[0]
        return (
            v.reshape(rows, pairs, group_size, 2, HD).swapaxes(2, 3).reshape(rows, query_width)
        )

    def gather_tokens(v):
        mine = lax.dynamic_slice_in_dim(v, me_t * half, half)
        other = lax.dynamic_slice_in_dim(v, (1 - me_t) * half, half)
        got = {0: mine}
        for k in order:
            lo, hi = low_bit(k), high_bit(k)
            if lo == hi:
                got[k] = hop(mine, k)
            else:
                cut = half // 2
                got[k] = jnp.concatenate(
                    [hop(got[k ^ lo][:cut], lo), hop(got[k ^ hi][cut:], hi)]
                )
        return jnp.concatenate(
            [mine, other] + [v for k in range(1, group) for v in (got[k], swap(got[k]))]
        )

    def scatter_tokens(v):
        cut = half // 2
        total = {}
        for k in reversed([0] + order):
            start = 2 * k * half
            mine, other = v[start : start + half], v[start + half : start + 2 * half]
            total[k] = mine.astype(wide) + swap(other).astype(wide)
        for k in reversed(order):
            lo, hi = low_bit(k), high_bit(k)
            sent = total[k].astype(low)
            if lo == hi:
                total[0] = total[0] + hop(sent, k).astype(wide)
            else:
                for there, first, b in ((k ^ lo, True, lo), (k ^ hi, False, hi)):
                    piece = hop(sent[:cut] if first else sent[cut:], b).astype(wide)
                    base = total[there]
                    total[there] = jnp.concatenate(
                        [base[:cut] + piece, base[cut:]]
                        if first
                        else [base[:cut], base[cut:] + piece]
                    )
        own = total[0].astype(low)
        other = swap(own)
        return jnp.where(
            me_t == 0, jnp.concatenate([own, other]), jnp.concatenate([other, own])
        )

    x = by_ctx(inputs.reshape(tokens, model_width))
    cot = by_ctx(cotangent.reshape(tokens, model_width))
    positions = me_c * local_rows + jnp.arange(local_rows, dtype=jnp.int32)
    cosines, sines = rope_tables(positions, HD)
    cosines, sines = jnp.tile(cosines, (1, 2)), jnp.tile(sines, (1, 2))

    gains = jnp.pad(jnp.stack([norm1_gain, norm2_gain]).astype(wide), ((0, 14), (0, 0)))
    lined, held = start_exchange(
        fsdp,
        ctx,
        group,
        [
            gains,
            jnp.concatenate([pair_heads(w_query), w_key, w_value], 1),
            pair_heads(w_out),
        ],
        [[w_gate, w_up], [w_down]],
    )
    far_groups = [[h * group + g for h in range(far)] for g in range(group)]
    near_groups = [[h * group + g for g in range(group)] for h in range(far)]

    def whole_width(v):
        if far > 1:
            v = lax.all_gather(v, "fsdp", axis=0, tiled=False, axis_index_groups=far_groups)
        return lax.all_gather(v, "ctx", axis=0, tiled=False).reshape(model_width, -1)

    both_full, down_full = [whole_width(v) for v in held]
    gain_rows, qkv_full = spread_weights(fsdp, ctx, lined[:2])
    gain_rows = gain_rows.reshape(ctx * fsdp, 16, shard)
    gain_one = gain_rows[:, 0].reshape(1, model_width)
    gain_two = gain_rows[:, 1].reshape(1, model_width)

    (ff_grad,) = by_rows(
        partial(cot_kernel, dims, local_rows),
        128,
        [(lengths, "smem"), (cot, "rows")],
        [((tokens, model_width), low)],
    )
    ff_grad, gain_one = lax.optimization_barrier((ff_grad, gain_one))
    ff_grad_all = gather_tokens(ff_grad)

    first_normed, query, kv_own = by_rows(
        partial(qkv_kernel, dims),
        128,
        [
            (x, "rows"),
            (qkv_full, "whole"),
            (gain_one, "whole"),
            (cosines, "cycle"),
            (sines, "cycle"),
        ],
        [
            ((tokens, model_width), low),
            ((tokens, query_width), low),
            ((tokens, 2 * kv_width), low),
        ],
        flops=2 * tokens * model_width * kv_end,
    )
    out_full, kv_all = spread_weights(fsdp, ctx, lined[2:], kv_own)
    attended, lse = attend(lengths, query, kv_all)
    attn_part = jnp.einsum(
        "tj,dj->td", attended, out_full, preferred_element_type=wide
    ).astype(low)
    middle, second_normed = by_rows(
        partial(middle_kernel, dims),
        128,
        [(x, "rows"), (attn_part, "rows"), (swap(attn_part), "rows"), (gain_two, "whole")],
        [((tokens, model_width), wide), ((tokens, model_width), low)],
    )
    normed_all = gather_tokens(second_normed)

    many = group * tokens
    hidden, both_grad, second_part, ff_part = by_rows(
        swiglu_kernel,
        256,
        [
            (normed_all, "rows"),
            (ff_grad_all, "rows"),
            (both_full, "whole"),
            (down_full, "whole"),
        ],
        [
            ((many, units), low),
            ((many, 2 * units), low),
            ((many, model_width), low),
            ((many, model_width), low),
        ],
        flops=12 * many * model_width * units,
        limit=56,
    )

    def unit_term(left, right):
        return jnp.einsum("td,tf->df", left, right, preferred_element_type=wide).astype(low)

    def return_units(term):
        own = lax.psum_scatter(
            term.reshape(ctx, fsdp, shard, units), "ctx", scatter_dimension=0, tiled=False
        )
        if far > 1:
            own = lax.psum_scatter(
                own.reshape(far, group, shard, units),
                "fsdp",
                scatter_dimension=0,
                tiled=False,
                axis_index_groups=far_groups,
            )
        return lax.all_to_all(
            own.reshape(group * shard, units),
            "fsdp",
            0,
            1,
            tiled=True,
            axis_index_groups=near_groups if far > 1 else None,
        ).astype(wide)

    down_term = unit_term(ff_grad_all, hidden)
    second_grad = scatter_tokens(second_part)
    gate_term = unit_term(normed_all, both_grad[:, :units])
    up_term = unit_term(normed_all, both_grad[:, units:])
    second_grad, ff_part, _, _, _ = lax.optimization_barrier(
        (second_grad, ff_part, down_term, gate_term, up_term)
    )
    ff_branch = scatter_tokens(ff_part)
    w_down_grad = return_units(down_term)
    w_gate_grad = return_units(gate_term)
    w_up_grad = return_units(up_term)
    (output,) = by_rows(
        partial(output_kernel, back_dims, local_rows),
        128,
        [(lengths, "smem"), (middle, "rows"), (ff_branch, "rows")],
        [((tokens, model_width), low)],
    )

    middle_grad, attn_grad, gain_two_term = by_rows(
        partial(middle_back_kernel, dims, local_rows),
        128,
        [
            (lengths, "smem"),
            (cot, "rows"),
            (middle, "rows"),
            (second_grad, "rows"),
            (gain_two, "whole"),
        ],
        [((tokens, model_width), wide), ((tokens, model_width), low), ((1, model_width), wide)],
    )
    attended_grad = jnp.dot(attn_grad, out_full, preferred_element_type=wide).astype(low)
    query_grad, kv_parts = attend_back(
        lengths, query, attended_grad, lse, cosines, sines, kv_all
    )
    out_term = jnp.einsum("td,tj->dj", attn_grad, attended, preferred_element_type=wide)
    w_out_grad, kv_grad = sum_weights(
        fsdp, ctx, [out_term.astype(low)], (kv_parts, cosines, sines)
    )
    qkv_grad = jnp.concatenate([query_grad, kv_grad], -1)
    qkv_term = jnp.einsum("td,tj->dj", first_normed, qkv_grad, preferred_element_type=wide)
    first_part = jnp.einsum(
        "tj,dj->td", qkv_grad, qkv_full, preferred_element_type=wide
    ).astype(low)
    input_grad, gain_one_term = by_rows(
        partial(input_back_kernel, dims),
        128,
        [
            (x, "rows"),
            (first_part, "rows"),
            (swap(first_part), "rows"),
            (middle_grad, "rows"),
            (gain_one, "whole"),
        ],
        [((tokens, model_width), low), ((1, model_width), wide)],
    )
    gain_terms = jnp.stack(
        [gain_one_term.reshape(-1, shard), gain_two_term.reshape(-1, shard)], 1
    )
    gain_terms = jnp.pad(gain_terms, ((0, 0), (0, 14), (0, 0))).reshape(-1, shard)
    qkv_term, w_down_grad, w_gate_grad, w_up_grad = lax.optimization_barrier(
        (qkv_term.astype(low), w_down_grad, w_gate_grad, w_up_grad)
    )
    gain_own, qkv_own = sum_weights(fsdp, ctx, [gain_terms, qkv_term])
    return (
        by_fsdp(output).reshape(inputs.shape),
        by_fsdp(input_grad).reshape(inputs.shape),
        gain_own[0],
        plain_heads(qkv_own[:, :query_width]),
        qkv_own[:, query_width : query_width + kv_width],
        qkv_own[:, query_width + kv_width :],
        plain_heads(w_out_grad),
        gain_own[1],
        w_gate_grad,
        w_up_grad,
        w_down_grad,
    )


def solution(mesh):
    placed = (
        P("fsdp", "ctx", None),
        P("fsdp"),
        P("fsdp", "ctx", None),
        P(("fsdp", "ctx")),
        P(("fsdp", "ctx"), "tp"),
        P(("fsdp", "ctx"), "tp"),
        P(("fsdp", "ctx"), "tp"),
        P(("fsdp", "ctx"), "tp"),
        P(("fsdp", "ctx")),
        P(("fsdp", "ctx"), "tp"),
        P(("fsdp", "ctx"), "tp"),
        P(("fsdp", "ctx"), "tp"),
    )
    return jax.shard_map(
        local,
        mesh=mesh,
        in_specs=placed,
        out_specs=(
            P("fsdp", "ctx", None),
            P("fsdp", "ctx", None),
            P(("fsdp", "ctx")),
            P(("fsdp", "ctx"), "tp"),
            P(("fsdp", "ctx"), "tp"),
            P(("fsdp", "ctx"), "tp"),
            P(("fsdp", "ctx"), "tp"),
            P(("fsdp", "ctx")),
            P(("fsdp", "ctx"), "tp"),
            P(("fsdp", "ctx"), "tp"),
            P(("fsdp", "ctx"), "tp"),
        ),
        check_vma=False,
    )
```

```python
from functools import partial

import jax
import jax.numpy as jnp
from jax import lax
from jax.experimental import pallas as pl
from jax.experimental.pallas import tpu as pltpu
from jax.sharding import PartitionSpec as P

HD = 64


norm_eps = 1e-05
residual_scale = 0.22
score_scale = 1.0 / 64.0
rope_base = 10000000.0
masked_score = -1e30


def rope_tables(positions, head_dim):
    half_dim = head_dim // 2
    frequency = rope_base ** (-(jnp.arange(half_dim, dtype=jnp.float32) * 2.0) / head_dim)
    angles = positions.astype(jnp.float32)[:, None] * frequency[None, :]
    return (
        jnp.concatenate([jnp.cos(angles), jnp.cos(angles)], -1),
        jnp.concatenate([jnp.sin(angles), jnp.sin(angles)], -1),
    )


def rotate(values_in, cosines, sines):
    half_dim = values_in.shape[-1] // 2
    turned = jnp.concatenate([-values_in[..., half_dim:], values_in[..., :half_dim]], -1)
    return values_in * cosines + turned * sines


def unrotate(grad_in, cosines, sines):
    half_dim = grad_in.shape[-1] // 2
    scaled = grad_in * sines
    return grad_in * cosines + jnp.concatenate(
        [scaled[..., half_dim:], -scaled[..., :half_dim]], -1
    )


def rms_scale(values_in):
    return lax.rsqrt(jnp.mean(values_in * values_in, -1, keepdims=True) + norm_eps)


def norm_back(grad_normed, values_in, scale, gain):
    scaled_grad = grad_normed * gain
    return scale * scaled_grad - values_in * scale**3 * jnp.mean(
        scaled_grad * values_in, -1, keepdims=True
    )


MESH_ID = pl.DeviceIdType.MESH
NT = (((1,), (1,)), ((), ()))
TN = (((0,), (0,)), ((), ()))
SMEM = pltpu.SMEM


def mul(left, right, dims=(((1,), (0,)), ((), ()))):
    return lax.dot_general(left, right, dims, preferred_element_type=jnp.float32)


def reorder(v, first, second, width):
    if width % 128:
        return v
    pieces = []
    for b in range(second):
        for a in range(first):
            start = (a * second + b) * width
            pieces.append(v[:, start : start + width])
    return jnp.concatenate(pieces, 1)


def turn(t, sign):
    lane = lax.broadcasted_iota(jnp.int32, t.shape, 1)
    ahead = pltpu.roll(t, 128 - HD // 2, 1)
    behind = pltpu.roll(t, HD // 2, 1)
    return jnp.where(lax.rem(lane, HD) < HD // 2, -sign * ahead, sign * behind)


def row_valid(len_ref, rows, local_rows):
    step = pl.program_id(0)
    start = step * rows
    seq = start // local_rows
    place = (
        lax.axis_index("ctx") * local_rows
        + lax.rem(start, local_rows)
        + lax.broadcasted_iota(jnp.int32, (rows, 1), 0)
    )
    return (place < len_ref[seq]).astype(jnp.float32)


def qkv_kernel(dims, x_ref, w_ref, gain_ref, cos_ref, sin_ref, normed_ref, q_ref, kv_ref):
    x = reorder(x_ref[...].astype(jnp.float32), *dims)
    normed = (x * rms_scale(x) * gain_ref[...]).astype(jnp.bfloat16)
    normed_ref[...] = normed
    lin = mul(normed, w_ref[...])
    cosines, sines = cos_ref[...], sin_ref[...]
    width = q_ref.shape[1]
    half = kv_ref.shape[1] // 2
    for start in range(0, width + half, 128):
        t = lin[:, start : start + 128]
        t = (t * cosines + turn(t, 1.0) * sines).astype(jnp.bfloat16)
        if start < width:
            q_ref[:, start : start + 128] = t
        else:
            kv_ref[:, start - width : start - width + 128] = t
    kv_ref[:, half:] = lin[:, width + half :].astype(jnp.bfloat16)


def key_biases(len_ref, rows, ctx):
    length = len_ref[pl.program_id(0)]
    me = lax.axis_index("ctx")
    row = lax.broadcasted_iota(jnp.int32, (rows, rows), 0)
    col = lax.broadcasted_iota(jnp.int32, (rows, rows), 1)
    first = jnp.where((col <= row) & (me * rows + col < length), 0.0, masked_score)
    out = [first]
    for s in range(1, ctx):
        place = (me - s) * rows + lax.broadcasted_iota(jnp.int32, (1, rows), 1)
        out.append(jnp.where((place >= 0) & (place < length), 0.0, masked_score))
    return out


def attend_kernel(ctx, len_ref, q_ref, *refs):
    keys, values = refs[:ctx], refs[ctx : 2 * ctx]
    o_ref, lse_ref = refs[2 * ctx :]
    rows = q_ref.shape[0]
    biases = key_biases(len_ref, rows, ctx)
    lane = lax.broadcasted_iota(jnp.int32, (rows, 128), 1)
    lse_all = jnp.zeros((rows, 128), jnp.float32)
    for j in range(q_ref.shape[1] // 128):
        q_pair = q_ref[:, j * 128 : (j + 1) * 128] * jnp.bfloat16(score_scale)
        outs = []
        for g in range(2):
            mine = (lane < HD) if g == 0 else (lane >= HD)
            q_head = jnp.where(mine, q_pair, jnp.zeros_like(q_pair))
            scores = [mul(q_head, k[...], NT) + b for k, b in zip(keys, biases)]
            top = scores[0].max(-1, keepdims=True)
            for s in scores[1:]:
                top = jnp.maximum(top, s.max(-1, keepdims=True))
            mass, out = 0.0, 0.0
            for s, v in zip(scores, values):
                p = jnp.exp(s - top)
                mass = mass + p.sum(-1, keepdims=True)
                out = out + mul(p.astype(jnp.bfloat16), v[...])
            outs.append(out / mass)
            lse_all = jnp.where(lane == 2 * j + g, top + jnp.log(mass), lse_all)
        o_ref[:, j * 128 : (j + 1) * 128] = jnp.where(lane < HD, outs[0], outs[1]).astype(
            jnp.bfloat16
        )
    lse_ref[...] = lse_all


def attend_back_kernel(ctx, len_ref, q_ref, do_ref, lse_ref, cos_ref, sin_ref, *refs):
    keys, values = refs[:ctx], refs[ctx : 2 * ctx]
    dq_ref, dkv_ref, dk_sum, dv_sum = refs[2 * ctx :]
    rows = q_ref.shape[0]
    biases = key_biases(len_ref, rows, ctx)
    lane = lax.broadcasted_iota(jnp.int32, (rows, 128), 1)
    dk_sum[...] = jnp.zeros_like(dk_sum)
    dv_sum[...] = jnp.zeros_like(dv_sum)
    lse_all = lse_ref[...]
    for j in range(q_ref.shape[1] // 128):
        q_pair = q_ref[:, j * 128 : (j + 1) * 128] * jnp.bfloat16(score_scale)
        do_pair = do_ref[:, j * 128 : (j + 1) * 128]
        dqs = []
        for g in range(2):
            mine = (lane < HD) if g == 0 else (lane >= HD)
            q_head = jnp.where(mine, q_pair, jnp.zeros_like(q_pair))
            do_head = jnp.where(mine, do_pair, jnp.zeros_like(do_pair))
            h = 2 * j + g
            lse = lse_all[:, h : h + 1]
            probs, grads, total = [], [], 0.0
            for s in range(ctx):
                p = jnp.exp(mul(q_head, keys[s][...], NT) + (biases[s] - lse))
                dp = mul(do_head, values[s][...], NT)
                total = total + (p * dp).sum(-1, keepdims=True)
                probs.append(p)
                grads.append(dp)
            dq = 0.0
            for s in range(ctx):
                ds = (probs[s] * (grads[s] - total)).astype(jnp.bfloat16)
                dv_sum[s] += mul(probs[s].astype(jnp.bfloat16), do_head, TN)
                dk_sum[s] += mul(ds, q_head, TN)
                dq = dq + mul(ds, keys[s][...])
            dqs.append(dq)
        dq = jnp.where(lane < HD, dqs[0], dqs[1]) * score_scale
        dq = dq * cos_ref[...] + turn(dq * sin_ref[...], -1.0)
        dq_ref[:, j * 128 : (j + 1) * 128] = dq.astype(jnp.bfloat16)
    for s in range(ctx):
        dkv_ref[s, 0] = dk_sum[s].astype(dkv_ref.dtype)
        dkv_ref[s, 1] = dv_sum[s].astype(dkv_ref.dtype)


def cot_kernel(dims, local_rows, len_ref, cot_ref, ff_ref):
    rows = cot_ref.shape[0]
    back = cot_ref[...].astype(jnp.float32) * row_valid(len_ref, rows, local_rows)
    ff_ref[...] = reorder((residual_scale * back).astype(jnp.bfloat16), *dims)


def middle_kernel(dims, x_ref, part_ref, other_ref, gain_ref, middle_ref, normed_ref):
    branch = part_ref[...].astype(jnp.float32) + other_ref[...].astype(jnp.float32)
    middle = reorder(x_ref[...].astype(jnp.float32), *dims) + residual_scale * branch
    middle_ref[...] = middle
    normed_ref[...] = (middle * rms_scale(middle) * gain_ref[...]).astype(jnp.bfloat16)


def middle_back_kernel(
    dims, local_rows, len_ref, cot_ref, middle_ref, grad_ref, gain_ref, back_ref, attn_ref, gain_sum
):
    rows = cot_ref.shape[0]
    back = cot_ref[...].astype(jnp.float32) * row_valid(len_ref, rows, local_rows)
    middle = middle_ref[...]
    grad = grad_ref[...].astype(jnp.float32)
    scale = rms_scale(middle)
    out = reorder(back, *dims) + norm_back(grad, middle, scale, gain_ref[...])
    back_ref[...] = out
    attn_ref[...] = (residual_scale * out).astype(jnp.bfloat16)

    @pl.when(pl.program_id(0) == 0)
    def _():
        gain_sum[...] = jnp.zeros_like(gain_sum)

    gain_sum[...] += (grad * middle * scale).sum(0, keepdims=True)


def output_kernel(dims, local_rows, len_ref, middle_ref, ff_ref, out_ref):
    rows = middle_ref.shape[0]
    out = middle_ref[...] + residual_scale * ff_ref[...].astype(jnp.float32)
    out = (out * row_valid(len_ref, rows, local_rows)).astype(jnp.bfloat16)
    out_ref[...] = reorder(out, *dims)


def input_back_kernel(
    dims, x_ref, part_ref, other_ref, back_ref, gain_ref, out_ref, gain_sum
):
    first, second, width = dims
    x = reorder(x_ref[...].astype(jnp.float32), *dims)
    grad = (part_ref[...].astype(jnp.float32) + other_ref[...].astype(jnp.float32))
    scale = rms_scale(x)
    out = back_ref[...] + norm_back(grad, x, scale, gain_ref[...])
    out_ref[...] = reorder(out.astype(jnp.bfloat16), second, first, width)

    @pl.when(pl.program_id(0) == 0)
    def _():
        gain_sum[...] = jnp.zeros_like(gain_sum)

    gain_sum[...] += (grad * x * scale).sum(0, keepdims=True)


def by_rows(kernel, rows, ins, outs, flops=0, limit=40):
    total = max(v.shape[0] for v, kind in ins if kind == "rows")
    in_specs = []
    moved = 0
    for v, kind in ins:
        moved += v.size * v.dtype.itemsize
        if kind == "rows":
            in_specs.append(pl.BlockSpec((rows, v.shape[1]), lambda i: (i, 0)))
        elif kind == "cycle":
            period = v.shape[0] // rows
            in_specs.append(
                pl.BlockSpec((rows, v.shape[1]), lambda i, period=period: (lax.rem(i, period), 0))
            )
        elif kind == "smem":
            in_specs.append(pl.BlockSpec(memory_space=SMEM))
        else:
            in_specs.append(
                pl.BlockSpec(v.shape, lambda i: (0, 0), pipeline_mode=pl.Buffered(1))
            )
    out_specs = []
    for shape, dtype in outs:
        moved += shape[0] * shape[1] * jnp.dtype(dtype).itemsize
        if shape[0] == 1:
            out_specs.append(pl.BlockSpec(shape, lambda i: (0, 0)))
        else:
            out_specs.append(pl.BlockSpec((rows, shape[1]), lambda i: (i, 0)))
    return pl.pallas_call(
        kernel,
        grid=(total // rows,),
        in_specs=in_specs,
        out_specs=out_specs,
        out_shape=[jax.ShapeDtypeStruct(shape, dtype) for shape, dtype in outs],
        compiler_params=pltpu.CompilerParams(vmem_limit_bytes=limit * 1024 * 1024),
        cost_estimate=pl.CostEstimate(flops=flops, bytes_accessed=moved, transcendentals=0),
    )(*[v for v, _ in ins])


def kv_specs(ctx, rows, pairs):
    def spec(slot, start):
        return pl.BlockSpec((None, rows, 128), lambda s, p: (slot, s, start + p))

    return [spec(slot, start) for start in (0, pairs) for slot in range(ctx)]


def attend(lengths, query, kv_all):
    ctx = kv_all.shape[0]
    seqs = lengths.shape[0]
    rows = query.shape[0] // seqs
    pairs = kv_all.shape[2] // 256
    wide = query.shape[1] // pairs
    flops = 4 * query.shape[0] * query.shape[1] * rows * ctx
    return pl.pallas_call(
        partial(attend_kernel, ctx),
        grid=(seqs, pairs),
        in_specs=[
            pl.BlockSpec(memory_space=SMEM),
            pl.BlockSpec((rows, wide), lambda s, p: (s, p)),
        ]
        + kv_specs(ctx, rows, pairs),
        out_specs=[
            pl.BlockSpec((rows, wide), lambda s, p: (s, p)),
            pl.BlockSpec((rows, 128), lambda s, p: (s, p)),
        ],
        out_shape=[
            jax.ShapeDtypeStruct(query.shape, jnp.bfloat16),
            jax.ShapeDtypeStruct((query.shape[0], 128 * pairs), jnp.float32),
        ],
        compiler_params=pltpu.CompilerParams(vmem_limit_bytes=40 * 1024 * 1024),
        cost_estimate=pl.CostEstimate(flops=4 * flops, bytes_accessed=6 << 20, transcendentals=0),
    )(lengths, query, *[kv_all] * (2 * ctx))


def attend_back(lengths, query, out_grad, lse, cosines, sines, kv_all):
    ctx = kv_all.shape[0]
    seqs = lengths.shape[0]
    rows = query.shape[0] // seqs
    pairs = kv_all.shape[2] // 256
    wide = query.shape[1] // pairs
    flops = 10 * query.shape[0] * query.shape[1] * rows * ctx
    return pl.pallas_call(
        partial(attend_back_kernel, ctx),
        grid=(seqs, pairs),
        in_specs=[
            pl.BlockSpec(memory_space=SMEM),
            pl.BlockSpec((rows, wide), lambda s, p: (s, p)),
            pl.BlockSpec((rows, wide), lambda s, p: (s, p)),
            pl.BlockSpec((rows, 128), lambda s, p: (s, p)),
            pl.BlockSpec((rows, 128), lambda s, p: (0, 0)),
            pl.BlockSpec((rows, 128), lambda s, p: (0, 0)),
        ]
        + kv_specs(ctx, rows, pairs),
        out_specs=[
            pl.BlockSpec((rows, wide), lambda s, p: (s, p)),
            pl.BlockSpec((ctx, 2, rows, 128), lambda s, p: (0, 0, s, p)),
        ],
        out_shape=[
            jax.ShapeDtypeStruct(query.shape, jnp.bfloat16),
            jax.ShapeDtypeStruct((ctx, 2, query.shape[0], 128 * pairs), jnp.bfloat16),
        ],
        scratch_shapes=[pltpu.VMEM((ctx, rows, 128), jnp.float32)] * 2,
        compiler_params=pltpu.CompilerParams(vmem_limit_bytes=40 * 1024 * 1024),
        cost_estimate=pl.CostEstimate(flops=4 * flops, bytes_accessed=10 << 20, transcendentals=0),
    )(lengths, query, out_grad, lse, cosines, sines, *[kv_all] * (2 * ctx))


def low_bit(k):
    return k & -k


def high_bit(k):
    return 1 << (k.bit_length() - 1)


def fsdp_order(fsdp):
    return sorted(range(1, fsdp), key=lambda k: (bin(k).count("1"), k))


def flip_index(me, k, fsdp):
    out = me
    for i in range(fsdp.bit_length() - 1):
        b = 1 << i
        if k & b:
            out = out + b - 2 * b * lax.rem(me // b, 2)
    return out


def line_neighbours(me, count):
    return (me > 0).astype(jnp.int32) + (me < count - 1).astype(jnp.int32)


def line_kernel(fsdp, ctx, group, lines, swaps, spots, *refs):
    line_in = refs[:lines]
    swap_in = refs[lines : lines + swaps]
    line_out = refs[lines + swaps : 2 * lines + swaps]
    swap_out = refs[2 * lines + swaps : -5]
    own_sem, z_send, z_recv, f_send, f_recv = refs[-5:]
    me_f = lax.axis_index("fsdp")
    me_c = lax.axis_index("ctx")
    me_t = lax.axis_index("tp")

    def along(step, act):
        there = me_c + step

        @pl.when((there >= 0) & (there < ctx))
        def _():
            act(there)

    barrier = pltpu.get_barrier_semaphore()
    for k in range(1, group):
        pl.semaphore_signal(
            barrier, inc=1, device_id=(flip_index(me_f, k, fsdp), me_c, me_t), device_id_type=MESH_ID
        )
    for step in (-1, 1):
        along(
            step,
            lambda there: pl.semaphore_signal(
                barrier, inc=1, device_id=(me_f, there, me_t), device_id_type=MESH_ID
            ),
        )
    pl.semaphore_wait(barrier, group - 1 + line_neighbours(me_c, ctx))

    def z_copy(i, shard, step, src=None):
        place = line_out[i].at[shard]
        way = 0 if step > 0 else 1
        return pltpu.make_async_remote_copy(
            src_ref=place if src is None else src,
            dst_ref=place,
            send_sem=z_send.at[i, way, shard],
            recv_sem=z_recv.at[i, way, shard],
            device_id=(me_f, me_c + step, me_t),
            device_id_type=MESH_ID,
        )

    def landing(i, f):
        out, start = spots[i]
        width = swap_in[i].shape[1] // group
        return swap_out[out].at[lax.rem(f, group), :, pl.ds(start, width)]

    def columns(i, f):
        width = swap_in[i].shape[1] // group
        return swap_in[i].at[:, pl.ds(pl.multiple_of(lax.rem(f, group) * width, 128), width)]

    def f_copy(i, k):
        there = flip_index(me_f, k, fsdp)
        return pltpu.make_async_remote_copy(
            src_ref=columns(i, there),
            dst_ref=landing(i, me_f),
            send_sem=f_send.at[i, k],
            recv_sem=f_recv.at[i, k],
            device_id=(there, me_c, me_t),
            device_id_type=MESH_ID,
        )

    def f_arrival(i, k):
        there = flip_index(me_f, k, fsdp)
        return pltpu.make_async_remote_copy(
            src_ref=landing(i, there),
            dst_ref=landing(i, there),
            send_sem=f_send.at[i, k],
            recv_sem=f_recv.at[i, k],
            device_id=(there, me_c, me_t),
            device_id_type=MESH_ID,
        )

    for i in range(lines):
        for step in (1, -1):
            along(step, lambda there: z_copy(i, me_c, step, line_in[i]).start())
    order = fsdp_order(group)
    for i in range(swaps):
        for k in order:
            f_copy(i, k).start()
    own = [
        pltpu.make_async_copy(line_in[i], line_out[i].at[me_c], own_sem.at[i])
        for i in range(lines)
    ] + [
        pltpu.make_async_copy(columns(i, me_f), landing(i, me_f), own_sem.at[lines + i])
        for i in range(swaps)
    ]
    for copy in own:
        copy.start()
    for distance in range(1, ctx):
        for i in range(lines):
            for step in (1, -1):
                shard = me_c - step * distance

                @pl.when((shard >= 0) & (shard < ctx))
                def _():
                    z_copy(i, shard, step).wait_recv()
                    along(step, lambda there: z_copy(i, shard, step).start())

    for i in range(swaps):
        for k in order:
            f_arrival(i, k).wait_recv()
            f_copy(i, k).wait_send()
    for copy in own:
        copy.wait()
    for i in range(lines):
        for step in (1, -1):
            along(step, lambda there: z_copy(i, me_c, step, line_in[i]).wait_send())
            for distance in range(1, ctx - 1):
                shard = me_c - step * distance

                @pl.when((shard >= 0) & (shard < ctx))
                def _():
                    along(step, lambda there: z_copy(i, shard, step).wait_send())


def start_exchange(fsdp, ctx, group, lines, swap_sets):
    sems = pltpu.SemaphoreType.DMA
    out_shape = [jax.ShapeDtypeStruct((ctx,) + v.shape, v.dtype) for v in lines]
    swaps, spots = [], []
    for out, arrays in enumerate(swap_sets):
        start = 0
        for v in arrays:
            spots.append((out, start))
            swaps.append(v)
            start += v.shape[1] // group
        out_shape.append(
            jax.ShapeDtypeStruct((group, arrays[0].shape[0], start), arrays[0].dtype)
        )
    count = len(lines) + len(swaps)
    outs = pl.pallas_call(
        partial(line_kernel, fsdp, ctx, group, len(lines), len(swaps), spots),
        out_shape=out_shape,
        in_specs=[pl.BlockSpec(memory_space=pltpu.VMEM)] * count,
        out_specs=[pl.BlockSpec(memory_space=pl.ANY)] * len(out_shape),
        scratch_shapes=[
            sems((count,)),
            sems((len(lines), 2, ctx)),
            sems((len(lines), 2, ctx)),
            sems((len(swaps), group)),
            sems((len(swaps), group)),
        ],
        compiler_params=pltpu.CompilerParams(
            collective_id=0, has_side_effects=True, vmem_limit_bytes=24 * 1024 * 1024
        ),
    )(*lines, *swaps)
    return outs[: len(lines)], outs[len(lines) :]


class TokenGather:
    def __init__(self, group, fsdp, v_ref, out_ref, own_sem, f_send, f_recv, t_send, t_recv):
        self.order = fsdp_order(group)
        self.bits = [1 << i for i in range(group.bit_length() - 1)]
        self.out_ref = out_ref
        self.sems = (f_send, f_recv, t_send, t_recv)
        self.fsdp = fsdp
        half = out_ref.shape[2]
        self.half = half
        me_t = lax.axis_index("tp")
        self.mine = v_ref.at[pl.ds(pl.multiple_of(me_t * half, half), half)]
        other = v_ref.at[pl.ds(pl.multiple_of((1 - me_t) * half, half), half)]
        self.own = [
            pltpu.make_async_copy(self.mine, out_ref.at[0, 0], own_sem.at[0]),
            pltpu.make_async_copy(other, out_ref.at[0, 1], own_sem.at[1]),
        ]

    def peer(self, k):
        me_f = lax.axis_index("fsdp")
        return (flip_index(me_f, k, self.fsdp), lax.axis_index("ctx"), lax.axis_index("tp"))

    def rows(self, k, part):
        if k == low_bit(k):
            return pl.ds(0, self.half)
        return pl.ds(part * (self.half // 2), self.half // 2)

    def f_copy(self, have, b):
        k = have | b
        part = 1 if have and b == high_bit(k) else 0
        place = self.out_ref.at[k, 0, self.rows(k, part)]
        src = self.out_ref.at[have, 0, self.rows(k, part)] if have else self.mine
        return pltpu.make_async_remote_copy(
            src_ref=src,
            dst_ref=place,
            send_sem=self.sems[0].at[k, part],
            recv_sem=self.sems[1].at[k, part],
            device_id=self.peer(b),
            device_id_type=MESH_ID,
        )

    def ways(self, have):
        return [
            b
            for b in self.bits
            if not have & b and (not have or b in (low_bit(have | b), high_bit(have | b)))
        ]

    def swap(self, k):
        me_f, me_c, me_t = self.peer(0)
        return pltpu.make_async_remote_copy(
            src_ref=self.out_ref.at[k, 0],
            dst_ref=self.out_ref.at[k, 1],
            send_sem=self.sems[2].at[k],
            recv_sem=self.sems[3].at[k],
            device_id=(me_f, me_c, 1 - me_t),
            device_id_type=MESH_ID,
        )

    def start(self):
        for b in self.ways(0):
            self.f_copy(0, b).start()
        for copy in self.own:
            copy.start()

    def relay(self, k):
        parts = [(0, k)] if k == low_bit(k) else [(0, low_bit(k)), (1, high_bit(k))]
        for part, b in parts:
            place = self.out_ref.at[k, 0, self.rows(k, part)]
            pltpu.make_async_remote_copy(
                src_ref=place,
                dst_ref=place,
                send_sem=self.sems[0].at[k, part],
                recv_sem=self.sems[1].at[k, part],
                device_id=self.peer(b),
                device_id_type=MESH_ID,
            ).wait_recv()
        for b in self.ways(k):
            self.f_copy(k, b).start()
        self.swap(k).start()

    def finish(self):
        for copy in self.own:
            copy.wait()
        for have in [0] + self.order:
            for b in self.ways(have):
                self.f_copy(have, b).wait_send()
        me_f, me_c, me_t = self.peer(0)
        for k in self.order:
            pltpu.make_async_remote_copy(
                src_ref=self.out_ref.at[k, 1],
                dst_ref=self.out_ref.at[k, 1],
                send_sem=self.sems[2].at[k],
                recv_sem=self.sems[3].at[k],
                device_id=(me_f, me_c, 1 - me_t),
                device_id_type=MESH_ID,
            ).wait_recv()
            self.swap(k).wait_send()


def token_sems(group):
    sems = pltpu.SemaphoreType.DMA
    return [sems((2,)), sems((group, 2)), sems((group, 2)), sems((group,)), sems((group,))]


def token_shape(group, v):
    return jax.ShapeDtypeStruct((group, 2, v.shape[0] // 2, v.shape[1]), v.dtype)


def tokens_kernel(group, fsdp, v_ref, out_ref, *sems):
    gather = TokenGather(group, fsdp, v_ref, out_ref, *sems)
    me_f, me_c, me_t = gather.peer(0)
    barrier = pltpu.get_barrier_semaphore()
    for b in gather.bits:
        pl.semaphore_signal(barrier, inc=1, device_id=gather.peer(b), device_id_type=MESH_ID)
    pl.semaphore_signal(
        barrier, inc=1, device_id=(me_f, me_c, 1 - me_t), device_id_type=MESH_ID
    )
    pl.semaphore_wait(barrier, len(gather.bits) + 1)
    gather.start()
    for k in gather.order:
        gather.relay(k)
    gather.finish()


def gather_tokens(group, fsdp, v):
    out = pl.pallas_call(
        partial(tokens_kernel, group, fsdp),
        out_shape=token_shape(group, v),
        in_specs=[pl.BlockSpec(memory_space=pltpu.VMEM)],
        out_specs=pl.BlockSpec(memory_space=pl.ANY),
        scratch_shapes=token_sems(group),
        compiler_params=pltpu.CompilerParams(
            collective_id=5, has_side_effects=True, vmem_limit_bytes=24 * 1024 * 1024
        ),
    )(v)
    return out.reshape(-1, v.shape[1])


def swiglu_kernel(
    fsdp,
    group,
    n_ref,
    g_ref,
    both_ref,
    down_ref,
    hidden_ref,
    grads_ref,
    ff_ref,
    own_ref,
    s_out,
    f_out,
    s_in,
    f_in,
    total,
    got,
    t_send,
    t_recv,
    f_send,
    f_recv,
    own_sem,
):
    half = n_ref.shape[0]
    units = hidden_ref.shape[1]
    step = pl.program_id(0)
    me_f = lax.axis_index("fsdp")
    me_c = lax.axis_index("ctx")
    me_t = lax.axis_index("tp")
    bits = [1 << i for i in range(group.bit_length() - 1)]
    order = fsdp_order(group)
    core = (me_f, me_c, 1 - me_t)

    def peer(k):
        return (flip_index(me_f, k, fsdp), me_c, me_t)

    @pl.when(step == 0)
    def _():
        barrier = pltpu.get_barrier_semaphore()
        for b in bits:
            pl.semaphore_signal(barrier, inc=1, device_id=peer(b), device_id_type=MESH_ID)
        pl.semaphore_signal(barrier, inc=1, device_id=core, device_id_type=MESH_ID)
        pl.semaphore_wait(barrier, len(bits) + 1)

    def core_copies(k):
        slot = k % 2
        return [
            pltpu.make_async_remote_copy(
                src_ref=out.at[slot],
                dst_ref=into.at[slot],
                send_sem=t_send.at[which, k],
                recv_sem=t_recv.at[which, k],
                device_id=core,
                device_id_type=MESH_ID,
            )
            for which, (out, into) in enumerate(((s_out, s_in), (f_out, f_in)))
        ]

    def ways(k):
        return [(0, k)] if k == low_bit(k) else [(0, low_bit(k)), (1, high_bit(k))]

    def span(k, part):
        return pl.ds(0, half) if k == low_bit(k) else pl.ds(part * (half // 2), half // 2)

    def f_copy(k, part, b):
        return pltpu.make_async_remote_copy(
            src_ref=total.at[k, span(k, part)],
            dst_ref=got.at[k, span(k, part)],
            send_sem=f_send.at[k, part],
            recv_sem=f_recv.at[k, part],
            device_id=peer(b),
            device_id_type=MESH_ID,
        )

    def own_copy():
        return pltpu.make_async_remote_copy(
            src_ref=total.at[0],
            dst_ref=own_ref.at[me_t],
            send_sem=own_sem.at[0],
            recv_sem=own_sem.at[1],
            device_id=core,
            device_id_type=MESH_ID,
        )

    lin = mul(n_ref[...], both_ref[...])
    gate, up = lin[:, :units], lin[:, units:]
    sig = jax.nn.sigmoid(gate)
    act = gate * sig
    hidden = (act * up).astype(jnp.bfloat16)
    hidden_ref[...] = hidden
    hidden_grad = mul(g_ref[...], down_ref[...])
    grads_ref[:, :units] = (hidden_grad * up * sig * (1.0 + gate * (1.0 - sig))).astype(
        jnp.bfloat16
    )
    grads_ref[:, units:] = (hidden_grad * act).astype(jnp.bfloat16)
    second = mul(grads_ref[...], both_ref[...], NT)
    ff = mul(hidden, down_ref[...], NT)

    for k in reversed(range(group)):
        slot = k % 2

        @pl.when(step == 2 * (group - 1 - k))
        def _():
            if k + 2 < group:
                for copy in core_copies(k + 2):
                    copy.wait_send()
            s_out[slot] = second.astype(jnp.bfloat16)
            f_out[slot] = ff.astype(jnp.bfloat16)
            for copy in core_copies(k):
                copy.start()

        @pl.when(step == 2 * (group - 1 - k) + 1)
        def _():
            for copy in core_copies(k):
                copy.wait_recv()
            ff_ref[...] = (ff + f_in[slot].astype(jnp.float32)).astype(jnp.bfloat16)
            total[k] = (second + s_in[slot].astype(jnp.float32)).astype(jnp.bfloat16)
            for far in order:
                for part, b in ways(far):
                    if far ^ b == k:
                        f_copy(far, part, b).wait_recv()
                        rows = span(far, part)
                        total[k, rows] = (
                            total[k, rows].astype(jnp.float32)
                            + got[far, rows].astype(jnp.float32)
                        ).astype(jnp.bfloat16)
            if k:
                for part, b in ways(k):
                    f_copy(k, part, b).start()
            else:
                own_copy().start()
                local = pltpu.make_async_copy(total.at[0], own_ref.at[me_t], own_sem.at[2])
                local.start()
                local.wait()
                other = own_ref.at[1 - me_t]
                pltpu.make_async_remote_copy(
                    src_ref=other,
                    dst_ref=other,
                    send_sem=own_sem.at[0],
                    recv_sem=own_sem.at[1],
                    device_id=core,
                    device_id_type=MESH_ID,
                ).wait_recv()
                own_copy().wait_send()
                for far in order:
                    for part, b in ways(far):
                        f_copy(far, part, b).wait_send()
                for late in range(min(2, group)):
                    for copy in core_copies(late):
                        copy.wait_send()


def swiglu(fsdp, group, normed, grads, both, down):
    many, width = normed.shape
    half = many // (2 * group)
    units = down.shape[1]
    low = jnp.bfloat16
    last = 2 * group - 1
    sems = pltpu.SemaphoreType.DMA
    block = (half, width)

    def rows(cols):
        return pl.BlockSpec((half, cols), lambda i: (last - i, 0))

    def whole(v):
        return pl.BlockSpec(v.shape, lambda i: (0, 0), pipeline_mode=pl.Buffered(1))

    return pl.pallas_call(
        partial(swiglu_kernel, fsdp, group),
        grid=(2 * group,),
        in_specs=[rows(width), rows(width), whole(both), whole(down)],
        out_specs=[
            rows(units),
            rows(2 * units),
            pl.BlockSpec(block, lambda i: (group - 1 - i // 2, 0)),
            pl.BlockSpec(memory_space=pl.ANY),
        ],
        out_shape=[
            jax.ShapeDtypeStruct((many, units), low),
            jax.ShapeDtypeStruct((many, 2 * units), low),
            jax.ShapeDtypeStruct((group * half, width), low),
            jax.ShapeDtypeStruct((2,) + block, low),
        ],
        scratch_shapes=[pltpu.VMEM((2,) + block, low)] * 4
        + [pltpu.VMEM((group,) + block, low)] * 2
        + [
            sems((2, group)),
            sems((2, group)),
            sems((group, 2)),
            sems((group, 2)),
            sems((3,)),
        ],
        compiler_params=pltpu.CompilerParams(
            collective_id=6, has_side_effects=True, vmem_limit_bytes=58 * 1024 * 1024
        ),
        cost_estimate=pl.CostEstimate(
            flops=12 * many * width * units, bytes_accessed=50 << 20, transcendentals=0
        ),
    )(normed, grads, both, down)


def spread_kernel(fsdp, ctx, group, count, chain, *refs):
    ins = refs[:count]
    outs = refs[count + chain : 2 * count + chain]
    sems = refs[2 * (count + chain) :]
    own_sem, f_send, f_recv, c_own, c_send, c_recv = sems[:6]
    me_f = lax.axis_index("fsdp")
    me_c = lax.axis_index("ctx")
    me_t = lax.axis_index("tp")
    bits = [1 << i for i in range(fsdp.bit_length() - 1)]
    order = fsdp_order(fsdp)

    def peer(k):
        return (flip_index(me_f, k, fsdp), me_c, me_t)

    barrier = pltpu.get_barrier_semaphore()
    for b in bits:
        pl.semaphore_signal(barrier, inc=1, device_id=peer(b), device_id_type=MESH_ID)
    if chain:
        chain_in, chain_out = refs[count], refs[2 * count + chain]
        gather = TokenGather(
            group, fsdp, refs[count + 1], refs[2 * count + chain + 1], *sems[6:]
        )
        pl.semaphore_signal(
            barrier, inc=1, device_id=(me_f, me_c, 1 - me_t), device_id_type=MESH_ID
        )
        for step in (-1, 1):
            there = me_c + step

            @pl.when((there >= 0) & (there < ctx))
            def _():
                pl.semaphore_signal(
                    barrier, inc=1, device_id=(me_f, there, me_t), device_id_type=MESH_ID
                )

        pl.semaphore_wait(barrier, len(bits) + 1 + line_neighbours(me_c, ctx))
    else:
        pl.semaphore_wait(barrier, len(bits))

    def quarters(rows):
        return [pl.ds(i * (rows // 4), rows // 4) for i in range(4)]

    def climb(s):
        return [
            pltpu.make_async_remote_copy(
                src_ref=chain_out.at[s, part] if s else chain_in.at[part],
                dst_ref=chain_out.at[s + 1, part],
                send_sem=c_send.at[s, i],
                recv_sem=c_recv.at[s + 1, i],
                device_id=(me_f, me_c + 1, me_t),
                device_id_type=MESH_ID,
            )
            for i, part in enumerate(quarters(chain_in.shape[0]))
        ]

    def keep(s):
        return pltpu.make_async_copy(chain_in, chain_out.at[s], c_own.at[s])

    def send_up(s):
        @pl.when((me_c >= s) & (me_c < ctx - 1))
        def _():
            for copy in climb(s):
                copy.start()

    def take_up(s):
        @pl.when(me_c >= s)
        def _():
            for i, part in enumerate(quarters(chain_in.shape[0])):
                pltpu.make_async_remote_copy(
                    src_ref=chain_out.at[s, part],
                    dst_ref=chain_out.at[s, part],
                    send_sem=c_send.at[s - 1, i],
                    recv_sem=c_recv.at[s, i],
                    device_id=(me_f, me_c - 1, me_t),
                    device_id_type=MESH_ID,
                ).wait_recv()

        if s < ctx - 1:
            send_up(s)

    if chain:
        send_up(0)
        keep(0).start()
        for s in range(1, ctx):
            @pl.when(me_c < s)
            def _():
                keep(s).start()

    def place(i, shard, have, k, part):
        block = outs[i].at[shard, flip_index(me_f, have, fsdp)]
        half = ins[i].shape[1] // 2
        return block if k == low_bit(k) else block.at[pl.ds(part * half, half)]

    def f_copy(i, shard, have, b):
        k = have | b
        part = 1 if have and b == high_bit(k) else 0
        block = place(i, shard, have, k, part)
        return pltpu.make_async_remote_copy(
            src_ref=block if have else ins[i].at[shard],
            dst_ref=block,
            send_sem=f_send.at[i, shard, k, part],
            recv_sem=f_recv.at[i, shard, k, part],
            device_id=peer(b),
            device_id_type=MESH_ID,
        )

    def ways(have):
        return [
            b
            for b in bits
            if not have & b and (not have or b in (low_bit(have | b), high_bit(have | b)))
        ]

    own = [
        pltpu.make_async_copy(ins[i], outs[i].at[:, me_f], own_sem.at[i]) for i in range(count)
    ]
    for i in range(count):
        for shard in range(ctx):
            for b in ways(0):
                f_copy(i, shard, 0, b).start()
        own[i].start()
    if chain:
        gather.start()
    climbed = 1
    for i in range(count):
        for k in order:
            if chain and climbed < ctx:
                take_up(climbed)
                climbed += 1
            if chain and k < group and i == 0:
                gather.relay(k)
            parts = [(0, k)] if k == low_bit(k) else [(0, low_bit(k)), (1, high_bit(k))]
            for shard in range(ctx):
                for part, b in parts:
                    block = place(i, shard, k, k, part)
                    pltpu.make_async_remote_copy(
                        src_ref=block,
                        dst_ref=block,
                        send_sem=f_send.at[i, shard, k, part],
                        recv_sem=f_recv.at[i, shard, k, part],
                        device_id=peer(b),
                        device_id_type=MESH_ID,
                    ).wait_recv()
                for b in ways(k):
                    f_copy(i, shard, k, b).start()
    if chain:
        for s in range(climbed, ctx):
            take_up(s)
        gather.finish()
        keep(0).wait()
        for s in range(ctx):
            if s:

                @pl.when(me_c < s)
                def _():
                    keep(s).wait()

            if s < ctx - 1:

                @pl.when((me_c >= s) & (me_c < ctx - 1))
                def _():
                    for copy in climb(s):
                        copy.wait_send()

    for i in range(count):
        own[i].wait()
        for have in [0] + order:
            for shard in range(ctx):
                for b in ways(have):
                    f_copy(i, shard, have, b).wait_send()


def spread_weights(fsdp, ctx, group, arrays, chain=()):
    count = len(arrays)
    sems = pltpu.SemaphoreType.DMA
    outs = pl.pallas_call(
        partial(spread_kernel, fsdp, ctx, group, count, len(chain)),
        out_shape=[
            jax.ShapeDtypeStruct((ctx, fsdp) + v.shape[1:], v.dtype) for v in arrays
        ]
        + [jax.ShapeDtypeStruct((ctx,) + v.shape, v.dtype) for v in chain[:1]]
        + [token_shape(group, v) for v in chain[1:]],
        in_specs=[pl.BlockSpec(memory_space=pltpu.VMEM)] * (count + len(chain)),
        out_specs=[pl.BlockSpec(memory_space=pl.ANY)] * (count + len(chain)),
        scratch_shapes=[
            sems((count,)),
            sems((count, ctx, fsdp, 2)),
            sems((count, ctx, fsdp, 2)),
            sems((ctx,)),
            sems((ctx, 4)),
            sems((ctx, 4)),
        ]
        + (token_sems(group) if chain else []),
        compiler_params=pltpu.CompilerParams(
            collective_id=3 if chain else 1,
            has_side_effects=True,
            vmem_limit_bytes=24 * 1024 * 1024,
        ),
    )(*arrays, *chain)
    return (
        [o.reshape(-1, v.shape[-1]) for o, v in zip(outs, arrays)]
        + list(outs[count : count + 1])
        + [o.reshape(-1, o.shape[-1]) for o in outs[count + 1 :]]
    )


def sum_kernel(fsdp, ctx, group, count, chain, *refs):
    weights = count - 1 if chain else count
    ins = refs[:count]
    if chain:
        parts_ref, cos_ref, sin_ref = refs[count : count + 3]
        refs = refs[:count] + refs[count + 3 :]
        kv_ref = refs[2 * count]
        refs = refs[: 2 * count] + refs[2 * count + 1 :]
    outs = refs[count : 2 * count]
    held = refs[2 * count : 3 * count]
    got = refs[3 * count : 4 * count]
    line = refs[4 * count : 4 * count + weights]
    refs = refs[4 * count + weights :]
    in_sem, f_send, f_recv, z_send, z_recv = refs[:5]
    if chain:
        kv_parts, kv_got, kv_sem, c_send, c_recv = refs[5:]
    me_f = lax.axis_index("fsdp")
    me_c = lax.axis_index("ctx")
    me_t = lax.axis_index("tp")
    bits = [1 << i for i in range(fsdp.bit_length() - 1)]
    order = fsdp_order(fsdp)
    near = fsdp_order(group)

    def steps_of(i):
        return order if i < weights else near

    def shards_of(i):
        return shards if i < weights else [0]

    def peer(k):
        return (flip_index(me_f, k, fsdp), me_c, me_t)

    def along(step, act):
        there = me_c + step

        @pl.when((there >= 0) & (there < ctx))
        def _():
            act(there)

    loads = {}
    if chain:
        kv_load = pltpu.make_async_copy(parts_ref, kv_parts, kv_sem.at[0])
        kv_load.start()
    for i in range(count):
        for k in reversed([0] + steps_of(i)):
            block = ins[i].at[:, flip_index(me_f, k, fsdp)] if i < weights else ins[i].at[k]
            loads[i, k] = pltpu.make_async_copy(block, held[i].at[k], in_sem.at[i, k])
            loads[i, k].start()

    barrier = pltpu.get_barrier_semaphore()
    for b in bits:
        pl.semaphore_signal(barrier, inc=1, device_id=peer(b), device_id_type=MESH_ID)
    for step in (-1, 1):
        along(
            step,
            lambda there: pl.semaphore_signal(
                barrier, inc=1, device_id=(me_f, there, me_t), device_id_type=MESH_ID
            ),
        )
    pl.semaphore_wait(barrier, len(bits) + line_neighbours(me_c, ctx))

    def ways(k):
        return [(0, k)] if k == low_bit(k) else [(0, low_bit(k)), (1, high_bit(k))]

    def piece(i, k, part):
        rows = ins[i].shape[2]
        return pl.ds(0, rows) if k == low_bit(k) else pl.ds(part * (rows // 2), rows // 2)

    def f_copy(i, shard, k, part, b):
        span = piece(i, k, part)
        return pltpu.make_async_remote_copy(
            src_ref=held[i].at[k, shard, span],
            dst_ref=got[i].at[k, shard, span],
            send_sem=f_send.at[i, shard, k, part],
            recv_sem=f_recv.at[i, shard, k, part],
            device_id=peer(b),
            device_id_type=MESH_ID,
        )

    def add(into, other):
        tile = 16 if into.dtype == jnp.bfloat16 else 8

        def body(r, _):
            span = pl.ds(pl.multiple_of(r * tile, tile), tile)
            into[span] = (
                into[span].astype(jnp.float32) + other[span].astype(jnp.float32)
            ).astype(into.dtype)
            return 0

        lax.fori_loop(0, into.shape[0] // tile, body, 0)

    def collect(i, shard, k):
        for far in steps_of(i):
            for part, b in ways(far):
                if far ^ b == k:
                    f_copy(i, shard, far, part, b).wait_recv()
                    span = piece(i, far, part)
                    add(held[i].at[k, shard, span], got[i].at[far, shard, span])

    def z_copy(i, shard, step):
        way = 0 if step > 0 else 1
        return pltpu.make_async_remote_copy(
            src_ref=held[i].at[0, shard],
            dst_ref=line[i].at[way, shard],
            send_sem=z_send.at[i, way, shard],
            recv_sem=z_recv.at[i, way, shard],
            device_id=(me_f, me_c + step, me_t),
            device_id_type=MESH_ID,
        )

    def give(i, shard):
        def body(r, _):
            span = pl.ds(pl.multiple_of(r * 16, 16), 16)
            outs[i][span] = held[i][0, shard, span].astype(outs[i].dtype)
            return 0

        lax.fori_loop(0, outs[i].shape[0] // 16, body, 0)

    def on_line(i, shard, step):
        way = 0 if step > 0 else 1

        @pl.when((me_c - step >= 0) & (me_c - step < ctx))
        def _():
            z_copy(i, shard, step).wait_recv()
            add(held[i].at[0, shard], line[i].at[way, shard])

        @pl.when(step * (shard - me_c) > 0)
        def _():
            z_copy(i, shard, step).start()

    def quarters():
        rows = kv_parts.shape[2] // 2
        return [(side, pl.ds(i * rows, rows)) for side in range(2) for i in range(2)]

    def descend(s):
        return [
            pltpu.make_async_remote_copy(
                src_ref=kv_parts.at[s, side, part],
                dst_ref=kv_got.at[s - 1, side, part],
                send_sem=c_send.at[s, i],
                recv_sem=c_recv.at[s - 1, i],
                device_id=(me_f, me_c - 1, me_t),
                device_id_type=MESH_ID,
            )
            for i, (side, part) in enumerate(quarters())
        ]

    def chain_step(s):
        if s < ctx - 1:

            @pl.when((me_c >= s) & (me_c < ctx - 1))
            def _():
                for i, (side, part) in enumerate(quarters()):
                    pltpu.make_async_remote_copy(
                        src_ref=kv_got.at[s, side, part],
                        dst_ref=kv_got.at[s, side, part],
                        send_sem=c_send.at[s + 1, i],
                        recv_sem=c_recv.at[s, i],
                        device_id=(me_f, me_c + 1, me_t),
                        device_id_type=MESH_ID,
                    ).wait_recv()
                    add(kv_parts.at[s, side, part], kv_got.at[s, side, part])

        if s:

            @pl.when(me_c >= s)
            def _():
                for copy in descend(s):
                    copy.start()

    def chain_result():
        width = kv_parts.shape[3]
        rows = cos_ref.shape[0]
        for seq in range(kv_parts.shape[2] // rows):
            span = pl.ds(seq * rows, rows)
            for start in range(0, width, 128):
                cols = slice(start, start + 128)
                t = kv_parts[0, 0, span, cols].astype(jnp.float32)
                t = t * cos_ref[...] + turn(t * sin_ref[...], -1.0)
                kv_ref[span, cols] = t.astype(kv_ref.dtype)
            kv_ref[span, width:] = kv_parts[0, 1, span]

    steps = list(reversed(range(ctx))) if chain else []

    def next_step():
        if steps:
            s = steps.pop(0)
            chain_step(s)
            if s == 0:
                chain_result()

    if chain:
        kv_load.wait()
        next_step()
    shards = sorted(range(ctx), key=lambda c: -abs(2 * c - ctx + 1))
    work = [[(i, shard) for i in range(weights)] for shard in shards]
    work += [[(i, 0)] for i in range(weights, count)]
    levels = sorted({bin(k).count("1") for k in order}, reverse=True)
    waited = set()

    def loaded(i, k):
        if (i, k) not in waited:
            waited.add((i, k))
            loads[i, k].wait()

    def advance(stage, item):
        for i, shard in item:
            if stage == len(levels):
                loaded(i, 0)
                collect(i, shard, 0)
                if i >= weights:
                    give(i, shard)
                continue
            for k in steps_of(i):
                if bin(k).count("1") == levels[stage]:
                    loaded(i, k)
                    collect(i, shard, k)
                    for part, b in ways(k):
                        f_copy(i, shard, k, part, b).start()

    def line_tick(item, hops):
        for i, shard in item:
            if i >= weights:
                continue
            for step, there in ((1, hops), (-1, ctx - 1 - hops)):
                if step * (shard - there) >= 0:

                    @pl.when(me_c == there)
                    def _():
                        on_line(i, shard, step)

            if hops == max(shard, ctx - 1 - shard):

                @pl.when(me_c == shard)
                def _():
                    give(i, shard)

    stages = len(levels) + 1
    for tick in range(len(work) + stages + ctx - 2):
        for stage in range(stages):
            if 0 <= tick - stage < len(work):
                advance(stage, work[tick - stage])
        for hops in range(ctx):
            place = tick - stages + 1 - hops
            if 0 <= place < len(work):
                line_tick(work[place], hops)
        next_step()
    while steps:
        next_step()
    for i, shard in [pair for item in work for pair in item]:
        for k in steps_of(i):
            for part, b in ways(k):
                f_copy(i, shard, k, part, b).wait_send()
        for step in (1, -1) if i < weights else ():

            @pl.when(step * (shard - me_c) > 0)
            def _():
                z_copy(i, shard, step).wait_send()

    if chain:
        for s in range(1, ctx):

            @pl.when(me_c >= s)
            def _():
                for copy in descend(s):
                    copy.wait_send()


def sum_weights(fsdp, ctx, group, arrays, chain=()):
    sems = pltpu.SemaphoreType.DMA
    vmem = pltpu.VMEM
    shards = [v.reshape(ctx, fsdp, -1, v.shape[-1]) for v in arrays]
    blocks = [(fsdp, ctx) + v.shape[2:] for v in shards]
    out_shape = [jax.ShapeDtypeStruct(v.shape[2:], jnp.float32) for v in shards]
    lines = [vmem((2,) + b[1:], v.dtype) for b, v in zip(blocks, shards)]
    extra = []
    if chain:
        rows, parts, cosines, sines = chain
        shards.append(rows[:, None])
        blocks.append(shards[-1].shape)
        out_shape.append(jax.ShapeDtypeStruct(rows.shape[1:], rows.dtype))
        out_shape.append(jax.ShapeDtypeStruct((parts.shape[2], 2 * parts.shape[3]), parts.dtype))
        extra = [
            vmem(parts.shape, parts.dtype),
            vmem((ctx - 1,) + parts.shape[1:], parts.dtype),
            sems((1,)),
            sems((ctx, 4)),
            sems((ctx, 4)),
        ]
    count = len(shards)
    held = [vmem(b, v.dtype) for b, v in zip(blocks, shards)]
    return pl.pallas_call(
        partial(sum_kernel, fsdp, ctx, group, count, bool(chain)),
        out_shape=out_shape,
        in_specs=[pl.BlockSpec(memory_space=pl.ANY)] * (count + len(chain[1:2]))
        + [pl.BlockSpec(memory_space=pltpu.VMEM)] * len(chain[2:]),
        out_specs=[pl.BlockSpec(memory_space=pltpu.VMEM)] * len(out_shape),
        scratch_shapes=held
        + held
        + lines
        + [
            sems((count, fsdp)),
            sems((count, ctx, fsdp, 2)),
            sems((count, ctx, fsdp, 2)),
            sems((count, 2, ctx)),
            sems((count, 2, ctx)),
        ]
        + extra,
        compiler_params=pltpu.CompilerParams(
            collective_id=4 if chain else 2,
            has_side_effects=True,
            vmem_limit_bytes=52 * 1024 * 1024,
        ),
    )(*shards, *chain[1:])


def local(
    inputs,
    lengths,
    cotangent,
    norm1_gain,
    w_query,
    w_key,
    w_value,
    w_out,
    norm2_gain,
    w_gate,
    w_up,
    w_down,
):
    seq_count, local_rows, model_width = inputs.shape
    tokens = seq_count * local_rows
    half = tokens // 2
    fsdp = lax.axis_size("fsdp")
    ctx = lax.axis_size("ctx")
    shard = w_query.shape[0]
    query_width = w_query.shape[1]
    kv_width = w_key.shape[1]
    kv_end = query_width + 2 * kv_width
    pairs = kv_width // (2 * HD)
    group_size = query_width // kv_width
    group = min(fsdp, 4)
    far = fsdp // group
    units = w_gate.shape[1] // group
    me_c = lax.axis_index("ctx")
    me_t = lax.axis_index("tp")
    low = jnp.bfloat16
    wide = jnp.float32

    def swap(v):
        return lax.ppermute(v, "tp", [(0, 1), (1, 0)])

    inside = shard % 128 == 0
    dims = (fsdp, ctx, shard)
    back_dims = (ctx, fsdp, shard)

    def by_ctx(v):
        if inside:
            return v
        rows = v.shape[0]
        return v.reshape(rows, fsdp, ctx, shard).swapaxes(1, 2).reshape(rows, model_width)

    def by_fsdp(v):
        if inside:
            return v
        rows = v.shape[0]
        return v.reshape(rows, ctx, fsdp, shard).swapaxes(1, 2).reshape(rows, model_width)

    def pair_heads(v):
        rows = v.shape[0]
        return (
            v.reshape(rows, pairs, 2, group_size, HD).swapaxes(2, 3).reshape(rows, query_width)
        )

    def plain_heads(v):
        rows = v.shape[0]
        return (
            v.reshape(rows, pairs, group_size, 2, HD).swapaxes(2, 3).reshape(rows, query_width)
        )

    def both_halves(own):
        other = swap(own)
        return jnp.where(
            me_t == 0, jnp.concatenate([own, other]), jnp.concatenate([other, own])
        )

    x = by_ctx(inputs.reshape(tokens, model_width))
    cot = by_ctx(cotangent.reshape(tokens, model_width))
    positions = me_c * local_rows + jnp.arange(local_rows, dtype=jnp.int32)
    cosines, sines = rope_tables(positions, HD)
    cosines, sines = jnp.tile(cosines, (1, 2)), jnp.tile(sines, (1, 2))

    gains = jnp.pad(jnp.stack([norm1_gain, norm2_gain]).astype(wide), ((0, 14), (0, 0)))
    lined, held = start_exchange(
        fsdp,
        ctx,
        group,
        [
            jnp.concatenate([pair_heads(w_query), w_key, w_value], 1),
            gains,
            pair_heads(w_out),
        ],
        [[w_gate, w_up], [w_down]],
    )
    far_groups = [[h * group + g for h in range(far)] for g in range(group)]
    near_groups = [[h * group + g for g in range(group)] for h in range(far)]

    def whole_width(v):
        if far > 1:
            v = lax.all_gather(v, "fsdp", axis=0, tiled=False, axis_index_groups=far_groups)
        return lax.all_gather(v, "ctx", axis=0, tiled=False).reshape(model_width, -1)

    both_full, down_full = [whole_width(v) for v in held]
    qkv_full, gain_rows = spread_weights(fsdp, ctx, group, lined[:2])
    gain_rows = gain_rows.reshape(ctx * fsdp, 16, shard)
    gain_one = gain_rows[:, 0].reshape(1, model_width)
    gain_two = gain_rows[:, 1].reshape(1, model_width)

    (ff_grad,) = by_rows(
        partial(cot_kernel, dims, local_rows),
        128,
        [(lengths, "smem"), (cot, "rows")],
        [((tokens, model_width), low)],
    )
    first_normed, query, kv_own = by_rows(
        partial(qkv_kernel, dims),
        128,
        [
            (x, "rows"),
            (qkv_full, "whole"),
            (gain_one, "whole"),
            (cosines, "cycle"),
            (sines, "cycle"),
        ],
        [
            ((tokens, model_width), low),
            ((tokens, query_width), low),
            ((tokens, 2 * kv_width), low),
        ],
        flops=2 * tokens * model_width * kv_end,
    )
    out_full, kv_all, ff_grad_all = spread_weights(
        fsdp, ctx, group, lined[2:], (kv_own, ff_grad)
    )
    attended, lse = attend(lengths, query, kv_all)
    attn_part = jnp.einsum(
        "tj,dj->td", attended, out_full, preferred_element_type=wide
    ).astype(low)
    middle, second_normed = by_rows(
        partial(middle_kernel, dims),
        128,
        [(x, "rows"), (attn_part, "rows"), (swap(attn_part), "rows"), (gain_two, "whole")],
        [((tokens, model_width), wide), ((tokens, model_width), low)],
    )
    normed_all = gather_tokens(group, fsdp, second_normed)

    hidden, both_grad, ff_sums, second_grad = swiglu(
        fsdp, group, normed_all, ff_grad_all, both_full, down_full
    )
    second_grad = second_grad.reshape(tokens, model_width)

    def unit_term(left, right):
        return jnp.einsum("td,tf->df", left, right, preferred_element_type=wide).astype(low)

    def own_units(term):
        own = lax.psum_scatter(
            term.reshape(ctx, fsdp, shard, units), "ctx", scatter_dimension=0, tiled=False
        )
        if far > 1:
            own = lax.psum_scatter(
                own.reshape(far, group, shard, units),
                "fsdp",
                scatter_dimension=0,
                tiled=False,
                axis_index_groups=far_groups,
            )
        return own

    def return_units(own):
        return lax.all_to_all(
            own.reshape(group * shard, units),
            "fsdp",
            0,
            1,
            tiled=True,
            axis_index_groups=near_groups if far > 1 else None,
        ).astype(wide)

    down_term = unit_term(ff_grad_all, hidden)
    second_grad, down_after = lax.optimization_barrier((second_grad, down_term))
    w_down_grad = return_units(own_units(down_term))

    middle_grad, attn_grad, gain_two_term = by_rows(
        partial(middle_back_kernel, dims, local_rows),
        128,
        [
            (lengths, "smem"),
            (cot, "rows"),
            (middle, "rows"),
            (second_grad, "rows"),
            (gain_two, "whole"),
        ],
        [((tokens, model_width), wide), ((tokens, model_width), low), ((1, model_width), wide)],
    )
    attended_grad = jnp.dot(attn_grad, out_full, preferred_element_type=wide).astype(low)
    query_grad, kv_parts = attend_back(
        lengths, query, attended_grad, lse, cosines, sines, kv_all
    )
    query_grad, normed_all, both_grad = lax.optimization_barrier(
        (query_grad, normed_all, both_grad)
    )
    gate_term = unit_term(normed_all, both_grad[:, :units])
    w_gate_grad = return_units(own_units(gate_term))
    ff_sums = ff_sums.reshape(group, half, model_width)
    out_term = jnp.einsum("td,tj->dj", attn_grad, attended, preferred_element_type=wide)
    kv_parts, gate_after = lax.optimization_barrier((kv_parts, gate_term))
    w_out_grad, ff_own, kv_grad = sum_weights(
        fsdp, ctx, group, [out_term.astype(low)], (ff_sums, kv_parts, cosines, sines)
    )
    (output,) = by_rows(
        partial(output_kernel, back_dims, local_rows),
        128,
        [(lengths, "smem"), (middle, "rows"), (both_halves(ff_own), "rows")],
        [((tokens, model_width), low)],
    )
    kv_grad, normed_all, both_grad = lax.optimization_barrier((kv_grad, normed_all, both_grad))
    up_term = unit_term(normed_all, both_grad[:, units:])
    up_own = own_units(up_term)
    qkv_grad = jnp.concatenate([query_grad, kv_grad], -1)
    qkv_term = jnp.einsum("td,tj->dj", first_normed, qkv_grad, preferred_element_type=wide)
    first_part = jnp.einsum(
        "tj,dj->td", qkv_grad, qkv_full, preferred_element_type=wide
    ).astype(low)
    input_grad, gain_one_term = by_rows(
        partial(input_back_kernel, dims),
        128,
        [
            (x, "rows"),
            (first_part, "rows"),
            (swap(first_part), "rows"),
            (middle_grad, "rows"),
            (gain_one, "whole"),
        ],
        [((tokens, model_width), low), ((1, model_width), wide)],
    )
    gain_terms = jnp.stack(
        [gain_one_term.reshape(-1, shard), gain_two_term.reshape(-1, shard)], 1
    )
    gain_terms = jnp.pad(gain_terms, ((0, 0), (0, 14), (0, 0))).reshape(-1, shard)
    qkv_term, w_down_grad, w_gate_grad, up_after = lax.optimization_barrier(
        (qkv_term.astype(low), w_down_grad, w_gate_grad, up_term)
    )
    qkv_own, gain_own = sum_weights(fsdp, ctx, group, [qkv_term, gain_terms])
    up_own, qkv_own = lax.optimization_barrier((up_own, qkv_own))
    w_up_grad = return_units(up_own)
    return (
        by_fsdp(output).reshape(inputs.shape),
        by_fsdp(input_grad).reshape(inputs.shape),
        gain_own[0],
        plain_heads(qkv_own[:, :query_width]),
        qkv_own[:, query_width : query_width + kv_width],
        qkv_own[:, query_width + kv_width :],
        plain_heads(w_out_grad),
        gain_own[1],
        w_gate_grad,
        w_up_grad,
        w_down_grad,
    )


def solution(mesh):
    placed = (
        P("fsdp", "ctx", None),
        P("fsdp"),
        P("fsdp", "ctx", None),
        P(("fsdp", "ctx")),
        P(("fsdp", "ctx"), "tp"),
        P(("fsdp", "ctx"), "tp"),
        P(("fsdp", "ctx"), "tp"),
        P(("fsdp", "ctx"), "tp"),
        P(("fsdp", "ctx")),
        P(("fsdp", "ctx"), "tp"),
        P(("fsdp", "ctx"), "tp"),
        P(("fsdp", "ctx"), "tp"),
    )
    return jax.shard_map(
        local,
        mesh=mesh,
        in_specs=placed,
        out_specs=(
            P("fsdp", "ctx", None),
            P("fsdp", "ctx", None),
            P(("fsdp", "ctx")),
            P(("fsdp", "ctx"), "tp"),
            P(("fsdp", "ctx"), "tp"),
            P(("fsdp", "ctx"), "tp"),
            P(("fsdp", "ctx"), "tp"),
            P(("fsdp", "ctx")),
            P(("fsdp", "ctx"), "tp"),
            P(("fsdp", "ctx"), "tp"),
            P(("fsdp", "ctx"), "tp"),
        ),
        check_vma=False,
    )
```

```python
from functools import partial

import jax
import jax.numpy as jnp
from jax import lax
from jax.experimental import pallas as pl
from jax.experimental.pallas import tpu as pltpu
from jax.sharding import PartitionSpec as P

HD = 64


norm_eps = 1e-05
residual_scale = 0.22
score_scale = 1.0 / 64.0
rope_base = 10000000.0
masked_score = -1e30


def rope_tables(positions, head_dim):
    half_dim = head_dim // 2
    frequency = rope_base ** (-(jnp.arange(half_dim, dtype=jnp.float32) * 2.0) / head_dim)
    angles = positions.astype(jnp.float32)[:, None] * frequency[None, :]
    return (
        jnp.concatenate([jnp.cos(angles), jnp.cos(angles)], -1),
        jnp.concatenate([jnp.sin(angles), jnp.sin(angles)], -1),
    )


def rotate(values_in, cosines, sines):
    half_dim = values_in.shape[-1] // 2
    turned = jnp.concatenate([-values_in[..., half_dim:], values_in[..., :half_dim]], -1)
    return values_in * cosines + turned * sines


def unrotate(grad_in, cosines, sines):
    half_dim = grad_in.shape[-1] // 2
    scaled = grad_in * sines
    return grad_in * cosines + jnp.concatenate(
        [scaled[..., half_dim:], -scaled[..., :half_dim]], -1
    )


def rms_scale(values_in):
    return lax.rsqrt(jnp.mean(values_in * values_in, -1, keepdims=True) + norm_eps)


def norm_back(grad_normed, values_in, scale, gain):
    scaled_grad = grad_normed * gain
    return scale * scaled_grad - values_in * scale**3 * jnp.mean(
        scaled_grad * values_in, -1, keepdims=True
    )


MESH_ID = pl.DeviceIdType.MESH
FIRST_EIGHTHS = 4
NT = (((1,), (1,)), ((), ()))
TN = (((0,), (0,)), ((), ()))
SMEM = pltpu.SMEM


def mul(left, right, dims=(((1,), (0,)), ((), ()))):
    return lax.dot_general(left, right, dims, preferred_element_type=jnp.float32)


def reorder(v, first, second, width):
    if width % 128:
        return v
    pieces = []
    for b in range(second):
        for a in range(first):
            start = (a * second + b) * width
            pieces.append(v[:, start : start + width])
    return jnp.concatenate(pieces, 1)


def turn(t, sign):
    lane = lax.broadcasted_iota(jnp.int32, t.shape, 1)
    ahead = pltpu.roll(t, 128 - HD // 2, 1)
    behind = pltpu.roll(t, HD // 2, 1)
    return jnp.where(lax.rem(lane, HD) < HD // 2, -sign * ahead, sign * behind)


def row_valid(len_ref, rows, local_rows):
    step = pl.program_id(0)
    start = step * rows
    seq = start // local_rows
    place = (
        lax.axis_index("ctx") * local_rows
        + lax.rem(start, local_rows)
        + lax.broadcasted_iota(jnp.int32, (rows, 1), 0)
    )
    return (place < len_ref[seq]).astype(jnp.float32)


def qkv_kernel(dims, x_ref, w_ref, gain_ref, cos_ref, sin_ref, normed_ref, q_ref, kv_ref):
    x = reorder(x_ref[...].astype(jnp.float32), *dims)
    normed = (x * rms_scale(x) * gain_ref[...]).astype(jnp.bfloat16)
    normed_ref[...] = normed
    lin = mul(normed, w_ref[...])
    cosines, sines = cos_ref[...], sin_ref[...]
    width = q_ref.shape[1]
    half = kv_ref.shape[1] // 2
    for start in range(0, width + half, 128):
        t = lin[:, start : start + 128]
        t = (t * cosines + turn(t, 1.0) * sines).astype(jnp.bfloat16)
        if start < width:
            q_ref[:, start : start + 128] = t
        else:
            kv_ref[:, start - width : start - width + 128] = t
    kv_ref[:, half:] = lin[:, width + half :].astype(jnp.bfloat16)


def key_biases(len_ref, rows, ctx):
    length = len_ref[pl.program_id(0)]
    me = lax.axis_index("ctx")
    row = lax.broadcasted_iota(jnp.int32, (rows, rows), 0)
    col = lax.broadcasted_iota(jnp.int32, (rows, rows), 1)
    first = jnp.where((col <= row) & (me * rows + col < length), 0.0, masked_score)
    out = [first]
    for s in range(1, ctx):
        place = (me - s) * rows + lax.broadcasted_iota(jnp.int32, (1, rows), 1)
        out.append(jnp.where((place >= 0) & (place < length), 0.0, masked_score))
    return out


def attend_kernel(ctx, len_ref, q_ref, *refs):
    keys, values = refs[:ctx], refs[ctx : 2 * ctx]
    o_ref, lse_ref = refs[2 * ctx :]
    rows = q_ref.shape[0]
    biases = key_biases(len_ref, rows, ctx)
    lane = lax.broadcasted_iota(jnp.int32, (rows, 128), 1)
    lse_all = jnp.zeros((rows, 128), jnp.float32)
    for j in range(q_ref.shape[1] // 128):
        q_pair = q_ref[:, j * 128 : (j + 1) * 128] * jnp.bfloat16(score_scale)
        outs = []
        for g in range(2):
            mine = (lane < HD) if g == 0 else (lane >= HD)
            q_head = jnp.where(mine, q_pair, jnp.zeros_like(q_pair))
            scores = [mul(q_head, k[...], NT) + b for k, b in zip(keys, biases)]
            top = scores[0].max(-1, keepdims=True)
            for s in scores[1:]:
                top = jnp.maximum(top, s.max(-1, keepdims=True))
            mass, out = 0.0, 0.0
            for s, v in zip(scores, values):
                p = jnp.exp(s - top)
                mass = mass + p.sum(-1, keepdims=True)
                out = out + mul(p.astype(jnp.bfloat16), v[...])
            outs.append(out / mass)
            lse_all = jnp.where(lane == 2 * j + g, top + jnp.log(mass), lse_all)
        o_ref[:, j * 128 : (j + 1) * 128] = jnp.where(lane < HD, outs[0], outs[1]).astype(
            jnp.bfloat16
        )
    lse_ref[...] = lse_all


class RowSum:
    def __init__(
        self, group, fsdp, rows_ref, own_ref, held, got, in_sem, f_send, f_recv, own_sem
    ):
        self.group, self.fsdp = group, fsdp
        self.order = fsdp_order(group)
        self.bits = [1 << i for i in range(group.bit_length() - 1)]
        self.own_ref, self.held, self.got = own_ref, held, got
        self.f_send, self.f_recv, self.own_sem = f_send, f_recv, own_sem
        self.half = rows_ref.shape[1]
        self.loads = [
            pltpu.make_async_copy(rows_ref.at[k], held.at[k], in_sem.at[k]) for k in range(group)
        ]

    def peer(self, k):
        me_f = lax.axis_index("fsdp")
        return (flip_index(me_f, k, self.fsdp), lax.axis_index("ctx"), lax.axis_index("tp"))

    def core(self):
        me_f, me_c, me_t = self.peer(0)
        return (me_f, me_c, 1 - me_t)

    def ways(self, k):
        return [(0, k)] if k == low_bit(k) else [(0, low_bit(k)), (1, high_bit(k))]

    def span(self, k, part):
        half = self.half
        return pl.ds(0, half) if k == low_bit(k) else pl.ds(part * (half // 2), half // 2)

    def copy(self, k, part, b):
        return pltpu.make_async_remote_copy(
            src_ref=self.held.at[k, self.span(k, part)],
            dst_ref=self.got.at[k, self.span(k, part)],
            send_sem=self.f_send.at[k, part],
            recv_sem=self.f_recv.at[k, part],
            device_id=self.peer(b),
            device_id_type=MESH_ID,
        )

    def own_copy(self, place):
        return pltpu.make_async_remote_copy(
            src_ref=self.held.at[0],
            dst_ref=self.own_ref.at[place],
            send_sem=self.own_sem.at[0],
            recv_sem=self.own_sem.at[1],
            device_id=self.core(),
            device_id_type=MESH_ID,
        )

    def collect(self, k):
        for far in self.order:
            for part, b in self.ways(far):
                if far ^ b == k:
                    self.copy(far, part, b).wait_recv()
                    rows = self.span(far, part)
                    self.held[k, rows] = (
                        self.held[k, rows].astype(jnp.float32)
                        + self.got[far, rows].astype(jnp.float32)
                    ).astype(self.held.dtype)

    def send(self, k):
        for part, b in self.ways(k):
            self.copy(k, part, b).start()

    def start(self):
        barrier = pltpu.get_barrier_semaphore()
        for b in self.bits:
            pl.semaphore_signal(barrier, inc=1, device_id=self.peer(b), device_id_type=MESH_ID)
        pl.semaphore_signal(barrier, inc=1, device_id=self.core(), device_id_type=MESH_ID)
        for load in self.loads:
            load.start()
        pl.semaphore_wait(barrier, len(self.bits) + 1)
        for load in self.loads:
            load.wait()
        for k in self.order:
            if k != low_bit(k):
                self.send(k)

    def relay(self):
        for k in self.order:
            if k == low_bit(k):
                self.collect(k)
                self.send(k)

    def finish(self):
        self.collect(0)
        me_t = lax.axis_index("tp")
        self.own_copy(me_t).start()
        local = pltpu.make_async_copy(
            self.held.at[0], self.own_ref.at[me_t], self.own_sem.at[2]
        )
        local.start()
        local.wait()
        self.own_copy(1 - me_t).wait_recv()
        self.own_copy(me_t).wait_send()
        for k in self.order:
            for part, b in self.ways(k):
                self.copy(k, part, b).wait_send()


def attend_back_kernel(
    ctx, fsdp, group, len_ref, q_ref, do_ref, lse_ref, cos_ref, sin_ref, rows_ref, *refs
):
    keys, values = refs[:ctx], refs[ctx : 2 * ctx]
    dq_ref, dkv_ref, own_ref, dk_sum, dv_sum = refs[2 * ctx : 2 * ctx + 5]
    step = pl.program_id(0) * pl.num_programs(1) + pl.program_id(1)
    sums = RowSum(group, fsdp, rows_ref, own_ref, *refs[2 * ctx + 5 :])

    @pl.when(step == 0)
    def _():
        sums.start()

    rows = q_ref.shape[0]
    biases = key_biases(len_ref, rows, ctx)
    lane = lax.broadcasted_iota(jnp.int32, (rows, 128), 1)
    dk_sum[...] = jnp.zeros_like(dk_sum)
    dv_sum[...] = jnp.zeros_like(dv_sum)
    lse_all = lse_ref[...]
    for j in range(q_ref.shape[1] // 128):
        q_pair = q_ref[:, j * 128 : (j + 1) * 128] * jnp.bfloat16(score_scale)
        do_pair = do_ref[:, j * 128 : (j + 1) * 128]
        dqs = []
        for g in range(2):
            mine = (lane < HD) if g == 0 else (lane >= HD)
            q_head = jnp.where(mine, q_pair, jnp.zeros_like(q_pair))
            do_head = jnp.where(mine, do_pair, jnp.zeros_like(do_pair))
            h = 2 * j + g
            lse = lse_all[:, h : h + 1]
            probs, grads, total = [], [], 0.0
            for s in range(ctx):
                p = jnp.exp(mul(q_head, keys[s][...], NT) + (biases[s] - lse))
                dp = mul(do_head, values[s][...], NT)
                total = total + (p * dp).sum(-1, keepdims=True)
                probs.append(p)
                grads.append(dp)
            dq = 0.0
            for s in range(ctx):
                ds = (probs[s] * (grads[s] - total)).astype(jnp.bfloat16)
                dv_sum[s] += mul(probs[s].astype(jnp.bfloat16), do_head, TN)
                dk_sum[s] += mul(ds, q_head, TN)
                dq = dq + mul(ds, keys[s][...])
            dqs.append(dq)
        dq = jnp.where(lane < HD, dqs[0], dqs[1]) * score_scale
        dq = dq * cos_ref[...] + turn(dq * sin_ref[...], -1.0)
        dq_ref[:, j * 128 : (j + 1) * 128] = dq.astype(jnp.bfloat16)
        if j == 1:

            @pl.when(step == 1)
            def _():
                sums.relay()

    for s in range(ctx):
        dkv_ref[s, 0] = dk_sum[s].astype(dkv_ref.dtype)
        dkv_ref[s, 1] = dv_sum[s].astype(dkv_ref.dtype)

    @pl.when(step == pl.num_programs(0) * pl.num_programs(1) - 1)
    def _():
        sums.finish()


def cot_kernel(dims, local_rows, len_ref, cot_ref, ff_ref):
    rows = cot_ref.shape[0]
    back = cot_ref[...].astype(jnp.float32) * row_valid(len_ref, rows, local_rows)
    ff_ref[...] = reorder((residual_scale * back).astype(jnp.bfloat16), *dims)


def middle_kernel(dims, x_ref, part_ref, other_ref, gain_ref, middle_ref, normed_ref):
    branch = part_ref[...].astype(jnp.float32) + other_ref[...].astype(jnp.float32)
    middle = reorder(x_ref[...].astype(jnp.float32), *dims) + residual_scale * branch
    middle_ref[...] = middle
    normed_ref[...] = (middle * rms_scale(middle) * gain_ref[...]).astype(jnp.bfloat16)


def middle_back_kernel(
    dims, local_rows, len_ref, cot_ref, middle_ref, grad_ref, gain_ref, back_ref, attn_ref, gain_sum
):
    rows = cot_ref.shape[0]
    back = cot_ref[...].astype(jnp.float32) * row_valid(len_ref, rows, local_rows)
    middle = middle_ref[...]
    grad = grad_ref[...].astype(jnp.float32)
    scale = rms_scale(middle)
    out = reorder(back, *dims) + norm_back(grad, middle, scale, gain_ref[...])
    back_ref[...] = out
    attn_ref[...] = (residual_scale * out).astype(jnp.bfloat16)

    @pl.when(pl.program_id(0) == 0)
    def _():
        gain_sum[...] = jnp.zeros_like(gain_sum)

    gain_sum[...] += (grad * middle * scale).sum(0, keepdims=True)


def output_kernel(dims, local_rows, len_ref, middle_ref, ff_ref, out_ref):
    rows = middle_ref.shape[0]
    out = middle_ref[...] + residual_scale * ff_ref[...].astype(jnp.float32)
    out = (out * row_valid(len_ref, rows, local_rows)).astype(jnp.bfloat16)
    out_ref[...] = reorder(out, *dims)


def input_back_kernel(
    dims, x_ref, part_ref, other_ref, back_ref, gain_ref, out_ref, gain_sum
):
    first, second, width = dims
    x = reorder(x_ref[...].astype(jnp.float32), *dims)
    grad = (part_ref[...].astype(jnp.float32) + other_ref[...].astype(jnp.float32))
    scale = rms_scale(x)
    out = back_ref[...] + norm_back(grad, x, scale, gain_ref[...])
    out_ref[...] = reorder(out.astype(jnp.bfloat16), second, first, width)

    @pl.when(pl.program_id(0) == 0)
    def _():
        gain_sum[...] = jnp.zeros_like(gain_sum)

    gain_sum[...] += (grad * x * scale).sum(0, keepdims=True)


def by_rows(kernel, rows, ins, outs, flops=0, limit=40):
    total = max(v.shape[0] for v, kind in ins if kind == "rows")
    in_specs = []
    moved = 0
    for v, kind in ins:
        moved += v.size * v.dtype.itemsize
        if kind == "rows":
            in_specs.append(pl.BlockSpec((rows, v.shape[1]), lambda i: (i, 0)))
        elif kind == "cycle":
            period = v.shape[0] // rows
            in_specs.append(
                pl.BlockSpec((rows, v.shape[1]), lambda i, period=period: (lax.rem(i, period), 0))
            )
        elif kind == "smem":
            in_specs.append(pl.BlockSpec(memory_space=SMEM))
        else:
            in_specs.append(
                pl.BlockSpec(v.shape, lambda i: (0, 0), pipeline_mode=pl.Buffered(1))
            )
    out_specs = []
    for shape, dtype in outs:
        moved += shape[0] * shape[1] * jnp.dtype(dtype).itemsize
        if shape[0] == 1:
            out_specs.append(pl.BlockSpec(shape, lambda i: (0, 0)))
        else:
            out_specs.append(pl.BlockSpec((rows, shape[1]), lambda i: (i, 0)))
    return pl.pallas_call(
        kernel,
        grid=(total // rows,),
        in_specs=in_specs,
        out_specs=out_specs,
        out_shape=[jax.ShapeDtypeStruct(shape, dtype) for shape, dtype in outs],
        compiler_params=pltpu.CompilerParams(vmem_limit_bytes=limit * 1024 * 1024),
        cost_estimate=pl.CostEstimate(flops=flops, bytes_accessed=moved, transcendentals=0),
    )(*[v for v, _ in ins])


def kv_specs(ctx, rows, pairs):
    def spec(slot, start):
        return pl.BlockSpec((None, rows, 128), lambda s, p: (slot, s, start + p))

    return [spec(slot, start) for start in (0, pairs) for slot in range(ctx)]


def attend(lengths, query, kv_all):
    ctx = kv_all.shape[0]
    seqs = lengths.shape[0]
    rows = query.shape[0] // seqs
    pairs = kv_all.shape[2] // 256
    wide = query.shape[1] // pairs
    flops = 4 * query.shape[0] * query.shape[1] * rows * ctx
    return pl.pallas_call(
        partial(attend_kernel, ctx),
        grid=(seqs, pairs),
        in_specs=[
            pl.BlockSpec(memory_space=SMEM),
            pl.BlockSpec((rows, wide), lambda s, p: (s, p)),
        ]
        + kv_specs(ctx, rows, pairs),
        out_specs=[
            pl.BlockSpec((rows, wide), lambda s, p: (s, p)),
            pl.BlockSpec((rows, 128), lambda s, p: (s, p)),
        ],
        out_shape=[
            jax.ShapeDtypeStruct(query.shape, jnp.bfloat16),
            jax.ShapeDtypeStruct((query.shape[0], 128 * pairs), jnp.float32),
        ],
        compiler_params=pltpu.CompilerParams(vmem_limit_bytes=40 * 1024 * 1024),
        cost_estimate=pl.CostEstimate(flops=4 * flops, bytes_accessed=6 << 20, transcendentals=0),
    )(lengths, query, *[kv_all] * (2 * ctx))


def attend_back(fsdp, group, lengths, query, out_grad, lse, cosines, sines, kv_all, row_blocks):
    ctx = kv_all.shape[0]
    block = row_blocks.shape[1:]
    low = jnp.bfloat16
    sems = pltpu.SemaphoreType.DMA
    seqs = lengths.shape[0]
    rows = query.shape[0] // seqs
    pairs = kv_all.shape[2] // 256
    wide = query.shape[1] // pairs
    flops = 10 * query.shape[0] * query.shape[1] * rows * ctx
    return pl.pallas_call(
        partial(attend_back_kernel, ctx, fsdp, group),
        grid=(seqs, pairs),
        in_specs=[
            pl.BlockSpec(memory_space=SMEM),
            pl.BlockSpec((rows, wide), lambda s, p: (s, p)),
            pl.BlockSpec((rows, wide), lambda s, p: (s, p)),
            pl.BlockSpec((rows, 128), lambda s, p: (s, p)),
            pl.BlockSpec((rows, 128), lambda s, p: (0, 0)),
            pl.BlockSpec((rows, 128), lambda s, p: (0, 0)),
            pl.BlockSpec(memory_space=pl.ANY),
        ]
        + kv_specs(ctx, rows, pairs),
        out_specs=[
            pl.BlockSpec((rows, wide), lambda s, p: (s, p)),
            pl.BlockSpec((ctx, 2, rows, 128), lambda s, p: (0, 0, s, p)),
            pl.BlockSpec(memory_space=pl.ANY),
        ],
        out_shape=[
            jax.ShapeDtypeStruct(query.shape, jnp.bfloat16),
            jax.ShapeDtypeStruct((ctx, 2, query.shape[0], 128 * pairs), low),
            jax.ShapeDtypeStruct((2,) + block, low),
        ],
        scratch_shapes=[pltpu.VMEM((ctx, rows, 128), jnp.float32)] * 2
        + [pltpu.VMEM((group,) + block, low)] * 2
        + [sems((group,)), sems((group, 2)), sems((group, 2)), sems((3,))],
        compiler_params=pltpu.CompilerParams(
            collective_id=7, has_side_effects=True, vmem_limit_bytes=44 * 1024 * 1024
        ),
        cost_estimate=pl.CostEstimate(flops=4 * flops, bytes_accessed=10 << 20, transcendentals=0),
    )(lengths, query, out_grad, lse, cosines, sines, row_blocks, *[kv_all] * (2 * ctx))


def low_bit(k):
    return k & -k


def high_bit(k):
    return 1 << (k.bit_length() - 1)


def fsdp_order(fsdp):
    return sorted(range(1, fsdp), key=lambda k: (bin(k).count("1"), k))


def flip_index(me, k, fsdp):
    out = me
    for i in range(fsdp.bit_length() - 1):
        b = 1 << i
        if k & b:
            out = out + b - 2 * b * lax.rem(me // b, 2)
    return out


def line_neighbours(me, count):
    return (me > 0).astype(jnp.int32) + (me < count - 1).astype(jnp.int32)


def line_kernel(fsdp, ctx, group, lines, swaps, widths, *refs):
    line_in = refs[:lines]
    swap_in = refs[lines : lines + swaps]
    line_out = refs[lines + swaps : 2 * lines + swaps]
    swap_out = refs[2 * lines + swaps : -5]
    own_sem, z_send, z_recv, f_send, f_recv = refs[-5:]
    parts = len(widths)
    me_f = lax.axis_index("fsdp")
    me_c = lax.axis_index("ctx")
    me_t = lax.axis_index("tp")

    def along(step, act):
        there = me_c + step

        @pl.when((there >= 0) & (there < ctx))
        def _():
            act(there)

    barrier = pltpu.get_barrier_semaphore()
    for k in range(1, group):
        pl.semaphore_signal(
            barrier, inc=1, device_id=(flip_index(me_f, k, fsdp), me_c, me_t), device_id_type=MESH_ID
        )
    for step in (-1, 1):
        along(
            step,
            lambda there: pl.semaphore_signal(
                barrier, inc=1, device_id=(me_f, there, me_t), device_id_type=MESH_ID
            ),
        )
    pl.semaphore_wait(barrier, group - 1 + line_neighbours(me_c, ctx))

    def z_copy(i, shard, step, src=None):
        place = line_out[i].at[shard]
        way = 0 if step > 0 else 1
        return pltpu.make_async_remote_copy(
            src_ref=place if src is None else src,
            dst_ref=place,
            send_sem=z_send.at[i, way, shard],
            recv_sem=z_recv.at[i, way, shard],
            device_id=(me_f, me_c + step, me_t),
            device_id_type=MESH_ID,
        )

    def landing(i, part, f):
        width = widths[part]
        return swap_out[part].at[lax.rem(f, group), :, pl.ds(i * width, width)]

    def columns(i, part, f):
        start = lax.rem(f, group) * sum(widths) + sum(widths[:part])
        return swap_in[i].at[:, pl.ds(pl.multiple_of(start, 128), widths[part])]

    def f_copy(i, part, k):
        there = flip_index(me_f, k, fsdp)
        return pltpu.make_async_remote_copy(
            src_ref=columns(i, part, there),
            dst_ref=landing(i, part, me_f),
            send_sem=f_send.at[i * parts + part, k],
            recv_sem=f_recv.at[i * parts + part, k],
            device_id=(there, me_c, me_t),
            device_id_type=MESH_ID,
        )

    def f_arrival(i, part, k):
        there = flip_index(me_f, k, fsdp)
        return pltpu.make_async_remote_copy(
            src_ref=landing(i, part, there),
            dst_ref=landing(i, part, there),
            send_sem=f_send.at[i * parts + part, k],
            recv_sem=f_recv.at[i * parts + part, k],
            device_id=(there, me_c, me_t),
            device_id_type=MESH_ID,
        )

    pieces = [(i, part) for part in range(parts) for i in range(swaps)]
    for i in range(lines):
        for step in (1, -1):
            along(step, lambda there: z_copy(i, me_c, step, line_in[i]).start())
    order = fsdp_order(group)
    for i, part in pieces:
        for k in order:
            f_copy(i, part, k).start()
    own = [
        pltpu.make_async_copy(line_in[i], line_out[i].at[me_c], own_sem.at[i])
        for i in range(lines)
    ] + [
        pltpu.make_async_copy(
            columns(i, part, me_f),
            landing(i, part, me_f),
            own_sem.at[lines + i * parts + part],
        )
        for i, part in pieces
    ]
    for copy in own:
        copy.start()
    for distance in range(1, ctx):
        for i in range(lines):
            for step in (1, -1):
                shard = me_c - step * distance

                @pl.when((shard >= 0) & (shard < ctx))
                def _():
                    z_copy(i, shard, step).wait_recv()
                    along(step, lambda there: z_copy(i, shard, step).start())

    for i, part in pieces:
        for k in order:
            f_arrival(i, part, k).wait_recv()
            f_copy(i, part, k).wait_send()
    for copy in own:
        copy.wait()
    for i in range(lines):
        for step in (1, -1):
            along(step, lambda there: z_copy(i, me_c, step, line_in[i]).wait_send())
            for distance in range(1, ctx - 1):
                shard = me_c - step * distance

                @pl.when((shard >= 0) & (shard < ctx))
                def _():
                    along(step, lambda there: z_copy(i, shard, step).wait_send())


def start_exchange(fsdp, ctx, group, lines, swaps, widths):
    parts = len(widths)
    sems = pltpu.SemaphoreType.DMA
    rows = swaps[0].shape[0]
    out_shape = [jax.ShapeDtypeStruct((ctx,) + v.shape, v.dtype) for v in lines]
    out_shape += [
        jax.ShapeDtypeStruct((group, rows, len(swaps) * w), swaps[0].dtype) for w in widths
    ]
    count = len(lines) + len(swaps)
    outs = pl.pallas_call(
        partial(line_kernel, fsdp, ctx, group, len(lines), len(swaps), tuple(widths)),
        out_shape=out_shape,
        in_specs=[pl.BlockSpec(memory_space=pltpu.VMEM)] * count,
        out_specs=[pl.BlockSpec(memory_space=pl.ANY)] * len(out_shape),
        scratch_shapes=[
            sems((len(lines) + len(swaps) * parts,)),
            sems((len(lines), 2, ctx)),
            sems((len(lines), 2, ctx)),
            sems((len(swaps) * parts, group)),
            sems((len(swaps) * parts, group)),
        ],
        compiler_params=pltpu.CompilerParams(
            collective_id=0, has_side_effects=True, vmem_limit_bytes=24 * 1024 * 1024
        ),
    )(*lines, *swaps)
    return outs[: len(lines)], outs[len(lines) :]


class TokenGather:
    def __init__(self, group, fsdp, v_ref, out_ref, own_sem, f_send, f_recv, t_send, t_recv):
        self.order = fsdp_order(group)
        self.bits = [1 << i for i in range(group.bit_length() - 1)]
        self.out_ref = out_ref
        self.sems = (f_send, f_recv, t_send, t_recv)
        self.fsdp = fsdp
        half = out_ref.shape[2]
        self.half = half
        me_t = lax.axis_index("tp")
        self.mine = v_ref.at[pl.ds(pl.multiple_of(me_t * half, half), half)]
        other = v_ref.at[pl.ds(pl.multiple_of((1 - me_t) * half, half), half)]
        self.own = [
            pltpu.make_async_copy(self.mine, out_ref.at[0, 0], own_sem.at[0]),
            pltpu.make_async_copy(other, out_ref.at[0, 1], own_sem.at[1]),
        ]

    def peer(self, k):
        me_f = lax.axis_index("fsdp")
        return (flip_index(me_f, k, self.fsdp), lax.axis_index("ctx"), lax.axis_index("tp"))

    def rows(self, k, part):
        if k == low_bit(k):
            return pl.ds(0, self.half)
        return pl.ds(part * (self.half // 2), self.half // 2)

    def f_copy(self, have, b):
        k = have | b
        part = 1 if have and b == high_bit(k) else 0
        place = self.out_ref.at[k, 0, self.rows(k, part)]
        src = self.out_ref.at[have, 0, self.rows(k, part)] if have else self.mine
        return pltpu.make_async_remote_copy(
            src_ref=src,
            dst_ref=place,
            send_sem=self.sems[0].at[k, part],
            recv_sem=self.sems[1].at[k, part],
            device_id=self.peer(b),
            device_id_type=MESH_ID,
        )

    def ways(self, have):
        return [
            b
            for b in self.bits
            if not have & b and (not have or b in (low_bit(have | b), high_bit(have | b)))
        ]

    def swap(self, k):
        me_f, me_c, me_t = self.peer(0)
        return pltpu.make_async_remote_copy(
            src_ref=self.out_ref.at[k, 0],
            dst_ref=self.out_ref.at[k, 1],
            send_sem=self.sems[2].at[k],
            recv_sem=self.sems[3].at[k],
            device_id=(me_f, me_c, 1 - me_t),
            device_id_type=MESH_ID,
        )

    def start(self):
        for b in self.ways(0):
            self.f_copy(0, b).start()
        for copy in self.own:
            copy.start()

    def relay(self, k):
        parts = [(0, k)] if k == low_bit(k) else [(0, low_bit(k)), (1, high_bit(k))]
        for part, b in parts:
            place = self.out_ref.at[k, 0, self.rows(k, part)]
            pltpu.make_async_remote_copy(
                src_ref=place,
                dst_ref=place,
                send_sem=self.sems[0].at[k, part],
                recv_sem=self.sems[1].at[k, part],
                device_id=self.peer(b),
                device_id_type=MESH_ID,
            ).wait_recv()
        for b in self.ways(k):
            self.f_copy(k, b).start()
        self.swap(k).start()

    def finish(self):
        for copy in self.own:
            copy.wait()
        for have in [0] + self.order:
            for b in self.ways(have):
                self.f_copy(have, b).wait_send()
        me_f, me_c, me_t = self.peer(0)
        for k in self.order:
            pltpu.make_async_remote_copy(
                src_ref=self.out_ref.at[k, 1],
                dst_ref=self.out_ref.at[k, 1],
                send_sem=self.sems[2].at[k],
                recv_sem=self.sems[3].at[k],
                device_id=(me_f, me_c, 1 - me_t),
                device_id_type=MESH_ID,
            ).wait_recv()
            self.swap(k).wait_send()


def token_sems(group):
    sems = pltpu.SemaphoreType.DMA
    return [sems((2,)), sems((group, 2)), sems((group, 2)), sems((group,)), sems((group,))]


def token_shape(group, v):
    return jax.ShapeDtypeStruct((group, 2, v.shape[0] // 2, v.shape[1]), v.dtype)


def tokens_kernel(group, fsdp, v_ref, out_ref, *sems):
    gather = TokenGather(group, fsdp, v_ref, out_ref, *sems)
    me_f, me_c, me_t = gather.peer(0)
    barrier = pltpu.get_barrier_semaphore()
    for b in gather.bits:
        pl.semaphore_signal(barrier, inc=1, device_id=gather.peer(b), device_id_type=MESH_ID)
    pl.semaphore_signal(
        barrier, inc=1, device_id=(me_f, me_c, 1 - me_t), device_id_type=MESH_ID
    )
    pl.semaphore_wait(barrier, len(gather.bits) + 1)
    gather.start()
    for k in gather.order:
        gather.relay(k)
    gather.finish()


def gather_tokens(group, fsdp, v):
    out = pl.pallas_call(
        partial(tokens_kernel, group, fsdp),
        out_shape=token_shape(group, v),
        in_specs=[pl.BlockSpec(memory_space=pltpu.VMEM)],
        out_specs=pl.BlockSpec(memory_space=pl.ANY),
        scratch_shapes=token_sems(group),
        compiler_params=pltpu.CompilerParams(
            collective_id=5, has_side_effects=True, vmem_limit_bytes=24 * 1024 * 1024
        ),
    )(v)
    return out.reshape(-1, v.shape[1])


def swiglu_parts(n_ref, g_ref, w_ref, hidden_ref, grads_ref):
    units = hidden_ref.shape[1]
    both = w_ref[:, : 2 * units]
    down = w_ref[:, 2 * units :]
    lin = mul(n_ref[...], both)
    gate, up = lin[:, :units], lin[:, units:]
    sig = jax.nn.sigmoid(gate)
    act = gate * sig
    hidden = (act * up).astype(jnp.bfloat16)
    hidden_ref[...] = hidden
    hidden_grad = mul(g_ref[...], down)
    grads_ref[:, :units] = (hidden_grad * up * sig * (1.0 + gate * (1.0 - sig))).astype(
        jnp.bfloat16
    )
    grads_ref[:, units:] = (hidden_grad * act).astype(jnp.bfloat16)
    return mul(grads_ref[...], both, NT), mul(hidden, down, NT)


def swiglu_first_kernel(n_ref, g_ref, w_ref, hidden_ref, grads_ref, second_ref, ff_ref):
    second, ff = swiglu_parts(n_ref, g_ref, w_ref, hidden_ref, grads_ref)
    second_ref[...] = second.astype(jnp.bfloat16)
    ff_ref[...] = ff.astype(jnp.bfloat16)


def swiglu_kernel(
    fsdp,
    group,
    n_ref,
    g_ref,
    w_ref,
    second_ref,
    ff_first_ref,
    hidden_ref,
    grads_ref,
    ff_ref,
    own_ref,
    s_out,
    f_out,
    s_in,
    f_in,
    total,
    got,
    t_send,
    t_recv,
    f_send,
    f_recv,
    own_sem,
):
    half = n_ref.shape[0]
    step = pl.program_id(0)
    me_f = lax.axis_index("fsdp")
    me_c = lax.axis_index("ctx")
    me_t = lax.axis_index("tp")
    bits = [1 << i for i in range(group.bit_length() - 1)]
    order = fsdp_order(group)
    core = (me_f, me_c, 1 - me_t)

    def peer(k):
        return (flip_index(me_f, k, fsdp), me_c, me_t)

    @pl.when(step == 0)
    def _():
        barrier = pltpu.get_barrier_semaphore()
        for b in bits:
            pl.semaphore_signal(barrier, inc=1, device_id=peer(b), device_id_type=MESH_ID)
        pl.semaphore_signal(barrier, inc=1, device_id=core, device_id_type=MESH_ID)
        pl.semaphore_wait(barrier, len(bits) + 1)

    def core_copies(k):
        slot = k % 2
        return [
            pltpu.make_async_remote_copy(
                src_ref=out.at[slot],
                dst_ref=into.at[slot],
                send_sem=t_send.at[which, k],
                recv_sem=t_recv.at[which, k],
                device_id=core,
                device_id_type=MESH_ID,
            )
            for which, (out, into) in enumerate(((s_out, s_in), (f_out, f_in)))
        ]

    def ways(k):
        return [(0, k)] if k == low_bit(k) else [(0, low_bit(k)), (1, high_bit(k))]

    def span(k, part):
        return pl.ds(0, half) if k == low_bit(k) else pl.ds(part * (half // 2), half // 2)

    def f_copy(k, part, b):
        return pltpu.make_async_remote_copy(
            src_ref=total.at[k, span(k, part)],
            dst_ref=got.at[k, span(k, part)],
            send_sem=f_send.at[k, part],
            recv_sem=f_recv.at[k, part],
            device_id=peer(b),
            device_id_type=MESH_ID,
        )

    def own_copy():
        return pltpu.make_async_remote_copy(
            src_ref=total.at[0],
            dst_ref=own_ref.at[me_t],
            send_sem=own_sem.at[0],
            recv_sem=own_sem.at[1],
            device_id=core,
            device_id_type=MESH_ID,
        )

    second, ff = swiglu_parts(n_ref, g_ref, w_ref, hidden_ref, grads_ref)
    second = second + second_ref[...].astype(jnp.float32)
    ff = ff + ff_first_ref[...].astype(jnp.float32)

    for k in reversed(range(group)):
        slot = k % 2

        @pl.when(step == 2 * (group - 1 - k))
        def _():
            if k + 2 < group:
                for copy in core_copies(k + 2):
                    copy.wait_send()
            s_out[slot] = second.astype(jnp.bfloat16)
            f_out[slot] = ff.astype(jnp.bfloat16)
            for copy in core_copies(k):
                copy.start()

        @pl.when(step == 2 * (group - 1 - k) + 1)
        def _():
            for copy in core_copies(k):
                copy.wait_recv()
            ff_ref[...] = (ff + f_in[slot].astype(jnp.float32)).astype(jnp.bfloat16)
            total[k] = (second + s_in[slot].astype(jnp.float32)).astype(jnp.bfloat16)
            for far in order:
                for part, b in ways(far):
                    if far ^ b == k:
                        f_copy(far, part, b).wait_recv()
                        rows = span(far, part)
                        total[k, rows] = (
                            total[k, rows].astype(jnp.float32)
                            + got[far, rows].astype(jnp.float32)
                        ).astype(jnp.bfloat16)
            if k:
                for part, b in ways(k):
                    f_copy(k, part, b).start()
            else:
                own_copy().start()
                local = pltpu.make_async_copy(total.at[0], own_ref.at[me_t], own_sem.at[2])
                local.start()
                local.wait()
                other = own_ref.at[1 - me_t]
                pltpu.make_async_remote_copy(
                    src_ref=other,
                    dst_ref=other,
                    send_sem=own_sem.at[0],
                    recv_sem=own_sem.at[1],
                    device_id=core,
                    device_id_type=MESH_ID,
                ).wait_recv()
                own_copy().wait_send()
                for far in order:
                    for part, b in ways(far):
                        f_copy(far, part, b).wait_send()
                for late in range(min(2, group)):
                    for copy in core_copies(late):
                        copy.wait_send()


def swiglu(fsdp, group, normed, grads, weights, second, ff):
    many, width = normed.shape
    half = many // (2 * group)
    units = weights.shape[1] // 3
    low = jnp.bfloat16
    last = 2 * group - 1
    sems = pltpu.SemaphoreType.DMA
    block = (half, width)

    def rows(cols):
        return pl.BlockSpec((half, cols), lambda i: (last - i, 0))

    def whole(v):
        return pl.BlockSpec(v.shape, lambda i: (0, 0), pipeline_mode=pl.Buffered(1))

    return pl.pallas_call(
        partial(swiglu_kernel, fsdp, group),
        grid=(2 * group,),
        in_specs=[rows(width), rows(width), whole(weights), rows(width), rows(width)],
        out_specs=[
            rows(units),
            rows(2 * units),
            pl.BlockSpec(block, lambda i: (group - 1 - i // 2, 0)),
            pl.BlockSpec(memory_space=pl.ANY),
        ],
        out_shape=[
            jax.ShapeDtypeStruct((many, units), low),
            jax.ShapeDtypeStruct((many, 2 * units), low),
            jax.ShapeDtypeStruct((group * half, width), low),
            jax.ShapeDtypeStruct((2,) + block, low),
        ],
        scratch_shapes=[pltpu.VMEM((2,) + block, low)] * 4
        + [pltpu.VMEM((group,) + block, low)] * 2
        + [
            sems((2, group)),
            sems((2, group)),
            sems((group, 2)),
            sems((group, 2)),
            sems((3,)),
        ],
        compiler_params=pltpu.CompilerParams(
            collective_id=6, has_side_effects=True, vmem_limit_bytes=58 * 1024 * 1024
        ),
        cost_estimate=pl.CostEstimate(
            flops=12 * many * width * units, bytes_accessed=50 << 20, transcendentals=0
        ),
    )(normed, grads, weights, second, ff)


def spread_kernel(fsdp, ctx, group, count, chain, *refs):
    ins = refs[:count]
    outs = refs[count + chain : 2 * count + chain]
    sems = refs[2 * (count + chain) :]
    own_sem, f_send, f_recv, c_own, c_send, c_recv = sems[:6]
    me_f = lax.axis_index("fsdp")
    me_c = lax.axis_index("ctx")
    me_t = lax.axis_index("tp")
    bits = [1 << i for i in range(fsdp.bit_length() - 1)]
    order = fsdp_order(fsdp)

    def peer(k):
        return (flip_index(me_f, k, fsdp), me_c, me_t)

    barrier = pltpu.get_barrier_semaphore()
    for b in bits:
        pl.semaphore_signal(barrier, inc=1, device_id=peer(b), device_id_type=MESH_ID)
    if chain:
        chain_in, chain_out = refs[count], refs[2 * count + chain]
        gather = TokenGather(
            group, fsdp, refs[count + 1], refs[2 * count + chain + 1], *sems[6:]
        )
        pl.semaphore_signal(
            barrier, inc=1, device_id=(me_f, me_c, 1 - me_t), device_id_type=MESH_ID
        )
        for step in (-1, 1):
            there = me_c + step

            @pl.when((there >= 0) & (there < ctx))
            def _():
                pl.semaphore_signal(
                    barrier, inc=1, device_id=(me_f, there, me_t), device_id_type=MESH_ID
                )

        pl.semaphore_wait(barrier, len(bits) + 1 + line_neighbours(me_c, ctx))
    else:
        pl.semaphore_wait(barrier, len(bits))

    def quarters(rows):
        return [pl.ds(i * (rows // 4), rows // 4) for i in range(4)]

    def climb(s):
        return [
            pltpu.make_async_remote_copy(
                src_ref=chain_out.at[s, part] if s else chain_in.at[part],
                dst_ref=chain_out.at[s + 1, part],
                send_sem=c_send.at[s, i],
                recv_sem=c_recv.at[s + 1, i],
                device_id=(me_f, me_c + 1, me_t),
                device_id_type=MESH_ID,
            )
            for i, part in enumerate(quarters(chain_in.shape[0]))
        ]

    def keep(s):
        return pltpu.make_async_copy(chain_in, chain_out.at[s], c_own.at[s])

    def send_up(s):
        @pl.when((me_c >= s) & (me_c < ctx - 1))
        def _():
            for copy in climb(s):
                copy.start()

    def take_up(s):
        @pl.when(me_c >= s)
        def _():
            for i, part in enumerate(quarters(chain_in.shape[0])):
                pltpu.make_async_remote_copy(
                    src_ref=chain_out.at[s, part],
                    dst_ref=chain_out.at[s, part],
                    send_sem=c_send.at[s - 1, i],
                    recv_sem=c_recv.at[s, i],
                    device_id=(me_f, me_c - 1, me_t),
                    device_id_type=MESH_ID,
                ).wait_recv()

        if s < ctx - 1:
            send_up(s)

    if chain:
        send_up(0)
        keep(0).start()
        for s in range(1, ctx):
            @pl.when(me_c < s)
            def _():
                keep(s).start()

    def place(i, shard, have, k, part):
        block = outs[i].at[shard, flip_index(me_f, have, fsdp)]
        half = ins[i].shape[1] // 2
        return block if k == low_bit(k) else block.at[pl.ds(part * half, half)]

    def f_copy(i, shard, have, b):
        k = have | b
        part = 1 if have and b == high_bit(k) else 0
        block = place(i, shard, have, k, part)
        return pltpu.make_async_remote_copy(
            src_ref=block if have else ins[i].at[shard],
            dst_ref=block,
            send_sem=f_send.at[i, shard, k, part],
            recv_sem=f_recv.at[i, shard, k, part],
            device_id=peer(b),
            device_id_type=MESH_ID,
        )

    def ways(have):
        return [
            b
            for b in bits
            if not have & b and (not have or b in (low_bit(have | b), high_bit(have | b)))
        ]

    own = [
        pltpu.make_async_copy(ins[i], outs[i].at[:, me_f], own_sem.at[i]) for i in range(count)
    ]
    for i in range(count):
        for shard in range(ctx):
            for b in ways(0):
                f_copy(i, shard, 0, b).start()
        own[i].start()
    if chain:
        gather.start()
    climbed = 1
    for i in range(count):
        for k in order:
            if chain and climbed < ctx:
                take_up(climbed)
                climbed += 1
            if chain and k < group and i == 0:
                gather.relay(k)
            parts = [(0, k)] if k == low_bit(k) else [(0, low_bit(k)), (1, high_bit(k))]
            for shard in range(ctx):
                for part, b in parts:
                    block = place(i, shard, k, k, part)
                    pltpu.make_async_remote_copy(
                        src_ref=block,
                        dst_ref=block,
                        send_sem=f_send.at[i, shard, k, part],
                        recv_sem=f_recv.at[i, shard, k, part],
                        device_id=peer(b),
                        device_id_type=MESH_ID,
                    ).wait_recv()
                for b in ways(k):
                    f_copy(i, shard, k, b).start()
    if chain:
        for s in range(climbed, ctx):
            take_up(s)
        gather.finish()
        keep(0).wait()
        for s in range(ctx):
            if s:

                @pl.when(me_c < s)
                def _():
                    keep(s).wait()

            if s < ctx - 1:

                @pl.when((me_c >= s) & (me_c < ctx - 1))
                def _():
                    for copy in climb(s):
                        copy.wait_send()

    for i in range(count):
        own[i].wait()
        for have in [0] + order:
            for shard in range(ctx):
                for b in ways(have):
                    f_copy(i, shard, have, b).wait_send()


def spread_weights(fsdp, ctx, group, arrays, chain=()):
    count = len(arrays)
    sems = pltpu.SemaphoreType.DMA
    outs = pl.pallas_call(
        partial(spread_kernel, fsdp, ctx, group, count, len(chain)),
        out_shape=[
            jax.ShapeDtypeStruct((ctx, fsdp) + v.shape[1:], v.dtype) for v in arrays
        ]
        + [jax.ShapeDtypeStruct((ctx,) + v.shape, v.dtype) for v in chain[:1]]
        + [token_shape(group, v) for v in chain[1:]],
        in_specs=[pl.BlockSpec(memory_space=pltpu.VMEM)] * (count + len(chain)),
        out_specs=[pl.BlockSpec(memory_space=pl.ANY)] * (count + len(chain)),
        scratch_shapes=[
            sems((count,)),
            sems((count, ctx, fsdp, 2)),
            sems((count, ctx, fsdp, 2)),
            sems((ctx,)),
            sems((ctx, 4)),
            sems((ctx, 4)),
        ]
        + (token_sems(group) if chain else []),
        compiler_params=pltpu.CompilerParams(
            collective_id=3 if chain else 1,
            has_side_effects=True,
            vmem_limit_bytes=24 * 1024 * 1024,
        ),
    )(*arrays, *chain)
    return (
        [o.reshape(-1, v.shape[-1]) for o, v in zip(outs, arrays)]
        + list(outs[count : count + 1])
        + [o.reshape(-1, o.shape[-1]) for o in outs[count + 1 :]]
    )


def sum_kernel(fsdp, ctx, count, chain, *refs):
    ins = refs[:count]
    if chain:
        parts_ref, cos_ref, sin_ref = refs[count : count + 3]
        refs = refs[:count] + refs[count + 3 :]
        kv_ref = refs[2 * count]
        refs = refs[: 2 * count] + refs[2 * count + 1 :]
    outs = refs[count : 2 * count]
    held = refs[2 * count : 3 * count]
    got = refs[3 * count : 4 * count]
    line = refs[4 * count : 5 * count]
    refs = refs[5 * count :]
    in_sem, f_send, f_recv, z_send, z_recv = refs[:5]
    if chain:
        kv_parts, kv_got, kv_sem, c_send, c_recv = refs[5:]
    me_f = lax.axis_index("fsdp")
    me_c = lax.axis_index("ctx")
    me_t = lax.axis_index("tp")
    bits = [1 << i for i in range(fsdp.bit_length() - 1)]
    order = fsdp_order(fsdp)

    def peer(k):
        return (flip_index(me_f, k, fsdp), me_c, me_t)

    def along(step, act):
        there = me_c + step

        @pl.when((there >= 0) & (there < ctx))
        def _():
            act(there)

    loads = {}
    if chain:
        kv_load = pltpu.make_async_copy(parts_ref, kv_parts, kv_sem.at[0])
        kv_load.start()
    for i in range(count):
        for k in reversed([0] + order):
            block = ins[i].at[:, flip_index(me_f, k, fsdp)]
            loads[i, k] = pltpu.make_async_copy(block, held[i].at[k], in_sem.at[i, k])
            loads[i, k].start()

    barrier = pltpu.get_barrier_semaphore()
    for b in bits:
        pl.semaphore_signal(barrier, inc=1, device_id=peer(b), device_id_type=MESH_ID)
    for step in (-1, 1):
        along(
            step,
            lambda there: pl.semaphore_signal(
                barrier, inc=1, device_id=(me_f, there, me_t), device_id_type=MESH_ID
            ),
        )
    pl.semaphore_wait(barrier, len(bits) + line_neighbours(me_c, ctx))

    def ways(k):
        return [(0, k)] if k == low_bit(k) else [(0, low_bit(k)), (1, high_bit(k))]

    def piece(i, k, part):
        rows = ins[i].shape[2]
        return pl.ds(0, rows) if k == low_bit(k) else pl.ds(part * (rows // 2), rows // 2)

    def f_copy(i, shard, k, part, b):
        span = piece(i, k, part)
        return pltpu.make_async_remote_copy(
            src_ref=held[i].at[k, shard, span],
            dst_ref=got[i].at[k, shard, span],
            send_sem=f_send.at[i, shard, k, part],
            recv_sem=f_recv.at[i, shard, k, part],
            device_id=peer(b),
            device_id_type=MESH_ID,
        )

    def add(into, other):
        tile = 16 if into.dtype == jnp.bfloat16 else 8

        def body(r, _):
            span = pl.ds(pl.multiple_of(r * tile, tile), tile)
            into[span] = (
                into[span].astype(jnp.float32) + other[span].astype(jnp.float32)
            ).astype(into.dtype)
            return 0

        lax.fori_loop(0, into.shape[0] // tile, body, 0)

    def collect(i, shard, k):
        for far in order:
            for part, b in ways(far):
                if far ^ b == k:
                    f_copy(i, shard, far, part, b).wait_recv()
                    span = piece(i, far, part)
                    add(held[i].at[k, shard, span], got[i].at[far, shard, span])

    def z_copy(i, shard, step):
        way = 0 if step > 0 else 1
        return pltpu.make_async_remote_copy(
            src_ref=held[i].at[0, shard],
            dst_ref=line[i].at[way, shard],
            send_sem=z_send.at[i, way, shard],
            recv_sem=z_recv.at[i, way, shard],
            device_id=(me_f, me_c + step, me_t),
            device_id_type=MESH_ID,
        )

    def give(i, shard):
        def body(r, _):
            span = pl.ds(pl.multiple_of(r * 16, 16), 16)
            outs[i][span] = held[i][0, shard, span].astype(outs[i].dtype)
            return 0

        lax.fori_loop(0, outs[i].shape[0] // 16, body, 0)

    def on_line(i, shard, step):
        way = 0 if step > 0 else 1

        @pl.when((me_c - step >= 0) & (me_c - step < ctx))
        def _():
            z_copy(i, shard, step).wait_recv()
            add(held[i].at[0, shard], line[i].at[way, shard])

        @pl.when(step * (shard - me_c) > 0)
        def _():
            z_copy(i, shard, step).start()

    def quarters():
        rows = kv_parts.shape[2] // 2
        return [(side, pl.ds(i * rows, rows)) for side in range(2) for i in range(2)]

    def descend(s):
        return [
            pltpu.make_async_remote_copy(
                src_ref=kv_parts.at[s, side, part],
                dst_ref=kv_got.at[s - 1, side, part],
                send_sem=c_send.at[s, i],
                recv_sem=c_recv.at[s - 1, i],
                device_id=(me_f, me_c - 1, me_t),
                device_id_type=MESH_ID,
            )
            for i, (side, part) in enumerate(quarters())
        ]

    def chain_step(s):
        if s < ctx - 1:

            @pl.when((me_c >= s) & (me_c < ctx - 1))
            def _():
                for i, (side, part) in enumerate(quarters()):
                    pltpu.make_async_remote_copy(
                        src_ref=kv_got.at[s, side, part],
                        dst_ref=kv_got.at[s, side, part],
                        send_sem=c_send.at[s + 1, i],
                        recv_sem=c_recv.at[s, i],
                        device_id=(me_f, me_c + 1, me_t),
                        device_id_type=MESH_ID,
                    ).wait_recv()
                    add(kv_parts.at[s, side, part], kv_got.at[s, side, part])

        if s:

            @pl.when(me_c >= s)
            def _():
                for copy in descend(s):
                    copy.start()

    def chain_result():
        width = kv_parts.shape[3]
        rows = cos_ref.shape[0]
        for seq in range(kv_parts.shape[2] // rows):
            span = pl.ds(seq * rows, rows)
            for start in range(0, width, 128):
                cols = slice(start, start + 128)
                t = kv_parts[0, 0, span, cols].astype(jnp.float32)
                t = t * cos_ref[...] + turn(t * sin_ref[...], -1.0)
                kv_ref[span, cols] = t.astype(kv_ref.dtype)
            kv_ref[span, width:] = kv_parts[0, 1, span]

    steps = list(reversed(range(ctx))) if chain else []

    def next_step():
        if steps:
            s = steps.pop(0)
            chain_step(s)
            if s == 0:
                chain_result()

    if chain:
        kv_load.wait()
        next_step()
    shards = sorted(range(ctx), key=lambda c: -abs(2 * c - ctx + 1))
    work = [[(i, shard) for i in range(count)] for shard in shards]
    levels = sorted({bin(k).count("1") for k in order}, reverse=True)
    waited = set()

    def loaded(i, k):
        if (i, k) not in waited:
            waited.add((i, k))
            loads[i, k].wait()

    def advance(stage, item):
        for i, shard in item:
            if stage == len(levels):
                loaded(i, 0)
                collect(i, shard, 0)
                continue
            for k in order:
                if bin(k).count("1") == levels[stage]:
                    loaded(i, k)
                    collect(i, shard, k)
                    for part, b in ways(k):
                        f_copy(i, shard, k, part, b).start()

    def line_tick(item, hops):
        for i, shard in item:
            for step, there in ((1, hops), (-1, ctx - 1 - hops)):
                if step * (shard - there) >= 0:

                    @pl.when(me_c == there)
                    def _():
                        on_line(i, shard, step)

            if hops == max(shard, ctx - 1 - shard):

                @pl.when(me_c == shard)
                def _():
                    give(i, shard)

    stages = len(levels) + 1
    for tick in range(len(work) + stages + ctx - 2):
        for stage in range(stages):
            if 0 <= tick - stage < len(work):
                advance(stage, work[tick - stage])
        for hops in range(ctx):
            place = tick - stages + 1 - hops
            if 0 <= place < len(work):
                line_tick(work[place], hops)
        next_step()
    while steps:
        next_step()
    for i, shard in [pair for item in work for pair in item]:
        for k in order:
            for part, b in ways(k):
                f_copy(i, shard, k, part, b).wait_send()
        for step in (1, -1):

            @pl.when(step * (shard - me_c) > 0)
            def _():
                z_copy(i, shard, step).wait_send()

    if chain:
        for s in range(1, ctx):

            @pl.when(me_c >= s)
            def _():
                for copy in descend(s):
                    copy.wait_send()


def sum_weights(fsdp, ctx, arrays, chain=()):
    sems = pltpu.SemaphoreType.DMA
    vmem = pltpu.VMEM
    shards = [v.reshape(ctx, fsdp, -1, v.shape[-1]) for v in arrays]
    blocks = [(fsdp, ctx) + v.shape[2:] for v in shards]
    out_shape = [jax.ShapeDtypeStruct(v.shape[2:], jnp.float32) for v in shards]
    lines = [vmem((2,) + b[1:], v.dtype) for b, v in zip(blocks, shards)]
    extra = []
    if chain:
        parts = chain[0]
        out_shape.append(jax.ShapeDtypeStruct((parts.shape[2], 2 * parts.shape[3]), parts.dtype))
        extra = [
            vmem(parts.shape, parts.dtype),
            vmem((ctx - 1,) + parts.shape[1:], parts.dtype),
            sems((1,)),
            sems((ctx, 4)),
            sems((ctx, 4)),
        ]
    count = len(shards)
    held = [vmem(b, v.dtype) for b, v in zip(blocks, shards)]
    return pl.pallas_call(
        partial(sum_kernel, fsdp, ctx, count, bool(chain)),
        out_shape=out_shape,
        in_specs=[pl.BlockSpec(memory_space=pl.ANY)] * (count + len(chain[:1]))
        + [pl.BlockSpec(memory_space=pltpu.VMEM)] * len(chain[1:]),
        out_specs=[pl.BlockSpec(memory_space=pltpu.VMEM)] * len(out_shape),
        scratch_shapes=held
        + held
        + lines
        + [
            sems((count, fsdp)),
            sems((count, ctx, fsdp, 2)),
            sems((count, ctx, fsdp, 2)),
            sems((count, 2, ctx)),
            sems((count, 2, ctx)),
        ]
        + extra,
        compiler_params=pltpu.CompilerParams(
            collective_id=4 if chain else 2,
            has_side_effects=True,
            vmem_limit_bytes=52 * 1024 * 1024,
        ),
    )(*shards, *chain)


def place_kernel(group, count, *refs):
    parts, outs = refs[:count], refs[count:]
    span = sum(v.shape[3] for v in parts)
    for i, out in enumerate(outs):
        for f in range(group):
            start = f * span
            for v in parts:
                width = v.shape[3]
                out[:, start : start + width] = v[f, i].astype(out.dtype)
                start += width


def place_units(parts):
    group, arrays, rows, _ = parts[0].shape
    cols = group * sum(v.shape[3] for v in parts)
    vmem = pl.BlockSpec(memory_space=pltpu.VMEM)
    return pl.pallas_call(
        partial(place_kernel, group, len(parts)),
        out_shape=[jax.ShapeDtypeStruct((rows, cols), jnp.float32)] * arrays,
        in_specs=[vmem] * len(parts),
        out_specs=[vmem] * arrays,
        compiler_params=pltpu.CompilerParams(vmem_limit_bytes=24 * 1024 * 1024),
        cost_estimate=pl.CostEstimate(
            flops=0, bytes_accessed=6 * rows * cols * arrays, transcendentals=0
        ),
    )(*parts)


def local(
    inputs,
    lengths,
    cotangent,
    norm1_gain,
    w_query,
    w_key,
    w_value,
    w_out,
    norm2_gain,
    w_gate,
    w_up,
    w_down,
):
    seq_count, local_rows, model_width = inputs.shape
    tokens = seq_count * local_rows
    half = tokens // 2
    fsdp = lax.axis_size("fsdp")
    ctx = lax.axis_size("ctx")
    shard = w_query.shape[0]
    query_width = w_query.shape[1]
    kv_width = w_key.shape[1]
    kv_end = query_width + 2 * kv_width
    pairs = kv_width // (2 * HD)
    group_size = query_width // kv_width
    group = min(fsdp, 4)
    far = fsdp // group
    own = w_gate.shape[1] // group
    first_units = own * FIRST_EIGHTHS // 8
    widths = (first_units, own - first_units)
    me_c = lax.axis_index("ctx")
    me_t = lax.axis_index("tp")
    low = jnp.bfloat16
    wide = jnp.float32

    def swap(v):
        return lax.ppermute(v, "tp", [(0, 1), (1, 0)])

    inside = shard % 128 == 0
    dims = (fsdp, ctx, shard)
    back_dims = (ctx, fsdp, shard)

    def by_ctx(v):
        if inside:
            return v
        rows = v.shape[0]
        return v.reshape(rows, fsdp, ctx, shard).swapaxes(1, 2).reshape(rows, model_width)

    def by_fsdp(v):
        if inside:
            return v
        rows = v.shape[0]
        return v.reshape(rows, ctx, fsdp, shard).swapaxes(1, 2).reshape(rows, model_width)

    def pair_heads(v):
        rows = v.shape[0]
        return (
            v.reshape(rows, pairs, 2, group_size, HD).swapaxes(2, 3).reshape(rows, query_width)
        )

    def plain_heads(v):
        rows = v.shape[0]
        return (
            v.reshape(rows, pairs, group_size, 2, HD).swapaxes(2, 3).reshape(rows, query_width)
        )

    x = by_ctx(inputs.reshape(tokens, model_width))
    cot = by_ctx(cotangent.reshape(tokens, model_width))
    positions = me_c * local_rows + jnp.arange(local_rows, dtype=jnp.int32)
    cosines, sines = rope_tables(positions, HD)
    cosines, sines = jnp.tile(cosines, (1, 2)), jnp.tile(sines, (1, 2))

    gains = jnp.pad(jnp.stack([norm1_gain, norm2_gain]).astype(wide), ((0, 14), (0, 0)))
    lined, held = start_exchange(
        fsdp,
        ctx,
        group,
        [
            jnp.concatenate([pair_heads(w_query), w_key, w_value], 1),
            gains,
            pair_heads(w_out),
        ],
        [w_gate, w_up, w_down],
        widths,
    )
    far_groups = [[h * group + g for h in range(far)] for g in range(group)]
    near_groups = [[h * group + g for g in range(group)] for h in range(far)]

    def whole_width(v):
        if far > 1:
            v = lax.all_gather(v, "fsdp", axis=0, tiled=False, axis_index_groups=far_groups)
        return lax.all_gather(v, "ctx", axis=0, tiled=False).reshape(model_width, -1)

    first_full = whole_width(held[0])
    qkv_full, gain_rows = spread_weights(fsdp, ctx, group, lined[:2])
    late_held, gain_rows = lax.optimization_barrier((held[1], gain_rows))
    late_full = whole_width(late_held)
    gain_rows = gain_rows.reshape(ctx * fsdp, 16, shard)
    gain_one = gain_rows[:, 0].reshape(1, model_width)
    gain_two = gain_rows[:, 1].reshape(1, model_width)

    (ff_grad,) = by_rows(
        partial(cot_kernel, dims, local_rows),
        128,
        [(lengths, "smem"), (cot, "rows")],
        [((tokens, model_width), low)],
    )
    first_normed, query, kv_own = by_rows(
        partial(qkv_kernel, dims),
        128,
        [
            (x, "rows"),
            (qkv_full, "whole"),
            (gain_one, "whole"),
            (cosines, "cycle"),
            (sines, "cycle"),
        ],
        [
            ((tokens, model_width), low),
            ((tokens, query_width), low),
            ((tokens, 2 * kv_width), low),
        ],
        flops=2 * tokens * model_width * kv_end,
    )
    out_full, kv_all, ff_grad_all = spread_weights(
        fsdp, ctx, group, lined[2:], (kv_own, ff_grad)
    )
    attended, lse = attend(lengths, query, kv_all)
    attn_part = jnp.einsum(
        "tj,dj->td", attended, out_full, preferred_element_type=wide
    ).astype(low)
    middle, second_normed = by_rows(
        partial(middle_kernel, dims),
        128,
        [(x, "rows"), (attn_part, "rows"), (swap(attn_part), "rows"), (gain_two, "whole")],
        [((tokens, model_width), wide), ((tokens, model_width), low)],
    )
    normed_all = gather_tokens(group, fsdp, second_normed)

    def unit_term(left, right):
        return jnp.einsum("td,tf->df", left, right, preferred_element_type=wide).astype(low)

    def own_units(term):
        width = term.shape[1]
        own = lax.psum_scatter(
            term.reshape(ctx, fsdp, shard, width), "ctx", scatter_dimension=0, tiled=False
        )
        if far > 1:
            own = lax.psum_scatter(
                own.reshape(far, group, shard, width),
                "fsdp",
                scatter_dimension=0,
                tiled=False,
                axis_index_groups=far_groups,
            )
        return own

    def return_units(both, down):
        units = down.shape[-1]
        pieces = jnp.concatenate([both[..., :units], both[..., units:], down], 1)
        back = lax.all_to_all(
            pieces.reshape(group * 3 * shard, units),
            "fsdp",
            0,
            0,
            tiled=True,
            axis_index_groups=near_groups if far > 1 else None,
        )
        return back.reshape(group, 3, shard, units)

    many = group * tokens
    first_hidden, first_grads, second_part, ff_part = by_rows(
        swiglu_first_kernel,
        256,
        [(normed_all, "rows"), (ff_grad_all, "rows"), (first_full, "whole")],
        [
            ((many, first_units), low),
            ((many, 2 * first_units), low),
            ((many, model_width), low),
            ((many, model_width), low),
        ],
        flops=12 * many * model_width * first_units,
        limit=56,
    )
    first_both = unit_term(normed_all, first_grads)
    first_down = unit_term(ff_grad_all, first_hidden)
    first_own = (own_units(first_both), own_units(first_down))
    second_part, ff_part, _, _ = lax.optimization_barrier(
        (second_part, ff_part, first_both, first_down)
    )
    hidden, both_grad, ff_sums, second_grad = swiglu(
        fsdp, group, normed_all, ff_grad_all, late_full, second_part, ff_part
    )
    second_grad = second_grad.reshape(tokens, model_width)

    middle_grad, attn_grad, gain_two_term = by_rows(
        partial(middle_back_kernel, dims, local_rows),
        128,
        [
            (lengths, "smem"),
            (cot, "rows"),
            (middle, "rows"),
            (second_grad, "rows"),
            (gain_two, "whole"),
        ],
        [((tokens, model_width), wide), ((tokens, model_width), low), ((1, model_width), wide)],
    )
    attended_grad = jnp.dot(attn_grad, out_full, preferred_element_type=wide).astype(low)
    query_grad, kv_parts, ff_branch = attend_back(
        fsdp,
        group,
        lengths,
        query,
        attended_grad,
        lse,
        cosines,
        sines,
        kv_all,
        ff_sums.reshape(group, half, model_width),
    )
    query_grad, normed_all, ff_grad_all, both_grad, hidden = lax.optimization_barrier(
        (query_grad, normed_all, ff_grad_all, both_grad, hidden)
    )
    late_down = unit_term(ff_grad_all, hidden)
    late_down_own = own_units(late_down)
    out_term = jnp.einsum("td,tj->dj", attn_grad, attended, preferred_element_type=wide)
    kv_parts, _ = lax.optimization_barrier((kv_parts, late_down))
    w_out_grad, kv_grad = sum_weights(
        fsdp, ctx, [out_term.astype(low)], (kv_parts, cosines, sines)
    )
    (output,) = by_rows(
        partial(output_kernel, back_dims, local_rows),
        128,
        [(lengths, "smem"), (middle, "rows"), (ff_branch.reshape(tokens, model_width), "rows")],
        [((tokens, model_width), low)],
    )
    kv_grad, normed_all, both_grad = lax.optimization_barrier((kv_grad, normed_all, both_grad))
    late_both = unit_term(normed_all, both_grad)
    late_both_own = own_units(late_both)
    qkv_grad = jnp.concatenate([query_grad, kv_grad], -1)
    qkv_term = jnp.einsum("td,tj->dj", first_normed, qkv_grad, preferred_element_type=wide)
    first_part = jnp.einsum(
        "tj,dj->td", qkv_grad, qkv_full, preferred_element_type=wide
    ).astype(low)
    input_grad, gain_one_term = by_rows(
        partial(input_back_kernel, dims),
        128,
        [
            (x, "rows"),
            (first_part, "rows"),
            (swap(first_part), "rows"),
            (middle_grad, "rows"),
            (gain_one, "whole"),
        ],
        [((tokens, model_width), low), ((1, model_width), wide)],
    )
    gain_terms = jnp.stack(
        [gain_one_term.reshape(-1, shard), gain_two_term.reshape(-1, shard)], 1
    )
    gain_terms = jnp.pad(gain_terms, ((0, 0), (0, 14), (0, 0))).reshape(-1, shard)
    first_back = return_units(*first_own)
    qkv_term, first_back, _ = lax.optimization_barrier(
        (qkv_term.astype(low), first_back, late_both)
    )
    qkv_own, gain_own = sum_weights(fsdp, ctx, [qkv_term, gain_terms])
    late_both_own, late_down_own, qkv_own = lax.optimization_barrier(
        (late_both_own, late_down_own, qkv_own)
    )
    late_back = return_units(late_both_own, late_down_own)
    w_gate_grad, w_up_grad, w_down_grad = place_units([first_back, late_back])
    return (
        by_fsdp(output).reshape(inputs.shape),
        by_fsdp(input_grad).reshape(inputs.shape),
        gain_own[0],
        plain_heads(qkv_own[:, :query_width]),
        qkv_own[:, query_width : query_width + kv_width],
        qkv_own[:, query_width + kv_width :],
        plain_heads(w_out_grad),
        gain_own[1],
        w_gate_grad,
        w_up_grad,
        w_down_grad,
    )


def solution(mesh):
    placed = (
        P("fsdp", "ctx", None),
        P("fsdp"),
        P("fsdp", "ctx", None),
        P(("fsdp", "ctx")),
        P(("fsdp", "ctx"), "tp"),
        P(("fsdp", "ctx"), "tp"),
        P(("fsdp", "ctx"), "tp"),
        P(("fsdp", "ctx"), "tp"),
        P(("fsdp", "ctx")),
        P(("fsdp", "ctx"), "tp"),
        P(("fsdp", "ctx"), "tp"),
        P(("fsdp", "ctx"), "tp"),
    )
    return jax.shard_map(
        local,
        mesh=mesh,
        in_specs=placed,
        out_specs=(
            P("fsdp", "ctx", None),
            P("fsdp", "ctx", None),
            P(("fsdp", "ctx")),
            P(("fsdp", "ctx"), "tp"),
            P(("fsdp", "ctx"), "tp"),
            P(("fsdp", "ctx"), "tp"),
            P(("fsdp", "ctx"), "tp"),
            P(("fsdp", "ctx")),
            P(("fsdp", "ctx"), "tp"),
            P(("fsdp", "ctx"), "tp"),
            P(("fsdp", "ctx"), "tp"),
        ),
        check_vma=False,
    )
```

```python
from functools import partial

import jax
import jax.numpy as jnp
from jax import lax
from jax.experimental import pallas as pl
from jax.experimental.pallas import tpu as pltpu
from jax.sharding import PartitionSpec as P

HD = 64


norm_eps = 1e-05
residual_scale = 0.22
score_scale = 1.0 / 64.0
rope_base = 10000000.0
masked_score = -1e30


def rope_tables(positions, head_dim):
    half_dim = head_dim // 2
    frequency = rope_base ** (-(jnp.arange(half_dim, dtype=jnp.float32) * 2.0) / head_dim)
    angles = positions.astype(jnp.float32)[:, None] * frequency[None, :]
    return (
        jnp.concatenate([jnp.cos(angles), jnp.cos(angles)], -1),
        jnp.concatenate([jnp.sin(angles), jnp.sin(angles)], -1),
    )


def rotate(values_in, cosines, sines):
    half_dim = values_in.shape[-1] // 2
    turned = jnp.concatenate([-values_in[..., half_dim:], values_in[..., :half_dim]], -1)
    return values_in * cosines + turned * sines


def unrotate(grad_in, cosines, sines):
    half_dim = grad_in.shape[-1] // 2
    scaled = grad_in * sines
    return grad_in * cosines + jnp.concatenate(
        [scaled[..., half_dim:], -scaled[..., :half_dim]], -1
    )


def rms_scale(values_in):
    return lax.rsqrt(jnp.mean(values_in * values_in, -1, keepdims=True) + norm_eps)


def norm_back(grad_normed, values_in, scale, gain):
    scaled_grad = grad_normed * gain
    return scale * scaled_grad - values_in * scale**3 * jnp.mean(
        scaled_grad * values_in, -1, keepdims=True
    )


MESH_ID = pl.DeviceIdType.MESH
FIRST_EIGHTHS = 4
NT = (((1,), (1,)), ((), ()))
TN = (((0,), (0,)), ((), ()))
SMEM = pltpu.SMEM


def mul(left, right, dims=(((1,), (0,)), ((), ()))):
    return lax.dot_general(left, right, dims, preferred_element_type=jnp.float32)


def reorder(v, first, second, width):
    if width % 128:
        return v
    pieces = []
    for b in range(second):
        for a in range(first):
            start = (a * second + b) * width
            pieces.append(v[:, start : start + width])
    return jnp.concatenate(pieces, 1)


def turn(t, sign):
    lane = lax.broadcasted_iota(jnp.int32, t.shape, 1)
    ahead = pltpu.roll(t, 128 - HD // 2, 1)
    behind = pltpu.roll(t, HD // 2, 1)
    return jnp.where(lax.rem(lane, HD) < HD // 2, -sign * ahead, sign * behind)


def row_valid(len_ref, rows, local_rows):
    step = pl.program_id(0)
    start = step * rows
    seq = start // local_rows
    place = (
        lax.axis_index("ctx") * local_rows
        + lax.rem(start, local_rows)
        + lax.broadcasted_iota(jnp.int32, (rows, 1), 0)
    )
    return (place < len_ref[seq]).astype(jnp.float32)


def qkv_kernel(dims, x_ref, w_ref, gain_ref, cos_ref, sin_ref, normed_ref, q_ref, kv_ref):
    x = reorder(x_ref[...].astype(jnp.float32), *dims)
    normed = (x * rms_scale(x) * gain_ref[...]).astype(jnp.bfloat16)
    normed_ref[...] = normed
    lin = mul(normed, w_ref[...])
    cosines, sines = cos_ref[...], sin_ref[...]
    width = q_ref.shape[1]
    half = kv_ref.shape[1] // 2
    for start in range(0, width + half, 128):
        t = lin[:, start : start + 128]
        t = (t * cosines + turn(t, 1.0) * sines).astype(jnp.bfloat16)
        if start < width:
            q_ref[:, start : start + 128] = t
        else:
            kv_ref[:, start - width : start - width + 128] = t
    kv_ref[:, half:] = lin[:, width + half :].astype(jnp.bfloat16)


def key_biases(len_ref, rows, ctx):
    length = len_ref[pl.program_id(0)]
    me = lax.axis_index("ctx")
    row = lax.broadcasted_iota(jnp.int32, (rows, rows), 0)
    col = lax.broadcasted_iota(jnp.int32, (rows, rows), 1)
    first = jnp.where((col <= row) & (me * rows + col < length), 0.0, masked_score)
    out = [first]
    for s in range(1, ctx):
        place = (me - s) * rows + lax.broadcasted_iota(jnp.int32, (1, rows), 1)
        out.append(jnp.where((place >= 0) & (place < length), 0.0, masked_score))
    return out


def attend_kernel(ctx, len_ref, q_ref, *refs):
    keys, values = refs[:ctx], refs[ctx : 2 * ctx]
    o_ref, lse_ref = refs[2 * ctx :]
    rows = q_ref.shape[0]
    biases = key_biases(len_ref, rows, ctx)
    lane = lax.broadcasted_iota(jnp.int32, (rows, 128), 1)
    lse_all = jnp.zeros((rows, 128), jnp.float32)
    for j in range(q_ref.shape[1] // 128):
        q_pair = q_ref[:, j * 128 : (j + 1) * 128] * jnp.bfloat16(score_scale)
        outs = []
        for g in range(2):
            mine = (lane < HD) if g == 0 else (lane >= HD)
            q_head = jnp.where(mine, q_pair, jnp.zeros_like(q_pair))
            scores = [mul(q_head, k[...], NT) + b for k, b in zip(keys, biases)]
            top = scores[0].max(-1, keepdims=True)
            for s in scores[1:]:
                top = jnp.maximum(top, s.max(-1, keepdims=True))
            mass, out = 0.0, 0.0
            for s, v in zip(scores, values):
                p = jnp.exp(s - top)
                mass = mass + p.sum(-1, keepdims=True)
                out = out + mul(p.astype(jnp.bfloat16), v[...])
            outs.append(out / mass)
            lse_all = jnp.where(lane == 2 * j + g, top + jnp.log(mass), lse_all)
        o_ref[:, j * 128 : (j + 1) * 128] = jnp.where(lane < HD, outs[0], outs[1]).astype(
            jnp.bfloat16
        )
    lse_ref[...] = lse_all


class RowSum:
    def __init__(
        self, group, fsdp, rows_ref, own_ref, held, got, in_sem, f_send, f_recv, own_sem
    ):
        self.group, self.fsdp = group, fsdp
        self.order = fsdp_order(group)
        self.bits = [1 << i for i in range(group.bit_length() - 1)]
        self.own_ref, self.held, self.got = own_ref, held, got
        self.f_send, self.f_recv, self.own_sem = f_send, f_recv, own_sem
        self.half = rows_ref.shape[1]
        self.loads = [
            pltpu.make_async_copy(rows_ref.at[k], held.at[k], in_sem.at[k]) for k in range(group)
        ]

    def peer(self, k):
        me_f = lax.axis_index("fsdp")
        return (flip_index(me_f, k, self.fsdp), lax.axis_index("ctx"), lax.axis_index("tp"))

    def core(self):
        me_f, me_c, me_t = self.peer(0)
        return (me_f, me_c, 1 - me_t)

    def ways(self, k):
        return [(0, k)] if k == low_bit(k) else [(0, low_bit(k)), (1, high_bit(k))]

    def span(self, k, part):
        half = self.half
        return pl.ds(0, half) if k == low_bit(k) else pl.ds(part * (half // 2), half // 2)

    def copy(self, k, part, b):
        return pltpu.make_async_remote_copy(
            src_ref=self.held.at[k, self.span(k, part)],
            dst_ref=self.got.at[k, self.span(k, part)],
            send_sem=self.f_send.at[k, part],
            recv_sem=self.f_recv.at[k, part],
            device_id=self.peer(b),
            device_id_type=MESH_ID,
        )

    def own_copy(self, place):
        return pltpu.make_async_remote_copy(
            src_ref=self.held.at[0],
            dst_ref=self.own_ref.at[place],
            send_sem=self.own_sem.at[0],
            recv_sem=self.own_sem.at[1],
            device_id=self.core(),
            device_id_type=MESH_ID,
        )

    def collect(self, k):
        for far in self.order:
            for part, b in self.ways(far):
                if far ^ b == k:
                    self.copy(far, part, b).wait_recv()
                    rows = self.span(far, part)
                    self.held[k, rows] = (
                        self.held[k, rows].astype(jnp.float32)
                        + self.got[far, rows].astype(jnp.float32)
                    ).astype(self.held.dtype)

    def send(self, k):
        for part, b in self.ways(k):
            self.copy(k, part, b).start()

    def start(self):
        barrier = pltpu.get_barrier_semaphore()
        for b in self.bits:
            pl.semaphore_signal(barrier, inc=1, device_id=self.peer(b), device_id_type=MESH_ID)
        pl.semaphore_signal(barrier, inc=1, device_id=self.core(), device_id_type=MESH_ID)
        for load in self.loads:
            load.start()
        pl.semaphore_wait(barrier, len(self.bits) + 1)
        for load in self.loads:
            load.wait()
        for k in self.order:
            if k != low_bit(k):
                self.send(k)

    def relay(self):
        for k in self.order:
            if k == low_bit(k):
                self.collect(k)
                self.send(k)

    def finish(self):
        self.collect(0)
        me_t = lax.axis_index("tp")
        self.own_copy(me_t).start()
        local = pltpu.make_async_copy(
            self.held.at[0], self.own_ref.at[me_t], self.own_sem.at[2]
        )
        local.start()
        local.wait()
        self.own_copy(1 - me_t).wait_recv()
        self.own_copy(me_t).wait_send()
        for k in self.order:
            for part, b in self.ways(k):
                self.copy(k, part, b).wait_send()


def attend_back_kernel(
    ctx, fsdp, group, len_ref, q_ref, do_ref, lse_ref, cos_ref, sin_ref, rows_ref, *refs
):
    keys, values = refs[:ctx], refs[ctx : 2 * ctx]
    dq_ref, dkv_ref, own_ref, dk_sum, dv_sum = refs[2 * ctx : 2 * ctx + 5]
    step = pl.program_id(0) * pl.num_programs(1) + pl.program_id(1)
    sums = RowSum(group, fsdp, rows_ref, own_ref, *refs[2 * ctx + 5 :])

    @pl.when(step == 0)
    def _():
        sums.start()

    rows = q_ref.shape[0]
    biases = key_biases(len_ref, rows, ctx)
    lane = lax.broadcasted_iota(jnp.int32, (rows, 128), 1)
    dk_sum[...] = jnp.zeros_like(dk_sum)
    dv_sum[...] = jnp.zeros_like(dv_sum)
    lse_all = lse_ref[...]
    for j in range(q_ref.shape[1] // 128):
        q_pair = q_ref[:, j * 128 : (j + 1) * 128] * jnp.bfloat16(score_scale)
        do_pair = do_ref[:, j * 128 : (j + 1) * 128]
        dqs = []
        for g in range(2):
            mine = (lane < HD) if g == 0 else (lane >= HD)
            q_head = jnp.where(mine, q_pair, jnp.zeros_like(q_pair))
            do_head = jnp.where(mine, do_pair, jnp.zeros_like(do_pair))
            h = 2 * j + g
            lse = lse_all[:, h : h + 1]
            probs, grads, total = [], [], 0.0
            for s in range(ctx):
                p = jnp.exp(mul(q_head, keys[s][...], NT) + (biases[s] - lse))
                dp = mul(do_head, values[s][...], NT)
                total = total + (p * dp).sum(-1, keepdims=True)
                probs.append(p)
                grads.append(dp)
            dq = 0.0
            for s in range(ctx):
                ds = (probs[s] * (grads[s] - total)).astype(jnp.bfloat16)
                dv_sum[s] += mul(probs[s].astype(jnp.bfloat16), do_head, TN)
                dk_sum[s] += mul(ds, q_head, TN)
                dq = dq + mul(ds, keys[s][...])
            dqs.append(dq)
        dq = jnp.where(lane < HD, dqs[0], dqs[1]) * score_scale
        dq = dq * cos_ref[...] + turn(dq * sin_ref[...], -1.0)
        dq_ref[:, j * 128 : (j + 1) * 128] = dq.astype(jnp.bfloat16)
        if j == 1:

            @pl.when(step == 1)
            def _():
                sums.relay()

    for s in range(ctx):
        dkv_ref[s, 0] = dk_sum[s].astype(dkv_ref.dtype)
        dkv_ref[s, 1] = dv_sum[s].astype(dkv_ref.dtype)

    @pl.when(step == pl.num_programs(0) * pl.num_programs(1) - 1)
    def _():
        sums.finish()


def cot_kernel(dims, local_rows, len_ref, cot_ref, ff_ref):
    rows = cot_ref.shape[0]
    back = cot_ref[...].astype(jnp.float32) * row_valid(len_ref, rows, local_rows)
    ff_ref[...] = reorder((residual_scale * back).astype(jnp.bfloat16), *dims)


def middle_kernel(dims, x_ref, part_ref, other_ref, gain_ref, middle_ref, normed_ref):
    branch = part_ref[...].astype(jnp.float32) + other_ref[...].astype(jnp.float32)
    middle = reorder(x_ref[...].astype(jnp.float32), *dims) + residual_scale * branch
    middle_ref[...] = middle
    normed_ref[...] = (middle * rms_scale(middle) * gain_ref[...]).astype(jnp.bfloat16)


def middle_back_kernel(
    dims, local_rows, len_ref, cot_ref, middle_ref, grad_ref, gain_ref, back_ref, attn_ref, gain_sum
):
    rows = cot_ref.shape[0]
    back = cot_ref[...].astype(jnp.float32) * row_valid(len_ref, rows, local_rows)
    middle = middle_ref[...]
    grad = grad_ref[...].astype(jnp.float32)
    scale = rms_scale(middle)
    out = reorder(back, *dims) + norm_back(grad, middle, scale, gain_ref[...])
    back_ref[...] = out
    attn_ref[...] = (residual_scale * out).astype(jnp.bfloat16)

    @pl.when(pl.program_id(0) == 0)
    def _():
        gain_sum[...] = jnp.zeros_like(gain_sum)

    gain_sum[...] += (grad * middle * scale).sum(0, keepdims=True)


def output_kernel(dims, local_rows, len_ref, middle_ref, ff_ref, out_ref):
    rows = middle_ref.shape[0]
    out = middle_ref[...] + residual_scale * ff_ref[...].astype(jnp.float32)
    out = (out * row_valid(len_ref, rows, local_rows)).astype(jnp.bfloat16)
    out_ref[...] = reorder(out, *dims)


def input_back_kernel(
    dims, x_ref, part_ref, other_ref, back_ref, gain_ref, out_ref, gain_sum
):
    first, second, width = dims
    x = reorder(x_ref[...].astype(jnp.float32), *dims)
    grad = (part_ref[...].astype(jnp.float32) + other_ref[...].astype(jnp.float32))
    scale = rms_scale(x)
    out = back_ref[...] + norm_back(grad, x, scale, gain_ref[...])
    out_ref[...] = reorder(out.astype(jnp.bfloat16), second, first, width)

    @pl.when(pl.program_id(0) == 0)
    def _():
        gain_sum[...] = jnp.zeros_like(gain_sum)

    gain_sum[...] += (grad * x * scale).sum(0, keepdims=True)


def by_rows(kernel, rows, ins, outs, flops=0, limit=40):
    total = max(v.shape[0] for v, kind in ins if kind == "rows")
    in_specs = []
    moved = 0
    for v, kind in ins:
        moved += v.size * v.dtype.itemsize
        if kind == "rows":
            in_specs.append(pl.BlockSpec((rows, v.shape[1]), lambda i: (i, 0)))
        elif kind == "cycle":
            period = v.shape[0] // rows
            in_specs.append(
                pl.BlockSpec((rows, v.shape[1]), lambda i, period=period: (lax.rem(i, period), 0))
            )
        elif kind == "smem":
            in_specs.append(pl.BlockSpec(memory_space=SMEM))
        else:
            in_specs.append(
                pl.BlockSpec(v.shape, lambda i: (0, 0), pipeline_mode=pl.Buffered(1))
            )
    out_specs = []
    for shape, dtype in outs:
        moved += shape[0] * shape[1] * jnp.dtype(dtype).itemsize
        if shape[0] == 1:
            out_specs.append(pl.BlockSpec(shape, lambda i: (0, 0)))
        else:
            out_specs.append(pl.BlockSpec((rows, shape[1]), lambda i: (i, 0)))
    return pl.pallas_call(
        kernel,
        grid=(total // rows,),
        in_specs=in_specs,
        out_specs=out_specs,
        out_shape=[jax.ShapeDtypeStruct(shape, dtype) for shape, dtype in outs],
        compiler_params=pltpu.CompilerParams(vmem_limit_bytes=limit * 1024 * 1024),
        cost_estimate=pl.CostEstimate(flops=flops, bytes_accessed=moved, transcendentals=0),
    )(*[v for v, _ in ins])


def kv_specs(ctx, rows, pairs):
    def spec(slot, start):
        return pl.BlockSpec((None, rows, 128), lambda s, p: (slot, s, start + p))

    return [spec(slot, start) for start in (0, pairs) for slot in range(ctx)]


def attend(lengths, query, kv_all):
    ctx = kv_all.shape[0]
    seqs = lengths.shape[0]
    rows = query.shape[0] // seqs
    pairs = kv_all.shape[2] // 256
    wide = query.shape[1] // pairs
    flops = 4 * query.shape[0] * query.shape[1] * rows * ctx
    return pl.pallas_call(
        partial(attend_kernel, ctx),
        grid=(seqs, pairs),
        in_specs=[
            pl.BlockSpec(memory_space=SMEM),
            pl.BlockSpec((rows, wide), lambda s, p: (s, p)),
        ]
        + kv_specs(ctx, rows, pairs),
        out_specs=[
            pl.BlockSpec((rows, wide), lambda s, p: (s, p)),
            pl.BlockSpec((rows, 128), lambda s, p: (s, p)),
        ],
        out_shape=[
            jax.ShapeDtypeStruct(query.shape, jnp.bfloat16),
            jax.ShapeDtypeStruct((query.shape[0], 128 * pairs), jnp.float32),
        ],
        compiler_params=pltpu.CompilerParams(vmem_limit_bytes=40 * 1024 * 1024),
        cost_estimate=pl.CostEstimate(flops=4 * flops, bytes_accessed=6 << 20, transcendentals=0),
    )(lengths, query, *[kv_all] * (2 * ctx))


def attend_back(fsdp, group, lengths, query, out_grad, lse, cosines, sines, kv_all, row_blocks):
    ctx = kv_all.shape[0]
    block = row_blocks.shape[1:]
    low = jnp.bfloat16
    sems = pltpu.SemaphoreType.DMA
    seqs = lengths.shape[0]
    rows = query.shape[0] // seqs
    pairs = kv_all.shape[2] // 256
    wide = query.shape[1] // pairs
    flops = 10 * query.shape[0] * query.shape[1] * rows * ctx
    return pl.pallas_call(
        partial(attend_back_kernel, ctx, fsdp, group),
        grid=(seqs, pairs),
        in_specs=[
            pl.BlockSpec(memory_space=SMEM),
            pl.BlockSpec((rows, wide), lambda s, p: (s, p)),
            pl.BlockSpec((rows, wide), lambda s, p: (s, p)),
            pl.BlockSpec((rows, 128), lambda s, p: (s, p)),
            pl.BlockSpec((rows, 128), lambda s, p: (0, 0)),
            pl.BlockSpec((rows, 128), lambda s, p: (0, 0)),
            pl.BlockSpec(memory_space=pl.ANY),
        ]
        + kv_specs(ctx, rows, pairs),
        out_specs=[
            pl.BlockSpec((rows, wide), lambda s, p: (s, p)),
            pl.BlockSpec((ctx, 2, rows, 128), lambda s, p: (0, 0, s, p)),
            pl.BlockSpec(memory_space=pl.ANY),
        ],
        out_shape=[
            jax.ShapeDtypeStruct(query.shape, jnp.bfloat16),
            jax.ShapeDtypeStruct((ctx, 2, query.shape[0], 128 * pairs), low),
            jax.ShapeDtypeStruct((2,) + block, low),
        ],
        scratch_shapes=[pltpu.VMEM((ctx, rows, 128), jnp.float32)] * 2
        + [pltpu.VMEM((group,) + block, low)] * 2
        + [sems((group,)), sems((group, 2)), sems((group, 2)), sems((3,))],
        compiler_params=pltpu.CompilerParams(
            collective_id=7, has_side_effects=True, vmem_limit_bytes=44 * 1024 * 1024
        ),
        cost_estimate=pl.CostEstimate(flops=4 * flops, bytes_accessed=10 << 20, transcendentals=0),
    )(lengths, query, out_grad, lse, cosines, sines, row_blocks, *[kv_all] * (2 * ctx))


def low_bit(k):
    return k & -k


def high_bit(k):
    return 1 << (k.bit_length() - 1)


def fsdp_order(fsdp):
    return sorted(range(1, fsdp), key=lambda k: (bin(k).count("1"), k))


def flip_index(me, k, fsdp):
    out = me
    for i in range(fsdp.bit_length() - 1):
        b = 1 << i
        if k & b:
            out = out + b - 2 * b * lax.rem(me // b, 2)
    return out


def line_neighbours(me, count):
    return (me > 0).astype(jnp.int32) + (me < count - 1).astype(jnp.int32)


def line_kernel(fsdp, ctx, group, lines, swaps, widths, *refs):
    line_in = refs[:lines]
    swap_in = refs[lines : lines + swaps]
    line_out = refs[lines + swaps : 2 * lines + swaps]
    swap_out = refs[2 * lines + swaps : -5]
    own_sem, z_send, z_recv, f_send, f_recv = refs[-5:]
    parts = len(widths)
    me_f = lax.axis_index("fsdp")
    me_c = lax.axis_index("ctx")
    me_t = lax.axis_index("tp")

    def along(step, act):
        there = me_c + step

        @pl.when((there >= 0) & (there < ctx))
        def _():
            act(there)

    barrier = pltpu.get_barrier_semaphore()
    for k in range(1, group):
        pl.semaphore_signal(
            barrier, inc=1, device_id=(flip_index(me_f, k, fsdp), me_c, me_t), device_id_type=MESH_ID
        )
    for step in (-1, 1):
        along(
            step,
            lambda there: pl.semaphore_signal(
                barrier, inc=1, device_id=(me_f, there, me_t), device_id_type=MESH_ID
            ),
        )
    pl.semaphore_wait(barrier, group - 1 + line_neighbours(me_c, ctx))

    def z_copy(i, shard, step, src=None):
        place = line_out[i].at[shard]
        way = 0 if step > 0 else 1
        return pltpu.make_async_remote_copy(
            src_ref=place if src is None else src,
            dst_ref=place,
            send_sem=z_send.at[i, way, shard],
            recv_sem=z_recv.at[i, way, shard],
            device_id=(me_f, me_c + step, me_t),
            device_id_type=MESH_ID,
        )

    def landing(i, part, f):
        width = widths[part]
        return swap_out[part].at[lax.rem(f, group), :, pl.ds(i * width, width)]

    def columns(i, part, f):
        start = lax.rem(f, group) * sum(widths) + sum(widths[:part])
        return swap_in[i].at[:, pl.ds(pl.multiple_of(start, 128), widths[part])]

    def f_copy(i, part, k):
        there = flip_index(me_f, k, fsdp)
        return pltpu.make_async_remote_copy(
            src_ref=columns(i, part, there),
            dst_ref=landing(i, part, me_f),
            send_sem=f_send.at[i * parts + part, k],
            recv_sem=f_recv.at[i * parts + part, k],
            device_id=(there, me_c, me_t),
            device_id_type=MESH_ID,
        )

    def f_arrival(i, part, k):
        there = flip_index(me_f, k, fsdp)
        return pltpu.make_async_remote_copy(
            src_ref=landing(i, part, there),
            dst_ref=landing(i, part, there),
            send_sem=f_send.at[i * parts + part, k],
            recv_sem=f_recv.at[i * parts + part, k],
            device_id=(there, me_c, me_t),
            device_id_type=MESH_ID,
        )

    pieces = [(i, part) for part in range(parts) for i in range(swaps)]
    for i in range(lines):
        for step in (1, -1):
            along(step, lambda there: z_copy(i, me_c, step, line_in[i]).start())
    order = fsdp_order(group)
    for i, part in pieces:
        for k in order:
            f_copy(i, part, k).start()
    own = [
        pltpu.make_async_copy(line_in[i], line_out[i].at[me_c], own_sem.at[i])
        for i in range(lines)
    ] + [
        pltpu.make_async_copy(
            columns(i, part, me_f),
            landing(i, part, me_f),
            own_sem.at[lines + i * parts + part],
        )
        for i, part in pieces
    ]
    for copy in own:
        copy.start()
    for distance in range(1, ctx):
        for i in range(lines):
            for step in (1, -1):
                shard = me_c - step * distance

                @pl.when((shard >= 0) & (shard < ctx))
                def _():
                    z_copy(i, shard, step).wait_recv()
                    along(step, lambda there: z_copy(i, shard, step).start())

    for i, part in pieces:
        for k in order:
            f_arrival(i, part, k).wait_recv()
            f_copy(i, part, k).wait_send()
    for copy in own:
        copy.wait()
    for i in range(lines):
        for step in (1, -1):
            along(step, lambda there: z_copy(i, me_c, step, line_in[i]).wait_send())
            for distance in range(1, ctx - 1):
                shard = me_c - step * distance

                @pl.when((shard >= 0) & (shard < ctx))
                def _():
                    along(step, lambda there: z_copy(i, shard, step).wait_send())


def start_exchange(fsdp, ctx, group, lines, swaps, widths):
    parts = len(widths)
    sems = pltpu.SemaphoreType.DMA
    rows = swaps[0].shape[0]
    out_shape = [jax.ShapeDtypeStruct((ctx,) + v.shape, v.dtype) for v in lines]
    out_shape += [
        jax.ShapeDtypeStruct((group, rows, len(swaps) * w), swaps[0].dtype) for w in widths
    ]
    count = len(lines) + len(swaps)
    outs = pl.pallas_call(
        partial(line_kernel, fsdp, ctx, group, len(lines), len(swaps), tuple(widths)),
        out_shape=out_shape,
        in_specs=[pl.BlockSpec(memory_space=pltpu.VMEM)] * count,
        out_specs=[pl.BlockSpec(memory_space=pl.ANY)] * len(out_shape),
        scratch_shapes=[
            sems((len(lines) + len(swaps) * parts,)),
            sems((len(lines), 2, ctx)),
            sems((len(lines), 2, ctx)),
            sems((len(swaps) * parts, group)),
            sems((len(swaps) * parts, group)),
        ],
        compiler_params=pltpu.CompilerParams(
            collective_id=0, has_side_effects=True, vmem_limit_bytes=24 * 1024 * 1024
        ),
    )(*lines, *swaps)
    return outs[: len(lines)], outs[len(lines) :]


class TokenGather:
    def __init__(self, group, fsdp, v_ref, out_ref, own_sem, f_send, f_recv, t_send, t_recv):
        self.order = fsdp_order(group)
        self.bits = [1 << i for i in range(group.bit_length() - 1)]
        self.out_ref = out_ref
        self.sems = (f_send, f_recv, t_send, t_recv)
        self.fsdp = fsdp
        half = out_ref.shape[2]
        self.half = half
        me_t = lax.axis_index("tp")
        self.mine = v_ref.at[pl.ds(pl.multiple_of(me_t * half, half), half)]
        other = v_ref.at[pl.ds(pl.multiple_of((1 - me_t) * half, half), half)]
        self.own = [
            pltpu.make_async_copy(self.mine, out_ref.at[0, 0], own_sem.at[0]),
            pltpu.make_async_copy(other, out_ref.at[0, 1], own_sem.at[1]),
        ]

    def peer(self, k):
        me_f = lax.axis_index("fsdp")
        return (flip_index(me_f, k, self.fsdp), lax.axis_index("ctx"), lax.axis_index("tp"))

    def rows(self, k, part):
        if k == low_bit(k):
            return pl.ds(0, self.half)
        return pl.ds(part * (self.half // 2), self.half // 2)

    def f_copy(self, have, b):
        k = have | b
        part = 1 if have and b == high_bit(k) else 0
        place = self.out_ref.at[k, 0, self.rows(k, part)]
        src = self.out_ref.at[have, 0, self.rows(k, part)] if have else self.mine
        return pltpu.make_async_remote_copy(
            src_ref=src,
            dst_ref=place,
            send_sem=self.sems[0].at[k, part],
            recv_sem=self.sems[1].at[k, part],
            device_id=self.peer(b),
            device_id_type=MESH_ID,
        )

    def ways(self, have):
        return [
            b
            for b in self.bits
            if not have & b and (not have or b in (low_bit(have | b), high_bit(have | b)))
        ]

    def swap(self, k):
        me_f, me_c, me_t = self.peer(0)
        return pltpu.make_async_remote_copy(
            src_ref=self.out_ref.at[k, 0],
            dst_ref=self.out_ref.at[k, 1],
            send_sem=self.sems[2].at[k],
            recv_sem=self.sems[3].at[k],
            device_id=(me_f, me_c, 1 - me_t),
            device_id_type=MESH_ID,
        )

    def start(self):
        for b in self.ways(0):
            self.f_copy(0, b).start()
        for copy in self.own:
            copy.start()

    def relay(self, k):
        parts = [(0, k)] if k == low_bit(k) else [(0, low_bit(k)), (1, high_bit(k))]
        for part, b in parts:
            place = self.out_ref.at[k, 0, self.rows(k, part)]
            pltpu.make_async_remote_copy(
                src_ref=place,
                dst_ref=place,
                send_sem=self.sems[0].at[k, part],
                recv_sem=self.sems[1].at[k, part],
                device_id=self.peer(b),
                device_id_type=MESH_ID,
            ).wait_recv()
        for b in self.ways(k):
            self.f_copy(k, b).start()
        self.swap(k).start()

    def finish(self):
        for copy in self.own:
            copy.wait()
        for have in [0] + self.order:
            for b in self.ways(have):
                self.f_copy(have, b).wait_send()
        me_f, me_c, me_t = self.peer(0)
        for k in self.order:
            pltpu.make_async_remote_copy(
                src_ref=self.out_ref.at[k, 1],
                dst_ref=self.out_ref.at[k, 1],
                send_sem=self.sems[2].at[k],
                recv_sem=self.sems[3].at[k],
                device_id=(me_f, me_c, 1 - me_t),
                device_id_type=MESH_ID,
            ).wait_recv()
            self.swap(k).wait_send()


def token_sems(group):
    sems = pltpu.SemaphoreType.DMA
    return [sems((2,)), sems((group, 2)), sems((group, 2)), sems((group,)), sems((group,))]


def token_shape(group, v):
    return jax.ShapeDtypeStruct((group, 2, v.shape[0] // 2, v.shape[1]), v.dtype)


def tokens_kernel(group, fsdp, v_ref, out_ref, *sems):
    gather = TokenGather(group, fsdp, v_ref, out_ref, *sems)
    me_f, me_c, me_t = gather.peer(0)
    barrier = pltpu.get_barrier_semaphore()
    for b in gather.bits:
        pl.semaphore_signal(barrier, inc=1, device_id=gather.peer(b), device_id_type=MESH_ID)
    pl.semaphore_signal(
        barrier, inc=1, device_id=(me_f, me_c, 1 - me_t), device_id_type=MESH_ID
    )
    pl.semaphore_wait(barrier, len(gather.bits) + 1)
    gather.start()
    for k in gather.order:
        gather.relay(k)
    gather.finish()


def gather_tokens(group, fsdp, v):
    out = pl.pallas_call(
        partial(tokens_kernel, group, fsdp),
        out_shape=token_shape(group, v),
        in_specs=[pl.BlockSpec(memory_space=pltpu.VMEM)],
        out_specs=pl.BlockSpec(memory_space=pl.ANY),
        scratch_shapes=token_sems(group),
        compiler_params=pltpu.CompilerParams(
            collective_id=5, has_side_effects=True, vmem_limit_bytes=24 * 1024 * 1024
        ),
    )(v)
    return out.reshape(-1, v.shape[1])


def swiglu_parts(n_ref, g_ref, w_ref, hidden_ref, grads_ref):
    units = hidden_ref.shape[1]
    both = w_ref[:, : 2 * units]
    down = w_ref[:, 2 * units :]
    lin = mul(n_ref[...], both)
    gate, up = lin[:, :units], lin[:, units:]
    sig = jax.nn.sigmoid(gate)
    act = gate * sig
    hidden = (act * up).astype(jnp.bfloat16)
    hidden_ref[...] = hidden
    hidden_grad = mul(g_ref[...], down)
    grads_ref[:, :units] = (hidden_grad * up * sig * (1.0 + gate * (1.0 - sig))).astype(
        jnp.bfloat16
    )
    grads_ref[:, units:] = (hidden_grad * act).astype(jnp.bfloat16)
    return mul(grads_ref[...], both, NT), mul(hidden, down, NT)


def swiglu_first_kernel(n_ref, g_ref, w_ref, hidden_ref, grads_ref, second_ref, ff_ref):
    second, ff = swiglu_parts(n_ref, g_ref, w_ref, hidden_ref, grads_ref)
    second_ref[...] = second.astype(jnp.bfloat16)
    ff_ref[...] = ff.astype(jnp.bfloat16)


def swiglu_kernel(
    fsdp,
    group,
    n_ref,
    g_ref,
    w_ref,
    second_ref,
    ff_first_ref,
    hidden_ref,
    grads_ref,
    ff_ref,
    own_ref,
    s_out,
    f_out,
    s_in,
    f_in,
    total,
    got,
    t_send,
    t_recv,
    f_send,
    f_recv,
    own_sem,
):
    half = n_ref.shape[0]
    step = pl.program_id(0)
    me_f = lax.axis_index("fsdp")
    me_c = lax.axis_index("ctx")
    me_t = lax.axis_index("tp")
    bits = [1 << i for i in range(group.bit_length() - 1)]
    order = fsdp_order(group)
    core = (me_f, me_c, 1 - me_t)

    def peer(k):
        return (flip_index(me_f, k, fsdp), me_c, me_t)

    @pl.when(step == 0)
    def _():
        barrier = pltpu.get_barrier_semaphore()
        for b in bits:
            pl.semaphore_signal(barrier, inc=1, device_id=peer(b), device_id_type=MESH_ID)
        pl.semaphore_signal(barrier, inc=1, device_id=core, device_id_type=MESH_ID)
        pl.semaphore_wait(barrier, len(bits) + 1)

    def core_copies(k):
        slot = k % 2
        return [
            pltpu.make_async_remote_copy(
                src_ref=out.at[slot],
                dst_ref=into.at[slot],
                send_sem=t_send.at[which, k],
                recv_sem=t_recv.at[which, k],
                device_id=core,
                device_id_type=MESH_ID,
            )
            for which, (out, into) in enumerate(((s_out, s_in), (f_out, f_in)))
        ]

    def ways(k):
        return [(0, k)] if k == low_bit(k) else [(0, low_bit(k)), (1, high_bit(k))]

    def span(k, part):
        return pl.ds(0, half) if k == low_bit(k) else pl.ds(part * (half // 2), half // 2)

    def f_copy(k, part, b):
        return pltpu.make_async_remote_copy(
            src_ref=total.at[k, span(k, part)],
            dst_ref=got.at[k, span(k, part)],
            send_sem=f_send.at[k, part],
            recv_sem=f_recv.at[k, part],
            device_id=peer(b),
            device_id_type=MESH_ID,
        )

    def own_copy():
        return pltpu.make_async_remote_copy(
            src_ref=total.at[0],
            dst_ref=own_ref.at[me_t],
            send_sem=own_sem.at[0],
            recv_sem=own_sem.at[1],
            device_id=core,
            device_id_type=MESH_ID,
        )

    second, ff = swiglu_parts(n_ref, g_ref, w_ref, hidden_ref, grads_ref)
    second = second + second_ref[...].astype(jnp.float32)
    ff = ff + ff_first_ref[...].astype(jnp.float32)

    for k in reversed(range(group)):
        slot = k % 2

        @pl.when(step == 2 * (group - 1 - k))
        def _():
            if k + 2 < group:
                for copy in core_copies(k + 2):
                    copy.wait_send()
            s_out[slot] = second.astype(jnp.bfloat16)
            f_out[slot] = ff.astype(jnp.bfloat16)
            for copy in core_copies(k):
                copy.start()

        @pl.when(step == 2 * (group - 1 - k) + 1)
        def _():
            for copy in core_copies(k):
                copy.wait_recv()
            ff_ref[...] = (ff + f_in[slot].astype(jnp.float32)).astype(jnp.bfloat16)
            total[k] = (second + s_in[slot].astype(jnp.float32)).astype(jnp.bfloat16)
            for far in order:
                for part, b in ways(far):
                    if far ^ b == k:
                        f_copy(far, part, b).wait_recv()
                        rows = span(far, part)
                        total[k, rows] = (
                            total[k, rows].astype(jnp.float32)
                            + got[far, rows].astype(jnp.float32)
                        ).astype(jnp.bfloat16)
            if k:
                for part, b in ways(k):
                    f_copy(k, part, b).start()
            else:
                own_copy().start()
                local = pltpu.make_async_copy(total.at[0], own_ref.at[me_t], own_sem.at[2])
                local.start()
                local.wait()
                other = own_ref.at[1 - me_t]
                pltpu.make_async_remote_copy(
                    src_ref=other,
                    dst_ref=other,
                    send_sem=own_sem.at[0],
                    recv_sem=own_sem.at[1],
                    device_id=core,
                    device_id_type=MESH_ID,
                ).wait_recv()
                own_copy().wait_send()
                for far in order:
                    for part, b in ways(far):
                        f_copy(far, part, b).wait_send()
                for late in range(min(2, group)):
                    for copy in core_copies(late):
                        copy.wait_send()


def swiglu(fsdp, group, normed, grads, weights, second, ff):
    many, width = normed.shape
    half = many // (2 * group)
    units = weights.shape[1] // 3
    low = jnp.bfloat16
    last = 2 * group - 1
    sems = pltpu.SemaphoreType.DMA
    block = (half, width)

    def rows(cols):
        return pl.BlockSpec((half, cols), lambda i: (last - i, 0))

    def whole(v):
        return pl.BlockSpec(v.shape, lambda i: (0, 0), pipeline_mode=pl.Buffered(1))

    return pl.pallas_call(
        partial(swiglu_kernel, fsdp, group),
        grid=(2 * group,),
        in_specs=[rows(width), rows(width), whole(weights), rows(width), rows(width)],
        out_specs=[
            rows(units),
            rows(2 * units),
            pl.BlockSpec(block, lambda i: (group - 1 - i // 2, 0)),
            pl.BlockSpec(memory_space=pl.ANY),
        ],
        out_shape=[
            jax.ShapeDtypeStruct((many, units), low),
            jax.ShapeDtypeStruct((many, 2 * units), low),
            jax.ShapeDtypeStruct((group * half, width), low),
            jax.ShapeDtypeStruct((2,) + block, low),
        ],
        scratch_shapes=[pltpu.VMEM((2,) + block, low)] * 4
        + [pltpu.VMEM((group,) + block, low)] * 2
        + [
            sems((2, group)),
            sems((2, group)),
            sems((group, 2)),
            sems((group, 2)),
            sems((3,)),
        ],
        compiler_params=pltpu.CompilerParams(
            collective_id=6, has_side_effects=True, vmem_limit_bytes=58 * 1024 * 1024
        ),
        cost_estimate=pl.CostEstimate(
            flops=12 * many * width * units, bytes_accessed=50 << 20, transcendentals=0
        ),
    )(normed, grads, weights, second, ff)


def spread_kernel(fsdp, ctx, group, count, chain, *refs):
    ins = refs[:count]
    outs = refs[count + chain : 2 * count + chain]
    sems = refs[2 * (count + chain) :]
    own_sem, f_send, f_recv, c_own, c_send, c_recv = sems[:6]
    me_f = lax.axis_index("fsdp")
    me_c = lax.axis_index("ctx")
    me_t = lax.axis_index("tp")
    bits = [1 << i for i in range(fsdp.bit_length() - 1)]
    order = fsdp_order(fsdp)

    def peer(k):
        return (flip_index(me_f, k, fsdp), me_c, me_t)

    barrier = pltpu.get_barrier_semaphore()
    for b in bits:
        pl.semaphore_signal(barrier, inc=1, device_id=peer(b), device_id_type=MESH_ID)
    if chain:
        chain_in, chain_out = refs[count], refs[2 * count + chain]
        gather = TokenGather(
            group, fsdp, refs[count + 1], refs[2 * count + chain + 1], *sems[6:]
        )
        pl.semaphore_signal(
            barrier, inc=1, device_id=(me_f, me_c, 1 - me_t), device_id_type=MESH_ID
        )
        for step in (-1, 1):
            there = me_c + step

            @pl.when((there >= 0) & (there < ctx))
            def _():
                pl.semaphore_signal(
                    barrier, inc=1, device_id=(me_f, there, me_t), device_id_type=MESH_ID
                )

        pl.semaphore_wait(barrier, len(bits) + 1 + line_neighbours(me_c, ctx))
    else:
        pl.semaphore_wait(barrier, len(bits))

    def quarters(rows):
        return [pl.ds(i * (rows // 4), rows // 4) for i in range(4)]

    def climb(s):
        return [
            pltpu.make_async_remote_copy(
                src_ref=chain_out.at[s, part] if s else chain_in.at[part],
                dst_ref=chain_out.at[s + 1, part],
                send_sem=c_send.at[s, i],
                recv_sem=c_recv.at[s + 1, i],
                device_id=(me_f, me_c + 1, me_t),
                device_id_type=MESH_ID,
            )
            for i, part in enumerate(quarters(chain_in.shape[0]))
        ]

    def keep(s):
        return pltpu.make_async_copy(chain_in, chain_out.at[s], c_own.at[s])

    def send_up(s):
        @pl.when((me_c >= s) & (me_c < ctx - 1))
        def _():
            for copy in climb(s):
                copy.start()

    def take_up(s):
        @pl.when(me_c >= s)
        def _():
            for i, part in enumerate(quarters(chain_in.shape[0])):
                pltpu.make_async_remote_copy(
                    src_ref=chain_out.at[s, part],
                    dst_ref=chain_out.at[s, part],
                    send_sem=c_send.at[s - 1, i],
                    recv_sem=c_recv.at[s, i],
                    device_id=(me_f, me_c - 1, me_t),
                    device_id_type=MESH_ID,
                ).wait_recv()

        if s < ctx - 1:
            send_up(s)

    if chain:
        send_up(0)
        keep(0).start()
        for s in range(1, ctx):
            @pl.when(me_c < s)
            def _():
                keep(s).start()

    def place(i, shard, have, k, part):
        block = outs[i].at[shard, flip_index(me_f, have, fsdp)]
        half = ins[i].shape[1] // 2
        return block if k == low_bit(k) else block.at[pl.ds(part * half, half)]

    def f_copy(i, shard, have, b):
        k = have | b
        part = 1 if have and b == high_bit(k) else 0
        block = place(i, shard, have, k, part)
        return pltpu.make_async_remote_copy(
            src_ref=block if have else ins[i].at[shard],
            dst_ref=block,
            send_sem=f_send.at[i, shard, k, part],
            recv_sem=f_recv.at[i, shard, k, part],
            device_id=peer(b),
            device_id_type=MESH_ID,
        )

    def ways(have):
        return [
            b
            for b in bits
            if not have & b and (not have or b in (low_bit(have | b), high_bit(have | b)))
        ]

    own = [
        pltpu.make_async_copy(ins[i], outs[i].at[:, me_f], own_sem.at[i]) for i in range(count)
    ]
    for i in range(count):
        for shard in range(ctx):
            for b in ways(0):
                f_copy(i, shard, 0, b).start()
        own[i].start()
    if chain:
        gather.start()
    climbed = 1
    for i in range(count):
        for k in order:
            if chain and climbed < ctx:
                take_up(climbed)
                climbed += 1
            if chain and k < group and i == 0:
                gather.relay(k)
            parts = [(0, k)] if k == low_bit(k) else [(0, low_bit(k)), (1, high_bit(k))]
            for shard in range(ctx):
                for part, b in parts:
                    block = place(i, shard, k, k, part)
                    pltpu.make_async_remote_copy(
                        src_ref=block,
                        dst_ref=block,
                        send_sem=f_send.at[i, shard, k, part],
                        recv_sem=f_recv.at[i, shard, k, part],
                        device_id=peer(b),
                        device_id_type=MESH_ID,
                    ).wait_recv()
                for b in ways(k):
                    f_copy(i, shard, k, b).start()
    if chain:
        for s in range(climbed, ctx):
            take_up(s)
        gather.finish()
        keep(0).wait()
        for s in range(ctx):
            if s:

                @pl.when(me_c < s)
                def _():
                    keep(s).wait()

            if s < ctx - 1:

                @pl.when((me_c >= s) & (me_c < ctx - 1))
                def _():
                    for copy in climb(s):
                        copy.wait_send()

    for i in range(count):
        own[i].wait()
        for have in [0] + order:
            for shard in range(ctx):
                for b in ways(have):
                    f_copy(i, shard, have, b).wait_send()


def spread_weights(fsdp, ctx, group, arrays, chain=()):
    count = len(arrays)
    sems = pltpu.SemaphoreType.DMA
    outs = pl.pallas_call(
        partial(spread_kernel, fsdp, ctx, group, count, len(chain)),
        out_shape=[
            jax.ShapeDtypeStruct((ctx, fsdp) + v.shape[1:], v.dtype) for v in arrays
        ]
        + [jax.ShapeDtypeStruct((ctx,) + v.shape, v.dtype) for v in chain[:1]]
        + [token_shape(group, v) for v in chain[1:]],
        in_specs=[pl.BlockSpec(memory_space=pltpu.VMEM)] * (count + len(chain)),
        out_specs=[pl.BlockSpec(memory_space=pl.ANY)] * (count + len(chain)),
        scratch_shapes=[
            sems((count,)),
            sems((count, ctx, fsdp, 2)),
            sems((count, ctx, fsdp, 2)),
            sems((ctx,)),
            sems((ctx, 4)),
            sems((ctx, 4)),
        ]
        + (token_sems(group) if chain else []),
        compiler_params=pltpu.CompilerParams(
            collective_id=3 if chain else 1,
            has_side_effects=True,
            vmem_limit_bytes=24 * 1024 * 1024,
        ),
    )(*arrays, *chain)
    return (
        [o.reshape(-1, v.shape[-1]) for o, v in zip(outs, arrays)]
        + list(outs[count : count + 1])
        + [o.reshape(-1, o.shape[-1]) for o in outs[count + 1 :]]
    )


def sum_kernel(fsdp, ctx, count, chain, products, *refs):
    inner = []
    if products:
        first = count + 3
        pairs = refs[first : first + 2 * products]
        place = first + 2 * products + count + 1
        results = refs[place : place + products]
        inner = refs[-2 * products - 1 :]
        refs = refs[:first] + refs[first + 2 * products : place] + refs[place + products :]
        refs = refs[: -2 * products - 1]
    ins = refs[:count]
    if chain:
        parts_ref, cos_ref, sin_ref = refs[count : count + 3]
        refs = refs[:count] + refs[count + 3 :]
        kv_ref = refs[2 * count]
        refs = refs[: 2 * count] + refs[2 * count + 1 :]
    outs = refs[count : 2 * count]
    held = refs[2 * count : 3 * count]
    got = refs[3 * count : 4 * count]
    line = refs[4 * count : 5 * count]
    refs = refs[5 * count :]
    in_sem, f_send, f_recv, z_send, z_recv = refs[:5]
    if chain:
        kv_parts, kv_got, kv_sem, c_send, c_recv = refs[5:]
    me_f = lax.axis_index("fsdp")
    me_c = lax.axis_index("ctx")
    me_t = lax.axis_index("tp")
    bits = [1 << i for i in range(fsdp.bit_length() - 1)]
    order = fsdp_order(fsdp)

    def peer(k):
        return (flip_index(me_f, k, fsdp), me_c, me_t)

    def along(step, act):
        there = me_c + step

        @pl.when((there >= 0) & (there < ctx))
        def _():
            act(there)

    loads = {}
    if chain:
        kv_load = pltpu.make_async_copy(parts_ref, kv_parts, kv_sem.at[0])
        kv_load.start()
    inner_loads = [
        pltpu.make_async_copy(pairs[i], inner[i], inner[-1].at[i]) for i in range(2 * products)
    ]
    for i in range(count):
        for k in reversed([0] + order):
            block = ins[i].at[:, flip_index(me_f, k, fsdp)]
            loads[i, k] = pltpu.make_async_copy(block, held[i].at[k], in_sem.at[i, k])
            loads[i, k].start()

    barrier = pltpu.get_barrier_semaphore()
    for b in bits:
        pl.semaphore_signal(barrier, inc=1, device_id=peer(b), device_id_type=MESH_ID)
    for step in (-1, 1):
        along(
            step,
            lambda there: pl.semaphore_signal(
                barrier, inc=1, device_id=(me_f, there, me_t), device_id_type=MESH_ID
            ),
        )
    pl.semaphore_wait(barrier, len(bits) + line_neighbours(me_c, ctx))

    def ways(k):
        return [(0, k)] if k == low_bit(k) else [(0, low_bit(k)), (1, high_bit(k))]

    def piece(i, k, part):
        rows = ins[i].shape[2]
        return pl.ds(0, rows) if k == low_bit(k) else pl.ds(part * (rows // 2), rows // 2)

    def f_copy(i, shard, k, part, b):
        span = piece(i, k, part)
        return pltpu.make_async_remote_copy(
            src_ref=held[i].at[k, shard, span],
            dst_ref=got[i].at[k, shard, span],
            send_sem=f_send.at[i, shard, k, part],
            recv_sem=f_recv.at[i, shard, k, part],
            device_id=peer(b),
            device_id_type=MESH_ID,
        )

    def add(into, other):
        tile = 16 if into.dtype == jnp.bfloat16 else 8

        def body(r, _):
            span = pl.ds(pl.multiple_of(r * tile, tile), tile)
            into[span] = (
                into[span].astype(jnp.float32) + other[span].astype(jnp.float32)
            ).astype(into.dtype)
            return 0

        lax.fori_loop(0, into.shape[0] // tile, body, 0)

    def collect(i, shard, k):
        for far in order:
            for part, b in ways(far):
                if far ^ b == k:
                    f_copy(i, shard, far, part, b).wait_recv()
                    span = piece(i, far, part)
                    add(held[i].at[k, shard, span], got[i].at[far, shard, span])

    def z_copy(i, shard, step):
        way = 0 if step > 0 else 1
        return pltpu.make_async_remote_copy(
            src_ref=held[i].at[0, shard],
            dst_ref=line[i].at[way, shard],
            send_sem=z_send.at[i, way, shard],
            recv_sem=z_recv.at[i, way, shard],
            device_id=(me_f, me_c + step, me_t),
            device_id_type=MESH_ID,
        )

    def give(i, shard):
        def body(r, _):
            span = pl.ds(pl.multiple_of(r * 16, 16), 16)
            outs[i][span] = held[i][0, shard, span].astype(outs[i].dtype)
            return 0

        lax.fori_loop(0, outs[i].shape[0] // 16, body, 0)

    def on_line(i, shard, step):
        way = 0 if step > 0 else 1

        @pl.when((me_c - step >= 0) & (me_c - step < ctx))
        def _():
            z_copy(i, shard, step).wait_recv()
            add(held[i].at[0, shard], line[i].at[way, shard])

        @pl.when(step * (shard - me_c) > 0)
        def _():
            z_copy(i, shard, step).start()

    def quarters():
        rows = kv_parts.shape[2] // 2
        return [(side, pl.ds(i * rows, rows)) for side in range(2) for i in range(2)]

    def descend(s):
        return [
            pltpu.make_async_remote_copy(
                src_ref=kv_parts.at[s, side, part],
                dst_ref=kv_got.at[s - 1, side, part],
                send_sem=c_send.at[s, i],
                recv_sem=c_recv.at[s - 1, i],
                device_id=(me_f, me_c - 1, me_t),
                device_id_type=MESH_ID,
            )
            for i, (side, part) in enumerate(quarters())
        ]

    def chain_step(s):
        if s < ctx - 1:

            @pl.when((me_c >= s) & (me_c < ctx - 1))
            def _():
                for i, (side, part) in enumerate(quarters()):
                    pltpu.make_async_remote_copy(
                        src_ref=kv_got.at[s, side, part],
                        dst_ref=kv_got.at[s, side, part],
                        send_sem=c_send.at[s + 1, i],
                        recv_sem=c_recv.at[s, i],
                        device_id=(me_f, me_c + 1, me_t),
                        device_id_type=MESH_ID,
                    ).wait_recv()
                    add(kv_parts.at[s, side, part], kv_got.at[s, side, part])

        if s:

            @pl.when(me_c >= s)
            def _():
                for copy in descend(s):
                    copy.start()

    def chain_result():
        width = kv_parts.shape[3]
        rows = cos_ref.shape[0]
        for seq in range(kv_parts.shape[2] // rows):
            span = pl.ds(seq * rows, rows)
            for start in range(0, width, 128):
                cols = slice(start, start + 128)
                t = kv_parts[0, 0, span, cols].astype(jnp.float32)
                t = t * cos_ref[...] + turn(t * sin_ref[...], -1.0)
                kv_ref[span, cols] = t.astype(kv_ref.dtype)
            kv_ref[span, width:] = kv_parts[0, 1, span]

    steps = list(reversed(range(ctx))) if chain else []

    def next_step():
        if steps:
            s = steps.pop(0)
            chain_step(s)
            if s == 0:
                chain_result()

    turns = 4

    def make_products(turn):
        if turn == 0:
            for load in inner_loads:
                load.wait()
        for i in range(products):
            left, right, result = inner[2 * i], inner[2 * i + 1], results[i]
            tiles = left.shape[1] // 256
            per = -(-tiles // turns)

            def body(t, _):
                cols = pl.ds(pl.multiple_of(t * 256, 256), 256)
                result[cols, :] = mul(left[:, cols], right[...], TN).astype(result.dtype)
                return 0

            lax.fori_loop(min(turn * per, tiles), min((turn + 1) * per, tiles), body, 0)

    if chain:
        kv_load.wait()
        next_step()
    for load in inner_loads:
        load.start()
    shards = sorted(range(ctx), key=lambda c: -abs(2 * c - ctx + 1))
    work = [[(i, shard) for i in range(count)] for shard in shards]
    levels = sorted({bin(k).count("1") for k in order}, reverse=True)
    waited = set()

    def loaded(i, k):
        if (i, k) not in waited:
            waited.add((i, k))
            loads[i, k].wait()

    def advance(stage, item):
        for i, shard in item:
            if stage == len(levels):
                loaded(i, 0)
                collect(i, shard, 0)
                continue
            for k in order:
                if bin(k).count("1") == levels[stage]:
                    loaded(i, k)
                    collect(i, shard, k)
                    for part, b in ways(k):
                        f_copy(i, shard, k, part, b).start()

    def line_tick(item, hops):
        for i, shard in item:
            for step, there in ((1, hops), (-1, ctx - 1 - hops)):
                if step * (shard - there) >= 0:

                    @pl.when(me_c == there)
                    def _():
                        on_line(i, shard, step)

            if hops == max(shard, ctx - 1 - shard):

                @pl.when(me_c == shard)
                def _():
                    give(i, shard)

    stages = len(levels) + 1
    for tick in range(len(work) + stages + ctx - 2):
        for stage in range(stages):
            if 0 <= tick - stage < len(work):
                advance(stage, work[tick - stage])
        for hops in range(ctx):
            place = tick - stages + 1 - hops
            if 0 <= place < len(work):
                line_tick(work[place], hops)
        if products and tick < turns:
            make_products(tick)
        next_step()
    while steps:
        next_step()
    for i, shard in [pair for item in work for pair in item]:
        for k in order:
            for part, b in ways(k):
                f_copy(i, shard, k, part, b).wait_send()
        for step in (1, -1):

            @pl.when(step * (shard - me_c) > 0)
            def _():
                z_copy(i, shard, step).wait_send()

    if chain:
        for s in range(1, ctx):

            @pl.when(me_c >= s)
            def _():
                for copy in descend(s):
                    copy.wait_send()


def sum_weights(fsdp, ctx, arrays, chain=(), products=()):
    sems = pltpu.SemaphoreType.DMA
    vmem = pltpu.VMEM
    shards = [v.reshape(ctx, fsdp, -1, v.shape[-1]) for v in arrays]
    blocks = [(fsdp, ctx) + v.shape[2:] for v in shards]
    out_shape = [jax.ShapeDtypeStruct(v.shape[2:], jnp.float32) for v in shards]
    lines = [vmem((2,) + b[1:], v.dtype) for b, v in zip(blocks, shards)]
    extra = []
    if chain:
        parts = chain[0]
        out_shape.append(jax.ShapeDtypeStruct((parts.shape[2], 2 * parts.shape[3]), parts.dtype))
        extra = [
            vmem(parts.shape, parts.dtype),
            vmem((ctx - 1,) + parts.shape[1:], parts.dtype),
            sems((1,)),
            sems((ctx, 4)),
            sems((ctx, 4)),
        ]
    count = len(shards)
    flat = [v for pair in products for v in pair]
    for left, right in products:
        out_shape.append(jax.ShapeDtypeStruct((left.shape[1], right.shape[1]), left.dtype))
    if products:
        extra = extra + [vmem(v.shape, v.dtype) for v in flat] + [sems((len(flat),))]
    held = [vmem(b, v.dtype) for b, v in zip(blocks, shards)]
    return pl.pallas_call(
        partial(sum_kernel, fsdp, ctx, count, bool(chain), len(products)),
        out_shape=out_shape,
        in_specs=[pl.BlockSpec(memory_space=pl.ANY)] * (count + len(chain[:1]))
        + [pl.BlockSpec(memory_space=pltpu.VMEM)] * len(chain[1:])
        + [pl.BlockSpec(memory_space=pl.ANY)] * len(flat),
        out_specs=[pl.BlockSpec(memory_space=pltpu.VMEM)] * len(out_shape),
        scratch_shapes=held
        + held
        + lines
        + [
            sems((count, fsdp)),
            sems((count, ctx, fsdp, 2)),
            sems((count, ctx, fsdp, 2)),
            sems((count, 2, ctx)),
            sems((count, 2, ctx)),
        ]
        + extra,
        compiler_params=pltpu.CompilerParams(
            collective_id=4 if chain else 2,
            has_side_effects=True,
            vmem_limit_bytes=58 * 1024 * 1024,
        ),
    )(*shards, *chain, *flat)


def heads_kernel(group_size, qkv_ref, out_ref, *outs):
    width = outs[0].shape[1]
    for source, target in ((qkv_ref, outs[0]), (out_ref, outs[3])):
        for block in range(width // 128):
            pair, rest = divmod(2 * block, 2 * group_size)
            g, j = divmod(rest, group_size)
            start = (pair * group_size + j) * 128
            left = source[:, start : start + 128]
            right = source[:, start + 128 : start + 256]
            if g:
                left = pltpu.roll(left, HD, 1)
            else:
                right = pltpu.roll(right, HD, 1)
            lane = lax.broadcasted_iota(jnp.int32, left.shape, 1)
            target[:, block * 128 : (block + 1) * 128] = jnp.where(lane < HD, left, right)
    kv_width = outs[1].shape[1]
    outs[1][...] = qkv_ref[:, width : width + kv_width]
    outs[2][...] = qkv_ref[:, width + kv_width :]


def plain_grads(group_size, qkv, out, kv_width):
    rows, width = out.shape
    vmem = pl.BlockSpec(memory_space=pltpu.VMEM)
    return pl.pallas_call(
        partial(heads_kernel, group_size),
        out_shape=[
            jax.ShapeDtypeStruct((rows, w), out.dtype) for w in (width, kv_width, kv_width, width)
        ],
        in_specs=[vmem] * 2,
        out_specs=[vmem] * 4,
        cost_estimate=pl.CostEstimate(flops=0, bytes_accessed=4 << 20, transcendentals=0),
    )(qkv, out)


def place_kernel(group, count, *refs):
    parts, outs = refs[:count], refs[count:]
    span = sum(v.shape[3] for v in parts)
    for i, out in enumerate(outs):
        for f in range(group):
            start = f * span
            for v in parts:
                width = v.shape[3]
                out[:, start : start + width] = v[f, i].astype(out.dtype)
                start += width


def place_units(parts):
    group, arrays, rows, _ = parts[0].shape
    cols = group * sum(v.shape[3] for v in parts)
    vmem = pl.BlockSpec(memory_space=pltpu.VMEM)
    return pl.pallas_call(
        partial(place_kernel, group, len(parts)),
        out_shape=[jax.ShapeDtypeStruct((rows, cols), jnp.float32)] * arrays,
        in_specs=[vmem] * len(parts),
        out_specs=[vmem] * arrays,
        compiler_params=pltpu.CompilerParams(vmem_limit_bytes=24 * 1024 * 1024),
        cost_estimate=pl.CostEstimate(
            flops=0, bytes_accessed=6 * rows * cols * arrays, transcendentals=0
        ),
    )(*parts)


def local(
    inputs,
    lengths,
    cotangent,
    norm1_gain,
    w_query,
    w_key,
    w_value,
    w_out,
    norm2_gain,
    w_gate,
    w_up,
    w_down,
):
    seq_count, local_rows, model_width = inputs.shape
    tokens = seq_count * local_rows
    half = tokens // 2
    fsdp = lax.axis_size("fsdp")
    ctx = lax.axis_size("ctx")
    shard = w_query.shape[0]
    query_width = w_query.shape[1]
    kv_width = w_key.shape[1]
    kv_end = query_width + 2 * kv_width
    pairs = kv_width // (2 * HD)
    group_size = query_width // kv_width
    group = min(fsdp, 4)
    far = fsdp // group
    own = w_gate.shape[1] // group
    first_units = own * FIRST_EIGHTHS // 8
    widths = (first_units, own - first_units)
    me_c = lax.axis_index("ctx")
    me_t = lax.axis_index("tp")
    low = jnp.bfloat16
    wide = jnp.float32

    def swap(v):
        return lax.ppermute(v, "tp", [(0, 1), (1, 0)])

    inside = shard % 128 == 0
    dims = (fsdp, ctx, shard)
    back_dims = (ctx, fsdp, shard)

    def by_ctx(v):
        if inside:
            return v
        rows = v.shape[0]
        return v.reshape(rows, fsdp, ctx, shard).swapaxes(1, 2).reshape(rows, model_width)

    def by_fsdp(v):
        if inside:
            return v
        rows = v.shape[0]
        return v.reshape(rows, ctx, fsdp, shard).swapaxes(1, 2).reshape(rows, model_width)

    def pair_heads(v):
        rows = v.shape[0]
        return (
            v.reshape(rows, pairs, 2, group_size, HD).swapaxes(2, 3).reshape(rows, query_width)
        )

    x = by_ctx(inputs.reshape(tokens, model_width))
    cot = by_ctx(cotangent.reshape(tokens, model_width))
    positions = me_c * local_rows + jnp.arange(local_rows, dtype=jnp.int32)
    cosines, sines = rope_tables(positions, HD)
    cosines, sines = jnp.tile(cosines, (1, 2)), jnp.tile(sines, (1, 2))

    gains = jnp.pad(jnp.stack([norm1_gain, norm2_gain]).astype(wide), ((0, 14), (0, 0)))
    lined, held = start_exchange(
        fsdp,
        ctx,
        group,
        [
            jnp.concatenate([pair_heads(w_query), w_key, w_value], 1),
            gains,
            pair_heads(w_out),
        ],
        [w_gate, w_up, w_down],
        widths,
    )
    far_groups = [[h * group + g for h in range(far)] for g in range(group)]
    near_groups = [[h * group + g for g in range(group)] for h in range(far)]

    def whole_width(v):
        if far > 1:
            v = lax.all_gather(v, "fsdp", axis=0, tiled=False, axis_index_groups=far_groups)
        return lax.all_gather(v, "ctx", axis=0, tiled=False).reshape(model_width, -1)

    first_full = whole_width(held[0])
    qkv_full, gain_rows = spread_weights(fsdp, ctx, group, lined[:2])
    late_held, gain_rows = lax.optimization_barrier((held[1], gain_rows))
    late_full = whole_width(late_held)
    gain_rows = gain_rows.reshape(ctx * fsdp, 16, shard)
    gain_one = gain_rows[:, 0].reshape(1, model_width)
    gain_two = gain_rows[:, 1].reshape(1, model_width)

    (ff_grad,) = by_rows(
        partial(cot_kernel, dims, local_rows),
        128,
        [(lengths, "smem"), (cot, "rows")],
        [((tokens, model_width), low)],
    )
    first_normed, query, kv_own = by_rows(
        partial(qkv_kernel, dims),
        128,
        [
            (x, "rows"),
            (qkv_full, "whole"),
            (gain_one, "whole"),
            (cosines, "cycle"),
            (sines, "cycle"),
        ],
        [
            ((tokens, model_width), low),
            ((tokens, query_width), low),
            ((tokens, 2 * kv_width), low),
        ],
        flops=2 * tokens * model_width * kv_end,
    )
    out_full, kv_all, ff_grad_all = spread_weights(
        fsdp, ctx, group, lined[2:], (kv_own, ff_grad)
    )
    attended, lse = attend(lengths, query, kv_all)
    attn_part = jnp.einsum(
        "tj,dj->td", attended, out_full, preferred_element_type=wide
    ).astype(low)
    middle, second_normed = by_rows(
        partial(middle_kernel, dims),
        128,
        [(x, "rows"), (attn_part, "rows"), (swap(attn_part), "rows"), (gain_two, "whole")],
        [((tokens, model_width), wide), ((tokens, model_width), low)],
    )
    normed_all = gather_tokens(group, fsdp, second_normed)

    def unit_term(left, right):
        return jnp.einsum("td,tf->df", left, right, preferred_element_type=wide).astype(low)

    def own_units(term):
        width = term.shape[1]
        own = lax.psum_scatter(
            term.reshape(ctx, fsdp, shard, width), "ctx", scatter_dimension=0, tiled=False
        )
        if far > 1:
            own = lax.psum_scatter(
                own.reshape(far, group, shard, width),
                "fsdp",
                scatter_dimension=0,
                tiled=False,
                axis_index_groups=far_groups,
            )
        return own

    def return_units(both, down):
        units = down.shape[-1]
        pieces = jnp.concatenate([both[..., :units], both[..., units:], down], 1)
        back = lax.all_to_all(
            pieces.reshape(group * 3 * shard, units),
            "fsdp",
            0,
            0,
            tiled=True,
            axis_index_groups=near_groups if far > 1 else None,
        )
        return back.reshape(group, 3, shard, units)

    many = group * tokens
    first_hidden, first_grads, second_part, ff_part = by_rows(
        swiglu_first_kernel,
        256,
        [(normed_all, "rows"), (ff_grad_all, "rows"), (first_full, "whole")],
        [
            ((many, first_units), low),
            ((many, 2 * first_units), low),
            ((many, model_width), low),
            ((many, model_width), low),
        ],
        flops=12 * many * model_width * first_units,
        limit=56,
    )
    first_both = unit_term(normed_all, first_grads)
    first_down = unit_term(ff_grad_all, first_hidden)
    first_own = (own_units(first_both), own_units(first_down))
    second_part, ff_part, _, _ = lax.optimization_barrier(
        (second_part, ff_part, first_both, first_down)
    )
    hidden, both_grad, ff_sums, second_grad = swiglu(
        fsdp, group, normed_all, ff_grad_all, late_full, second_part, ff_part
    )
    second_grad = second_grad.reshape(tokens, model_width)

    middle_grad, attn_grad, gain_two_term = by_rows(
        partial(middle_back_kernel, dims, local_rows),
        128,
        [
            (lengths, "smem"),
            (cot, "rows"),
            (middle, "rows"),
            (second_grad, "rows"),
            (gain_two, "whole"),
        ],
        [((tokens, model_width), wide), ((tokens, model_width), low), ((1, model_width), wide)],
    )
    attended_grad = jnp.dot(attn_grad, out_full, preferred_element_type=wide).astype(low)
    query_grad, kv_parts, ff_branch = attend_back(
        fsdp,
        group,
        lengths,
        query,
        attended_grad,
        lse,
        cosines,
        sines,
        kv_all,
        ff_sums.reshape(group, half, model_width),
    )
    out_term = jnp.einsum("td,tj->dj", attn_grad, attended, preferred_element_type=wide)
    w_out_grad, kv_grad, late_both, late_down = sum_weights(
        fsdp,
        ctx,
        [out_term.astype(low)],
        (kv_parts, cosines, sines),
        ((normed_all, both_grad), (ff_grad_all, hidden)),
    )
    late_both_own = own_units(late_both)
    late_down_own = own_units(late_down)
    (output,) = by_rows(
        partial(output_kernel, back_dims, local_rows),
        128,
        [(lengths, "smem"), (middle, "rows"), (ff_branch.reshape(tokens, model_width), "rows")],
        [((tokens, model_width), low)],
    )
    qkv_grad = jnp.concatenate([query_grad, kv_grad], -1)
    qkv_term = jnp.einsum("td,tj->dj", first_normed, qkv_grad, preferred_element_type=wide)
    first_part = jnp.einsum(
        "tj,dj->td", qkv_grad, qkv_full, preferred_element_type=wide
    ).astype(low)
    input_grad, gain_one_term = by_rows(
        partial(input_back_kernel, dims),
        128,
        [
            (x, "rows"),
            (first_part, "rows"),
            (swap(first_part), "rows"),
            (middle_grad, "rows"),
            (gain_one, "whole"),
        ],
        [((tokens, model_width), low), ((1, model_width), wide)],
    )
    gain_terms = jnp.stack(
        [gain_one_term.reshape(-1, shard), gain_two_term.reshape(-1, shard)], 1
    )
    gain_terms = jnp.pad(gain_terms, ((0, 0), (0, 14), (0, 0))).reshape(-1, shard)
    first_back = return_units(*first_own)
    qkv_term, first_back, _ = lax.optimization_barrier(
        (qkv_term.astype(low), first_back, late_both)
    )
    qkv_own, gain_own = sum_weights(fsdp, ctx, [qkv_term, gain_terms])
    w_query_grad, w_key_grad, w_value_grad, w_out_grad = plain_grads(
        group_size, qkv_own, w_out_grad, kv_width
    )
    late_both_own, late_down_own, qkv_own = lax.optimization_barrier(
        (late_both_own, late_down_own, qkv_own)
    )
    late_back = return_units(late_both_own, late_down_own)
    w_gate_grad, w_up_grad, w_down_grad = place_units([first_back, late_back])
    return (
        by_fsdp(output).reshape(inputs.shape),
        by_fsdp(input_grad).reshape(inputs.shape),
        gain_own[0],
        w_query_grad,
        w_key_grad,
        w_value_grad,
        w_out_grad,
        gain_own[1],
        w_gate_grad,
        w_up_grad,
        w_down_grad,
    )


def solution(mesh):
    placed = (
        P("fsdp", "ctx", None),
        P("fsdp"),
        P("fsdp", "ctx", None),
        P(("fsdp", "ctx")),
        P(("fsdp", "ctx"), "tp"),
        P(("fsdp", "ctx"), "tp"),
        P(("fsdp", "ctx"), "tp"),
        P(("fsdp", "ctx"), "tp"),
        P(("fsdp", "ctx")),
        P(("fsdp", "ctx"), "tp"),
        P(("fsdp", "ctx"), "tp"),
        P(("fsdp", "ctx"), "tp"),
    )
    return jax.shard_map(
        local,
        mesh=mesh,
        in_specs=placed,
        out_specs=(
            P("fsdp", "ctx", None),
            P("fsdp", "ctx", None),
            P(("fsdp", "ctx")),
            P(("fsdp", "ctx"), "tp"),
            P(("fsdp", "ctx"), "tp"),
            P(("fsdp", "ctx"), "tp"),
            P(("fsdp", "ctx"), "tp"),
            P(("fsdp", "ctx")),
            P(("fsdp", "ctx"), "tp"),
            P(("fsdp", "ctx"), "tp"),
            P(("fsdp", "ctx"), "tp"),
        ),
        check_vma=False,
    )
```

```python
from functools import partial

import jax
import jax.numpy as jnp
from jax import lax
from jax.experimental import pallas as pl
from jax.experimental.pallas import tpu as pltpu
from jax.sharding import PartitionSpec as P

HD = 64


norm_eps = 1e-05
residual_scale = 0.22
score_scale = 1.0 / 64.0
rope_base = 10000000.0
masked_score = -1e30


def rope_tables(positions, head_dim):
    half_dim = head_dim // 2
    frequency = rope_base ** (-(jnp.arange(half_dim, dtype=jnp.float32) * 2.0) / head_dim)
    angles = positions.astype(jnp.float32)[:, None] * frequency[None, :]
    return (
        jnp.concatenate([jnp.cos(angles), jnp.cos(angles)], -1),
        jnp.concatenate([jnp.sin(angles), jnp.sin(angles)], -1),
    )


def rotate(values_in, cosines, sines):
    half_dim = values_in.shape[-1] // 2
    turned = jnp.concatenate([-values_in[..., half_dim:], values_in[..., :half_dim]], -1)
    return values_in * cosines + turned * sines


def unrotate(grad_in, cosines, sines):
    half_dim = grad_in.shape[-1] // 2
    scaled = grad_in * sines
    return grad_in * cosines + jnp.concatenate(
        [scaled[..., half_dim:], -scaled[..., :half_dim]], -1
    )


def rms_scale(values_in):
    return lax.rsqrt(jnp.mean(values_in * values_in, -1, keepdims=True) + norm_eps)


def norm_back(grad_normed, values_in, scale, gain):
    scaled_grad = grad_normed * gain
    return scale * scaled_grad - values_in * scale**3 * jnp.mean(
        scaled_grad * values_in, -1, keepdims=True
    )


MESH_ID = pl.DeviceIdType.MESH
FIRST_EIGHTHS = 4
NT = (((1,), (1,)), ((), ()))
TN = (((0,), (0,)), ((), ()))
SMEM = pltpu.SMEM


def mul(left, right, dims=(((1,), (0,)), ((), ()))):
    return lax.dot_general(left, right, dims, preferred_element_type=jnp.float32)


def reorder(v, first, second, width):
    if width % 128:
        return v
    pieces = []
    for b in range(second):
        for a in range(first):
            start = (a * second + b) * width
            pieces.append(v[:, start : start + width])
    return jnp.concatenate(pieces, 1)


def turn(t, sign):
    lane = lax.broadcasted_iota(jnp.int32, t.shape, 1)
    ahead = pltpu.roll(t, 128 - HD // 2, 1)
    behind = pltpu.roll(t, HD // 2, 1)
    return jnp.where(lax.rem(lane, HD) < HD // 2, -sign * ahead, sign * behind)


def row_valid(len_ref, rows, local_rows):
    step = pl.program_id(0)
    start = step * rows
    seq = start // local_rows
    place = (
        lax.axis_index("ctx") * local_rows
        + lax.rem(start, local_rows)
        + lax.broadcasted_iota(jnp.int32, (rows, 1), 0)
    )
    return (place < len_ref[seq]).astype(jnp.float32)


def qkv_kernel(dims, x_ref, w_ref, gain_ref, cos_ref, sin_ref, normed_ref, q_ref, kv_ref):
    x = reorder(x_ref[...].astype(jnp.float32), *dims)
    normed = (x * rms_scale(x) * gain_ref[...]).astype(jnp.bfloat16)
    normed_ref[...] = normed
    lin = mul(normed, w_ref[...])
    cosines, sines = cos_ref[...], sin_ref[...]
    width = q_ref.shape[1]
    half = kv_ref.shape[1] // 2
    for start in range(0, width + half, 128):
        t = lin[:, start : start + 128]
        t = (t * cosines + turn(t, 1.0) * sines).astype(jnp.bfloat16)
        if start < width:
            q_ref[:, start : start + 128] = t
        else:
            kv_ref[:, start - width : start - width + 128] = t
    kv_ref[:, half:] = lin[:, width + half :].astype(jnp.bfloat16)


def key_biases(len_ref, rows, ctx):
    length = len_ref[pl.program_id(0)]
    me = lax.axis_index("ctx")
    row = lax.broadcasted_iota(jnp.int32, (rows, rows), 0)
    col = lax.broadcasted_iota(jnp.int32, (rows, rows), 1)
    first = jnp.where((col <= row) & (me * rows + col < length), 0.0, masked_score)
    out = [first]
    for s in range(1, ctx):
        place = (me - s) * rows + lax.broadcasted_iota(jnp.int32, (1, rows), 1)
        out.append(jnp.where((place >= 0) & (place < length), 0.0, masked_score))
    return out


def attend_kernel(ctx, len_ref, q_ref, *refs):
    keys, values = refs[:ctx], refs[ctx : 2 * ctx]
    o_ref, lse_ref = refs[2 * ctx :]
    rows = q_ref.shape[0]
    biases = key_biases(len_ref, rows, ctx)
    lane = lax.broadcasted_iota(jnp.int32, (rows, 128), 1)
    lse_all = jnp.zeros((rows, 128), jnp.float32)
    for j in range(q_ref.shape[1] // 128):
        q_pair = q_ref[:, j * 128 : (j + 1) * 128] * jnp.bfloat16(score_scale)
        outs = []
        for g in range(2):
            mine = (lane < HD) if g == 0 else (lane >= HD)
            q_head = jnp.where(mine, q_pair, jnp.zeros_like(q_pair))
            scores = [mul(q_head, k[...], NT) + b for k, b in zip(keys, biases)]
            top = scores[0].max(-1, keepdims=True)
            for s in scores[1:]:
                top = jnp.maximum(top, s.max(-1, keepdims=True))
            mass, out = 0.0, 0.0
            for s, v in zip(scores, values):
                p = jnp.exp(s - top)
                mass = mass + p.sum(-1, keepdims=True)
                out = out + mul(p.astype(jnp.bfloat16), v[...])
            outs.append(out / mass)
            lse_all = jnp.where(lane == 2 * j + g, top + jnp.log(mass), lse_all)
        o_ref[:, j * 128 : (j + 1) * 128] = jnp.where(lane < HD, outs[0], outs[1]).astype(
            jnp.bfloat16
        )
    lse_ref[...] = lse_all


class RowSum:
    def __init__(
        self, group, fsdp, rows_ref, own_ref, held, got, in_sem, f_send, f_recv, own_sem
    ):
        self.group, self.fsdp = group, fsdp
        self.order = fsdp_order(group)
        self.bits = [1 << i for i in range(group.bit_length() - 1)]
        self.own_ref, self.held, self.got = own_ref, held, got
        self.f_send, self.f_recv, self.own_sem = f_send, f_recv, own_sem
        self.half = rows_ref.shape[1]
        self.loads = [
            pltpu.make_async_copy(rows_ref.at[k], held.at[k], in_sem.at[k]) for k in range(group)
        ]

    def peer(self, k):
        me_f = lax.axis_index("fsdp")
        return (flip_index(me_f, k, self.fsdp), lax.axis_index("ctx"), lax.axis_index("tp"))

    def core(self):
        me_f, me_c, me_t = self.peer(0)
        return (me_f, me_c, 1 - me_t)

    def ways(self, k):
        return [(0, k)] if k == low_bit(k) else [(0, low_bit(k)), (1, high_bit(k))]

    def span(self, k, part):
        half = self.half
        return pl.ds(0, half) if k == low_bit(k) else pl.ds(part * (half // 2), half // 2)

    def copy(self, k, part, b):
        return pltpu.make_async_remote_copy(
            src_ref=self.held.at[k, self.span(k, part)],
            dst_ref=self.got.at[k, self.span(k, part)],
            send_sem=self.f_send.at[k, part],
            recv_sem=self.f_recv.at[k, part],
            device_id=self.peer(b),
            device_id_type=MESH_ID,
        )

    def own_copy(self, place):
        return pltpu.make_async_remote_copy(
            src_ref=self.held.at[0],
            dst_ref=self.own_ref.at[place],
            send_sem=self.own_sem.at[0],
            recv_sem=self.own_sem.at[1],
            device_id=self.core(),
            device_id_type=MESH_ID,
        )

    def collect(self, k):
        for far in self.order:
            for part, b in self.ways(far):
                if far ^ b == k:
                    self.copy(far, part, b).wait_recv()
                    rows = self.span(far, part)
                    self.held[k, rows] = (
                        self.held[k, rows].astype(jnp.float32)
                        + self.got[far, rows].astype(jnp.float32)
                    ).astype(self.held.dtype)

    def send(self, k):
        for part, b in self.ways(k):
            self.copy(k, part, b).start()

    def start(self):
        barrier = pltpu.get_barrier_semaphore()
        for b in self.bits:
            pl.semaphore_signal(barrier, inc=1, device_id=self.peer(b), device_id_type=MESH_ID)
        pl.semaphore_signal(barrier, inc=1, device_id=self.core(), device_id_type=MESH_ID)
        for load in self.loads:
            load.start()
        pl.semaphore_wait(barrier, len(self.bits) + 1)
        for load in self.loads:
            load.wait()
        for k in self.order:
            if k != low_bit(k):
                self.send(k)

    def relay(self):
        for k in self.order:
            if k == low_bit(k):
                self.collect(k)
                self.send(k)

    def finish(self):
        self.collect(0)
        me_t = lax.axis_index("tp")
        self.own_copy(me_t).start()
        local = pltpu.make_async_copy(
            self.held.at[0], self.own_ref.at[me_t], self.own_sem.at[2]
        )
        local.start()
        local.wait()
        self.own_copy(1 - me_t).wait_recv()
        self.own_copy(me_t).wait_send()
        for k in self.order:
            for part, b in self.ways(k):
                self.copy(k, part, b).wait_send()


def attend_back_kernel(
    ctx, fsdp, group, len_ref, q_ref, do_ref, lse_ref, cos_ref, sin_ref, rows_ref, *refs
):
    keys, values = refs[:ctx], refs[ctx : 2 * ctx]
    dq_ref, dkv_ref, own_ref, dk_sum, dv_sum = refs[2 * ctx : 2 * ctx + 5]
    step = pl.program_id(0) * pl.num_programs(1) + pl.program_id(1)
    sums = RowSum(group, fsdp, rows_ref, own_ref, *refs[2 * ctx + 5 :])

    @pl.when(step == 0)
    def _():
        sums.start()

    rows = q_ref.shape[0]
    biases = key_biases(len_ref, rows, ctx)
    lane = lax.broadcasted_iota(jnp.int32, (rows, 128), 1)
    dk_sum[...] = jnp.zeros_like(dk_sum)
    dv_sum[...] = jnp.zeros_like(dv_sum)
    lse_all = lse_ref[...]
    for j in range(q_ref.shape[1] // 128):
        q_pair = q_ref[:, j * 128 : (j + 1) * 128] * jnp.bfloat16(score_scale)
        do_pair = do_ref[:, j * 128 : (j + 1) * 128]
        dqs = []
        for g in range(2):
            mine = (lane < HD) if g == 0 else (lane >= HD)
            q_head = jnp.where(mine, q_pair, jnp.zeros_like(q_pair))
            do_head = jnp.where(mine, do_pair, jnp.zeros_like(do_pair))
            h = 2 * j + g
            lse = lse_all[:, h : h + 1]
            probs, grads, total = [], [], 0.0
            for s in range(ctx):
                p = jnp.exp(mul(q_head, keys[s][...], NT) + (biases[s] - lse))
                dp = mul(do_head, values[s][...], NT)
                total = total + (p * dp).sum(-1, keepdims=True)
                probs.append(p)
                grads.append(dp)
            dq = 0.0
            for s in range(ctx):
                ds = (probs[s] * (grads[s] - total)).astype(jnp.bfloat16)
                dv_sum[s] += mul(probs[s].astype(jnp.bfloat16), do_head, TN)
                dk_sum[s] += mul(ds, q_head, TN)
                dq = dq + mul(ds, keys[s][...])
            dqs.append(dq)
        dq = jnp.where(lane < HD, dqs[0], dqs[1]) * score_scale
        dq = dq * cos_ref[...] + turn(dq * sin_ref[...], -1.0)
        dq_ref[:, j * 128 : (j + 1) * 128] = dq.astype(jnp.bfloat16)
        if j == 1:

            @pl.when(step == 1)
            def _():
                sums.relay()

    for s in range(ctx):
        dkv_ref[s, 0] = dk_sum[s].astype(dkv_ref.dtype)
        dkv_ref[s, 1] = dv_sum[s].astype(dkv_ref.dtype)

    @pl.when(step == pl.num_programs(0) * pl.num_programs(1) - 1)
    def _():
        sums.finish()


def cot_kernel(dims, local_rows, len_ref, cot_ref, ff_ref):
    rows = cot_ref.shape[0]
    back = cot_ref[...].astype(jnp.float32) * row_valid(len_ref, rows, local_rows)
    ff_ref[...] = reorder((residual_scale * back).astype(jnp.bfloat16), *dims)


def middle_kernel(dims, x_ref, part_ref, other_ref, gain_ref, middle_ref, normed_ref):
    branch = part_ref[...].astype(jnp.float32) + other_ref[...].astype(jnp.float32)
    middle = reorder(x_ref[...].astype(jnp.float32), *dims) + residual_scale * branch
    middle_ref[...] = middle
    normed_ref[...] = (middle * rms_scale(middle) * gain_ref[...]).astype(jnp.bfloat16)


def middle_back_kernel(
    dims, local_rows, len_ref, cot_ref, middle_ref, grad_ref, gain_ref, back_ref, attn_ref, gain_sum
):
    rows = cot_ref.shape[0]
    back = cot_ref[...].astype(jnp.float32) * row_valid(len_ref, rows, local_rows)
    middle = middle_ref[...]
    grad = grad_ref[...].astype(jnp.float32)
    scale = rms_scale(middle)
    out = reorder(back, *dims) + norm_back(grad, middle, scale, gain_ref[...])
    back_ref[...] = out
    attn_ref[...] = (residual_scale * out).astype(jnp.bfloat16)

    @pl.when(pl.program_id(0) == 0)
    def _():
        gain_sum[...] = jnp.zeros_like(gain_sum)

    gain_sum[...] += (grad * middle * scale).sum(0, keepdims=True)


def output_kernel(dims, local_rows, len_ref, middle_ref, ff_ref, out_ref):
    rows = middle_ref.shape[0]
    out = middle_ref[...] + residual_scale * ff_ref[...].astype(jnp.float32)
    out = (out * row_valid(len_ref, rows, local_rows)).astype(jnp.bfloat16)
    out_ref[...] = reorder(out, *dims)


def input_back_kernel(
    dims, x_ref, part_ref, other_ref, back_ref, gain_ref, out_ref, gain_sum
):
    first, second, width = dims
    x = reorder(x_ref[...].astype(jnp.float32), *dims)
    grad = (part_ref[...].astype(jnp.float32) + other_ref[...].astype(jnp.float32))
    scale = rms_scale(x)
    out = back_ref[...] + norm_back(grad, x, scale, gain_ref[...])
    out_ref[...] = reorder(out.astype(jnp.bfloat16), second, first, width)

    @pl.when(pl.program_id(0) == 0)
    def _():
        gain_sum[...] = jnp.zeros_like(gain_sum)

    gain_sum[...] += (grad * x * scale).sum(0, keepdims=True)


def by_rows(kernel, rows, ins, outs, flops=0, limit=40):
    total = max(v.shape[0] for v, kind in ins if kind == "rows")
    in_specs = []
    moved = 0
    for v, kind in ins:
        moved += v.size * v.dtype.itemsize
        if kind == "rows":
            in_specs.append(pl.BlockSpec((rows, v.shape[1]), lambda i: (i, 0)))
        elif kind == "cycle":
            period = v.shape[0] // rows
            in_specs.append(
                pl.BlockSpec((rows, v.shape[1]), lambda i, period=period: (lax.rem(i, period), 0))
            )
        elif kind == "smem":
            in_specs.append(pl.BlockSpec(memory_space=SMEM))
        else:
            in_specs.append(
                pl.BlockSpec(v.shape, lambda i: (0, 0), pipeline_mode=pl.Buffered(1))
            )
    out_specs = []
    for shape, dtype in outs:
        moved += shape[0] * shape[1] * jnp.dtype(dtype).itemsize
        if shape[0] == 1:
            out_specs.append(pl.BlockSpec(shape, lambda i: (0, 0)))
        else:
            out_specs.append(pl.BlockSpec((rows, shape[1]), lambda i: (i, 0)))
    return pl.pallas_call(
        kernel,
        grid=(total // rows,),
        in_specs=in_specs,
        out_specs=out_specs,
        out_shape=[jax.ShapeDtypeStruct(shape, dtype) for shape, dtype in outs],
        compiler_params=pltpu.CompilerParams(vmem_limit_bytes=limit * 1024 * 1024),
        cost_estimate=pl.CostEstimate(flops=flops, bytes_accessed=moved, transcendentals=0),
    )(*[v for v, _ in ins])


def kv_specs(ctx, rows, pairs):
    def spec(slot, start):
        return pl.BlockSpec((None, rows, 128), lambda s, p: (slot, s, start + p))

    return [spec(slot, start) for start in (0, pairs) for slot in range(ctx)]


def attend(lengths, query, kv_all):
    ctx = kv_all.shape[0]
    seqs = lengths.shape[0]
    rows = query.shape[0] // seqs
    pairs = kv_all.shape[2] // 256
    wide = query.shape[1] // pairs
    flops = 4 * query.shape[0] * query.shape[1] * rows * ctx
    return pl.pallas_call(
        partial(attend_kernel, ctx),
        grid=(seqs, pairs),
        in_specs=[
            pl.BlockSpec(memory_space=SMEM),
            pl.BlockSpec((rows, wide), lambda s, p: (s, p)),
        ]
        + kv_specs(ctx, rows, pairs),
        out_specs=[
            pl.BlockSpec((rows, wide), lambda s, p: (s, p)),
            pl.BlockSpec((rows, 128), lambda s, p: (s, p)),
        ],
        out_shape=[
            jax.ShapeDtypeStruct(query.shape, jnp.bfloat16),
            jax.ShapeDtypeStruct((query.shape[0], 128 * pairs), jnp.float32),
        ],
        compiler_params=pltpu.CompilerParams(vmem_limit_bytes=40 * 1024 * 1024),
        cost_estimate=pl.CostEstimate(flops=4 * flops, bytes_accessed=6 << 20, transcendentals=0),
    )(lengths, query, *[kv_all] * (2 * ctx))


def attend_back(fsdp, group, lengths, query, out_grad, lse, cosines, sines, kv_all, row_blocks):
    ctx = kv_all.shape[0]
    block = row_blocks.shape[1:]
    low = jnp.bfloat16
    sems = pltpu.SemaphoreType.DMA
    seqs = lengths.shape[0]
    rows = query.shape[0] // seqs
    pairs = kv_all.shape[2] // 256
    wide = query.shape[1] // pairs
    flops = 10 * query.shape[0] * query.shape[1] * rows * ctx
    return pl.pallas_call(
        partial(attend_back_kernel, ctx, fsdp, group),
        grid=(seqs, pairs),
        in_specs=[
            pl.BlockSpec(memory_space=SMEM),
            pl.BlockSpec((rows, wide), lambda s, p: (s, p)),
            pl.BlockSpec((rows, wide), lambda s, p: (s, p)),
            pl.BlockSpec((rows, 128), lambda s, p: (s, p)),
            pl.BlockSpec((rows, 128), lambda s, p: (0, 0)),
            pl.BlockSpec((rows, 128), lambda s, p: (0, 0)),
            pl.BlockSpec(memory_space=pl.ANY),
        ]
        + kv_specs(ctx, rows, pairs),
        out_specs=[
            pl.BlockSpec((rows, wide), lambda s, p: (s, p)),
            pl.BlockSpec((ctx, 2, rows, 128), lambda s, p: (0, 0, s, p)),
            pl.BlockSpec(memory_space=pl.ANY),
        ],
        out_shape=[
            jax.ShapeDtypeStruct(query.shape, jnp.bfloat16),
            jax.ShapeDtypeStruct((ctx, 2, query.shape[0], 128 * pairs), low),
            jax.ShapeDtypeStruct((2,) + block, low),
        ],
        scratch_shapes=[pltpu.VMEM((ctx, rows, 128), jnp.float32)] * 2
        + [pltpu.VMEM((group,) + block, low)] * 2
        + [sems((group,)), sems((group, 2)), sems((group, 2)), sems((3,))],
        compiler_params=pltpu.CompilerParams(
            collective_id=7, has_side_effects=True, vmem_limit_bytes=44 * 1024 * 1024
        ),
        cost_estimate=pl.CostEstimate(flops=4 * flops, bytes_accessed=10 << 20, transcendentals=0),
    )(lengths, query, out_grad, lse, cosines, sines, row_blocks, *[kv_all] * (2 * ctx))


def low_bit(k):
    return k & -k


def high_bit(k):
    return 1 << (k.bit_length() - 1)


def fsdp_order(fsdp):
    return sorted(range(1, fsdp), key=lambda k: (bin(k).count("1"), k))


def flip_index(me, k, fsdp):
    out = me
    for i in range(fsdp.bit_length() - 1):
        b = 1 << i
        if k & b:
            out = out + b - 2 * b * lax.rem(me // b, 2)
    return out


def line_neighbours(me, count):
    return (me > 0).astype(jnp.int32) + (me < count - 1).astype(jnp.int32)


def line_kernel(fsdp, ctx, group, lines, swaps, widths, *refs):
    line_in = refs[:lines]
    swap_in = refs[lines : lines + swaps]
    line_out = refs[lines + swaps : 2 * lines + swaps]
    swap_out = refs[2 * lines + swaps : -5]
    own_sem, z_send, z_recv, f_send, f_recv = refs[-5:]
    parts = len(widths)
    me_f = lax.axis_index("fsdp")
    me_c = lax.axis_index("ctx")
    me_t = lax.axis_index("tp")

    def along(step, act):
        there = me_c + step

        @pl.when((there >= 0) & (there < ctx))
        def _():
            act(there)

    barrier = pltpu.get_barrier_semaphore()
    for k in range(1, group):
        pl.semaphore_signal(
            barrier, inc=1, device_id=(flip_index(me_f, k, fsdp), me_c, me_t), device_id_type=MESH_ID
        )
    for step in (-1, 1):
        along(
            step,
            lambda there: pl.semaphore_signal(
                barrier, inc=1, device_id=(me_f, there, me_t), device_id_type=MESH_ID
            ),
        )
    pl.semaphore_wait(barrier, group - 1 + line_neighbours(me_c, ctx))

    def z_copy(i, shard, step, src=None):
        place = line_out[i].at[shard]
        way = 0 if step > 0 else 1
        return pltpu.make_async_remote_copy(
            src_ref=place if src is None else src,
            dst_ref=place,
            send_sem=z_send.at[i, way, shard],
            recv_sem=z_recv.at[i, way, shard],
            device_id=(me_f, me_c + step, me_t),
            device_id_type=MESH_ID,
        )

    def landing(i, part, f):
        width = widths[part]
        return swap_out[part].at[lax.rem(f, group), :, pl.ds(i * width, width)]

    def columns(i, part, f):
        start = lax.rem(f, group) * sum(widths) + sum(widths[:part])
        return swap_in[i].at[:, pl.ds(pl.multiple_of(start, 128), widths[part])]

    def f_copy(i, part, k):
        there = flip_index(me_f, k, fsdp)
        return pltpu.make_async_remote_copy(
            src_ref=columns(i, part, there),
            dst_ref=landing(i, part, me_f),
            send_sem=f_send.at[i * parts + part, k],
            recv_sem=f_recv.at[i * parts + part, k],
            device_id=(there, me_c, me_t),
            device_id_type=MESH_ID,
        )

    def f_arrival(i, part, k):
        there = flip_index(me_f, k, fsdp)
        return pltpu.make_async_remote_copy(
            src_ref=landing(i, part, there),
            dst_ref=landing(i, part, there),
            send_sem=f_send.at[i * parts + part, k],
            recv_sem=f_recv.at[i * parts + part, k],
            device_id=(there, me_c, me_t),
            device_id_type=MESH_ID,
        )

    pieces = [(i, part) for part in range(parts) for i in range(swaps)]
    for i in range(lines):
        for step in (1, -1):
            along(step, lambda there: z_copy(i, me_c, step, line_in[i]).start())
    order = fsdp_order(group)
    for i, part in pieces:
        for k in order:
            f_copy(i, part, k).start()
    own = [
        pltpu.make_async_copy(line_in[i], line_out[i].at[me_c], own_sem.at[i])
        for i in range(lines)
    ] + [
        pltpu.make_async_copy(
            columns(i, part, me_f),
            landing(i, part, me_f),
            own_sem.at[lines + i * parts + part],
        )
        for i, part in pieces
    ]
    for copy in own:
        copy.start()
    for distance in range(1, ctx):
        for i in range(lines):
            for step in (1, -1):
                shard = me_c - step * distance

                @pl.when((shard >= 0) & (shard < ctx))
                def _():
                    z_copy(i, shard, step).wait_recv()
                    along(step, lambda there: z_copy(i, shard, step).start())

    for i, part in pieces:
        for k in order:
            f_arrival(i, part, k).wait_recv()
            f_copy(i, part, k).wait_send()
    for copy in own:
        copy.wait()
    for i in range(lines):
        for step in (1, -1):
            along(step, lambda there: z_copy(i, me_c, step, line_in[i]).wait_send())
            for distance in range(1, ctx - 1):
                shard = me_c - step * distance

                @pl.when((shard >= 0) & (shard < ctx))
                def _():
                    along(step, lambda there: z_copy(i, shard, step).wait_send())


def start_exchange(fsdp, ctx, group, lines, swaps, widths):
    parts = len(widths)
    sems = pltpu.SemaphoreType.DMA
    rows = swaps[0].shape[0]
    out_shape = [jax.ShapeDtypeStruct((ctx,) + v.shape, v.dtype) for v in lines]
    out_shape += [
        jax.ShapeDtypeStruct((group, rows, len(swaps) * w), swaps[0].dtype) for w in widths
    ]
    count = len(lines) + len(swaps)
    outs = pl.pallas_call(
        partial(line_kernel, fsdp, ctx, group, len(lines), len(swaps), tuple(widths)),
        out_shape=out_shape,
        in_specs=[pl.BlockSpec(memory_space=pltpu.VMEM)] * count,
        out_specs=[pl.BlockSpec(memory_space=pl.ANY)] * len(out_shape),
        scratch_shapes=[
            sems((len(lines) + len(swaps) * parts,)),
            sems((len(lines), 2, ctx)),
            sems((len(lines), 2, ctx)),
            sems((len(swaps) * parts, group)),
            sems((len(swaps) * parts, group)),
        ],
        compiler_params=pltpu.CompilerParams(
            collective_id=0, has_side_effects=True, vmem_limit_bytes=24 * 1024 * 1024
        ),
    )(*lines, *swaps)
    return outs[: len(lines)], outs[len(lines) :]


class TokenGather:
    def __init__(self, group, fsdp, v_ref, out_ref, own_sem, f_send, f_recv, t_send, t_recv):
        self.order = fsdp_order(group)
        self.bits = [1 << i for i in range(group.bit_length() - 1)]
        self.out_ref = out_ref
        self.sems = (f_send, f_recv, t_send, t_recv)
        self.fsdp = fsdp
        half = out_ref.shape[2]
        self.half = half
        me_t = lax.axis_index("tp")
        self.mine = v_ref.at[pl.ds(pl.multiple_of(me_t * half, half), half)]
        other = v_ref.at[pl.ds(pl.multiple_of((1 - me_t) * half, half), half)]
        self.own = [
            pltpu.make_async_copy(self.mine, out_ref.at[0, 0], own_sem.at[0]),
            pltpu.make_async_copy(other, out_ref.at[0, 1], own_sem.at[1]),
        ]

    def peer(self, k):
        me_f = lax.axis_index("fsdp")
        return (flip_index(me_f, k, self.fsdp), lax.axis_index("ctx"), lax.axis_index("tp"))

    def rows(self, k, part):
        if k == low_bit(k):
            return pl.ds(0, self.half)
        return pl.ds(part * (self.half // 2), self.half // 2)

    def f_copy(self, have, b):
        k = have | b
        part = 1 if have and b == high_bit(k) else 0
        place = self.out_ref.at[k, 0, self.rows(k, part)]
        src = self.out_ref.at[have, 0, self.rows(k, part)] if have else self.mine
        return pltpu.make_async_remote_copy(
            src_ref=src,
            dst_ref=place,
            send_sem=self.sems[0].at[k, part],
            recv_sem=self.sems[1].at[k, part],
            device_id=self.peer(b),
            device_id_type=MESH_ID,
        )

    def ways(self, have):
        return [
            b
            for b in self.bits
            if not have & b and (not have or b in (low_bit(have | b), high_bit(have | b)))
        ]

    def swap(self, k):
        me_f, me_c, me_t = self.peer(0)
        return pltpu.make_async_remote_copy(
            src_ref=self.out_ref.at[k, 0],
            dst_ref=self.out_ref.at[k, 1],
            send_sem=self.sems[2].at[k],
            recv_sem=self.sems[3].at[k],
            device_id=(me_f, me_c, 1 - me_t),
            device_id_type=MESH_ID,
        )

    def start(self):
        for b in self.ways(0):
            self.f_copy(0, b).start()
        for copy in self.own:
            copy.start()

    def relay(self, k):
        parts = [(0, k)] if k == low_bit(k) else [(0, low_bit(k)), (1, high_bit(k))]
        for part, b in parts:
            place = self.out_ref.at[k, 0, self.rows(k, part)]
            pltpu.make_async_remote_copy(
                src_ref=place,
                dst_ref=place,
                send_sem=self.sems[0].at[k, part],
                recv_sem=self.sems[1].at[k, part],
                device_id=self.peer(b),
                device_id_type=MESH_ID,
            ).wait_recv()
        for b in self.ways(k):
            self.f_copy(k, b).start()
        self.swap(k).start()

    def finish(self):
        for copy in self.own:
            copy.wait()
        for have in [0] + self.order:
            for b in self.ways(have):
                self.f_copy(have, b).wait_send()
        me_f, me_c, me_t = self.peer(0)
        for k in self.order:
            pltpu.make_async_remote_copy(
                src_ref=self.out_ref.at[k, 1],
                dst_ref=self.out_ref.at[k, 1],
                send_sem=self.sems[2].at[k],
                recv_sem=self.sems[3].at[k],
                device_id=(me_f, me_c, 1 - me_t),
                device_id_type=MESH_ID,
            ).wait_recv()
            self.swap(k).wait_send()


def token_sems(group):
    sems = pltpu.SemaphoreType.DMA
    return [sems((2,)), sems((group, 2)), sems((group, 2)), sems((group,)), sems((group,))]


def token_shape(group, v):
    return jax.ShapeDtypeStruct((group, 2, v.shape[0] // 2, v.shape[1]), v.dtype)


def tokens_kernel(group, fsdp, v_ref, out_ref, *sems):
    gather = TokenGather(group, fsdp, v_ref, out_ref, *sems)
    me_f, me_c, me_t = gather.peer(0)
    barrier = pltpu.get_barrier_semaphore()
    for b in gather.bits:
        pl.semaphore_signal(barrier, inc=1, device_id=gather.peer(b), device_id_type=MESH_ID)
    pl.semaphore_signal(
        barrier, inc=1, device_id=(me_f, me_c, 1 - me_t), device_id_type=MESH_ID
    )
    pl.semaphore_wait(barrier, len(gather.bits) + 1)
    gather.start()
    for k in gather.order:
        gather.relay(k)
    gather.finish()


def gather_tokens(group, fsdp, v):
    out = pl.pallas_call(
        partial(tokens_kernel, group, fsdp),
        out_shape=token_shape(group, v),
        in_specs=[pl.BlockSpec(memory_space=pltpu.VMEM)],
        out_specs=pl.BlockSpec(memory_space=pl.ANY),
        scratch_shapes=token_sems(group),
        compiler_params=pltpu.CompilerParams(
            collective_id=5, has_side_effects=True, vmem_limit_bytes=24 * 1024 * 1024
        ),
    )(v)
    return out.reshape(-1, v.shape[1])


def swiglu_parts(n_ref, g_ref, w_ref, hidden_ref, grads_ref):
    units = hidden_ref.shape[1]
    both = w_ref[:, : 2 * units]
    down = w_ref[:, 2 * units :]
    lin = mul(n_ref[...], both)
    gate, up = lin[:, :units], lin[:, units:]
    sig = jax.nn.sigmoid(gate)
    act = gate * sig
    hidden = (act * up).astype(jnp.bfloat16)
    hidden_ref[...] = hidden
    hidden_grad = mul(g_ref[...], down)
    grads_ref[:, :units] = (hidden_grad * up * sig * (1.0 + gate * (1.0 - sig))).astype(
        jnp.bfloat16
    )
    grads_ref[:, units:] = (hidden_grad * act).astype(jnp.bfloat16)
    return mul(grads_ref[...], both, NT), mul(hidden, down, NT)


def swiglu_first_kernel(n_ref, g_ref, w_ref, hidden_ref, grads_ref, second_ref, ff_ref):
    second, ff = swiglu_parts(n_ref, g_ref, w_ref, hidden_ref, grads_ref)
    second_ref[...] = second.astype(jnp.bfloat16)
    ff_ref[...] = ff.astype(jnp.bfloat16)


def swiglu_kernel(
    fsdp,
    group,
    n_ref,
    g_ref,
    w_ref,
    second_ref,
    ff_first_ref,
    left_ref,
    right_ref,
    hidden_ref,
    grads_ref,
    ff_ref,
    own_ref,
    product_ref,
    s_out,
    f_out,
    s_in,
    f_in,
    total,
    got,
    t_send,
    t_recv,
    f_send,
    f_recv,
    own_sem,
    left,
    right,
    product,
    inner_sem,
):
    half = n_ref.shape[0]
    step = pl.program_id(0)
    me_f = lax.axis_index("fsdp")
    me_c = lax.axis_index("ctx")
    me_t = lax.axis_index("tp")
    bits = [1 << i for i in range(group.bit_length() - 1)]
    order = fsdp_order(group)
    core = (me_f, me_c, 1 - me_t)

    def peer(k):
        return (flip_index(me_f, k, fsdp), me_c, me_t)

    @pl.when(step == 0)
    def _():
        barrier = pltpu.get_barrier_semaphore()
        for b in bits:
            pl.semaphore_signal(barrier, inc=1, device_id=peer(b), device_id_type=MESH_ID)
        pl.semaphore_signal(barrier, inc=1, device_id=core, device_id_type=MESH_ID)
        pl.semaphore_wait(barrier, len(bits) + 1)

    inner = [
        pltpu.make_async_copy(left_ref, left, inner_sem.at[0]),
        pltpu.make_async_copy(right_ref, right, inner_sem.at[1]),
    ]

    @pl.when(step == 1)
    def _():
        for copy in inner:
            copy.start()

    def make_product():
        for copy in inner:
            copy.wait()

        def body(t, _):
            cols = pl.ds(pl.multiple_of(t * 256, 256), 256)
            product[cols, :] = mul(left[:, cols], right[...], TN).astype(product.dtype)
            return 0

        lax.fori_loop(0, left.shape[1] // 256, body, 0)
        pltpu.make_async_copy(product, product_ref, inner_sem.at[2]).start()

    def core_copies(k):
        slot = k % 2
        return [
            pltpu.make_async_remote_copy(
                src_ref=out.at[slot],
                dst_ref=into.at[slot],
                send_sem=t_send.at[which, k],
                recv_sem=t_recv.at[which, k],
                device_id=core,
                device_id_type=MESH_ID,
            )
            for which, (out, into) in enumerate(((s_out, s_in), (f_out, f_in)))
        ]

    def ways(k):
        return [(0, k)] if k == low_bit(k) else [(0, low_bit(k)), (1, high_bit(k))]

    def span(k, part):
        return pl.ds(0, half) if k == low_bit(k) else pl.ds(part * (half // 2), half // 2)

    def f_copy(k, part, b):
        return pltpu.make_async_remote_copy(
            src_ref=total.at[k, span(k, part)],
            dst_ref=got.at[k, span(k, part)],
            send_sem=f_send.at[k, part],
            recv_sem=f_recv.at[k, part],
            device_id=peer(b),
            device_id_type=MESH_ID,
        )

    def own_copy():
        return pltpu.make_async_remote_copy(
            src_ref=total.at[0],
            dst_ref=own_ref.at[me_t],
            send_sem=own_sem.at[0],
            recv_sem=own_sem.at[1],
            device_id=core,
            device_id_type=MESH_ID,
        )

    second, ff = swiglu_parts(n_ref, g_ref, w_ref, hidden_ref, grads_ref)
    second = second + second_ref[...].astype(jnp.float32)
    ff = ff + ff_first_ref[...].astype(jnp.float32)

    for k in reversed(range(group)):
        slot = k % 2

        @pl.when(step == 2 * (group - 1 - k))
        def _():
            if k + 2 < group:
                for copy in core_copies(k + 2):
                    copy.wait_send()
            s_out[slot] = second.astype(jnp.bfloat16)
            f_out[slot] = ff.astype(jnp.bfloat16)
            for copy in core_copies(k):
                copy.start()

        @pl.when(step == 2 * (group - 1 - k) + 1)
        def _():
            for copy in core_copies(k):
                copy.wait_recv()
            ff_ref[...] = (ff + f_in[slot].astype(jnp.float32)).astype(jnp.bfloat16)
            total[k] = (second + s_in[slot].astype(jnp.float32)).astype(jnp.bfloat16)
            if k == 0:
                make_product()
            for far in order:
                for part, b in ways(far):
                    if far ^ b == k:
                        f_copy(far, part, b).wait_recv()
                        rows = span(far, part)
                        total[k, rows] = (
                            total[k, rows].astype(jnp.float32)
                            + got[far, rows].astype(jnp.float32)
                        ).astype(jnp.bfloat16)
            if k:
                for part, b in ways(k):
                    f_copy(k, part, b).start()
            else:
                own_copy().start()
                local = pltpu.make_async_copy(total.at[0], own_ref.at[me_t], own_sem.at[2])
                local.start()
                local.wait()
                other = own_ref.at[1 - me_t]
                pltpu.make_async_remote_copy(
                    src_ref=other,
                    dst_ref=other,
                    send_sem=own_sem.at[0],
                    recv_sem=own_sem.at[1],
                    device_id=core,
                    device_id_type=MESH_ID,
                ).wait_recv()
                own_copy().wait_send()
                for far in order:
                    for part, b in ways(far):
                        f_copy(far, part, b).wait_send()
                for late in range(min(2, group)):
                    for copy in core_copies(late):
                        copy.wait_send()
                pltpu.make_async_copy(product, product_ref, inner_sem.at[2]).wait()


def swiglu(fsdp, group, normed, grads, weights, second, ff, hidden):
    many, width = normed.shape
    half = many // (2 * group)
    units = weights.shape[1] // 3
    low = jnp.bfloat16
    last = 2 * group - 1
    sems = pltpu.SemaphoreType.DMA
    block = (half, width)

    def rows(cols):
        return pl.BlockSpec((half, cols), lambda i: (last - i, 0))

    def whole(v):
        return pl.BlockSpec(v.shape, lambda i: (0, 0), pipeline_mode=pl.Buffered(1))

    return pl.pallas_call(
        partial(swiglu_kernel, fsdp, group),
        grid=(2 * group,),
        in_specs=[rows(width), rows(width), whole(weights), rows(width), rows(width)]
        + [pl.BlockSpec(memory_space=pl.ANY)] * 2,
        out_specs=[
            rows(units),
            rows(2 * units),
            pl.BlockSpec(block, lambda i: (group - 1 - i // 2, 0)),
            pl.BlockSpec(memory_space=pl.ANY),
            pl.BlockSpec(memory_space=pl.ANY),
        ],
        out_shape=[
            jax.ShapeDtypeStruct((many, units), low),
            jax.ShapeDtypeStruct((many, 2 * units), low),
            jax.ShapeDtypeStruct((group * half, width), low),
            jax.ShapeDtypeStruct((2,) + block, low),
            jax.ShapeDtypeStruct((width, hidden.shape[1]), low),
        ],
        scratch_shapes=[pltpu.VMEM((2,) + block, low)] * 4
        + [pltpu.VMEM((group,) + block, low)] * 2
        + [
            sems((2, group)),
            sems((2, group)),
            sems((group, 2)),
            sems((group, 2)),
            sems((3,)),
            pltpu.VMEM(grads.shape, low),
            pltpu.VMEM(hidden.shape, low),
            pltpu.VMEM((width, hidden.shape[1]), low),
            sems((3,)),
        ],
        compiler_params=pltpu.CompilerParams(
            collective_id=6, has_side_effects=True, vmem_limit_bytes=58 * 1024 * 1024
        ),
        cost_estimate=pl.CostEstimate(
            flops=12 * many * width * units, bytes_accessed=50 << 20, transcendentals=0
        ),
    )(normed, grads, weights, second, ff, grads, hidden)


def spread_kernel(fsdp, ctx, group, count, chain, *refs):
    ins = refs[:count]
    outs = refs[count + chain : 2 * count + chain]
    sems = refs[2 * (count + chain) :]
    own_sem, f_send, f_recv, c_own, c_send, c_recv = sems[:6]
    me_f = lax.axis_index("fsdp")
    me_c = lax.axis_index("ctx")
    me_t = lax.axis_index("tp")
    bits = [1 << i for i in range(fsdp.bit_length() - 1)]
    order = fsdp_order(fsdp)

    def peer(k):
        return (flip_index(me_f, k, fsdp), me_c, me_t)

    barrier = pltpu.get_barrier_semaphore()
    for b in bits:
        pl.semaphore_signal(barrier, inc=1, device_id=peer(b), device_id_type=MESH_ID)
    if chain:
        chain_in, chain_out = refs[count], refs[2 * count + chain]
        gather = TokenGather(
            group, fsdp, refs[count + 1], refs[2 * count + chain + 1], *sems[6:]
        )
        pl.semaphore_signal(
            barrier, inc=1, device_id=(me_f, me_c, 1 - me_t), device_id_type=MESH_ID
        )
        for step in (-1, 1):
            there = me_c + step

            @pl.when((there >= 0) & (there < ctx))
            def _():
                pl.semaphore_signal(
                    barrier, inc=1, device_id=(me_f, there, me_t), device_id_type=MESH_ID
                )

        pl.semaphore_wait(barrier, len(bits) + 1 + line_neighbours(me_c, ctx))
    else:
        pl.semaphore_wait(barrier, len(bits))

    def quarters(rows):
        return [pl.ds(i * (rows // 4), rows // 4) for i in range(4)]

    def climb(s):
        return [
            pltpu.make_async_remote_copy(
                src_ref=chain_out.at[s, part] if s else chain_in.at[part],
                dst_ref=chain_out.at[s + 1, part],
                send_sem=c_send.at[s, i],
                recv_sem=c_recv.at[s + 1, i],
                device_id=(me_f, me_c + 1, me_t),
                device_id_type=MESH_ID,
            )
            for i, part in enumerate(quarters(chain_in.shape[0]))
        ]

    def keep(s):
        return pltpu.make_async_copy(chain_in, chain_out.at[s], c_own.at[s])

    def send_up(s):
        @pl.when((me_c >= s) & (me_c < ctx - 1))
        def _():
            for copy in climb(s):
                copy.start()

    def take_up(s):
        @pl.when(me_c >= s)
        def _():
            for i, part in enumerate(quarters(chain_in.shape[0])):
                pltpu.make_async_remote_copy(
                    src_ref=chain_out.at[s, part],
                    dst_ref=chain_out.at[s, part],
                    send_sem=c_send.at[s - 1, i],
                    recv_sem=c_recv.at[s, i],
                    device_id=(me_f, me_c - 1, me_t),
                    device_id_type=MESH_ID,
                ).wait_recv()

        if s < ctx - 1:
            send_up(s)

    if chain:
        send_up(0)
        keep(0).start()
        for s in range(1, ctx):
            @pl.when(me_c < s)
            def _():
                keep(s).start()

    def place(i, shard, have, k, part):
        block = outs[i].at[shard, flip_index(me_f, have, fsdp)]
        half = ins[i].shape[1] // 2
        return block if k == low_bit(k) else block.at[pl.ds(part * half, half)]

    def f_copy(i, shard, have, b):
        k = have | b
        part = 1 if have and b == high_bit(k) else 0
        block = place(i, shard, have, k, part)
        return pltpu.make_async_remote_copy(
            src_ref=block if have else ins[i].at[shard],
            dst_ref=block,
            send_sem=f_send.at[i, shard, k, part],
            recv_sem=f_recv.at[i, shard, k, part],
            device_id=peer(b),
            device_id_type=MESH_ID,
        )

    def ways(have):
        return [
            b
            for b in bits
            if not have & b and (not have or b in (low_bit(have | b), high_bit(have | b)))
        ]

    own = [
        pltpu.make_async_copy(ins[i], outs[i].at[:, me_f], own_sem.at[i]) for i in range(count)
    ]
    for i in range(count):
        for shard in range(ctx):
            for b in ways(0):
                f_copy(i, shard, 0, b).start()
        own[i].start()
    if chain:
        gather.start()
    climbed = 1
    for i in range(count):
        for k in order:
            if chain and climbed < ctx:
                take_up(climbed)
                climbed += 1
            if chain and k < group and i == 0:
                gather.relay(k)
            parts = [(0, k)] if k == low_bit(k) else [(0, low_bit(k)), (1, high_bit(k))]
            for shard in range(ctx):
                for part, b in parts:
                    block = place(i, shard, k, k, part)
                    pltpu.make_async_remote_copy(
                        src_ref=block,
                        dst_ref=block,
                        send_sem=f_send.at[i, shard, k, part],
                        recv_sem=f_recv.at[i, shard, k, part],
                        device_id=peer(b),
                        device_id_type=MESH_ID,
                    ).wait_recv()
                for b in ways(k):
                    f_copy(i, shard, k, b).start()
    if chain:
        for s in range(climbed, ctx):
            take_up(s)
        gather.finish()
        keep(0).wait()
        for s in range(ctx):
            if s:

                @pl.when(me_c < s)
                def _():
                    keep(s).wait()

            if s < ctx - 1:

                @pl.when((me_c >= s) & (me_c < ctx - 1))
                def _():
                    for copy in climb(s):
                        copy.wait_send()

    for i in range(count):
        own[i].wait()
        for have in [0] + order:
            for shard in range(ctx):
                for b in ways(have):
                    f_copy(i, shard, have, b).wait_send()


def spread_weights(fsdp, ctx, group, arrays, chain=()):
    count = len(arrays)
    sems = pltpu.SemaphoreType.DMA
    outs = pl.pallas_call(
        partial(spread_kernel, fsdp, ctx, group, count, len(chain)),
        out_shape=[
            jax.ShapeDtypeStruct((ctx, fsdp) + v.shape[1:], v.dtype) for v in arrays
        ]
        + [jax.ShapeDtypeStruct((ctx,) + v.shape, v.dtype) for v in chain[:1]]
        + [token_shape(group, v) for v in chain[1:]],
        in_specs=[pl.BlockSpec(memory_space=pltpu.VMEM)] * (count + len(chain)),
        out_specs=[pl.BlockSpec(memory_space=pl.ANY)] * (count + len(chain)),
        scratch_shapes=[
            sems((count,)),
            sems((count, ctx, fsdp, 2)),
            sems((count, ctx, fsdp, 2)),
            sems((ctx,)),
            sems((ctx, 4)),
            sems((ctx, 4)),
        ]
        + (token_sems(group) if chain else []),
        compiler_params=pltpu.CompilerParams(
            collective_id=3 if chain else 1,
            has_side_effects=True,
            vmem_limit_bytes=24 * 1024 * 1024,
        ),
    )(*arrays, *chain)
    return (
        [o.reshape(-1, v.shape[-1]) for o, v in zip(outs, arrays)]
        + list(outs[count : count + 1])
        + [o.reshape(-1, o.shape[-1]) for o in outs[count + 1 :]]
    )


def sum_kernel(fsdp, ctx, count, chain, products, *refs):
    inner = []
    if products:
        first = count + 3
        pairs = refs[first : first + 2 * products]
        place = first + 2 * products + count + 1
        results = refs[place : place + products]
        inner = refs[-2 * products - 1 :]
        refs = refs[:first] + refs[first + 2 * products : place] + refs[place + products :]
        refs = refs[: -2 * products - 1]
    ins = refs[:count]
    if chain:
        parts_ref, cos_ref, sin_ref = refs[count : count + 3]
        refs = refs[:count] + refs[count + 3 :]
        kv_ref = refs[2 * count]
        refs = refs[: 2 * count] + refs[2 * count + 1 :]
    outs = refs[count : 2 * count]
    held = refs[2 * count : 3 * count]
    got = refs[3 * count : 4 * count]
    line = refs[4 * count : 5 * count]
    refs = refs[5 * count :]
    in_sem, f_send, f_recv, z_send, z_recv = refs[:5]
    if chain:
        kv_parts, kv_got, kv_sem, c_send, c_recv = refs[5:]
    me_f = lax.axis_index("fsdp")
    me_c = lax.axis_index("ctx")
    me_t = lax.axis_index("tp")
    bits = [1 << i for i in range(fsdp.bit_length() - 1)]
    order = fsdp_order(fsdp)

    def peer(k):
        return (flip_index(me_f, k, fsdp), me_c, me_t)

    def along(step, act):
        there = me_c + step

        @pl.when((there >= 0) & (there < ctx))
        def _():
            act(there)

    loads = {}
    if chain:
        kv_load = pltpu.make_async_copy(parts_ref, kv_parts, kv_sem.at[0])
        kv_load.start()
    inner_loads = [
        pltpu.make_async_copy(pairs[i], inner[i], inner[-1].at[i]) for i in range(2 * products)
    ]
    for i in range(count):
        for k in reversed([0] + order):
            block = ins[i].at[:, flip_index(me_f, k, fsdp)]
            loads[i, k] = pltpu.make_async_copy(block, held[i].at[k], in_sem.at[i, k])
            loads[i, k].start()

    barrier = pltpu.get_barrier_semaphore()
    for b in bits:
        pl.semaphore_signal(barrier, inc=1, device_id=peer(b), device_id_type=MESH_ID)
    for step in (-1, 1):
        along(
            step,
            lambda there: pl.semaphore_signal(
                barrier, inc=1, device_id=(me_f, there, me_t), device_id_type=MESH_ID
            ),
        )
    pl.semaphore_wait(barrier, len(bits) + line_neighbours(me_c, ctx))

    def ways(k):
        return [(0, k)] if k == low_bit(k) else [(0, low_bit(k)), (1, high_bit(k))]

    def piece(i, k, part):
        rows = ins[i].shape[2]
        return pl.ds(0, rows) if k == low_bit(k) else pl.ds(part * (rows // 2), rows // 2)

    def f_copy(i, shard, k, part, b):
        span = piece(i, k, part)
        return pltpu.make_async_remote_copy(
            src_ref=held[i].at[k, shard, span],
            dst_ref=got[i].at[k, shard, span],
            send_sem=f_send.at[i, shard, k, part],
            recv_sem=f_recv.at[i, shard, k, part],
            device_id=peer(b),
            device_id_type=MESH_ID,
        )

    def add(into, other):
        tile = 16 if into.dtype == jnp.bfloat16 else 8

        def body(r, _):
            span = pl.ds(pl.multiple_of(r * tile, tile), tile)
            into[span] = (
                into[span].astype(jnp.float32) + other[span].astype(jnp.float32)
            ).astype(into.dtype)
            return 0

        lax.fori_loop(0, into.shape[0] // tile, body, 0)

    def collect(i, shard, k):
        for far in order:
            for part, b in ways(far):
                if far ^ b == k:
                    f_copy(i, shard, far, part, b).wait_recv()
                    span = piece(i, far, part)
                    add(held[i].at[k, shard, span], got[i].at[far, shard, span])

    def z_copy(i, shard, step):
        way = 0 if step > 0 else 1
        return pltpu.make_async_remote_copy(
            src_ref=held[i].at[0, shard],
            dst_ref=line[i].at[way, shard],
            send_sem=z_send.at[i, way, shard],
            recv_sem=z_recv.at[i, way, shard],
            device_id=(me_f, me_c + step, me_t),
            device_id_type=MESH_ID,
        )

    def give(i, shard):
        def body(r, _):
            span = pl.ds(pl.multiple_of(r * 16, 16), 16)
            outs[i][span] = held[i][0, shard, span].astype(outs[i].dtype)
            return 0

        lax.fori_loop(0, outs[i].shape[0] // 16, body, 0)

    def on_line(i, shard, step):
        way = 0 if step > 0 else 1

        @pl.when((me_c - step >= 0) & (me_c - step < ctx))
        def _():
            z_copy(i, shard, step).wait_recv()
            add(held[i].at[0, shard], line[i].at[way, shard])

        @pl.when(step * (shard - me_c) > 0)
        def _():
            z_copy(i, shard, step).start()

    def quarters():
        rows = kv_parts.shape[2] // 2
        return [(side, pl.ds(i * rows, rows)) for side in range(2) for i in range(2)]

    def descend(s):
        return [
            pltpu.make_async_remote_copy(
                src_ref=kv_parts.at[s, side, part],
                dst_ref=kv_got.at[s - 1, side, part],
                send_sem=c_send.at[s, i],
                recv_sem=c_recv.at[s - 1, i],
                device_id=(me_f, me_c - 1, me_t),
                device_id_type=MESH_ID,
            )
            for i, (side, part) in enumerate(quarters())
        ]

    def chain_step(s):
        if s < ctx - 1:

            @pl.when((me_c >= s) & (me_c < ctx - 1))
            def _():
                for i, (side, part) in enumerate(quarters()):
                    pltpu.make_async_remote_copy(
                        src_ref=kv_got.at[s, side, part],
                        dst_ref=kv_got.at[s, side, part],
                        send_sem=c_send.at[s + 1, i],
                        recv_sem=c_recv.at[s, i],
                        device_id=(me_f, me_c + 1, me_t),
                        device_id_type=MESH_ID,
                    ).wait_recv()
                    add(kv_parts.at[s, side, part], kv_got.at[s, side, part])

        if s:

            @pl.when(me_c >= s)
            def _():
                for copy in descend(s):
                    copy.start()

    def chain_result():
        width = kv_parts.shape[3]
        rows = cos_ref.shape[0]
        for seq in range(kv_parts.shape[2] // rows):
            span = pl.ds(seq * rows, rows)
            for start in range(0, width, 128):
                cols = slice(start, start + 128)
                t = kv_parts[0, 0, span, cols].astype(jnp.float32)
                t = t * cos_ref[...] + turn(t * sin_ref[...], -1.0)
                kv_ref[span, cols] = t.astype(kv_ref.dtype)
            kv_ref[span, width:] = kv_parts[0, 1, span]

    steps = list(reversed(range(ctx))) if chain else []

    def next_step():
        if steps:
            s = steps.pop(0)
            chain_step(s)
            if s == 0:
                chain_result()

    turns = 4

    def make_products(turn):
        if turn == 0:
            for load in inner_loads:
                load.wait()
        for i in range(products):
            left, right, result = inner[2 * i], inner[2 * i + 1], results[i]
            tiles = left.shape[1] // 256
            per = -(-tiles // turns)

            def body(t, _):
                cols = pl.ds(pl.multiple_of(t * 256, 256), 256)
                result[cols, :] = mul(left[:, cols], right[...], TN).astype(result.dtype)
                return 0

            lax.fori_loop(min(turn * per, tiles), min((turn + 1) * per, tiles), body, 0)

    if chain:
        kv_load.wait()
        next_step()
    for load in inner_loads:
        load.start()
    shards = sorted(range(ctx), key=lambda c: -abs(2 * c - ctx + 1))
    work = [[(i, shard) for i in range(count)] for shard in shards]
    levels = sorted({bin(k).count("1") for k in order}, reverse=True)
    waited = set()

    def loaded(i, k):
        if (i, k) not in waited:
            waited.add((i, k))
            loads[i, k].wait()

    def advance(stage, item):
        for i, shard in item:
            if stage == len(levels):
                loaded(i, 0)
                collect(i, shard, 0)
                continue
            for k in order:
                if bin(k).count("1") == levels[stage]:
                    loaded(i, k)
                    collect(i, shard, k)
                    for part, b in ways(k):
                        f_copy(i, shard, k, part, b).start()

    def line_tick(item, hops):
        for i, shard in item:
            for step, there in ((1, hops), (-1, ctx - 1 - hops)):
                if step * (shard - there) >= 0:

                    @pl.when(me_c == there)
                    def _():
                        on_line(i, shard, step)

            if hops == max(shard, ctx - 1 - shard):

                @pl.when(me_c == shard)
                def _():
                    give(i, shard)

    stages = len(levels) + 1
    for tick in range(len(work) + stages + ctx - 2):
        for stage in range(stages):
            if 0 <= tick - stage < len(work):
                advance(stage, work[tick - stage])
        for hops in range(ctx):
            place = tick - stages + 1 - hops
            if 0 <= place < len(work):
                line_tick(work[place], hops)
        if products and tick < turns:
            make_products(tick)
        next_step()
    while steps:
        next_step()
    for i, shard in [pair for item in work for pair in item]:
        for k in order:
            for part, b in ways(k):
                f_copy(i, shard, k, part, b).wait_send()
        for step in (1, -1):

            @pl.when(step * (shard - me_c) > 0)
            def _():
                z_copy(i, shard, step).wait_send()

    if chain:
        for s in range(1, ctx):

            @pl.when(me_c >= s)
            def _():
                for copy in descend(s):
                    copy.wait_send()


def sum_weights(fsdp, ctx, arrays, chain=(), products=()):
    sems = pltpu.SemaphoreType.DMA
    vmem = pltpu.VMEM
    shards = [v.reshape(ctx, fsdp, -1, v.shape[-1]) for v in arrays]
    blocks = [(fsdp, ctx) + v.shape[2:] for v in shards]
    out_shape = [jax.ShapeDtypeStruct(v.shape[2:], jnp.float32) for v in shards]
    lines = [vmem((2,) + b[1:], v.dtype) for b, v in zip(blocks, shards)]
    extra = []
    if chain:
        parts = chain[0]
        out_shape.append(jax.ShapeDtypeStruct((parts.shape[2], 2 * parts.shape[3]), parts.dtype))
        extra = [
            vmem(parts.shape, parts.dtype),
            vmem((ctx - 1,) + parts.shape[1:], parts.dtype),
            sems((1,)),
            sems((ctx, 4)),
            sems((ctx, 4)),
        ]
    count = len(shards)
    flat = [v for pair in products for v in pair]
    for left, right in products:
        out_shape.append(jax.ShapeDtypeStruct((left.shape[1], right.shape[1]), left.dtype))
    if products:
        extra = extra + [vmem(v.shape, v.dtype) for v in flat] + [sems((len(flat),))]
    held = [vmem(b, v.dtype) for b, v in zip(blocks, shards)]
    return pl.pallas_call(
        partial(sum_kernel, fsdp, ctx, count, bool(chain), len(products)),
        out_shape=out_shape,
        in_specs=[pl.BlockSpec(memory_space=pl.ANY)] * (count + len(chain[:1]))
        + [pl.BlockSpec(memory_space=pltpu.VMEM)] * len(chain[1:])
        + [pl.BlockSpec(memory_space=pl.ANY)] * len(flat),
        out_specs=[pl.BlockSpec(memory_space=pltpu.VMEM)] * len(out_shape),
        scratch_shapes=held
        + held
        + lines
        + [
            sems((count, fsdp)),
            sems((count, ctx, fsdp, 2)),
            sems((count, ctx, fsdp, 2)),
            sems((count, 2, ctx)),
            sems((count, 2, ctx)),
        ]
        + extra,
        compiler_params=pltpu.CompilerParams(
            collective_id=4 if chain else 2,
            has_side_effects=True,
            vmem_limit_bytes=58 * 1024 * 1024,
        ),
    )(*shards, *chain, *flat)


def heads_kernel(group_size, qkv_ref, out_ref, *outs):
    width = outs[0].shape[1]
    for source, target in ((qkv_ref, outs[0]), (out_ref, outs[3])):
        for block in range(width // 128):
            pair, rest = divmod(2 * block, 2 * group_size)
            g, j = divmod(rest, group_size)
            start = (pair * group_size + j) * 128
            left = source[:, start : start + 128]
            right = source[:, start + 128 : start + 256]
            if g:
                left = pltpu.roll(left, HD, 1)
            else:
                right = pltpu.roll(right, HD, 1)
            lane = lax.broadcasted_iota(jnp.int32, left.shape, 1)
            target[:, block * 128 : (block + 1) * 128] = jnp.where(lane < HD, left, right)
    kv_width = outs[1].shape[1]
    outs[1][...] = qkv_ref[:, width : width + kv_width]
    outs[2][...] = qkv_ref[:, width + kv_width :]


def plain_grads(group_size, qkv, out, kv_width):
    rows, width = out.shape
    vmem = pl.BlockSpec(memory_space=pltpu.VMEM)
    return pl.pallas_call(
        partial(heads_kernel, group_size),
        out_shape=[
            jax.ShapeDtypeStruct((rows, w), out.dtype) for w in (width, kv_width, kv_width, width)
        ],
        in_specs=[vmem] * 2,
        out_specs=[vmem] * 4,
        cost_estimate=pl.CostEstimate(flops=0, bytes_accessed=4 << 20, transcendentals=0),
    )(qkv, out)


def place_kernel(group, count, *refs):
    parts, outs = refs[:count], refs[count:]
    span = sum(v.shape[3] for v in parts)
    for i, out in enumerate(outs):
        for f in range(group):
            start = f * span
            for v in parts:
                width = v.shape[3]
                out[:, start : start + width] = v[f, i].astype(out.dtype)
                start += width


def place_units(parts):
    group, arrays, rows, _ = parts[0].shape
    cols = group * sum(v.shape[3] for v in parts)
    vmem = pl.BlockSpec(memory_space=pltpu.VMEM)
    return pl.pallas_call(
        partial(place_kernel, group, len(parts)),
        out_shape=[jax.ShapeDtypeStruct((rows, cols), jnp.float32)] * arrays,
        in_specs=[vmem] * len(parts),
        out_specs=[vmem] * arrays,
        compiler_params=pltpu.CompilerParams(vmem_limit_bytes=24 * 1024 * 1024),
        cost_estimate=pl.CostEstimate(
            flops=0, bytes_accessed=6 * rows * cols * arrays, transcendentals=0
        ),
    )(*parts)


def local(
    inputs,
    lengths,
    cotangent,
    norm1_gain,
    w_query,
    w_key,
    w_value,
    w_out,
    norm2_gain,
    w_gate,
    w_up,
    w_down,
):
    seq_count, local_rows, model_width = inputs.shape
    tokens = seq_count * local_rows
    half = tokens // 2
    fsdp = lax.axis_size("fsdp")
    ctx = lax.axis_size("ctx")
    shard = w_query.shape[0]
    query_width = w_query.shape[1]
    kv_width = w_key.shape[1]
    kv_end = query_width + 2 * kv_width
    pairs = kv_width // (2 * HD)
    group_size = query_width // kv_width
    group = min(fsdp, 4)
    far = fsdp // group
    own = w_gate.shape[1] // group
    first_units = own * FIRST_EIGHTHS // 8
    widths = (first_units, own - first_units)
    me_c = lax.axis_index("ctx")
    me_t = lax.axis_index("tp")
    low = jnp.bfloat16
    wide = jnp.float32

    def swap(v):
        return lax.ppermute(v, "tp", [(0, 1), (1, 0)])

    inside = shard % 128 == 0
    dims = (fsdp, ctx, shard)
    back_dims = (ctx, fsdp, shard)

    def by_ctx(v):
        if inside:
            return v
        rows = v.shape[0]
        return v.reshape(rows, fsdp, ctx, shard).swapaxes(1, 2).reshape(rows, model_width)

    def by_fsdp(v):
        if inside:
            return v
        rows = v.shape[0]
        return v.reshape(rows, ctx, fsdp, shard).swapaxes(1, 2).reshape(rows, model_width)

    def pair_heads(v):
        rows = v.shape[0]
        return (
            v.reshape(rows, pairs, 2, group_size, HD).swapaxes(2, 3).reshape(rows, query_width)
        )

    x = by_ctx(inputs.reshape(tokens, model_width))
    cot = by_ctx(cotangent.reshape(tokens, model_width))
    positions = me_c * local_rows + jnp.arange(local_rows, dtype=jnp.int32)
    cosines, sines = rope_tables(positions, HD)
    cosines, sines = jnp.tile(cosines, (1, 2)), jnp.tile(sines, (1, 2))

    gains = jnp.pad(jnp.stack([norm1_gain, norm2_gain]).astype(wide), ((0, 14), (0, 0)))
    lined, held = start_exchange(
        fsdp,
        ctx,
        group,
        [
            jnp.concatenate([pair_heads(w_query), w_key, w_value], 1),
            gains,
            pair_heads(w_out),
        ],
        [w_gate, w_up, w_down],
        widths,
    )
    far_groups = [[h * group + g for h in range(far)] for g in range(group)]
    near_groups = [[h * group + g for g in range(group)] for h in range(far)]

    def whole_width(v):
        if far > 1:
            v = lax.all_gather(v, "fsdp", axis=0, tiled=False, axis_index_groups=far_groups)
        return lax.all_gather(v, "ctx", axis=0, tiled=False).reshape(model_width, -1)

    first_full = whole_width(held[0])
    qkv_full, gain_rows = spread_weights(fsdp, ctx, group, lined[:2])
    gain_rows = gain_rows.reshape(ctx * fsdp, 16, shard)
    gain_one = gain_rows[:, 0].reshape(1, model_width)
    gain_two = gain_rows[:, 1].reshape(1, model_width)

    (ff_grad,) = by_rows(
        partial(cot_kernel, dims, local_rows),
        128,
        [(lengths, "smem"), (cot, "rows")],
        [((tokens, model_width), low)],
    )
    first_normed, query, kv_own = by_rows(
        partial(qkv_kernel, dims),
        128,
        [
            (x, "rows"),
            (qkv_full, "whole"),
            (gain_one, "whole"),
            (cosines, "cycle"),
            (sines, "cycle"),
        ],
        [
            ((tokens, model_width), low),
            ((tokens, query_width), low),
            ((tokens, 2 * kv_width), low),
        ],
        flops=2 * tokens * model_width * kv_end,
    )
    out_full, kv_all, ff_grad_all = spread_weights(
        fsdp, ctx, group, lined[2:], (kv_own, ff_grad)
    )
    late_held, kv_all = lax.optimization_barrier((held[1], kv_all))
    late_full = whole_width(late_held)
    attended, lse = attend(lengths, query, kv_all)
    attn_part = jnp.einsum(
        "tj,dj->td", attended, out_full, preferred_element_type=wide
    ).astype(low)
    middle, second_normed = by_rows(
        partial(middle_kernel, dims),
        128,
        [(x, "rows"), (attn_part, "rows"), (swap(attn_part), "rows"), (gain_two, "whole")],
        [((tokens, model_width), wide), ((tokens, model_width), low)],
    )
    normed_all = gather_tokens(group, fsdp, second_normed)

    def unit_term(left, right):
        return jnp.einsum("td,tf->df", left, right, preferred_element_type=wide).astype(low)

    def own_units(term):
        width = term.shape[1]
        own = lax.psum_scatter(
            term.reshape(ctx, fsdp, shard, width), "ctx", scatter_dimension=0, tiled=False
        )
        if far > 1:
            own = lax.psum_scatter(
                own.reshape(far, group, shard, width),
                "fsdp",
                scatter_dimension=0,
                tiled=False,
                axis_index_groups=far_groups,
            )
        return own

    def return_units(both, down):
        units = down.shape[-1]
        pieces = jnp.concatenate([both[..., :units], both[..., units:], down], 1)
        back = lax.all_to_all(
            pieces.reshape(group * 3 * shard, units),
            "fsdp",
            0,
            0,
            tiled=True,
            axis_index_groups=near_groups if far > 1 else None,
        )
        return back.reshape(group, 3, shard, units)

    many = group * tokens
    first_hidden, first_grads, second_part, ff_part = by_rows(
        swiglu_first_kernel,
        256,
        [(normed_all, "rows"), (ff_grad_all, "rows"), (first_full, "whole")],
        [
            ((many, first_units), low),
            ((many, 2 * first_units), low),
            ((many, model_width), low),
            ((many, model_width), low),
        ],
        flops=12 * many * model_width * first_units,
        limit=56,
    )
    first_both = unit_term(normed_all, first_grads)
    second_part, ff_part, _ = lax.optimization_barrier((second_part, ff_part, first_both))
    hidden, both_grad, ff_sums, second_grad, first_down = swiglu(
        fsdp,
        group,
        normed_all,
        ff_grad_all,
        late_full,
        second_part,
        ff_part,
        first_hidden,
    )
    first_own = (own_units(first_both), own_units(first_down))
    second_grad = second_grad.reshape(tokens, model_width)

    middle_grad, attn_grad, gain_two_term = by_rows(
        partial(middle_back_kernel, dims, local_rows),
        128,
        [
            (lengths, "smem"),
            (cot, "rows"),
            (middle, "rows"),
            (second_grad, "rows"),
            (gain_two, "whole"),
        ],
        [((tokens, model_width), wide), ((tokens, model_width), low), ((1, model_width), wide)],
    )
    attended_grad = jnp.dot(attn_grad, out_full, preferred_element_type=wide).astype(low)
    query_grad, kv_parts, ff_branch = attend_back(
        fsdp,
        group,
        lengths,
        query,
        attended_grad,
        lse,
        cosines,
        sines,
        kv_all,
        ff_sums.reshape(group, half, model_width),
    )
    out_term = jnp.einsum("td,tj->dj", attn_grad, attended, preferred_element_type=wide)
    w_out_grad, kv_grad, late_both, late_down = sum_weights(
        fsdp,
        ctx,
        [out_term.astype(low)],
        (kv_parts, cosines, sines),
        ((normed_all, both_grad), (ff_grad_all, hidden)),
    )
    late_both_own = own_units(late_both)
    late_down_own = own_units(late_down)
    (output,) = by_rows(
        partial(output_kernel, back_dims, local_rows),
        128,
        [(lengths, "smem"), (middle, "rows"), (ff_branch.reshape(tokens, model_width), "rows")],
        [((tokens, model_width), low)],
    )
    qkv_grad = jnp.concatenate([query_grad, kv_grad], -1)
    qkv_term = jnp.einsum("td,tj->dj", first_normed, qkv_grad, preferred_element_type=wide)
    first_part = jnp.einsum(
        "tj,dj->td", qkv_grad, qkv_full, preferred_element_type=wide
    ).astype(low)
    input_grad, gain_one_term = by_rows(
        partial(input_back_kernel, dims),
        128,
        [
            (x, "rows"),
            (first_part, "rows"),
            (swap(first_part), "rows"),
            (middle_grad, "rows"),
            (gain_one, "whole"),
        ],
        [((tokens, model_width), low), ((1, model_width), wide)],
    )
    gain_terms = jnp.stack(
        [gain_one_term.reshape(-1, shard), gain_two_term.reshape(-1, shard)], 1
    )
    gain_terms = jnp.pad(gain_terms, ((0, 0), (0, 14), (0, 0))).reshape(-1, shard)
    first_back = return_units(*first_own)
    qkv_term, first_back, _ = lax.optimization_barrier(
        (qkv_term.astype(low), first_back, late_both)
    )
    qkv_own, gain_own = sum_weights(fsdp, ctx, [qkv_term, gain_terms])
    w_query_grad, w_key_grad, w_value_grad, w_out_grad = plain_grads(
        group_size, qkv_own, w_out_grad, kv_width
    )
    late_both_own, late_down_own, qkv_own = lax.optimization_barrier(
        (late_both_own, late_down_own, qkv_own)
    )
    late_back = return_units(late_both_own, late_down_own)
    w_gate_grad, w_up_grad, w_down_grad = place_units([first_back, late_back])
    return (
        by_fsdp(output).reshape(inputs.shape),
        by_fsdp(input_grad).reshape(inputs.shape),
        gain_own[0],
        w_query_grad,
        w_key_grad,
        w_value_grad,
        w_out_grad,
        gain_own[1],
        w_gate_grad,
        w_up_grad,
        w_down_grad,
    )


def solution(mesh):
    placed = (
        P("fsdp", "ctx", None),
        P("fsdp"),
        P("fsdp", "ctx", None),
        P(("fsdp", "ctx")),
        P(("fsdp", "ctx"), "tp"),
        P(("fsdp", "ctx"), "tp"),
        P(("fsdp", "ctx"), "tp"),
        P(("fsdp", "ctx"), "tp"),
        P(("fsdp", "ctx")),
        P(("fsdp", "ctx"), "tp"),
        P(("fsdp", "ctx"), "tp"),
        P(("fsdp", "ctx"), "tp"),
    )
    return jax.shard_map(
        local,
        mesh=mesh,
        in_specs=placed,
        out_specs=(
            P("fsdp", "ctx", None),
            P("fsdp", "ctx", None),
            P(("fsdp", "ctx")),
            P(("fsdp", "ctx"), "tp"),
            P(("fsdp", "ctx"), "tp"),
            P(("fsdp", "ctx"), "tp"),
            P(("fsdp", "ctx"), "tp"),
            P(("fsdp", "ctx")),
            P(("fsdp", "ctx"), "tp"),
            P(("fsdp", "ctx"), "tp"),
            P(("fsdp", "ctx"), "tp"),
        ),
        check_vma=False,
    )
```

```python
from functools import partial

import jax
import jax.numpy as jnp
from jax import lax
from jax.experimental import pallas as pl
from jax.experimental.pallas import tpu as pltpu
from jax.sharding import PartitionSpec as P

HD = 64


norm_eps = 1e-05
residual_scale = 0.22
score_scale = 1.0 / 64.0
rope_base = 10000000.0
masked_score = -1e30


def rope_tables(positions, head_dim):
    half_dim = head_dim // 2
    frequency = rope_base ** (-(jnp.arange(half_dim, dtype=jnp.float32) * 2.0) / head_dim)
    angles = positions.astype(jnp.float32)[:, None] * frequency[None, :]
    return (
        jnp.concatenate([jnp.cos(angles), jnp.cos(angles)], -1),
        jnp.concatenate([jnp.sin(angles), jnp.sin(angles)], -1),
    )


def rotate(values_in, cosines, sines):
    half_dim = values_in.shape[-1] // 2
    turned = jnp.concatenate([-values_in[..., half_dim:], values_in[..., :half_dim]], -1)
    return values_in * cosines + turned * sines


def unrotate(grad_in, cosines, sines):
    half_dim = grad_in.shape[-1] // 2
    scaled = grad_in * sines
    return grad_in * cosines + jnp.concatenate(
        [scaled[..., half_dim:], -scaled[..., :half_dim]], -1
    )


def rms_scale(values_in):
    return lax.rsqrt(jnp.mean(values_in * values_in, -1, keepdims=True) + norm_eps)


def norm_back(grad_normed, values_in, scale, gain):
    scaled_grad = grad_normed * gain
    return scale * scaled_grad - values_in * scale**3 * jnp.mean(
        scaled_grad * values_in, -1, keepdims=True
    )


MESH_ID = pl.DeviceIdType.MESH
FIRST_EIGHTHS = 4
NT = (((1,), (1,)), ((), ()))
TN = (((0,), (0,)), ((), ()))
SMEM = pltpu.SMEM


def mul(left, right, dims=(((1,), (0,)), ((), ()))):
    return lax.dot_general(left, right, dims, preferred_element_type=jnp.float32)


def reorder(v, first, second, width):
    if width % 128:
        return v
    pieces = []
    for b in range(second):
        for a in range(first):
            start = (a * second + b) * width
            pieces.append(v[:, start : start + width])
    return jnp.concatenate(pieces, 1)


def turn(t, sign):
    lane = lax.broadcasted_iota(jnp.int32, t.shape, 1)
    ahead = pltpu.roll(t, 128 - HD // 2, 1)
    behind = pltpu.roll(t, HD // 2, 1)
    return jnp.where(lax.rem(lane, HD) < HD // 2, -sign * ahead, sign * behind)


def row_valid(len_ref, rows, local_rows):
    step = pl.program_id(0)
    start = step * rows
    seq = start // local_rows
    place = (
        lax.axis_index("ctx") * local_rows
        + lax.rem(start, local_rows)
        + lax.broadcasted_iota(jnp.int32, (rows, 1), 0)
    )
    return (place < len_ref[seq]).astype(jnp.float32)


def qkv_kernel(dims, x_ref, w_ref, gain_ref, cos_ref, sin_ref, normed_ref, q_ref, kv_ref):
    x = reorder(x_ref[...].astype(jnp.float32), *dims)
    normed = (x * rms_scale(x) * gain_ref[...]).astype(jnp.bfloat16)
    normed_ref[...] = normed
    lin = mul(normed, w_ref[...])
    cosines, sines = cos_ref[...], sin_ref[...]
    width = q_ref.shape[1]
    half = kv_ref.shape[1] // 2
    for start in range(0, width + half, 128):
        t = lin[:, start : start + 128]
        t = (t * cosines + turn(t, 1.0) * sines).astype(jnp.bfloat16)
        if start < width:
            q_ref[:, start : start + 128] = t
        else:
            kv_ref[:, start - width : start - width + 128] = t
    kv_ref[:, half:] = lin[:, width + half :].astype(jnp.bfloat16)


def key_biases(len_ref, rows, ctx):
    length = len_ref[pl.program_id(0)]
    me = lax.axis_index("ctx")
    row = lax.broadcasted_iota(jnp.int32, (rows, rows), 0)
    col = lax.broadcasted_iota(jnp.int32, (rows, rows), 1)
    first = jnp.where((col <= row) & (me * rows + col < length), 0.0, masked_score)
    out = [first]
    for s in range(1, ctx):
        place = (me - s) * rows + lax.broadcasted_iota(jnp.int32, (1, rows), 1)
        out.append(jnp.where((place >= 0) & (place < length), 0.0, masked_score))
    return out


def attend_kernel(ctx, len_ref, q_ref, *refs):
    keys, values = refs[:ctx], refs[ctx : 2 * ctx]
    o_ref, lse_ref = refs[2 * ctx :]
    rows = q_ref.shape[0]
    biases = key_biases(len_ref, rows, ctx)
    lane = lax.broadcasted_iota(jnp.int32, (rows, 128), 1)
    lse_all = jnp.zeros((rows, 128), jnp.float32)
    for j in range(q_ref.shape[1] // 128):
        q_pair = q_ref[:, j * 128 : (j + 1) * 128] * jnp.bfloat16(score_scale)
        outs = []
        for g in range(2):
            mine = (lane < HD) if g == 0 else (lane >= HD)
            q_head = jnp.where(mine, q_pair, jnp.zeros_like(q_pair))
            scores = [mul(q_head, k[...], NT) + b for k, b in zip(keys, biases)]
            top = scores[0].max(-1, keepdims=True)
            for s in scores[1:]:
                top = jnp.maximum(top, s.max(-1, keepdims=True))
            mass, out = 0.0, 0.0
            for s, v in zip(scores, values):
                p = jnp.exp(s - top)
                mass = mass + p.sum(-1, keepdims=True)
                out = out + mul(p.astype(jnp.bfloat16), v[...])
            outs.append(out / mass)
            lse_all = jnp.where(lane == 2 * j + g, top + jnp.log(mass), lse_all)
        o_ref[:, j * 128 : (j + 1) * 128] = jnp.where(lane < HD, outs[0], outs[1]).astype(
            jnp.bfloat16
        )
    lse_ref[...] = lse_all


class RowSum:
    def __init__(
        self, group, fsdp, rows_ref, own_ref, held, got, in_sem, f_send, f_recv, own_sem
    ):
        self.group, self.fsdp = group, fsdp
        self.order = fsdp_order(group)
        self.bits = [1 << i for i in range(group.bit_length() - 1)]
        self.own_ref, self.held, self.got = own_ref, held, got
        self.f_send, self.f_recv, self.own_sem = f_send, f_recv, own_sem
        self.half = rows_ref.shape[1]
        self.loads = [
            pltpu.make_async_copy(rows_ref.at[k], held.at[k], in_sem.at[k]) for k in range(group)
        ]

    def peer(self, k):
        me_f = lax.axis_index("fsdp")
        return (flip_index(me_f, k, self.fsdp), lax.axis_index("ctx"), lax.axis_index("tp"))

    def core(self):
        me_f, me_c, me_t = self.peer(0)
        return (me_f, me_c, 1 - me_t)

    def ways(self, k):
        return [(0, k)] if k == low_bit(k) else [(0, low_bit(k)), (1, high_bit(k))]

    def span(self, k, part):
        half = self.half
        return pl.ds(0, half) if k == low_bit(k) else pl.ds(part * (half // 2), half // 2)

    def copy(self, k, part, b):
        return pltpu.make_async_remote_copy(
            src_ref=self.held.at[k, self.span(k, part)],
            dst_ref=self.got.at[k, self.span(k, part)],
            send_sem=self.f_send.at[k, part],
            recv_sem=self.f_recv.at[k, part],
            device_id=self.peer(b),
            device_id_type=MESH_ID,
        )

    def own_copy(self, place):
        return pltpu.make_async_remote_copy(
            src_ref=self.held.at[0],
            dst_ref=self.own_ref.at[place],
            send_sem=self.own_sem.at[0],
            recv_sem=self.own_sem.at[1],
            device_id=self.core(),
            device_id_type=MESH_ID,
        )

    def collect(self, k):
        for far in self.order:
            for part, b in self.ways(far):
                if far ^ b == k:
                    self.copy(far, part, b).wait_recv()
                    rows = self.span(far, part)
                    self.held[k, rows] = (
                        self.held[k, rows].astype(jnp.float32)
                        + self.got[far, rows].astype(jnp.float32)
                    ).astype(self.held.dtype)

    def send(self, k):
        for part, b in self.ways(k):
            self.copy(k, part, b).start()

    def start(self):
        barrier = pltpu.get_barrier_semaphore()
        for b in self.bits:
            pl.semaphore_signal(barrier, inc=1, device_id=self.peer(b), device_id_type=MESH_ID)
        pl.semaphore_signal(barrier, inc=1, device_id=self.core(), device_id_type=MESH_ID)
        for load in self.loads:
            load.start()
        pl.semaphore_wait(barrier, len(self.bits) + 1)
        for load in self.loads:
            load.wait()
        for k in self.order:
            if k != low_bit(k):
                self.send(k)

    def relay(self):
        for k in self.order:
            if k == low_bit(k):
                self.collect(k)
                self.send(k)

    def finish(self):
        self.collect(0)
        me_t = lax.axis_index("tp")
        self.own_copy(me_t).start()
        local = pltpu.make_async_copy(
            self.held.at[0], self.own_ref.at[me_t], self.own_sem.at[2]
        )
        local.start()
        local.wait()
        self.own_copy(1 - me_t).wait_recv()
        self.own_copy(me_t).wait_send()
        for k in self.order:
            for part, b in self.ways(k):
                self.copy(k, part, b).wait_send()


def attend_back_kernel(
    ctx, fsdp, group, len_ref, q_ref, do_ref, lse_ref, cos_ref, sin_ref, rows_ref, *refs
):
    keys, values = refs[:ctx], refs[ctx : 2 * ctx]
    dq_ref, dkv_ref, own_ref, dk_sum, dv_sum = refs[2 * ctx : 2 * ctx + 5]
    step = pl.program_id(0) * pl.num_programs(1) + pl.program_id(1)
    sums = RowSum(group, fsdp, rows_ref, own_ref, *refs[2 * ctx + 5 :])

    @pl.when(step == 0)
    def _():
        sums.start()

    rows = q_ref.shape[0]
    biases = key_biases(len_ref, rows, ctx)
    lane = lax.broadcasted_iota(jnp.int32, (rows, 128), 1)
    dk_sum[...] = jnp.zeros_like(dk_sum)
    dv_sum[...] = jnp.zeros_like(dv_sum)
    lse_all = lse_ref[...]
    for j in range(q_ref.shape[1] // 128):
        q_pair = q_ref[:, j * 128 : (j + 1) * 128] * jnp.bfloat16(score_scale)
        do_pair = do_ref[:, j * 128 : (j + 1) * 128]
        dqs = []
        for g in range(2):
            mine = (lane < HD) if g == 0 else (lane >= HD)
            q_head = jnp.where(mine, q_pair, jnp.zeros_like(q_pair))
            do_head = jnp.where(mine, do_pair, jnp.zeros_like(do_pair))
            h = 2 * j + g
            lse = lse_all[:, h : h + 1]
            probs, grads, total = [], [], 0.0
            for s in range(ctx):
                p = jnp.exp(mul(q_head, keys[s][...], NT) + (biases[s] - lse))
                dp = mul(do_head, values[s][...], NT)
                total = total + (p * dp).sum(-1, keepdims=True)
                probs.append(p)
                grads.append(dp)
            dq = 0.0
            for s in range(ctx):
                ds = (probs[s] * (grads[s] - total)).astype(jnp.bfloat16)
                dv_sum[s] += mul(probs[s].astype(jnp.bfloat16), do_head, TN)
                dk_sum[s] += mul(ds, q_head, TN)
                dq = dq + mul(ds, keys[s][...])
            dqs.append(dq)
        dq = jnp.where(lane < HD, dqs[0], dqs[1]) * score_scale
        dq = dq * cos_ref[...] + turn(dq * sin_ref[...], -1.0)
        dq_ref[:, j * 128 : (j + 1) * 128] = dq.astype(jnp.bfloat16)
        if j == 1:

            @pl.when(step == 1)
            def _():
                sums.relay()

    for s in range(ctx):
        dkv_ref[s, 0] = dk_sum[s].astype(dkv_ref.dtype)
        dkv_ref[s, 1] = dv_sum[s].astype(dkv_ref.dtype)

    @pl.when(step == pl.num_programs(0) * pl.num_programs(1) - 1)
    def _():
        sums.finish()


def cot_kernel(dims, local_rows, len_ref, cot_ref, ff_ref):
    rows = cot_ref.shape[0]
    back = cot_ref[...].astype(jnp.float32) * row_valid(len_ref, rows, local_rows)
    ff_ref[...] = reorder((residual_scale * back).astype(jnp.bfloat16), *dims)


def middle_kernel(dims, x_ref, part_ref, other_ref, gain_ref, middle_ref, normed_ref):
    branch = part_ref[...].astype(jnp.float32) + other_ref[...].astype(jnp.float32)
    middle = reorder(x_ref[...].astype(jnp.float32), *dims) + residual_scale * branch
    middle_ref[...] = middle
    normed_ref[...] = (middle * rms_scale(middle) * gain_ref[...]).astype(jnp.bfloat16)


def middle_back_kernel(
    dims, local_rows, len_ref, cot_ref, middle_ref, grad_ref, gain_ref, back_ref, attn_ref, gain_sum
):
    rows = cot_ref.shape[0]
    back = cot_ref[...].astype(jnp.float32) * row_valid(len_ref, rows, local_rows)
    middle = middle_ref[...]
    grad = grad_ref[...].astype(jnp.float32)
    scale = rms_scale(middle)
    out = reorder(back, *dims) + norm_back(grad, middle, scale, gain_ref[...])
    back_ref[...] = out
    attn_ref[...] = (residual_scale * out).astype(jnp.bfloat16)

    @pl.when(pl.program_id(0) == 0)
    def _():
        gain_sum[...] = jnp.zeros_like(gain_sum)

    gain_sum[...] += (grad * middle * scale).sum(0, keepdims=True)


def output_kernel(dims, local_rows, len_ref, middle_ref, ff_ref, out_ref):
    rows = middle_ref.shape[0]
    out = middle_ref[...] + residual_scale * ff_ref[...].astype(jnp.float32)
    out = (out * row_valid(len_ref, rows, local_rows)).astype(jnp.bfloat16)
    out_ref[...] = reorder(out, *dims)


def input_back_kernel(
    dims, x_ref, part_ref, other_ref, back_ref, gain_ref, out_ref, gain_sum
):
    first, second, width = dims
    x = reorder(x_ref[...].astype(jnp.float32), *dims)
    grad = (part_ref[...].astype(jnp.float32) + other_ref[...].astype(jnp.float32))
    scale = rms_scale(x)
    out = back_ref[...] + norm_back(grad, x, scale, gain_ref[...])
    out_ref[...] = reorder(out.astype(jnp.bfloat16), second, first, width)

    @pl.when(pl.program_id(0) == 0)
    def _():
        gain_sum[...] = jnp.zeros_like(gain_sum)

    gain_sum[...] += (grad * x * scale).sum(0, keepdims=True)


def by_rows(kernel, rows, ins, outs, flops=0, limit=40):
    total = max(v.shape[0] for v, kind in ins if kind == "rows")
    in_specs = []
    moved = 0
    for v, kind in ins:
        moved += v.size * v.dtype.itemsize
        if kind == "rows":
            in_specs.append(pl.BlockSpec((rows, v.shape[1]), lambda i: (i, 0)))
        elif kind == "cycle":
            period = v.shape[0] // rows
            in_specs.append(
                pl.BlockSpec((rows, v.shape[1]), lambda i, period=period: (lax.rem(i, period), 0))
            )
        elif kind == "smem":
            in_specs.append(pl.BlockSpec(memory_space=SMEM))
        else:
            in_specs.append(
                pl.BlockSpec(v.shape, lambda i: (0, 0), pipeline_mode=pl.Buffered(1))
            )
    out_specs = []
    for shape, dtype in outs:
        moved += shape[0] * shape[1] * jnp.dtype(dtype).itemsize
        if shape[0] == 1:
            out_specs.append(pl.BlockSpec(shape, lambda i: (0, 0)))
        else:
            out_specs.append(pl.BlockSpec((rows, shape[1]), lambda i: (i, 0)))
    return pl.pallas_call(
        kernel,
        grid=(total // rows,),
        in_specs=in_specs,
        out_specs=out_specs,
        out_shape=[jax.ShapeDtypeStruct(shape, dtype) for shape, dtype in outs],
        compiler_params=pltpu.CompilerParams(vmem_limit_bytes=limit * 1024 * 1024),
        cost_estimate=pl.CostEstimate(flops=flops, bytes_accessed=moved, transcendentals=0),
    )(*[v for v, _ in ins])


def kv_specs(ctx, rows, pairs):
    def spec(slot, start):
        return pl.BlockSpec((None, rows, 128), lambda s, p: (slot, s, start + p))

    return [spec(slot, start) for start in (0, pairs) for slot in range(ctx)]


def attend(lengths, query, kv_all):
    ctx = kv_all.shape[0]
    seqs = lengths.shape[0]
    rows = query.shape[0] // seqs
    pairs = kv_all.shape[2] // 256
    wide = query.shape[1] // pairs
    flops = 4 * query.shape[0] * query.shape[1] * rows * ctx
    return pl.pallas_call(
        partial(attend_kernel, ctx),
        grid=(seqs, pairs),
        in_specs=[
            pl.BlockSpec(memory_space=SMEM),
            pl.BlockSpec((rows, wide), lambda s, p: (s, p)),
        ]
        + kv_specs(ctx, rows, pairs),
        out_specs=[
            pl.BlockSpec((rows, wide), lambda s, p: (s, p)),
            pl.BlockSpec((rows, 128), lambda s, p: (s, p)),
        ],
        out_shape=[
            jax.ShapeDtypeStruct(query.shape, jnp.bfloat16),
            jax.ShapeDtypeStruct((query.shape[0], 128 * pairs), jnp.float32),
        ],
        compiler_params=pltpu.CompilerParams(vmem_limit_bytes=40 * 1024 * 1024),
        cost_estimate=pl.CostEstimate(flops=4 * flops, bytes_accessed=6 << 20, transcendentals=0),
    )(lengths, query, *[kv_all] * (2 * ctx))


def attend_back(fsdp, group, lengths, query, out_grad, lse, cosines, sines, kv_all, row_blocks):
    ctx = kv_all.shape[0]
    block = row_blocks.shape[1:]
    low = jnp.bfloat16
    sems = pltpu.SemaphoreType.DMA
    seqs = lengths.shape[0]
    rows = query.shape[0] // seqs
    pairs = kv_all.shape[2] // 256
    wide = query.shape[1] // pairs
    flops = 10 * query.shape[0] * query.shape[1] * rows * ctx
    return pl.pallas_call(
        partial(attend_back_kernel, ctx, fsdp, group),
        grid=(seqs, pairs),
        in_specs=[
            pl.BlockSpec(memory_space=SMEM),
            pl.BlockSpec((rows, wide), lambda s, p: (s, p)),
            pl.BlockSpec((rows, wide), lambda s, p: (s, p)),
            pl.BlockSpec((rows, 128), lambda s, p: (s, p)),
            pl.BlockSpec((rows, 128), lambda s, p: (0, 0)),
            pl.BlockSpec((rows, 128), lambda s, p: (0, 0)),
            pl.BlockSpec(memory_space=pl.ANY),
        ]
        + kv_specs(ctx, rows, pairs),
        out_specs=[
            pl.BlockSpec((rows, wide), lambda s, p: (s, p)),
            pl.BlockSpec((ctx, 2, rows, 128), lambda s, p: (0, 0, s, p)),
            pl.BlockSpec(memory_space=pl.ANY),
        ],
        out_shape=[
            jax.ShapeDtypeStruct(query.shape, jnp.bfloat16),
            jax.ShapeDtypeStruct((ctx, 2, query.shape[0], 128 * pairs), low),
            jax.ShapeDtypeStruct((2,) + block, low),
        ],
        scratch_shapes=[pltpu.VMEM((ctx, rows, 128), jnp.float32)] * 2
        + [pltpu.VMEM((group,) + block, low)] * 2
        + [sems((group,)), sems((group, 2)), sems((group, 2)), sems((3,))],
        compiler_params=pltpu.CompilerParams(
            collective_id=7, has_side_effects=True, vmem_limit_bytes=44 * 1024 * 1024
        ),
        cost_estimate=pl.CostEstimate(flops=4 * flops, bytes_accessed=10 << 20, transcendentals=0),
    )(lengths, query, out_grad, lse, cosines, sines, row_blocks, *[kv_all] * (2 * ctx))


def low_bit(k):
    return k & -k


def high_bit(k):
    return 1 << (k.bit_length() - 1)


def fsdp_order(fsdp):
    return sorted(range(1, fsdp), key=lambda k: (bin(k).count("1"), k))


def flip_index(me, k, fsdp):
    out = me
    for i in range(fsdp.bit_length() - 1):
        b = 1 << i
        if k & b:
            out = out + b - 2 * b * lax.rem(me // b, 2)
    return out


def line_neighbours(me, count):
    return (me > 0).astype(jnp.int32) + (me < count - 1).astype(jnp.int32)


def line_kernel(fsdp, ctx, group, lines, swaps, widths, *refs):
    line_in = refs[:lines]
    swap_in = refs[lines : lines + swaps]
    line_out = refs[lines + swaps : 2 * lines + swaps]
    swap_out = refs[2 * lines + swaps : -5]
    own_sem, z_send, z_recv, f_send, f_recv = refs[-5:]
    parts = len(widths)
    me_f = lax.axis_index("fsdp")
    me_c = lax.axis_index("ctx")
    me_t = lax.axis_index("tp")

    def along(step, act):
        there = me_c + step

        @pl.when((there >= 0) & (there < ctx))
        def _():
            act(there)

    barrier = pltpu.get_barrier_semaphore()
    for k in range(1, group):
        pl.semaphore_signal(
            barrier, inc=1, device_id=(flip_index(me_f, k, fsdp), me_c, me_t), device_id_type=MESH_ID
        )
    for step in (-1, 1):
        along(
            step,
            lambda there: pl.semaphore_signal(
                barrier, inc=1, device_id=(me_f, there, me_t), device_id_type=MESH_ID
            ),
        )
    pl.semaphore_wait(barrier, group - 1 + line_neighbours(me_c, ctx))

    def z_copy(i, shard, step, src=None):
        place = line_out[i].at[shard]
        way = 0 if step > 0 else 1
        return pltpu.make_async_remote_copy(
            src_ref=place if src is None else src,
            dst_ref=place,
            send_sem=z_send.at[i, way, shard],
            recv_sem=z_recv.at[i, way, shard],
            device_id=(me_f, me_c + step, me_t),
            device_id_type=MESH_ID,
        )

    def landing(i, part, f):
        width = widths[part]
        return swap_out[part].at[lax.rem(f, group), :, pl.ds(i * width, width)]

    def columns(i, part, f):
        start = lax.rem(f, group) * sum(widths) + sum(widths[:part])
        return swap_in[i].at[:, pl.ds(pl.multiple_of(start, 128), widths[part])]

    def f_copy(i, part, k):
        there = flip_index(me_f, k, fsdp)
        return pltpu.make_async_remote_copy(
            src_ref=columns(i, part, there),
            dst_ref=landing(i, part, me_f),
            send_sem=f_send.at[i * parts + part, k],
            recv_sem=f_recv.at[i * parts + part, k],
            device_id=(there, me_c, me_t),
            device_id_type=MESH_ID,
        )

    def f_arrival(i, part, k):
        there = flip_index(me_f, k, fsdp)
        return pltpu.make_async_remote_copy(
            src_ref=landing(i, part, there),
            dst_ref=landing(i, part, there),
            send_sem=f_send.at[i * parts + part, k],
            recv_sem=f_recv.at[i * parts + part, k],
            device_id=(there, me_c, me_t),
            device_id_type=MESH_ID,
        )

    pieces = [(i, part) for part in range(parts) for i in range(swaps)]
    for i in range(lines):
        for step in (1, -1):
            along(step, lambda there: z_copy(i, me_c, step, line_in[i]).start())
    order = fsdp_order(group)
    for i, part in pieces:
        for k in order:
            f_copy(i, part, k).start()
    own = [
        pltpu.make_async_copy(line_in[i], line_out[i].at[me_c], own_sem.at[i])
        for i in range(lines)
    ] + [
        pltpu.make_async_copy(
            columns(i, part, me_f),
            landing(i, part, me_f),
            own_sem.at[lines + i * parts + part],
        )
        for i, part in pieces
    ]
    for copy in own:
        copy.start()
    for distance in range(1, ctx):
        for i in range(lines):
            for step in (1, -1):
                shard = me_c - step * distance

                @pl.when((shard >= 0) & (shard < ctx))
                def _():
                    z_copy(i, shard, step).wait_recv()
                    along(step, lambda there: z_copy(i, shard, step).start())

    for i, part in pieces:
        for k in order:
            f_arrival(i, part, k).wait_recv()
            f_copy(i, part, k).wait_send()
    for copy in own:
        copy.wait()
    for i in range(lines):
        for step in (1, -1):
            along(step, lambda there: z_copy(i, me_c, step, line_in[i]).wait_send())
            for distance in range(1, ctx - 1):
                shard = me_c - step * distance

                @pl.when((shard >= 0) & (shard < ctx))
                def _():
                    along(step, lambda there: z_copy(i, shard, step).wait_send())


def start_exchange(fsdp, ctx, group, lines, swaps, widths):
    parts = len(widths)
    sems = pltpu.SemaphoreType.DMA
    rows = swaps[0].shape[0]
    out_shape = [jax.ShapeDtypeStruct((ctx,) + v.shape, v.dtype) for v in lines]
    out_shape += [
        jax.ShapeDtypeStruct((group, rows, len(swaps) * w), swaps[0].dtype) for w in widths
    ]
    count = len(lines) + len(swaps)
    outs = pl.pallas_call(
        partial(line_kernel, fsdp, ctx, group, len(lines), len(swaps), tuple(widths)),
        out_shape=out_shape,
        in_specs=[pl.BlockSpec(memory_space=pltpu.VMEM)] * count,
        out_specs=[pl.BlockSpec(memory_space=pl.ANY)] * len(out_shape),
        scratch_shapes=[
            sems((len(lines) + len(swaps) * parts,)),
            sems((len(lines), 2, ctx)),
            sems((len(lines), 2, ctx)),
            sems((len(swaps) * parts, group)),
            sems((len(swaps) * parts, group)),
        ],
        compiler_params=pltpu.CompilerParams(
            collective_id=0, has_side_effects=True, vmem_limit_bytes=24 * 1024 * 1024
        ),
    )(*lines, *swaps)
    return outs[: len(lines)], outs[len(lines) :]


class TokenGather:
    def __init__(self, group, fsdp, v_ref, out_ref, own_sem, f_send, f_recv, t_send, t_recv):
        self.order = fsdp_order(group)
        self.bits = [1 << i for i in range(group.bit_length() - 1)]
        self.out_ref = out_ref
        self.sems = (f_send, f_recv, t_send, t_recv)
        self.fsdp = fsdp
        half = out_ref.shape[2]
        self.half = half
        me_t = lax.axis_index("tp")
        self.mine = v_ref.at[pl.ds(pl.multiple_of(me_t * half, half), half)]
        other = v_ref.at[pl.ds(pl.multiple_of((1 - me_t) * half, half), half)]
        self.own = [
            pltpu.make_async_copy(self.mine, out_ref.at[0, 0], own_sem.at[0]),
            pltpu.make_async_copy(other, out_ref.at[0, 1], own_sem.at[1]),
        ]

    def peer(self, k):
        me_f = lax.axis_index("fsdp")
        return (flip_index(me_f, k, self.fsdp), lax.axis_index("ctx"), lax.axis_index("tp"))

    def rows(self, k, part):
        if k == low_bit(k):
            return pl.ds(0, self.half)
        return pl.ds(part * (self.half // 2), self.half // 2)

    def f_copy(self, have, b):
        k = have | b
        part = 1 if have and b == high_bit(k) else 0
        place = self.out_ref.at[k, 0, self.rows(k, part)]
        src = self.out_ref.at[have, 0, self.rows(k, part)] if have else self.mine
        return pltpu.make_async_remote_copy(
            src_ref=src,
            dst_ref=place,
            send_sem=self.sems[0].at[k, part],
            recv_sem=self.sems[1].at[k, part],
            device_id=self.peer(b),
            device_id_type=MESH_ID,
        )

    def ways(self, have):
        return [
            b
            for b in self.bits
            if not have & b and (not have or b in (low_bit(have | b), high_bit(have | b)))
        ]

    def swap(self, k):
        me_f, me_c, me_t = self.peer(0)
        return pltpu.make_async_remote_copy(
            src_ref=self.out_ref.at[k, 0],
            dst_ref=self.out_ref.at[k, 1],
            send_sem=self.sems[2].at[k],
            recv_sem=self.sems[3].at[k],
            device_id=(me_f, me_c, 1 - me_t),
            device_id_type=MESH_ID,
        )

    def start(self):
        for b in self.ways(0):
            self.f_copy(0, b).start()
        for copy in self.own:
            copy.start()

    def relay(self, k):
        parts = [(0, k)] if k == low_bit(k) else [(0, low_bit(k)), (1, high_bit(k))]
        for part, b in parts:
            place = self.out_ref.at[k, 0, self.rows(k, part)]
            pltpu.make_async_remote_copy(
                src_ref=place,
                dst_ref=place,
                send_sem=self.sems[0].at[k, part],
                recv_sem=self.sems[1].at[k, part],
                device_id=self.peer(b),
                device_id_type=MESH_ID,
            ).wait_recv()
        for b in self.ways(k):
            self.f_copy(k, b).start()
        self.swap(k).start()

    def finish(self):
        for copy in self.own:
            copy.wait()
        for have in [0] + self.order:
            for b in self.ways(have):
                self.f_copy(have, b).wait_send()
        me_f, me_c, me_t = self.peer(0)
        for k in self.order:
            pltpu.make_async_remote_copy(
                src_ref=self.out_ref.at[k, 1],
                dst_ref=self.out_ref.at[k, 1],
                send_sem=self.sems[2].at[k],
                recv_sem=self.sems[3].at[k],
                device_id=(me_f, me_c, 1 - me_t),
                device_id_type=MESH_ID,
            ).wait_recv()
            self.swap(k).wait_send()


def token_sems(group):
    sems = pltpu.SemaphoreType.DMA
    return [sems((2,)), sems((group, 2)), sems((group, 2)), sems((group,)), sems((group,))]


def token_shape(group, v):
    return jax.ShapeDtypeStruct((group, 2, v.shape[0] // 2, v.shape[1]), v.dtype)


def tokens_kernel(group, fsdp, v_ref, out_ref, *sems):
    gather = TokenGather(group, fsdp, v_ref, out_ref, *sems)
    me_f, me_c, me_t = gather.peer(0)
    barrier = pltpu.get_barrier_semaphore()
    for b in gather.bits:
        pl.semaphore_signal(barrier, inc=1, device_id=gather.peer(b), device_id_type=MESH_ID)
    pl.semaphore_signal(
        barrier, inc=1, device_id=(me_f, me_c, 1 - me_t), device_id_type=MESH_ID
    )
    pl.semaphore_wait(barrier, len(gather.bits) + 1)
    gather.start()
    for k in gather.order:
        gather.relay(k)
    gather.finish()


def gather_tokens(group, fsdp, v):
    out = pl.pallas_call(
        partial(tokens_kernel, group, fsdp),
        out_shape=token_shape(group, v),
        in_specs=[pl.BlockSpec(memory_space=pltpu.VMEM)],
        out_specs=pl.BlockSpec(memory_space=pl.ANY),
        scratch_shapes=token_sems(group),
        compiler_params=pltpu.CompilerParams(
            collective_id=5, has_side_effects=True, vmem_limit_bytes=24 * 1024 * 1024
        ),
    )(v)
    return out.reshape(-1, v.shape[1])


def swiglu_parts(n_ref, g_ref, w_ref, hidden_ref, grads_ref):
    units = hidden_ref.shape[1]
    both = w_ref[:, : 2 * units]
    down = w_ref[:, 2 * units :]
    lin = mul(n_ref[...], both)
    gate, up = lin[:, :units], lin[:, units:]
    sig = jax.nn.sigmoid(gate)
    act = gate * sig
    hidden = (act * up).astype(jnp.bfloat16)
    hidden_ref[...] = hidden
    hidden_grad = mul(g_ref[...], down)
    grads_ref[:, :units] = (hidden_grad * up * sig * (1.0 + gate * (1.0 - sig))).astype(
        jnp.bfloat16
    )
    grads_ref[:, units:] = (hidden_grad * act).astype(jnp.bfloat16)
    return mul(grads_ref[...], both, NT), mul(hidden, down, NT)


def swiglu_first_kernel(n_ref, g_ref, w_ref, hidden_ref, grads_ref, second_ref, ff_ref):
    second, ff = swiglu_parts(n_ref, g_ref, w_ref, hidden_ref, grads_ref)
    second_ref[...] = second.astype(jnp.bfloat16)
    ff_ref[...] = ff.astype(jnp.bfloat16)


def swiglu_kernel(
    fsdp,
    group,
    n_ref,
    g_ref,
    w_ref,
    second_ref,
    ff_first_ref,
    left_ref,
    right_ref,
    hidden_ref,
    grads_ref,
    ff_ref,
    own_ref,
    product_ref,
    s_out,
    f_out,
    s_in,
    f_in,
    total,
    got,
    t_send,
    t_recv,
    f_send,
    f_recv,
    own_sem,
    left,
    right,
    product,
    inner_sem,
):
    half = n_ref.shape[0]
    step = pl.program_id(0)
    me_f = lax.axis_index("fsdp")
    me_c = lax.axis_index("ctx")
    me_t = lax.axis_index("tp")
    bits = [1 << i for i in range(group.bit_length() - 1)]
    order = fsdp_order(group)
    core = (me_f, me_c, 1 - me_t)

    def peer(k):
        return (flip_index(me_f, k, fsdp), me_c, me_t)

    @pl.when(step == 0)
    def _():
        barrier = pltpu.get_barrier_semaphore()
        for b in bits:
            pl.semaphore_signal(barrier, inc=1, device_id=peer(b), device_id_type=MESH_ID)
        pl.semaphore_signal(barrier, inc=1, device_id=core, device_id_type=MESH_ID)
        pl.semaphore_wait(barrier, len(bits) + 1)

    inner = [
        pltpu.make_async_copy(left_ref, left, inner_sem.at[0]),
        pltpu.make_async_copy(right_ref, right, inner_sem.at[1]),
    ]

    @pl.when(step == 1)
    def _():
        for copy in inner:
            copy.start()

    def make_product():
        for copy in inner:
            copy.wait()

        def body(t, _):
            cols = pl.ds(pl.multiple_of(t * 256, 256), 256)
            product[cols, :] = mul(left[:, cols], right[...], TN).astype(product.dtype)
            return 0

        lax.fori_loop(0, left.shape[1] // 256, body, 0)
        pltpu.make_async_copy(product, product_ref, inner_sem.at[2]).start()

    def core_copies(k):
        slot = k % 2
        return [
            pltpu.make_async_remote_copy(
                src_ref=out.at[slot],
                dst_ref=into.at[slot],
                send_sem=t_send.at[which, k],
                recv_sem=t_recv.at[which, k],
                device_id=core,
                device_id_type=MESH_ID,
            )
            for which, (out, into) in enumerate(((s_out, s_in), (f_out, f_in)))
        ]

    def ways(k):
        return [(0, k)] if k == low_bit(k) else [(0, low_bit(k)), (1, high_bit(k))]

    def span(k, part):
        return pl.ds(0, half) if k == low_bit(k) else pl.ds(part * (half // 2), half // 2)

    def f_copy(k, part, b):
        return pltpu.make_async_remote_copy(
            src_ref=total.at[k, span(k, part)],
            dst_ref=got.at[k, span(k, part)],
            send_sem=f_send.at[k, part],
            recv_sem=f_recv.at[k, part],
            device_id=peer(b),
            device_id_type=MESH_ID,
        )

    def own_copy():
        return pltpu.make_async_remote_copy(
            src_ref=total.at[0],
            dst_ref=own_ref.at[me_t],
            send_sem=own_sem.at[0],
            recv_sem=own_sem.at[1],
            device_id=core,
            device_id_type=MESH_ID,
        )

    second, ff = swiglu_parts(n_ref, g_ref, w_ref, hidden_ref, grads_ref)
    second = second + second_ref[...].astype(jnp.float32)
    ff = ff + ff_first_ref[...].astype(jnp.float32)

    for k in reversed(range(group)):
        slot = k % 2

        @pl.when(step == 2 * (group - 1 - k))
        def _():
            if k + 2 < group:
                for copy in core_copies(k + 2):
                    copy.wait_send()
            s_out[slot] = second.astype(jnp.bfloat16)
            f_out[slot] = ff.astype(jnp.bfloat16)
            for copy in core_copies(k):
                copy.start()

        @pl.when(step == 2 * (group - 1 - k) + 1)
        def _():
            for copy in core_copies(k):
                copy.wait_recv()
            ff_ref[...] = (ff + f_in[slot].astype(jnp.float32)).astype(jnp.bfloat16)
            total[k] = (second + s_in[slot].astype(jnp.float32)).astype(jnp.bfloat16)
            if k == 0:
                make_product()
            for far in order:
                for part, b in ways(far):
                    if far ^ b == k:
                        f_copy(far, part, b).wait_recv()
                        rows = span(far, part)
                        total[k, rows] = (
                            total[k, rows].astype(jnp.float32)
                            + got[far, rows].astype(jnp.float32)
                        ).astype(jnp.bfloat16)
            if k:
                for part, b in ways(k):
                    f_copy(k, part, b).start()
            else:
                own_copy().start()
                local = pltpu.make_async_copy(total.at[0], own_ref.at[me_t], own_sem.at[2])
                local.start()
                local.wait()
                other = own_ref.at[1 - me_t]
                pltpu.make_async_remote_copy(
                    src_ref=other,
                    dst_ref=other,
                    send_sem=own_sem.at[0],
                    recv_sem=own_sem.at[1],
                    device_id=core,
                    device_id_type=MESH_ID,
                ).wait_recv()
                own_copy().wait_send()
                for far in order:
                    for part, b in ways(far):
                        f_copy(far, part, b).wait_send()
                for late in range(min(2, group)):
                    for copy in core_copies(late):
                        copy.wait_send()
                pltpu.make_async_copy(product, product_ref, inner_sem.at[2]).wait()


def swiglu(fsdp, group, normed, grads, weights, second, ff, hidden):
    many, width = normed.shape
    half = many // (2 * group)
    units = weights.shape[1] // 3
    low = jnp.bfloat16
    last = 2 * group - 1
    sems = pltpu.SemaphoreType.DMA
    block = (half, width)

    def rows(cols):
        return pl.BlockSpec((half, cols), lambda i: (last - i, 0))

    def whole(v):
        return pl.BlockSpec(v.shape, lambda i: (0, 0), pipeline_mode=pl.Buffered(1))

    return pl.pallas_call(
        partial(swiglu_kernel, fsdp, group),
        grid=(2 * group,),
        in_specs=[rows(width), rows(width), whole(weights), rows(width), rows(width)]
        + [pl.BlockSpec(memory_space=pl.ANY)] * 2,
        out_specs=[
            rows(units),
            rows(2 * units),
            pl.BlockSpec(block, lambda i: (group - 1 - i // 2, 0)),
            pl.BlockSpec(memory_space=pl.ANY),
            pl.BlockSpec(memory_space=pl.ANY),
        ],
        out_shape=[
            jax.ShapeDtypeStruct((many, units), low),
            jax.ShapeDtypeStruct((many, 2 * units), low),
            jax.ShapeDtypeStruct((group * half, width), low),
            jax.ShapeDtypeStruct((2,) + block, low),
            jax.ShapeDtypeStruct((width, hidden.shape[1]), low),
        ],
        scratch_shapes=[pltpu.VMEM((2,) + block, low)] * 4
        + [pltpu.VMEM((group,) + block, low)] * 2
        + [
            sems((2, group)),
            sems((2, group)),
            sems((group, 2)),
            sems((group, 2)),
            sems((3,)),
            pltpu.VMEM(grads.shape, low),
            pltpu.VMEM(hidden.shape, low),
            pltpu.VMEM((width, hidden.shape[1]), low),
            sems((3,)),
        ],
        compiler_params=pltpu.CompilerParams(
            collective_id=6, has_side_effects=True, vmem_limit_bytes=58 * 1024 * 1024
        ),
        cost_estimate=pl.CostEstimate(
            flops=12 * many * width * units, bytes_accessed=50 << 20, transcendentals=0
        ),
    )(normed, grads, weights, second, ff, grads, hidden)


def spread_kernel(fsdp, ctx, group, count, chain, *refs):
    ins = refs[:count]
    outs = refs[count + chain : 2 * count + chain]
    sems = refs[2 * (count + chain) :]
    own_sem, f_send, f_recv, c_own, c_send, c_recv = sems[:6]
    me_f = lax.axis_index("fsdp")
    me_c = lax.axis_index("ctx")
    me_t = lax.axis_index("tp")
    bits = [1 << i for i in range(fsdp.bit_length() - 1)]
    order = fsdp_order(fsdp)

    def peer(k):
        return (flip_index(me_f, k, fsdp), me_c, me_t)

    barrier = pltpu.get_barrier_semaphore()
    for b in bits:
        pl.semaphore_signal(barrier, inc=1, device_id=peer(b), device_id_type=MESH_ID)
    if chain:
        chain_in, chain_out = refs[count], refs[2 * count + chain]
        gather = TokenGather(
            group, fsdp, refs[count + 1], refs[2 * count + chain + 1], *sems[6:]
        )
        pl.semaphore_signal(
            barrier, inc=1, device_id=(me_f, me_c, 1 - me_t), device_id_type=MESH_ID
        )
        for step in (-1, 1):
            there = me_c + step

            @pl.when((there >= 0) & (there < ctx))
            def _():
                pl.semaphore_signal(
                    barrier, inc=1, device_id=(me_f, there, me_t), device_id_type=MESH_ID
                )

        pl.semaphore_wait(barrier, len(bits) + 1 + line_neighbours(me_c, ctx))
    else:
        pl.semaphore_wait(barrier, len(bits))

    def quarters(rows):
        return [pl.ds(i * (rows // 4), rows // 4) for i in range(4)]

    def climb(s):
        return [
            pltpu.make_async_remote_copy(
                src_ref=chain_out.at[s, part] if s else chain_in.at[part],
                dst_ref=chain_out.at[s + 1, part],
                send_sem=c_send.at[s, i],
                recv_sem=c_recv.at[s + 1, i],
                device_id=(me_f, me_c + 1, me_t),
                device_id_type=MESH_ID,
            )
            for i, part in enumerate(quarters(chain_in.shape[0]))
        ]

    def keep(s):
        return pltpu.make_async_copy(chain_in, chain_out.at[s], c_own.at[s])

    def send_up(s):
        @pl.when((me_c >= s) & (me_c < ctx - 1))
        def _():
            for copy in climb(s):
                copy.start()

    def take_up(s):
        @pl.when(me_c >= s)
        def _():
            for i, part in enumerate(quarters(chain_in.shape[0])):
                pltpu.make_async_remote_copy(
                    src_ref=chain_out.at[s, part],
                    dst_ref=chain_out.at[s, part],
                    send_sem=c_send.at[s - 1, i],
                    recv_sem=c_recv.at[s, i],
                    device_id=(me_f, me_c - 1, me_t),
                    device_id_type=MESH_ID,
                ).wait_recv()

        if s < ctx - 1:
            send_up(s)

    if chain:
        send_up(0)
        keep(0).start()
        for s in range(1, ctx):
            @pl.when(me_c < s)
            def _():
                keep(s).start()

    def place(i, shard, have, k, part):
        block = outs[i].at[shard, flip_index(me_f, have, fsdp)]
        half = ins[i].shape[1] // 2
        return block if k == low_bit(k) else block.at[pl.ds(part * half, half)]

    def f_copy(i, shard, have, b):
        k = have | b
        part = 1 if have and b == high_bit(k) else 0
        block = place(i, shard, have, k, part)
        return pltpu.make_async_remote_copy(
            src_ref=block if have else ins[i].at[shard],
            dst_ref=block,
            send_sem=f_send.at[i, shard, k, part],
            recv_sem=f_recv.at[i, shard, k, part],
            device_id=peer(b),
            device_id_type=MESH_ID,
        )

    def ways(have):
        return [
            b
            for b in bits
            if not have & b and (not have or b in (low_bit(have | b), high_bit(have | b)))
        ]

    own = [
        pltpu.make_async_copy(ins[i], outs[i].at[:, me_f], own_sem.at[i]) for i in range(count)
    ]
    for i in range(count):
        for shard in range(ctx):
            for b in ways(0):
                f_copy(i, shard, 0, b).start()
        own[i].start()
    if chain:
        gather.start()
    climbed = 1
    for i in range(count):
        for k in order:
            if chain and climbed < ctx:
                take_up(climbed)
                climbed += 1
            if chain and k < group and i == 0:
                gather.relay(k)
            parts = [(0, k)] if k == low_bit(k) else [(0, low_bit(k)), (1, high_bit(k))]
            for shard in range(ctx):
                for part, b in parts:
                    block = place(i, shard, k, k, part)
                    pltpu.make_async_remote_copy(
                        src_ref=block,
                        dst_ref=block,
                        send_sem=f_send.at[i, shard, k, part],
                        recv_sem=f_recv.at[i, shard, k, part],
                        device_id=peer(b),
                        device_id_type=MESH_ID,
                    ).wait_recv()
                for b in ways(k):
                    f_copy(i, shard, k, b).start()
    if chain:
        for s in range(climbed, ctx):
            take_up(s)
        gather.finish()
        keep(0).wait()
        for s in range(ctx):
            if s:

                @pl.when(me_c < s)
                def _():
                    keep(s).wait()

            if s < ctx - 1:

                @pl.when((me_c >= s) & (me_c < ctx - 1))
                def _():
                    for copy in climb(s):
                        copy.wait_send()

    for i in range(count):
        own[i].wait()
        for have in [0] + order:
            for shard in range(ctx):
                for b in ways(have):
                    f_copy(i, shard, have, b).wait_send()


def spread_weights(fsdp, ctx, group, arrays, chain=()):
    count = len(arrays)
    sems = pltpu.SemaphoreType.DMA
    outs = pl.pallas_call(
        partial(spread_kernel, fsdp, ctx, group, count, len(chain)),
        out_shape=[
            jax.ShapeDtypeStruct((ctx, fsdp) + v.shape[1:], v.dtype) for v in arrays
        ]
        + [jax.ShapeDtypeStruct((ctx,) + v.shape, v.dtype) for v in chain[:1]]
        + [token_shape(group, v) for v in chain[1:]],
        in_specs=[pl.BlockSpec(memory_space=pltpu.VMEM)] * (count + len(chain)),
        out_specs=[pl.BlockSpec(memory_space=pl.ANY)] * (count + len(chain)),
        scratch_shapes=[
            sems((count,)),
            sems((count, ctx, fsdp, 2)),
            sems((count, ctx, fsdp, 2)),
            sems((ctx,)),
            sems((ctx, 4)),
            sems((ctx, 4)),
        ]
        + (token_sems(group) if chain else []),
        compiler_params=pltpu.CompilerParams(
            collective_id=3 if chain else 1,
            has_side_effects=True,
            vmem_limit_bytes=24 * 1024 * 1024,
        ),
    )(*arrays, *chain)
    return (
        [o.reshape(-1, v.shape[-1]) for o, v in zip(outs, arrays)]
        + list(outs[count : count + 1])
        + [o.reshape(-1, o.shape[-1]) for o in outs[count + 1 :]]
    )


def sum_kernel(fsdp, ctx, count, chain, products, *refs):
    inner = []
    if products:
        first = count + 3
        pairs = refs[first : first + 2 * products]
        place = first + 2 * products + count + 1
        results = refs[place : place + products]
        inner = refs[-2 * products - 1 :]
        refs = refs[:first] + refs[first + 2 * products : place] + refs[place + products :]
        refs = refs[: -2 * products - 1]
    ins = refs[:count]
    if chain:
        parts_ref, cos_ref, sin_ref = refs[count : count + 3]
        refs = refs[:count] + refs[count + 3 :]
        kv_ref = refs[2 * count]
        refs = refs[: 2 * count] + refs[2 * count + 1 :]
    outs = refs[count : 2 * count]
    held = refs[2 * count : 3 * count]
    got = refs[3 * count : 4 * count]
    line = refs[4 * count : 5 * count]
    refs = refs[5 * count :]
    in_sem, f_send, f_recv, z_send, z_recv = refs[:5]
    if chain:
        kv_parts, kv_got, kv_sem, c_send, c_recv = refs[5:]
    me_f = lax.axis_index("fsdp")
    me_c = lax.axis_index("ctx")
    me_t = lax.axis_index("tp")
    bits = [1 << i for i in range(fsdp.bit_length() - 1)]
    order = fsdp_order(fsdp)

    def peer(k):
        return (flip_index(me_f, k, fsdp), me_c, me_t)

    def along(step, act):
        there = me_c + step

        @pl.when((there >= 0) & (there < ctx))
        def _():
            act(there)

    loads = {}
    if chain:
        kv_load = pltpu.make_async_copy(parts_ref, kv_parts, kv_sem.at[0])
        kv_load.start()
    inner_loads = [
        pltpu.make_async_copy(pairs[i], inner[i], inner[-1].at[i]) for i in range(2 * products)
    ]
    for i in range(count):
        for k in reversed([0] + order):
            block = ins[i].at[:, flip_index(me_f, k, fsdp)]
            loads[i, k] = pltpu.make_async_copy(block, held[i].at[k], in_sem.at[i, k])
            loads[i, k].start()

    barrier = pltpu.get_barrier_semaphore()
    for b in bits:
        pl.semaphore_signal(barrier, inc=1, device_id=peer(b), device_id_type=MESH_ID)
    for step in (-1, 1):
        along(
            step,
            lambda there: pl.semaphore_signal(
                barrier, inc=1, device_id=(me_f, there, me_t), device_id_type=MESH_ID
            ),
        )
    pl.semaphore_wait(barrier, len(bits) + line_neighbours(me_c, ctx))

    def ways(k):
        return [(0, k)] if k == low_bit(k) else [(0, low_bit(k)), (1, high_bit(k))]

    def piece(i, k, part):
        rows = ins[i].shape[2]
        return pl.ds(0, rows) if k == low_bit(k) else pl.ds(part * (rows // 2), rows // 2)

    def f_copy(i, shard, k, part, b):
        span = piece(i, k, part)
        return pltpu.make_async_remote_copy(
            src_ref=held[i].at[k, shard, span],
            dst_ref=got[i].at[k, shard, span],
            send_sem=f_send.at[i, shard, k, part],
            recv_sem=f_recv.at[i, shard, k, part],
            device_id=peer(b),
            device_id_type=MESH_ID,
        )

    def add(into, other):
        tile = 16 if into.dtype == jnp.bfloat16 else 8

        def body(r, _):
            span = pl.ds(pl.multiple_of(r * tile, tile), tile)
            into[span] = (
                into[span].astype(jnp.float32) + other[span].astype(jnp.float32)
            ).astype(into.dtype)
            return 0

        lax.fori_loop(0, into.shape[0] // tile, body, 0)

    def collect(i, shard, k):
        for far in order:
            for part, b in ways(far):
                if far ^ b == k:
                    f_copy(i, shard, far, part, b).wait_recv()
                    span = piece(i, far, part)
                    add(held[i].at[k, shard, span], got[i].at[far, shard, span])

    def z_copy(i, shard, step):
        way = 0 if step > 0 else 1
        return pltpu.make_async_remote_copy(
            src_ref=held[i].at[0, shard],
            dst_ref=line[i].at[way, shard],
            send_sem=z_send.at[i, way, shard],
            recv_sem=z_recv.at[i, way, shard],
            device_id=(me_f, me_c + step, me_t),
            device_id_type=MESH_ID,
        )

    def give(i, shard):
        def body(r, _):
            span = pl.ds(pl.multiple_of(r * 16, 16), 16)
            outs[i][span] = held[i][0, shard, span].astype(outs[i].dtype)
            return 0

        lax.fori_loop(0, outs[i].shape[0] // 16, body, 0)

    def on_line(i, shard, step):
        way = 0 if step > 0 else 1

        @pl.when((me_c - step >= 0) & (me_c - step < ctx))
        def _():
            z_copy(i, shard, step).wait_recv()
            add(held[i].at[0, shard], line[i].at[way, shard])

        @pl.when(step * (shard - me_c) > 0)
        def _():
            z_copy(i, shard, step).start()

    def quarters():
        rows = kv_parts.shape[2] // 2
        return [(side, pl.ds(i * rows, rows)) for side in range(2) for i in range(2)]

    def descend(s):
        return [
            pltpu.make_async_remote_copy(
                src_ref=kv_parts.at[s, side, part],
                dst_ref=kv_got.at[s - 1, side, part],
                send_sem=c_send.at[s, i],
                recv_sem=c_recv.at[s - 1, i],
                device_id=(me_f, me_c - 1, me_t),
                device_id_type=MESH_ID,
            )
            for i, (side, part) in enumerate(quarters())
        ]

    def chain_step(s):
        if s < ctx - 1:

            @pl.when((me_c >= s) & (me_c < ctx - 1))
            def _():
                for i, (side, part) in enumerate(quarters()):
                    pltpu.make_async_remote_copy(
                        src_ref=kv_got.at[s, side, part],
                        dst_ref=kv_got.at[s, side, part],
                        send_sem=c_send.at[s + 1, i],
                        recv_sem=c_recv.at[s, i],
                        device_id=(me_f, me_c + 1, me_t),
                        device_id_type=MESH_ID,
                    ).wait_recv()
                    add(kv_parts.at[s, side, part], kv_got.at[s, side, part])

        if s:

            @pl.when(me_c >= s)
            def _():
                for copy in descend(s):
                    copy.start()

    def chain_result():
        width = kv_parts.shape[3]
        rows = cos_ref.shape[0]
        for seq in range(kv_parts.shape[2] // rows):
            span = pl.ds(seq * rows, rows)
            for start in range(0, width, 128):
                cols = slice(start, start + 128)
                t = kv_parts[0, 0, span, cols].astype(jnp.float32)
                t = t * cos_ref[...] + turn(t * sin_ref[...], -1.0)
                kv_ref[span, cols] = t.astype(kv_ref.dtype)
            kv_ref[span, width:] = kv_parts[0, 1, span]

    steps = list(reversed(range(ctx))) if chain else []

    def next_step():
        if steps:
            s = steps.pop(0)
            chain_step(s)
            if s == 0:
                chain_result()

    turns = 4

    def make_products(turn):
        if turn == 0:
            for load in inner_loads:
                load.wait()
        for i in range(products):
            left, right, result = inner[2 * i], inner[2 * i + 1], results[i]
            tiles = left.shape[1] // 256
            per = -(-tiles // turns)

            def body(t, _):
                cols = pl.ds(pl.multiple_of(t * 256, 256), 256)
                result[cols, :] = mul(left[:, cols], right[...], TN).astype(result.dtype)
                return 0

            lax.fori_loop(min(turn * per, tiles), min((turn + 1) * per, tiles), body, 0)

    if chain:
        kv_load.wait()
        next_step()
    for load in inner_loads:
        load.start()
    shards = sorted(range(ctx), key=lambda c: -abs(2 * c - ctx + 1))
    work = [[(i, shard) for i in range(count)] for shard in shards]
    levels = sorted({bin(k).count("1") for k in order}, reverse=True)
    waited = set()

    def loaded(i, k):
        if (i, k) not in waited:
            waited.add((i, k))
            loads[i, k].wait()

    def advance(stage, item):
        for i, shard in item:
            if stage == len(levels):
                loaded(i, 0)
                collect(i, shard, 0)
                continue
            for k in order:
                if bin(k).count("1") == levels[stage]:
                    loaded(i, k)
                    collect(i, shard, k)
                    for part, b in ways(k):
                        f_copy(i, shard, k, part, b).start()

    def line_tick(item, hops):
        for i, shard in item:
            for step, there in ((1, hops), (-1, ctx - 1 - hops)):
                if step * (shard - there) >= 0:

                    @pl.when(me_c == there)
                    def _():
                        on_line(i, shard, step)

            if hops == max(shard, ctx - 1 - shard):

                @pl.when(me_c == shard)
                def _():
                    give(i, shard)

    stages = len(levels) + 1
    for tick in range(len(work) + stages + ctx - 2):
        for stage in range(stages):
            if 0 <= tick - stage < len(work):
                advance(stage, work[tick - stage])
        for hops in range(ctx):
            place = tick - stages + 1 - hops
            if 0 <= place < len(work):
                line_tick(work[place], hops)
        if products and tick < turns:
            make_products(tick)
        next_step()
    while steps:
        next_step()
    for i, shard in [pair for item in work for pair in item]:
        for k in order:
            for part, b in ways(k):
                f_copy(i, shard, k, part, b).wait_send()
        for step in (1, -1):

            @pl.when(step * (shard - me_c) > 0)
            def _():
                z_copy(i, shard, step).wait_send()

    if chain:
        for s in range(1, ctx):

            @pl.when(me_c >= s)
            def _():
                for copy in descend(s):
                    copy.wait_send()


def sum_weights(fsdp, ctx, arrays, chain=(), products=()):
    sems = pltpu.SemaphoreType.DMA
    vmem = pltpu.VMEM
    shards = [v.reshape(ctx, fsdp, -1, v.shape[-1]) for v in arrays]
    blocks = [(fsdp, ctx) + v.shape[2:] for v in shards]
    out_shape = [jax.ShapeDtypeStruct(v.shape[2:], jnp.float32) for v in shards]
    lines = [vmem((2,) + b[1:], v.dtype) for b, v in zip(blocks, shards)]
    extra = []
    if chain:
        parts = chain[0]
        out_shape.append(jax.ShapeDtypeStruct((parts.shape[2], 2 * parts.shape[3]), parts.dtype))
        extra = [
            vmem(parts.shape, parts.dtype),
            vmem((ctx - 1,) + parts.shape[1:], parts.dtype),
            sems((1,)),
            sems((ctx, 4)),
            sems((ctx, 4)),
        ]
    count = len(shards)
    flat = [v for pair in products for v in pair]
    for left, right in products:
        out_shape.append(jax.ShapeDtypeStruct((left.shape[1], right.shape[1]), left.dtype))
    if products:
        extra = extra + [vmem(v.shape, v.dtype) for v in flat] + [sems((len(flat),))]
    held = [vmem(b, v.dtype) for b, v in zip(blocks, shards)]
    return pl.pallas_call(
        partial(sum_kernel, fsdp, ctx, count, bool(chain), len(products)),
        out_shape=out_shape,
        in_specs=[pl.BlockSpec(memory_space=pl.ANY)] * (count + len(chain[:1]))
        + [pl.BlockSpec(memory_space=pltpu.VMEM)] * len(chain[1:])
        + [pl.BlockSpec(memory_space=pl.ANY)] * len(flat),
        out_specs=[pl.BlockSpec(memory_space=pltpu.VMEM)] * len(out_shape),
        scratch_shapes=held
        + held
        + lines
        + [
            sems((count, fsdp)),
            sems((count, ctx, fsdp, 2)),
            sems((count, ctx, fsdp, 2)),
            sems((count, 2, ctx)),
            sems((count, 2, ctx)),
        ]
        + extra,
        compiler_params=pltpu.CompilerParams(
            collective_id=4 if chain else 2,
            has_side_effects=True,
            vmem_limit_bytes=58 * 1024 * 1024,
        ),
    )(*shards, *chain, *flat)


def heads_kernel(group_size, qkv_ref, out_ref, *outs):
    width = outs[0].shape[1]
    for source, target in ((qkv_ref, outs[0]), (out_ref, outs[3])):
        for block in range(width // 128):
            pair, rest = divmod(2 * block, 2 * group_size)
            g, j = divmod(rest, group_size)
            start = (pair * group_size + j) * 128
            left = source[:, start : start + 128]
            right = source[:, start + 128 : start + 256]
            if g:
                left = pltpu.roll(left, HD, 1)
            else:
                right = pltpu.roll(right, HD, 1)
            lane = lax.broadcasted_iota(jnp.int32, left.shape, 1)
            target[:, block * 128 : (block + 1) * 128] = jnp.where(lane < HD, left, right)
    kv_width = outs[1].shape[1]
    outs[1][...] = qkv_ref[:, width : width + kv_width]
    outs[2][...] = qkv_ref[:, width + kv_width :]


def plain_grads(group_size, qkv, out, kv_width):
    rows, width = out.shape
    vmem = pl.BlockSpec(memory_space=pltpu.VMEM)
    return pl.pallas_call(
        partial(heads_kernel, group_size),
        out_shape=[
            jax.ShapeDtypeStruct((rows, w), out.dtype) for w in (width, kv_width, kv_width, width)
        ],
        in_specs=[vmem] * 2,
        out_specs=[vmem] * 4,
        cost_estimate=pl.CostEstimate(flops=0, bytes_accessed=4 << 20, transcendentals=0),
    )(qkv, out)


def place_kernel(group, count, *refs):
    parts, outs = refs[:count], refs[count:]
    span = sum(v.shape[3] for v in parts)
    for i, out in enumerate(outs):
        for f in range(group):
            start = f * span
            for v in parts:
                width = v.shape[3]
                out[:, start : start + width] = v[f, i].astype(out.dtype)
                start += width


def place_units(parts):
    group, arrays, rows, _ = parts[0].shape
    cols = group * sum(v.shape[3] for v in parts)
    vmem = pl.BlockSpec(memory_space=pltpu.VMEM)
    return pl.pallas_call(
        partial(place_kernel, group, len(parts)),
        out_shape=[jax.ShapeDtypeStruct((rows, cols), jnp.float32)] * arrays,
        in_specs=[vmem] * len(parts),
        out_specs=[vmem] * arrays,
        compiler_params=pltpu.CompilerParams(vmem_limit_bytes=24 * 1024 * 1024),
        cost_estimate=pl.CostEstimate(
            flops=0, bytes_accessed=6 * rows * cols * arrays, transcendentals=0
        ),
    )(*parts)


def local(
    inputs,
    lengths,
    cotangent,
    norm1_gain,
    w_query,
    w_key,
    w_value,
    w_out,
    norm2_gain,
    w_gate,
    w_up,
    w_down,
):
    seq_count, local_rows, model_width = inputs.shape
    tokens = seq_count * local_rows
    half = tokens // 2
    fsdp = lax.axis_size("fsdp")
    ctx = lax.axis_size("ctx")
    shard = w_query.shape[0]
    query_width = w_query.shape[1]
    kv_width = w_key.shape[1]
    kv_end = query_width + 2 * kv_width
    pairs = kv_width // (2 * HD)
    group_size = query_width // kv_width
    group = min(fsdp, 4)
    far = fsdp // group
    own = w_gate.shape[1] // group
    first_units = own * FIRST_EIGHTHS // 8
    widths = (first_units, own - first_units)
    me_c = lax.axis_index("ctx")
    me_t = lax.axis_index("tp")
    low = jnp.bfloat16
    wide = jnp.float32

    def swap(v):
        return lax.ppermute(v, "tp", [(0, 1), (1, 0)])

    inside = shard % 128 == 0
    dims = (fsdp, ctx, shard)
    back_dims = (ctx, fsdp, shard)

    def by_ctx(v):
        if inside:
            return v
        rows = v.shape[0]
        return v.reshape(rows, fsdp, ctx, shard).swapaxes(1, 2).reshape(rows, model_width)

    def by_fsdp(v):
        if inside:
            return v
        rows = v.shape[0]
        return v.reshape(rows, ctx, fsdp, shard).swapaxes(1, 2).reshape(rows, model_width)

    def pair_heads(v):
        rows = v.shape[0]
        return (
            v.reshape(rows, pairs, 2, group_size, HD).swapaxes(2, 3).reshape(rows, query_width)
        )

    x = by_ctx(inputs.reshape(tokens, model_width))
    cot = by_ctx(cotangent.reshape(tokens, model_width))
    positions = me_c * local_rows + jnp.arange(local_rows, dtype=jnp.int32)
    cosines, sines = rope_tables(positions, HD)
    cosines, sines = jnp.tile(cosines, (1, 2)), jnp.tile(sines, (1, 2))

    gains = jnp.pad(jnp.stack([norm1_gain, norm2_gain]).astype(wide), ((0, 14), (0, 0)))
    lined, held = start_exchange(
        fsdp,
        ctx,
        group,
        [
            jnp.concatenate([pair_heads(w_query), w_key, w_value], 1),
            gains,
            pair_heads(w_out),
        ],
        [w_gate, w_up, w_down],
        widths,
    )
    far_groups = [[h * group + g for h in range(far)] for g in range(group)]
    near_groups = [[h * group + g for g in range(group)] for h in range(far)]

    def whole_width(v):
        if far > 1:
            v = lax.all_gather(v, "fsdp", axis=0, tiled=False, axis_index_groups=far_groups)
        return lax.all_gather(v, "ctx", axis=0, tiled=False).reshape(model_width, -1)

    first_full = whole_width(held[0])
    qkv_full, gain_rows = spread_weights(fsdp, ctx, group, lined[:2])
    gain_rows = gain_rows.reshape(ctx * fsdp, 16, shard)
    gain_one = gain_rows[:, 0].reshape(1, model_width)
    gain_two = gain_rows[:, 1].reshape(1, model_width)

    (ff_grad,) = by_rows(
        partial(cot_kernel, dims, local_rows),
        128,
        [(lengths, "smem"), (cot, "rows")],
        [((tokens, model_width), low)],
    )
    first_normed, query, kv_own = by_rows(
        partial(qkv_kernel, dims),
        128,
        [
            (x, "rows"),
            (qkv_full, "whole"),
            (gain_one, "whole"),
            (cosines, "cycle"),
            (sines, "cycle"),
        ],
        [
            ((tokens, model_width), low),
            ((tokens, query_width), low),
            ((tokens, 2 * kv_width), low),
        ],
        flops=2 * tokens * model_width * kv_end,
    )
    out_full, kv_all, ff_grad_all = spread_weights(
        fsdp, ctx, group, lined[2:], (kv_own, ff_grad)
    )
    late_held, kv_all = lax.optimization_barrier((held[1], kv_all))
    late_full = whole_width(late_held)
    attended, lse = attend(lengths, query, kv_all)
    attn_part = jnp.einsum(
        "tj,dj->td", attended, out_full, preferred_element_type=wide
    ).astype(low)
    middle, second_normed = by_rows(
        partial(middle_kernel, dims),
        128,
        [(x, "rows"), (attn_part, "rows"), (swap(attn_part), "rows"), (gain_two, "whole")],
        [((tokens, model_width), wide), ((tokens, model_width), low)],
    )
    normed_all = gather_tokens(group, fsdp, second_normed)

    def unit_term(left, right):
        return jnp.einsum("td,tf->df", left, right, preferred_element_type=wide).astype(low)

    def own_units(term):
        width = term.shape[1]
        own = lax.psum_scatter(
            term.reshape(ctx, fsdp, shard, width), "ctx", scatter_dimension=0, tiled=False
        )
        if far > 1:
            own = lax.psum_scatter(
                own.reshape(far, group, shard, width),
                "fsdp",
                scatter_dimension=0,
                tiled=False,
                axis_index_groups=far_groups,
            )
        return own

    def return_units(both, down):
        units = down.shape[-1]
        pieces = jnp.concatenate([both[..., :units], both[..., units:], down], 1)
        back = lax.all_to_all(
            pieces.reshape(group * 3 * shard, units),
            "fsdp",
            0,
            0,
            tiled=True,
            axis_index_groups=near_groups if far > 1 else None,
        )
        return back.reshape(group, 3, shard, units)

    many = group * tokens
    first_hidden, first_grads, second_part, ff_part = by_rows(
        swiglu_first_kernel,
        256,
        [(normed_all, "rows"), (ff_grad_all, "rows"), (first_full, "whole")],
        [
            ((many, first_units), low),
            ((many, 2 * first_units), low),
            ((many, model_width), low),
            ((many, model_width), low),
        ],
        flops=12 * many * model_width * first_units,
        limit=56,
    )
    first_both = unit_term(normed_all, first_grads)
    second_part, ff_part, _ = lax.optimization_barrier((second_part, ff_part, first_both))
    hidden, both_grad, ff_sums, second_grad, first_down = swiglu(
        fsdp,
        group,
        normed_all,
        ff_grad_all,
        late_full,
        second_part,
        ff_part,
        first_hidden,
    )
    first_own = (own_units(first_both), own_units(first_down))
    second_grad = second_grad.reshape(tokens, model_width)

    middle_grad, attn_grad, gain_two_term = by_rows(
        partial(middle_back_kernel, dims, local_rows),
        128,
        [
            (lengths, "smem"),
            (cot, "rows"),
            (middle, "rows"),
            (second_grad, "rows"),
            (gain_two, "whole"),
        ],
        [((tokens, model_width), wide), ((tokens, model_width), low), ((1, model_width), wide)],
    )
    attended_grad = jnp.dot(attn_grad, out_full, preferred_element_type=wide).astype(low)
    query_grad, kv_parts, ff_branch = attend_back(
        fsdp,
        group,
        lengths,
        query,
        attended_grad,
        lse,
        cosines,
        sines,
        kv_all,
        ff_sums.reshape(group, half, model_width),
    )
    query_grad, late_rows, late_hidden = lax.optimization_barrier(
        (query_grad, ff_grad_all, hidden)
    )
    late_down = unit_term(late_rows, late_hidden)
    late_down_own = own_units(late_down)
    kv_parts, _ = lax.optimization_barrier((kv_parts, late_down))
    out_term = jnp.einsum("td,tj->dj", attn_grad, attended, preferred_element_type=wide)
    w_out_grad, kv_grad, late_both = sum_weights(
        fsdp,
        ctx,
        [out_term.astype(low)],
        (kv_parts, cosines, sines),
        ((normed_all, both_grad),),
    )
    late_both_own = own_units(late_both)
    (output,) = by_rows(
        partial(output_kernel, back_dims, local_rows),
        128,
        [(lengths, "smem"), (middle, "rows"), (ff_branch.reshape(tokens, model_width), "rows")],
        [((tokens, model_width), low)],
    )
    qkv_grad = jnp.concatenate([query_grad, kv_grad], -1)
    qkv_term = jnp.einsum("td,tj->dj", first_normed, qkv_grad, preferred_element_type=wide)
    first_part = jnp.einsum(
        "tj,dj->td", qkv_grad, qkv_full, preferred_element_type=wide
    ).astype(low)
    input_grad, gain_one_term = by_rows(
        partial(input_back_kernel, dims),
        128,
        [
            (x, "rows"),
            (first_part, "rows"),
            (swap(first_part), "rows"),
            (middle_grad, "rows"),
            (gain_one, "whole"),
        ],
        [((tokens, model_width), low), ((1, model_width), wide)],
    )
    gain_terms = jnp.stack(
        [gain_one_term.reshape(-1, shard), gain_two_term.reshape(-1, shard)], 1
    )
    gain_terms = jnp.pad(gain_terms, ((0, 0), (0, 14), (0, 0))).reshape(-1, shard)
    first_back = return_units(*first_own)
    qkv_term, first_back, _ = lax.optimization_barrier(
        (qkv_term.astype(low), first_back, late_both)
    )
    qkv_own, gain_own = sum_weights(fsdp, ctx, [qkv_term, gain_terms])
    w_query_grad, w_key_grad, w_value_grad, w_out_grad = plain_grads(
        group_size, qkv_own, w_out_grad, kv_width
    )
    late_both_own, late_down_own, qkv_own = lax.optimization_barrier(
        (late_both_own, late_down_own, qkv_own)
    )
    late_back = return_units(late_both_own, late_down_own)
    w_gate_grad, w_up_grad, w_down_grad = place_units([first_back, late_back])
    return (
        by_fsdp(output).reshape(inputs.shape),
        by_fsdp(input_grad).reshape(inputs.shape),
        gain_own[0],
        w_query_grad,
        w_key_grad,
        w_value_grad,
        w_out_grad,
        gain_own[1],
        w_gate_grad,
        w_up_grad,
        w_down_grad,
    )


def solution(mesh):
    placed = (
        P("fsdp", "ctx", None),
        P("fsdp"),
        P("fsdp", "ctx", None),
        P(("fsdp", "ctx")),
        P(("fsdp", "ctx"), "tp"),
        P(("fsdp", "ctx"), "tp"),
        P(("fsdp", "ctx"), "tp"),
        P(("fsdp", "ctx"), "tp"),
        P(("fsdp", "ctx")),
        P(("fsdp", "ctx"), "tp"),
        P(("fsdp", "ctx"), "tp"),
        P(("fsdp", "ctx"), "tp"),
    )
    return jax.shard_map(
        local,
        mesh=mesh,
        in_specs=placed,
        out_specs=(
            P("fsdp", "ctx", None),
            P("fsdp", "ctx", None),
            P(("fsdp", "ctx")),
            P(("fsdp", "ctx"), "tp"),
            P(("fsdp", "ctx"), "tp"),
            P(("fsdp", "ctx"), "tp"),
            P(("fsdp", "ctx"), "tp"),
            P(("fsdp", "ctx")),
            P(("fsdp", "ctx"), "tp"),
            P(("fsdp", "ctx"), "tp"),
            P(("fsdp", "ctx"), "tp"),
        ),
        check_vma=False,
    )
```

```python
from functools import partial

import jax
import jax.numpy as jnp
from jax import lax
from jax.experimental import pallas as pl
from jax.experimental.pallas import tpu as pltpu
from jax.sharding import PartitionSpec as P

HD = 64


norm_eps = 1e-05
residual_scale = 0.22
score_scale = 1.0 / 64.0
rope_base = 10000000.0
masked_score = -1e30


def rope_tables(positions, head_dim):
    half_dim = head_dim // 2
    frequency = rope_base ** (-(jnp.arange(half_dim, dtype=jnp.float32) * 2.0) / head_dim)
    angles = positions.astype(jnp.float32)[:, None] * frequency[None, :]
    return (
        jnp.concatenate([jnp.cos(angles), jnp.cos(angles)], -1),
        jnp.concatenate([jnp.sin(angles), jnp.sin(angles)], -1),
    )


def rotate(values_in, cosines, sines):
    half_dim = values_in.shape[-1] // 2
    turned = jnp.concatenate([-values_in[..., half_dim:], values_in[..., :half_dim]], -1)
    return values_in * cosines + turned * sines


def unrotate(grad_in, cosines, sines):
    half_dim = grad_in.shape[-1] // 2
    scaled = grad_in * sines
    return grad_in * cosines + jnp.concatenate(
        [scaled[..., half_dim:], -scaled[..., :half_dim]], -1
    )


def rms_scale(values_in):
    return lax.rsqrt(jnp.mean(values_in * values_in, -1, keepdims=True) + norm_eps)


def norm_back(grad_normed, values_in, scale, gain):
    scaled_grad = grad_normed * gain
    return scale * scaled_grad - values_in * scale**3 * jnp.mean(
        scaled_grad * values_in, -1, keepdims=True
    )


MESH_ID = pl.DeviceIdType.MESH
FIRST_EIGHTHS = 4
NT = (((1,), (1,)), ((), ()))
TN = (((0,), (0,)), ((), ()))
SMEM = pltpu.SMEM


def mul(left, right, dims=(((1,), (0,)), ((), ()))):
    return lax.dot_general(left, right, dims, preferred_element_type=jnp.float32)


def reorder(v, first, second, width):
    if width % 128:
        return v
    pieces = []
    for b in range(second):
        for a in range(first):
            start = (a * second + b) * width
            pieces.append(v[:, start : start + width])
    return jnp.concatenate(pieces, 1)


def turn(t, sign):
    lane = lax.broadcasted_iota(jnp.int32, t.shape, 1)
    ahead = pltpu.roll(t, 128 - HD // 2, 1)
    behind = pltpu.roll(t, HD // 2, 1)
    return jnp.where(lax.rem(lane, HD) < HD // 2, -sign * ahead, sign * behind)


def row_valid(len_ref, rows, local_rows):
    step = pl.program_id(0)
    start = step * rows
    seq = start // local_rows
    place = (
        lax.axis_index("ctx") * local_rows
        + lax.rem(start, local_rows)
        + lax.broadcasted_iota(jnp.int32, (rows, 1), 0)
    )
    return (place < len_ref[seq]).astype(jnp.float32)


def qkv_kernel(dims, x_ref, w_ref, gain_ref, cos_ref, sin_ref, normed_ref, q_ref, kv_ref):
    x = reorder(x_ref[...].astype(jnp.float32), *dims)
    normed = (x * rms_scale(x) * gain_ref[...]).astype(jnp.bfloat16)
    normed_ref[...] = normed
    lin = mul(normed, w_ref[...])
    cosines, sines = cos_ref[...], sin_ref[...]
    width = q_ref.shape[1]
    half = kv_ref.shape[1] // 2
    for start in range(0, width + half, 128):
        t = lin[:, start : start + 128]
        t = (t * cosines + turn(t, 1.0) * sines).astype(jnp.bfloat16)
        if start < width:
            q_ref[:, start : start + 128] = t
        else:
            kv_ref[:, start - width : start - width + 128] = t
    kv_ref[:, half:] = lin[:, width + half :].astype(jnp.bfloat16)


def key_biases(len_ref, rows, ctx):
    length = len_ref[pl.program_id(0)]
    me = lax.axis_index("ctx")
    row = lax.broadcasted_iota(jnp.int32, (rows, rows), 0)
    col = lax.broadcasted_iota(jnp.int32, (rows, rows), 1)
    first = jnp.where((col <= row) & (me * rows + col < length), 0.0, masked_score)
    out = [first]
    for s in range(1, ctx):
        place = (me - s) * rows + lax.broadcasted_iota(jnp.int32, (1, rows), 1)
        out.append(jnp.where((place >= 0) & (place < length), 0.0, masked_score))
    return out


def attend_kernel(ctx, len_ref, q_ref, *refs):
    keys, values = refs[:ctx], refs[ctx : 2 * ctx]
    o_ref, lse_ref = refs[2 * ctx :]
    rows = q_ref.shape[0]
    biases = key_biases(len_ref, rows, ctx)
    lane = lax.broadcasted_iota(jnp.int32, (rows, 128), 1)
    lse_all = jnp.zeros((rows, 128), jnp.float32)
    for j in range(q_ref.shape[1] // 128):
        q_pair = q_ref[:, j * 128 : (j + 1) * 128] * jnp.bfloat16(score_scale)
        outs = []
        for g in range(2):
            mine = (lane < HD) if g == 0 else (lane >= HD)
            q_head = jnp.where(mine, q_pair, jnp.zeros_like(q_pair))
            scores = [mul(q_head, k[...], NT) + b for k, b in zip(keys, biases)]
            top = scores[0].max(-1, keepdims=True)
            for s in scores[1:]:
                top = jnp.maximum(top, s.max(-1, keepdims=True))
            mass, out = 0.0, 0.0
            for s, v in zip(scores, values):
                p = jnp.exp(s - top)
                mass = mass + p.sum(-1, keepdims=True)
                out = out + mul(p.astype(jnp.bfloat16), v[...])
            outs.append(out / mass)
            lse_all = jnp.where(lane == 2 * j + g, top + jnp.log(mass), lse_all)
        o_ref[:, j * 128 : (j + 1) * 128] = jnp.where(lane < HD, outs[0], outs[1]).astype(
            jnp.bfloat16
        )
    lse_ref[...] = lse_all


class RowSum:
    def __init__(
        self, group, fsdp, rows_ref, own_ref, held, got, in_sem, f_send, f_recv, own_sem
    ):
        self.group, self.fsdp = group, fsdp
        self.order = fsdp_order(group)
        self.bits = [1 << i for i in range(group.bit_length() - 1)]
        self.own_ref, self.held, self.got = own_ref, held, got
        self.f_send, self.f_recv, self.own_sem = f_send, f_recv, own_sem
        self.half = rows_ref.shape[1]
        self.loads = [
            pltpu.make_async_copy(rows_ref.at[k], held.at[k], in_sem.at[k]) for k in range(group)
        ]

    def peer(self, k):
        me_f = lax.axis_index("fsdp")
        return (flip_index(me_f, k, self.fsdp), lax.axis_index("ctx"), lax.axis_index("tp"))

    def core(self):
        me_f, me_c, me_t = self.peer(0)
        return (me_f, me_c, 1 - me_t)

    def ways(self, k):
        return [(0, k)] if k == low_bit(k) else [(0, low_bit(k)), (1, high_bit(k))]

    def span(self, k, part):
        half = self.half
        return pl.ds(0, half) if k == low_bit(k) else pl.ds(part * (half // 2), half // 2)

    def copy(self, k, part, b):
        return pltpu.make_async_remote_copy(
            src_ref=self.held.at[k, self.span(k, part)],
            dst_ref=self.got.at[k, self.span(k, part)],
            send_sem=self.f_send.at[k, part],
            recv_sem=self.f_recv.at[k, part],
            device_id=self.peer(b),
            device_id_type=MESH_ID,
        )

    def own_copy(self, place):
        return pltpu.make_async_remote_copy(
            src_ref=self.held.at[0],
            dst_ref=self.own_ref.at[place],
            send_sem=self.own_sem.at[0],
            recv_sem=self.own_sem.at[1],
            device_id=self.core(),
            device_id_type=MESH_ID,
        )

    def collect(self, k):
        for far in self.order:
            for part, b in self.ways(far):
                if far ^ b == k:
                    self.copy(far, part, b).wait_recv()
                    rows = self.span(far, part)
                    self.held[k, rows] = (
                        self.held[k, rows].astype(jnp.float32)
                        + self.got[far, rows].astype(jnp.float32)
                    ).astype(self.held.dtype)

    def send(self, k):
        for part, b in self.ways(k):
            self.copy(k, part, b).start()

    def start(self):
        barrier = pltpu.get_barrier_semaphore()
        for b in self.bits:
            pl.semaphore_signal(barrier, inc=1, device_id=self.peer(b), device_id_type=MESH_ID)
        pl.semaphore_signal(barrier, inc=1, device_id=self.core(), device_id_type=MESH_ID)
        for load in self.loads:
            load.start()
        pl.semaphore_wait(barrier, len(self.bits) + 1)
        for load in self.loads:
            load.wait()
        for k in self.order:
            if k != low_bit(k):
                self.send(k)

    def relay(self):
        for k in self.order:
            if k == low_bit(k):
                self.collect(k)
                self.send(k)

    def finish(self):
        self.collect(0)
        me_t = lax.axis_index("tp")
        self.own_copy(me_t).start()
        local = pltpu.make_async_copy(
            self.held.at[0], self.own_ref.at[me_t], self.own_sem.at[2]
        )
        local.start()
        local.wait()
        self.own_copy(1 - me_t).wait_recv()
        self.own_copy(me_t).wait_send()
        for k in self.order:
            for part, b in self.ways(k):
                self.copy(k, part, b).wait_send()


def attend_back_kernel(
    ctx, fsdp, group, len_ref, q_ref, do_ref, lse_ref, cos_ref, sin_ref, rows_ref, *refs
):
    keys, values = refs[:ctx], refs[ctx : 2 * ctx]
    dq_ref, dkv_ref, own_ref, dk_sum, dv_sum = refs[2 * ctx : 2 * ctx + 5]
    step = pl.program_id(0) * pl.num_programs(1) + pl.program_id(1)
    sums = RowSum(group, fsdp, rows_ref, own_ref, *refs[2 * ctx + 5 :])

    @pl.when(step == 0)
    def _():
        sums.start()

    rows = q_ref.shape[0]
    biases = key_biases(len_ref, rows, ctx)
    lane = lax.broadcasted_iota(jnp.int32, (rows, 128), 1)
    dk_sum[...] = jnp.zeros_like(dk_sum)
    dv_sum[...] = jnp.zeros_like(dv_sum)
    lse_all = lse_ref[...]
    for j in range(q_ref.shape[1] // 128):
        q_pair = q_ref[:, j * 128 : (j + 1) * 128] * jnp.bfloat16(score_scale)
        do_pair = do_ref[:, j * 128 : (j + 1) * 128]
        dqs = []
        for g in range(2):
            mine = (lane < HD) if g == 0 else (lane >= HD)
            q_head = jnp.where(mine, q_pair, jnp.zeros_like(q_pair))
            do_head = jnp.where(mine, do_pair, jnp.zeros_like(do_pair))
            h = 2 * j + g
            lse = lse_all[:, h : h + 1]
            probs, grads, total = [], [], 0.0
            for s in range(ctx):
                p = jnp.exp(mul(q_head, keys[s][...], NT) + (biases[s] - lse))
                dp = mul(do_head, values[s][...], NT)
                total = total + (p * dp).sum(-1, keepdims=True)
                probs.append(p)
                grads.append(dp)
            dq = 0.0
            for s in range(ctx):
                ds = (probs[s] * (grads[s] - total)).astype(jnp.bfloat16)
                dv_sum[s] += mul(probs[s].astype(jnp.bfloat16), do_head, TN)
                dk_sum[s] += mul(ds, q_head, TN)
                dq = dq + mul(ds, keys[s][...])
            dqs.append(dq)
        dq = jnp.where(lane < HD, dqs[0], dqs[1]) * score_scale
        dq = dq * cos_ref[...] + turn(dq * sin_ref[...], -1.0)
        dq_ref[:, j * 128 : (j + 1) * 128] = dq.astype(jnp.bfloat16)
        if j == 0:

            @pl.when(step == 1)
            def _():
                sums.relay()

    for s in range(ctx):
        dkv_ref[s, 0] = dk_sum[s].astype(dkv_ref.dtype)
        dkv_ref[s, 1] = dv_sum[s].astype(dkv_ref.dtype)

    @pl.when(step == pl.num_programs(0) * pl.num_programs(1) - 1)
    def _():
        sums.finish()


def cot_kernel(dims, local_rows, len_ref, cot_ref, ff_ref):
    rows = cot_ref.shape[0]
    back = cot_ref[...].astype(jnp.float32) * row_valid(len_ref, rows, local_rows)
    ff_ref[...] = reorder((residual_scale * back).astype(jnp.bfloat16), *dims)


def middle_kernel(dims, x_ref, part_ref, other_ref, gain_ref, middle_ref, normed_ref):
    branch = part_ref[...].astype(jnp.float32) + other_ref[...].astype(jnp.float32)
    middle = reorder(x_ref[...].astype(jnp.float32), *dims) + residual_scale * branch
    middle_ref[...] = middle
    normed_ref[...] = (middle * rms_scale(middle) * gain_ref[...]).astype(jnp.bfloat16)


def middle_back_kernel(
    dims, local_rows, len_ref, cot_ref, middle_ref, grad_ref, gain_ref, back_ref, attn_ref, gain_sum
):
    rows = cot_ref.shape[0]
    back = cot_ref[...].astype(jnp.float32) * row_valid(len_ref, rows, local_rows)
    middle = middle_ref[...]
    grad = grad_ref[...].astype(jnp.float32)
    scale = rms_scale(middle)
    out = reorder(back, *dims) + norm_back(grad, middle, scale, gain_ref[...])
    back_ref[...] = out
    attn_ref[...] = (residual_scale * out).astype(jnp.bfloat16)

    @pl.when(pl.program_id(0) == 0)
    def _():
        gain_sum[...] = jnp.zeros_like(gain_sum)

    gain_sum[...] += (grad * middle * scale).sum(0, keepdims=True)


def output_kernel(dims, local_rows, len_ref, middle_ref, ff_ref, out_ref):
    rows = middle_ref.shape[0]
    out = middle_ref[...] + residual_scale * ff_ref[...].astype(jnp.float32)
    out = (out * row_valid(len_ref, rows, local_rows)).astype(jnp.bfloat16)
    out_ref[...] = reorder(out, *dims)


def input_back_kernel(
    dims, x_ref, part_ref, other_ref, back_ref, gain_ref, out_ref, gain_sum
):
    first, second, width = dims
    x = reorder(x_ref[...].astype(jnp.float32), *dims)
    grad = (part_ref[...].astype(jnp.float32) + other_ref[...].astype(jnp.float32))
    scale = rms_scale(x)
    out = back_ref[...] + norm_back(grad, x, scale, gain_ref[...])
    out_ref[...] = reorder(out.astype(jnp.bfloat16), second, first, width)

    @pl.when(pl.program_id(0) == 0)
    def _():
        gain_sum[...] = jnp.zeros_like(gain_sum)

    gain_sum[...] += (grad * x * scale).sum(0, keepdims=True)


def by_rows(kernel, rows, ins, outs, flops=0, limit=40):
    total = max(v.shape[0] for v, kind in ins if kind == "rows")
    in_specs = []
    moved = 0
    for v, kind in ins:
        moved += v.size * v.dtype.itemsize
        if kind == "rows":
            in_specs.append(pl.BlockSpec((rows, v.shape[1]), lambda i: (i, 0)))
        elif kind == "cycle":
            period = v.shape[0] // rows
            in_specs.append(
                pl.BlockSpec((rows, v.shape[1]), lambda i, period=period: (lax.rem(i, period), 0))
            )
        elif kind == "smem":
            in_specs.append(pl.BlockSpec(memory_space=SMEM))
        else:
            in_specs.append(
                pl.BlockSpec(v.shape, lambda i: (0, 0), pipeline_mode=pl.Buffered(1))
            )
    out_specs = []
    for shape, dtype in outs:
        moved += shape[0] * shape[1] * jnp.dtype(dtype).itemsize
        if shape[0] == 1:
            out_specs.append(pl.BlockSpec(shape, lambda i: (0, 0)))
        else:
            out_specs.append(pl.BlockSpec((rows, shape[1]), lambda i: (i, 0)))
    return pl.pallas_call(
        kernel,
        grid=(total // rows,),
        in_specs=in_specs,
        out_specs=out_specs,
        out_shape=[jax.ShapeDtypeStruct(shape, dtype) for shape, dtype in outs],
        compiler_params=pltpu.CompilerParams(vmem_limit_bytes=limit * 1024 * 1024),
        cost_estimate=pl.CostEstimate(flops=flops, bytes_accessed=moved, transcendentals=0),
    )(*[v for v, _ in ins])


def kv_specs(ctx, rows, pairs):
    def spec(slot, start):
        return pl.BlockSpec((None, rows, 128), lambda s, p: (slot, s, start + p))

    return [spec(slot, start) for start in (0, pairs) for slot in range(ctx)]


def attend(lengths, query, kv_all):
    ctx = kv_all.shape[0]
    seqs = lengths.shape[0]
    rows = query.shape[0] // seqs
    pairs = kv_all.shape[2] // 256
    wide = query.shape[1] // pairs
    flops = 4 * query.shape[0] * query.shape[1] * rows * ctx
    return pl.pallas_call(
        partial(attend_kernel, ctx),
        grid=(seqs, pairs),
        in_specs=[
            pl.BlockSpec(memory_space=SMEM),
            pl.BlockSpec((rows, wide), lambda s, p: (s, p)),
        ]
        + kv_specs(ctx, rows, pairs),
        out_specs=[
            pl.BlockSpec((rows, wide), lambda s, p: (s, p)),
            pl.BlockSpec((rows, 128), lambda s, p: (s, p)),
        ],
        out_shape=[
            jax.ShapeDtypeStruct(query.shape, jnp.bfloat16),
            jax.ShapeDtypeStruct((query.shape[0], 128 * pairs), jnp.float32),
        ],
        compiler_params=pltpu.CompilerParams(vmem_limit_bytes=40 * 1024 * 1024),
        cost_estimate=pl.CostEstimate(flops=4 * flops, bytes_accessed=6 << 20, transcendentals=0),
    )(lengths, query, *[kv_all] * (2 * ctx))


def attend_back(fsdp, group, lengths, query, out_grad, lse, cosines, sines, kv_all, row_blocks):
    ctx = kv_all.shape[0]
    block = row_blocks.shape[1:]
    low = jnp.bfloat16
    sems = pltpu.SemaphoreType.DMA
    seqs = lengths.shape[0]
    rows = query.shape[0] // seqs
    pairs = kv_all.shape[2] // 256
    wide = query.shape[1] // pairs
    flops = 10 * query.shape[0] * query.shape[1] * rows * ctx
    return pl.pallas_call(
        partial(attend_back_kernel, ctx, fsdp, group),
        grid=(seqs, pairs),
        in_specs=[
            pl.BlockSpec(memory_space=SMEM),
            pl.BlockSpec((rows, wide), lambda s, p: (s, p)),
            pl.BlockSpec((rows, wide), lambda s, p: (s, p)),
            pl.BlockSpec((rows, 128), lambda s, p: (s, p)),
            pl.BlockSpec((rows, 128), lambda s, p: (0, 0)),
            pl.BlockSpec((rows, 128), lambda s, p: (0, 0)),
            pl.BlockSpec(memory_space=pl.ANY),
        ]
        + kv_specs(ctx, rows, pairs),
        out_specs=[
            pl.BlockSpec((rows, wide), lambda s, p: (s, p)),
            pl.BlockSpec((ctx, 2, rows, 128), lambda s, p: (0, 0, s, p)),
            pl.BlockSpec(memory_space=pl.ANY),
        ],
        out_shape=[
            jax.ShapeDtypeStruct(query.shape, jnp.bfloat16),
            jax.ShapeDtypeStruct((ctx, 2, query.shape[0], 128 * pairs), low),
            jax.ShapeDtypeStruct((2,) + block, low),
        ],
        scratch_shapes=[pltpu.VMEM((ctx, rows, 128), jnp.float32)] * 2
        + [pltpu.VMEM((group,) + block, low)] * 2
        + [sems((group,)), sems((group, 2)), sems((group, 2)), sems((3,))],
        compiler_params=pltpu.CompilerParams(
            collective_id=7, has_side_effects=True, vmem_limit_bytes=44 * 1024 * 1024
        ),
        cost_estimate=pl.CostEstimate(flops=4 * flops, bytes_accessed=10 << 20, transcendentals=0),
    )(lengths, query, out_grad, lse, cosines, sines, row_blocks, *[kv_all] * (2 * ctx))


def low_bit(k):
    return k & -k


def high_bit(k):
    return 1 << (k.bit_length() - 1)


def fsdp_order(fsdp):
    return sorted(range(1, fsdp), key=lambda k: (bin(k).count("1"), k))


def flip_index(me, k, fsdp):
    out = me
    for i in range(fsdp.bit_length() - 1):
        b = 1 << i
        if k & b:
            out = out + b - 2 * b * lax.rem(me // b, 2)
    return out


def line_neighbours(me, count):
    return (me > 0).astype(jnp.int32) + (me < count - 1).astype(jnp.int32)


def line_kernel(fsdp, ctx, group, lines, swaps, widths, *refs):
    line_in = refs[:lines]
    swap_in = refs[lines : lines + swaps]
    line_out = refs[lines + swaps : 2 * lines + swaps]
    swap_out = refs[2 * lines + swaps : -5]
    own_sem, z_send, z_recv, f_send, f_recv = refs[-5:]
    parts = len(widths)
    me_f = lax.axis_index("fsdp")
    me_c = lax.axis_index("ctx")
    me_t = lax.axis_index("tp")

    def along(step, act):
        there = me_c + step

        @pl.when((there >= 0) & (there < ctx))
        def _():
            act(there)

    barrier = pltpu.get_barrier_semaphore()
    for k in range(1, group):
        pl.semaphore_signal(
            barrier, inc=1, device_id=(flip_index(me_f, k, fsdp), me_c, me_t), device_id_type=MESH_ID
        )
    for step in (-1, 1):
        along(
            step,
            lambda there: pl.semaphore_signal(
                barrier, inc=1, device_id=(me_f, there, me_t), device_id_type=MESH_ID
            ),
        )
    pl.semaphore_wait(barrier, group - 1 + line_neighbours(me_c, ctx))

    def z_copy(i, shard, step, src=None):
        place = line_out[i].at[shard]
        way = 0 if step > 0 else 1
        return pltpu.make_async_remote_copy(
            src_ref=place if src is None else src,
            dst_ref=place,
            send_sem=z_send.at[i, way, shard],
            recv_sem=z_recv.at[i, way, shard],
            device_id=(me_f, me_c + step, me_t),
            device_id_type=MESH_ID,
        )

    def landing(i, part, f):
        width = widths[part]
        return swap_out[part].at[lax.rem(f, group), :, pl.ds(i * width, width)]

    def columns(i, part, f):
        start = lax.rem(f, group) * sum(widths) + sum(widths[:part])
        return swap_in[i].at[:, pl.ds(pl.multiple_of(start, 128), widths[part])]

    def f_copy(i, part, k):
        there = flip_index(me_f, k, fsdp)
        return pltpu.make_async_remote_copy(
            src_ref=columns(i, part, there),
            dst_ref=landing(i, part, me_f),
            send_sem=f_send.at[i * parts + part, k],
            recv_sem=f_recv.at[i * parts + part, k],
            device_id=(there, me_c, me_t),
            device_id_type=MESH_ID,
        )

    def f_arrival(i, part, k):
        there = flip_index(me_f, k, fsdp)
        return pltpu.make_async_remote_copy(
            src_ref=landing(i, part, there),
            dst_ref=landing(i, part, there),
            send_sem=f_send.at[i * parts + part, k],
            recv_sem=f_recv.at[i * parts + part, k],
            device_id=(there, me_c, me_t),
            device_id_type=MESH_ID,
        )

    pieces = [(i, part) for part in range(parts) for i in range(swaps)]
    for i in range(lines):
        for step in (1, -1):
            along(step, lambda there: z_copy(i, me_c, step, line_in[i]).start())
    order = fsdp_order(group)
    for i, part in pieces:
        for k in order:
            f_copy(i, part, k).start()
    own = [
        pltpu.make_async_copy(line_in[i], line_out[i].at[me_c], own_sem.at[i])
        for i in range(lines)
    ] + [
        pltpu.make_async_copy(
            columns(i, part, me_f),
            landing(i, part, me_f),
            own_sem.at[lines + i * parts + part],
        )
        for i, part in pieces
    ]
    for copy in own:
        copy.start()
    for distance in range(1, ctx):
        for i in range(lines):
            for step in (1, -1):
                shard = me_c - step * distance

                @pl.when((shard >= 0) & (shard < ctx))
                def _():
                    z_copy(i, shard, step).wait_recv()
                    along(step, lambda there: z_copy(i, shard, step).start())

    for i, part in pieces:
        for k in order:
            f_arrival(i, part, k).wait_recv()
            f_copy(i, part, k).wait_send()
    for copy in own:
        copy.wait()
    for i in range(lines):
        for step in (1, -1):
            along(step, lambda there: z_copy(i, me_c, step, line_in[i]).wait_send())
            for distance in range(1, ctx - 1):
                shard = me_c - step * distance

                @pl.when((shard >= 0) & (shard < ctx))
                def _():
                    along(step, lambda there: z_copy(i, shard, step).wait_send())


def start_exchange(fsdp, ctx, group, lines, swaps, widths):
    parts = len(widths)
    sems = pltpu.SemaphoreType.DMA
    rows = swaps[0].shape[0]
    out_shape = [jax.ShapeDtypeStruct((ctx,) + v.shape, v.dtype) for v in lines]
    out_shape += [
        jax.ShapeDtypeStruct((group, rows, len(swaps) * w), swaps[0].dtype) for w in widths
    ]
    count = len(lines) + len(swaps)
    outs = pl.pallas_call(
        partial(line_kernel, fsdp, ctx, group, len(lines), len(swaps), tuple(widths)),
        out_shape=out_shape,
        in_specs=[pl.BlockSpec(memory_space=pltpu.VMEM)] * count,
        out_specs=[pl.BlockSpec(memory_space=pl.ANY)] * len(out_shape),
        scratch_shapes=[
            sems((len(lines) + len(swaps) * parts,)),
            sems((len(lines), 2, ctx)),
            sems((len(lines), 2, ctx)),
            sems((len(swaps) * parts, group)),
            sems((len(swaps) * parts, group)),
        ],
        compiler_params=pltpu.CompilerParams(
            collective_id=0, has_side_effects=True, vmem_limit_bytes=24 * 1024 * 1024
        ),
    )(*lines, *swaps)
    return outs[: len(lines)], outs[len(lines) :]


class TokenGather:
    def __init__(self, group, fsdp, v_ref, out_ref, own_sem, f_send, f_recv, t_send, t_recv):
        self.order = fsdp_order(group)
        self.bits = [1 << i for i in range(group.bit_length() - 1)]
        self.out_ref = out_ref
        self.sems = (f_send, f_recv, t_send, t_recv)
        self.fsdp = fsdp
        half = out_ref.shape[2]
        self.half = half
        me_t = lax.axis_index("tp")
        self.mine = v_ref.at[pl.ds(pl.multiple_of(me_t * half, half), half)]
        other = v_ref.at[pl.ds(pl.multiple_of((1 - me_t) * half, half), half)]
        self.own = [
            pltpu.make_async_copy(self.mine, out_ref.at[0, 0], own_sem.at[0]),
            pltpu.make_async_copy(other, out_ref.at[0, 1], own_sem.at[1]),
        ]

    def peer(self, k):
        me_f = lax.axis_index("fsdp")
        return (flip_index(me_f, k, self.fsdp), lax.axis_index("ctx"), lax.axis_index("tp"))

    def rows(self, k, part):
        if k == low_bit(k):
            return pl.ds(0, self.half)
        return pl.ds(part * (self.half // 2), self.half // 2)

    def f_copy(self, have, b):
        k = have | b
        part = 1 if have and b == high_bit(k) else 0
        place = self.out_ref.at[k, 0, self.rows(k, part)]
        src = self.out_ref.at[have, 0, self.rows(k, part)] if have else self.mine
        return pltpu.make_async_remote_copy(
            src_ref=src,
            dst_ref=place,
            send_sem=self.sems[0].at[k, part],
            recv_sem=self.sems[1].at[k, part],
            device_id=self.peer(b),
            device_id_type=MESH_ID,
        )

    def ways(self, have):
        return [
            b
            for b in self.bits
            if not have & b and (not have or b in (low_bit(have | b), high_bit(have | b)))
        ]

    def swap(self, k):
        me_f, me_c, me_t = self.peer(0)
        return pltpu.make_async_remote_copy(
            src_ref=self.out_ref.at[k, 0],
            dst_ref=self.out_ref.at[k, 1],
            send_sem=self.sems[2].at[k],
            recv_sem=self.sems[3].at[k],
            device_id=(me_f, me_c, 1 - me_t),
            device_id_type=MESH_ID,
        )

    def start(self):
        for b in self.ways(0):
            self.f_copy(0, b).start()
        for copy in self.own:
            copy.start()

    def relay(self, k):
        parts = [(0, k)] if k == low_bit(k) else [(0, low_bit(k)), (1, high_bit(k))]
        for part, b in parts:
            place = self.out_ref.at[k, 0, self.rows(k, part)]
            pltpu.make_async_remote_copy(
                src_ref=place,
                dst_ref=place,
                send_sem=self.sems[0].at[k, part],
                recv_sem=self.sems[1].at[k, part],
                device_id=self.peer(b),
                device_id_type=MESH_ID,
            ).wait_recv()
        for b in self.ways(k):
            self.f_copy(k, b).start()
        self.swap(k).start()

    def finish(self):
        for copy in self.own:
            copy.wait()
        for have in [0] + self.order:
            for b in self.ways(have):
                self.f_copy(have, b).wait_send()
        me_f, me_c, me_t = self.peer(0)
        for k in self.order:
            pltpu.make_async_remote_copy(
                src_ref=self.out_ref.at[k, 1],
                dst_ref=self.out_ref.at[k, 1],
                send_sem=self.sems[2].at[k],
                recv_sem=self.sems[3].at[k],
                device_id=(me_f, me_c, 1 - me_t),
                device_id_type=MESH_ID,
            ).wait_recv()
            self.swap(k).wait_send()


def token_sems(group):
    sems = pltpu.SemaphoreType.DMA
    return [sems((2,)), sems((group, 2)), sems((group, 2)), sems((group,)), sems((group,))]


def token_shape(group, v):
    return jax.ShapeDtypeStruct((group, 2, v.shape[0] // 2, v.shape[1]), v.dtype)


def tokens_kernel(group, fsdp, v_ref, out_ref, *sems):
    gather = TokenGather(group, fsdp, v_ref, out_ref, *sems)
    me_f, me_c, me_t = gather.peer(0)
    barrier = pltpu.get_barrier_semaphore()
    for b in gather.bits:
        pl.semaphore_signal(barrier, inc=1, device_id=gather.peer(b), device_id_type=MESH_ID)
    pl.semaphore_signal(
        barrier, inc=1, device_id=(me_f, me_c, 1 - me_t), device_id_type=MESH_ID
    )
    pl.semaphore_wait(barrier, len(gather.bits) + 1)
    gather.start()
    for k in gather.order:
        gather.relay(k)
    gather.finish()


def gather_tokens(group, fsdp, v):
    out = pl.pallas_call(
        partial(tokens_kernel, group, fsdp),
        out_shape=token_shape(group, v),
        in_specs=[pl.BlockSpec(memory_space=pltpu.VMEM)],
        out_specs=pl.BlockSpec(memory_space=pl.ANY),
        scratch_shapes=token_sems(group),
        compiler_params=pltpu.CompilerParams(
            collective_id=5, has_side_effects=True, vmem_limit_bytes=24 * 1024 * 1024
        ),
    )(v)
    return out.reshape(-1, v.shape[1])


def swiglu_parts(n_ref, g_ref, w_ref, hidden_ref, grads_ref):
    units = hidden_ref.shape[1]
    both = w_ref[:, : 2 * units]
    down = w_ref[:, 2 * units :]
    lin = mul(n_ref[...], both)
    gate, up = lin[:, :units], lin[:, units:]
    sig = jax.nn.sigmoid(gate)
    act = gate * sig
    hidden = (act * up).astype(jnp.bfloat16)
    hidden_ref[...] = hidden
    hidden_grad = mul(g_ref[...], down)
    grads_ref[:, :units] = (hidden_grad * up * sig * (1.0 + gate * (1.0 - sig))).astype(
        jnp.bfloat16
    )
    grads_ref[:, units:] = (hidden_grad * act).astype(jnp.bfloat16)
    return mul(grads_ref[...], both, NT), mul(hidden, down, NT)


def swiglu_first_kernel(n_ref, g_ref, w_ref, hidden_ref, grads_ref, second_ref, ff_ref):
    second, ff = swiglu_parts(n_ref, g_ref, w_ref, hidden_ref, grads_ref)
    second_ref[...] = second.astype(jnp.bfloat16)
    ff_ref[...] = ff.astype(jnp.bfloat16)


def swiglu_kernel(
    fsdp,
    group,
    n_ref,
    g_ref,
    w_ref,
    second_ref,
    ff_first_ref,
    left_ref,
    right_ref,
    hidden_ref,
    grads_ref,
    ff_ref,
    own_ref,
    product_ref,
    s_out,
    f_out,
    s_in,
    f_in,
    total,
    got,
    t_send,
    t_recv,
    f_send,
    f_recv,
    own_sem,
    left,
    right,
    product,
    inner_sem,
):
    half = n_ref.shape[0]
    step = pl.program_id(0)
    me_f = lax.axis_index("fsdp")
    me_c = lax.axis_index("ctx")
    me_t = lax.axis_index("tp")
    bits = [1 << i for i in range(group.bit_length() - 1)]
    order = fsdp_order(group)
    core = (me_f, me_c, 1 - me_t)

    def peer(k):
        return (flip_index(me_f, k, fsdp), me_c, me_t)

    @pl.when(step == 0)
    def _():
        barrier = pltpu.get_barrier_semaphore()
        for b in bits:
            pl.semaphore_signal(barrier, inc=1, device_id=peer(b), device_id_type=MESH_ID)
        pl.semaphore_signal(barrier, inc=1, device_id=core, device_id_type=MESH_ID)
        pl.semaphore_wait(barrier, len(bits) + 1)

    inner = [
        pltpu.make_async_copy(left_ref, left, inner_sem.at[0]),
        pltpu.make_async_copy(right_ref, right, inner_sem.at[1]),
    ]

    @pl.when(step == 1)
    def _():
        for copy in inner:
            copy.start()

    def make_product():
        for copy in inner:
            copy.wait()

        def body(t, _):
            cols = pl.ds(pl.multiple_of(t * 256, 256), 256)
            product[cols, :] = mul(left[:, cols], right[...], TN).astype(product.dtype)
            return 0

        lax.fori_loop(0, left.shape[1] // 256, body, 0)
        pltpu.make_async_copy(product, product_ref, inner_sem.at[2]).start()

    def core_copies(k):
        slot = k % 2
        return [
            pltpu.make_async_remote_copy(
                src_ref=out.at[slot],
                dst_ref=into.at[slot],
                send_sem=t_send.at[which, k],
                recv_sem=t_recv.at[which, k],
                device_id=core,
                device_id_type=MESH_ID,
            )
            for which, (out, into) in enumerate(((s_out, s_in), (f_out, f_in)))
        ]

    def ways(k):
        return [(0, k)] if k == low_bit(k) else [(0, low_bit(k)), (1, high_bit(k))]

    def span(k, part):
        return pl.ds(0, half) if k == low_bit(k) else pl.ds(part * (half // 2), half // 2)

    def f_copy(k, part, b):
        return pltpu.make_async_remote_copy(
            src_ref=total.at[k, span(k, part)],
            dst_ref=got.at[k, span(k, part)],
            send_sem=f_send.at[k, part],
            recv_sem=f_recv.at[k, part],
            device_id=peer(b),
            device_id_type=MESH_ID,
        )

    def own_copy():
        return pltpu.make_async_remote_copy(
            src_ref=total.at[0],
            dst_ref=own_ref.at[me_t],
            send_sem=own_sem.at[0],
            recv_sem=own_sem.at[1],
            device_id=core,
            device_id_type=MESH_ID,
        )

    second, ff = swiglu_parts(n_ref, g_ref, w_ref, hidden_ref, grads_ref)
    second = second + second_ref[...].astype(jnp.float32)
    ff = ff + ff_first_ref[...].astype(jnp.float32)

    for k in reversed(range(group)):
        slot = k % 2

        @pl.when(step == 2 * (group - 1 - k))
        def _():
            if k + 2 < group:
                for copy in core_copies(k + 2):
                    copy.wait_send()
            s_out[slot] = second.astype(jnp.bfloat16)
            f_out[slot] = ff.astype(jnp.bfloat16)
            for copy in core_copies(k):
                copy.start()

        @pl.when(step == 2 * (group - 1 - k) + 1)
        def _():
            for copy in core_copies(k):
                copy.wait_recv()
            ff_ref[...] = (ff + f_in[slot].astype(jnp.float32)).astype(jnp.bfloat16)
            total[k] = (second + s_in[slot].astype(jnp.float32)).astype(jnp.bfloat16)
            if k == 0:
                make_product()
            for far in order:
                for part, b in ways(far):
                    if far ^ b == k:
                        f_copy(far, part, b).wait_recv()
                        rows = span(far, part)
                        total[k, rows] = (
                            total[k, rows].astype(jnp.float32)
                            + got[far, rows].astype(jnp.float32)
                        ).astype(jnp.bfloat16)
            if k:
                for part, b in ways(k):
                    f_copy(k, part, b).start()
            else:
                own_copy().start()
                local = pltpu.make_async_copy(total.at[0], own_ref.at[me_t], own_sem.at[2])
                local.start()
                local.wait()
                other = own_ref.at[1 - me_t]
                pltpu.make_async_remote_copy(
                    src_ref=other,
                    dst_ref=other,
                    send_sem=own_sem.at[0],
                    recv_sem=own_sem.at[1],
                    device_id=core,
                    device_id_type=MESH_ID,
                ).wait_recv()
                own_copy().wait_send()
                for far in order:
                    for part, b in ways(far):
                        f_copy(far, part, b).wait_send()
                for late in range(min(2, group)):
                    for copy in core_copies(late):
                        copy.wait_send()
                pltpu.make_async_copy(product, product_ref, inner_sem.at[2]).wait()


def swiglu(fsdp, group, normed, grads, weights, second, ff, hidden):
    many, width = normed.shape
    half = many // (2 * group)
    units = weights.shape[1] // 3
    low = jnp.bfloat16
    last = 2 * group - 1
    sems = pltpu.SemaphoreType.DMA
    block = (half, width)

    def rows(cols):
        return pl.BlockSpec((half, cols), lambda i: (last - i, 0))

    def whole(v):
        return pl.BlockSpec(v.shape, lambda i: (0, 0), pipeline_mode=pl.Buffered(1))

    return pl.pallas_call(
        partial(swiglu_kernel, fsdp, group),
        grid=(2 * group,),
        in_specs=[rows(width), rows(width), whole(weights), rows(width), rows(width)]
        + [pl.BlockSpec(memory_space=pl.ANY)] * 2,
        out_specs=[
            rows(units),
            rows(2 * units),
            pl.BlockSpec(block, lambda i: (group - 1 - i // 2, 0)),
            pl.BlockSpec(memory_space=pl.ANY),
            pl.BlockSpec(memory_space=pl.ANY),
        ],
        out_shape=[
            jax.ShapeDtypeStruct((many, units), low),
            jax.ShapeDtypeStruct((many, 2 * units), low),
            jax.ShapeDtypeStruct((group * half, width), low),
            jax.ShapeDtypeStruct((2,) + block, low),
            jax.ShapeDtypeStruct((width, hidden.shape[1]), low),
        ],
        scratch_shapes=[pltpu.VMEM((2,) + block, low)] * 4
        + [pltpu.VMEM((group,) + block, low)] * 2
        + [
            sems((2, group)),
            sems((2, group)),
            sems((group, 2)),
            sems((group, 2)),
            sems((3,)),
            pltpu.VMEM(grads.shape, low),
            pltpu.VMEM(hidden.shape, low),
            pltpu.VMEM((width, hidden.shape[1]), low),
            sems((3,)),
        ],
        compiler_params=pltpu.CompilerParams(
            collective_id=6, has_side_effects=True, vmem_limit_bytes=58 * 1024 * 1024
        ),
        cost_estimate=pl.CostEstimate(
            flops=12 * many * width * units, bytes_accessed=50 << 20, transcendentals=0
        ),
    )(normed, grads, weights, second, ff, grads, hidden)


def spread_kernel(fsdp, ctx, group, count, chain, *refs):
    ins = refs[:count]
    outs = refs[count + chain : 2 * count + chain]
    sems = refs[2 * (count + chain) :]
    own_sem, f_send, f_recv, c_own, c_send, c_recv = sems[:6]
    me_f = lax.axis_index("fsdp")
    me_c = lax.axis_index("ctx")
    me_t = lax.axis_index("tp")
    bits = [1 << i for i in range(fsdp.bit_length() - 1)]
    order = fsdp_order(fsdp)

    def peer(k):
        return (flip_index(me_f, k, fsdp), me_c, me_t)

    barrier = pltpu.get_barrier_semaphore()
    for b in bits:
        pl.semaphore_signal(barrier, inc=1, device_id=peer(b), device_id_type=MESH_ID)
    if chain:
        chain_in, chain_out = refs[count], refs[2 * count + chain]
        gather = TokenGather(
            group, fsdp, refs[count + 1], refs[2 * count + chain + 1], *sems[6:]
        )
        pl.semaphore_signal(
            barrier, inc=1, device_id=(me_f, me_c, 1 - me_t), device_id_type=MESH_ID
        )
        for step in (-1, 1):
            there = me_c + step

            @pl.when((there >= 0) & (there < ctx))
            def _():
                pl.semaphore_signal(
                    barrier, inc=1, device_id=(me_f, there, me_t), device_id_type=MESH_ID
                )

        pl.semaphore_wait(barrier, len(bits) + 1 + line_neighbours(me_c, ctx))
    else:
        pl.semaphore_wait(barrier, len(bits))

    def quarters(rows):
        return [pl.ds(i * (rows // 4), rows // 4) for i in range(4)]

    def climb(s):
        return [
            pltpu.make_async_remote_copy(
                src_ref=chain_out.at[s, part] if s else chain_in.at[part],
                dst_ref=chain_out.at[s + 1, part],
                send_sem=c_send.at[s, i],
                recv_sem=c_recv.at[s + 1, i],
                device_id=(me_f, me_c + 1, me_t),
                device_id_type=MESH_ID,
            )
            for i, part in enumerate(quarters(chain_in.shape[0]))
        ]

    def keep(s):
        return pltpu.make_async_copy(chain_in, chain_out.at[s], c_own.at[s])

    def send_up(s):
        @pl.when((me_c >= s) & (me_c < ctx - 1))
        def _():
            for copy in climb(s):
                copy.start()

    def take_up(s):
        @pl.when(me_c >= s)
        def _():
            for i, part in enumerate(quarters(chain_in.shape[0])):
                pltpu.make_async_remote_copy(
                    src_ref=chain_out.at[s, part],
                    dst_ref=chain_out.at[s, part],
                    send_sem=c_send.at[s - 1, i],
                    recv_sem=c_recv.at[s, i],
                    device_id=(me_f, me_c - 1, me_t),
                    device_id_type=MESH_ID,
                ).wait_recv()

        if s < ctx - 1:
            send_up(s)

    if chain:
        send_up(0)
        keep(0).start()
        for s in range(1, ctx):
            @pl.when(me_c < s)
            def _():
                keep(s).start()

    def place(i, shard, have, k, part):
        block = outs[i].at[shard, flip_index(me_f, have, fsdp)]
        half = ins[i].shape[1] // 2
        return block if k == low_bit(k) else block.at[pl.ds(part * half, half)]

    def f_copy(i, shard, have, b):
        k = have | b
        part = 1 if have and b == high_bit(k) else 0
        block = place(i, shard, have, k, part)
        return pltpu.make_async_remote_copy(
            src_ref=block if have else ins[i].at[shard],
            dst_ref=block,
            send_sem=f_send.at[i, shard, k, part],
            recv_sem=f_recv.at[i, shard, k, part],
            device_id=peer(b),
            device_id_type=MESH_ID,
        )

    def ways(have):
        return [
            b
            for b in bits
            if not have & b and (not have or b in (low_bit(have | b), high_bit(have | b)))
        ]

    own = [
        pltpu.make_async_copy(ins[i], outs[i].at[:, me_f], own_sem.at[i]) for i in range(count)
    ]
    for i in range(count):
        for shard in range(ctx):
            for b in ways(0):
                f_copy(i, shard, 0, b).start()
        own[i].start()
    if chain:
        gather.start()
    climbed = 1
    for i in range(count):
        for k in order:
            if chain and climbed < ctx:
                take_up(climbed)
                climbed += 1
            if chain and k < group and i == 0:
                gather.relay(k)
            parts = [(0, k)] if k == low_bit(k) else [(0, low_bit(k)), (1, high_bit(k))]
            for shard in range(ctx):
                for part, b in parts:
                    block = place(i, shard, k, k, part)
                    pltpu.make_async_remote_copy(
                        src_ref=block,
                        dst_ref=block,
                        send_sem=f_send.at[i, shard, k, part],
                        recv_sem=f_recv.at[i, shard, k, part],
                        device_id=peer(b),
                        device_id_type=MESH_ID,
                    ).wait_recv()
                for b in ways(k):
                    f_copy(i, shard, k, b).start()
    if chain:
        for s in range(climbed, ctx):
            take_up(s)
        gather.finish()
        keep(0).wait()
        for s in range(ctx):
            if s:

                @pl.when(me_c < s)
                def _():
                    keep(s).wait()

            if s < ctx - 1:

                @pl.when((me_c >= s) & (me_c < ctx - 1))
                def _():
                    for copy in climb(s):
                        copy.wait_send()

    for i in range(count):
        own[i].wait()
        for have in [0] + order:
            for shard in range(ctx):
                for b in ways(have):
                    f_copy(i, shard, have, b).wait_send()


def spread_weights(fsdp, ctx, group, arrays, chain=()):
    count = len(arrays)
    sems = pltpu.SemaphoreType.DMA
    outs = pl.pallas_call(
        partial(spread_kernel, fsdp, ctx, group, count, len(chain)),
        out_shape=[
            jax.ShapeDtypeStruct((ctx, fsdp) + v.shape[1:], v.dtype) for v in arrays
        ]
        + [jax.ShapeDtypeStruct((ctx,) + v.shape, v.dtype) for v in chain[:1]]
        + [token_shape(group, v) for v in chain[1:]],
        in_specs=[pl.BlockSpec(memory_space=pltpu.VMEM)] * (count + len(chain)),
        out_specs=[pl.BlockSpec(memory_space=pl.ANY)] * (count + len(chain)),
        scratch_shapes=[
            sems((count,)),
            sems((count, ctx, fsdp, 2)),
            sems((count, ctx, fsdp, 2)),
            sems((ctx,)),
            sems((ctx, 4)),
            sems((ctx, 4)),
        ]
        + (token_sems(group) if chain else []),
        compiler_params=pltpu.CompilerParams(
            collective_id=3 if chain else 1,
            has_side_effects=True,
            vmem_limit_bytes=24 * 1024 * 1024,
        ),
    )(*arrays, *chain)
    return (
        [o.reshape(-1, v.shape[-1]) for o, v in zip(outs, arrays)]
        + list(outs[count : count + 1])
        + [o.reshape(-1, o.shape[-1]) for o in outs[count + 1 :]]
    )


def sum_kernel(fsdp, ctx, count, chain, products, *refs):
    inner = []
    if products:
        first = count + 3
        pairs = refs[first : first + 2 * products]
        place = first + 2 * products + count + 1
        results = refs[place : place + products]
        inner = refs[-2 * products - 1 :]
        refs = refs[:first] + refs[first + 2 * products : place] + refs[place + products :]
        refs = refs[: -2 * products - 1]
    ins = refs[:count]
    if chain:
        parts_ref, cos_ref, sin_ref = refs[count : count + 3]
        refs = refs[:count] + refs[count + 3 :]
        kv_ref = refs[2 * count]
        refs = refs[: 2 * count] + refs[2 * count + 1 :]
    outs = refs[count : 2 * count]
    held = refs[2 * count : 3 * count]
    got = refs[3 * count : 4 * count]
    line = refs[4 * count : 5 * count]
    refs = refs[5 * count :]
    in_sem, f_send, f_recv, z_send, z_recv = refs[:5]
    if chain:
        kv_parts, kv_got, kv_sem, c_send, c_recv = refs[5:]
    me_f = lax.axis_index("fsdp")
    me_c = lax.axis_index("ctx")
    me_t = lax.axis_index("tp")
    bits = [1 << i for i in range(fsdp.bit_length() - 1)]
    order = fsdp_order(fsdp)

    def peer(k):
        return (flip_index(me_f, k, fsdp), me_c, me_t)

    def along(step, act):
        there = me_c + step

        @pl.when((there >= 0) & (there < ctx))
        def _():
            act(there)

    loads = {}
    if chain:
        kv_load = pltpu.make_async_copy(parts_ref, kv_parts, kv_sem.at[0])
        kv_load.start()
    inner_loads = [
        pltpu.make_async_copy(pairs[i], inner[i], inner[-1].at[i]) for i in range(2 * products)
    ]
    for i in range(count):
        for k in reversed([0] + order):
            block = ins[i].at[:, flip_index(me_f, k, fsdp)]
            loads[i, k] = pltpu.make_async_copy(block, held[i].at[k], in_sem.at[i, k])
            loads[i, k].start()

    barrier = pltpu.get_barrier_semaphore()
    for b in bits:
        pl.semaphore_signal(barrier, inc=1, device_id=peer(b), device_id_type=MESH_ID)
    for step in (-1, 1):
        along(
            step,
            lambda there: pl.semaphore_signal(
                barrier, inc=1, device_id=(me_f, there, me_t), device_id_type=MESH_ID
            ),
        )
    pl.semaphore_wait(barrier, len(bits) + line_neighbours(me_c, ctx))

    def ways(k):
        return [(0, k)] if k == low_bit(k) else [(0, low_bit(k)), (1, high_bit(k))]

    def piece(i, k, part):
        rows = ins[i].shape[2]
        return pl.ds(0, rows) if k == low_bit(k) else pl.ds(part * (rows // 2), rows // 2)

    def f_copy(i, shard, k, part, b):
        span = piece(i, k, part)
        return pltpu.make_async_remote_copy(
            src_ref=held[i].at[k, shard, span],
            dst_ref=got[i].at[k, shard, span],
            send_sem=f_send.at[i, shard, k, part],
            recv_sem=f_recv.at[i, shard, k, part],
            device_id=peer(b),
            device_id_type=MESH_ID,
        )

    def add(into, other):
        tile = 16 if into.dtype == jnp.bfloat16 else 8

        def body(r, _):
            span = pl.ds(pl.multiple_of(r * tile, tile), tile)
            into[span] = (
                into[span].astype(jnp.float32) + other[span].astype(jnp.float32)
            ).astype(into.dtype)
            return 0

        lax.fori_loop(0, into.shape[0] // tile, body, 0)

    def collect(i, shard, k):
        for far in order:
            for part, b in ways(far):
                if far ^ b == k:
                    f_copy(i, shard, far, part, b).wait_recv()
                    span = piece(i, far, part)
                    add(held[i].at[k, shard, span], got[i].at[far, shard, span])

    def z_copy(i, shard, step):
        way = 0 if step > 0 else 1
        return pltpu.make_async_remote_copy(
            src_ref=held[i].at[0, shard],
            dst_ref=line[i].at[way, shard],
            send_sem=z_send.at[i, way, shard],
            recv_sem=z_recv.at[i, way, shard],
            device_id=(me_f, me_c + step, me_t),
            device_id_type=MESH_ID,
        )

    def give(i, shard):
        def body(r, _):
            span = pl.ds(pl.multiple_of(r * 16, 16), 16)
            outs[i][span] = held[i][0, shard, span].astype(outs[i].dtype)
            return 0

        lax.fori_loop(0, outs[i].shape[0] // 16, body, 0)

    def on_line(i, shard, step):
        way = 0 if step > 0 else 1

        @pl.when((me_c - step >= 0) & (me_c - step < ctx))
        def _():
            z_copy(i, shard, step).wait_recv()
            add(held[i].at[0, shard], line[i].at[way, shard])

        @pl.when(step * (shard - me_c) > 0)
        def _():
            z_copy(i, shard, step).start()

    def quarters():
        rows = kv_parts.shape[2] // 2
        return [(side, pl.ds(i * rows, rows)) for side in range(2) for i in range(2)]

    def descend(s):
        return [
            pltpu.make_async_remote_copy(
                src_ref=kv_parts.at[s, side, part],
                dst_ref=kv_got.at[s - 1, side, part],
                send_sem=c_send.at[s, i],
                recv_sem=c_recv.at[s - 1, i],
                device_id=(me_f, me_c - 1, me_t),
                device_id_type=MESH_ID,
            )
            for i, (side, part) in enumerate(quarters())
        ]

    def chain_step(s):
        if s < ctx - 1:

            @pl.when((me_c >= s) & (me_c < ctx - 1))
            def _():
                for i, (side, part) in enumerate(quarters()):
                    pltpu.make_async_remote_copy(
                        src_ref=kv_got.at[s, side, part],
                        dst_ref=kv_got.at[s, side, part],
                        send_sem=c_send.at[s + 1, i],
                        recv_sem=c_recv.at[s, i],
                        device_id=(me_f, me_c + 1, me_t),
                        device_id_type=MESH_ID,
                    ).wait_recv()
                    add(kv_parts.at[s, side, part], kv_got.at[s, side, part])

        if s:

            @pl.when(me_c >= s)
            def _():
                for copy in descend(s):
                    copy.start()

    def chain_result():
        width = kv_parts.shape[3]
        rows = cos_ref.shape[0]
        for seq in range(kv_parts.shape[2] // rows):
            span = pl.ds(seq * rows, rows)
            for start in range(0, width, 128):
                cols = slice(start, start + 128)
                t = kv_parts[0, 0, span, cols].astype(jnp.float32)
                t = t * cos_ref[...] + turn(t * sin_ref[...], -1.0)
                kv_ref[span, cols] = t.astype(kv_ref.dtype)
            kv_ref[span, width:] = kv_parts[0, 1, span]

    steps = list(reversed(range(ctx))) if chain else []

    def next_step():
        if steps:
            s = steps.pop(0)
            chain_step(s)
            if s == 0:
                chain_result()

    turns = 4

    def make_products(turn):
        if turn == 0:
            for load in inner_loads:
                load.wait()
        for i in range(products):
            left, right, result = inner[2 * i], inner[2 * i + 1], results[i]
            tiles = left.shape[1] // 256
            per = -(-tiles // turns)

            def body(t, _):
                cols = pl.ds(pl.multiple_of(t * 256, 256), 256)
                result[cols, :] = mul(left[:, cols], right[...], TN).astype(result.dtype)
                return 0

            lax.fori_loop(min(turn * per, tiles), min((turn + 1) * per, tiles), body, 0)

    if chain:
        kv_load.wait()
        next_step()
    for load in inner_loads:
        load.start()
    shards = sorted(range(ctx), key=lambda c: -abs(2 * c - ctx + 1))
    work = [[(i, shard) for i in range(count)] for shard in shards]
    levels = sorted({bin(k).count("1") for k in order}, reverse=True)
    waited = set()

    def loaded(i, k):
        if (i, k) not in waited:
            waited.add((i, k))
            loads[i, k].wait()

    def advance(stage, item):
        for i, shard in item:
            if stage == len(levels):
                loaded(i, 0)
                collect(i, shard, 0)
                continue
            for k in order:
                if bin(k).count("1") == levels[stage]:
                    loaded(i, k)
                    collect(i, shard, k)
                    for part, b in ways(k):
                        f_copy(i, shard, k, part, b).start()

    def line_tick(item, hops):
        for i, shard in item:
            for step, there in ((1, hops), (-1, ctx - 1 - hops)):
                if step * (shard - there) >= 0:

                    @pl.when(me_c == there)
                    def _():
                        on_line(i, shard, step)

            if hops == max(shard, ctx - 1 - shard):

                @pl.when(me_c == shard)
                def _():
                    give(i, shard)

    stages = len(levels) + 1
    for tick in range(len(work) + stages + ctx - 2):
        for stage in range(stages):
            if 0 <= tick - stage < len(work):
                advance(stage, work[tick - stage])
        for hops in range(ctx):
            place = tick - stages + 1 - hops
            if 0 <= place < len(work):
                line_tick(work[place], hops)
        if products and tick < turns:
            make_products(tick)
        next_step()
    while steps:
        next_step()
    for i, shard in [pair for item in work for pair in item]:
        for k in order:
            for part, b in ways(k):
                f_copy(i, shard, k, part, b).wait_send()
        for step in (1, -1):

            @pl.when(step * (shard - me_c) > 0)
            def _():
                z_copy(i, shard, step).wait_send()

    if chain:
        for s in range(1, ctx):

            @pl.when(me_c >= s)
            def _():
                for copy in descend(s):
                    copy.wait_send()


def sum_weights(fsdp, ctx, arrays, chain=(), products=()):
    sems = pltpu.SemaphoreType.DMA
    vmem = pltpu.VMEM
    shards = [v.reshape(ctx, fsdp, -1, v.shape[-1]) for v in arrays]
    blocks = [(fsdp, ctx) + v.shape[2:] for v in shards]
    out_shape = [jax.ShapeDtypeStruct(v.shape[2:], jnp.float32) for v in shards]
    lines = [vmem((2,) + b[1:], v.dtype) for b, v in zip(blocks, shards)]
    extra = []
    if chain:
        parts = chain[0]
        out_shape.append(jax.ShapeDtypeStruct((parts.shape[2], 2 * parts.shape[3]), parts.dtype))
        extra = [
            vmem(parts.shape, parts.dtype),
            vmem((ctx - 1,) + parts.shape[1:], parts.dtype),
            sems((1,)),
            sems((ctx, 4)),
            sems((ctx, 4)),
        ]
    count = len(shards)
    flat = [v for pair in products for v in pair]
    for left, right in products:
        out_shape.append(jax.ShapeDtypeStruct((left.shape[1], right.shape[1]), left.dtype))
    if products:
        extra = extra + [vmem(v.shape, v.dtype) for v in flat] + [sems((len(flat),))]
    held = [vmem(b, v.dtype) for b, v in zip(blocks, shards)]
    return pl.pallas_call(
        partial(sum_kernel, fsdp, ctx, count, bool(chain), len(products)),
        out_shape=out_shape,
        in_specs=[pl.BlockSpec(memory_space=pl.ANY)] * (count + len(chain[:1]))
        + [pl.BlockSpec(memory_space=pltpu.VMEM)] * len(chain[1:])
        + [pl.BlockSpec(memory_space=pl.ANY)] * len(flat),
        out_specs=[pl.BlockSpec(memory_space=pltpu.VMEM)] * len(out_shape),
        scratch_shapes=held
        + held
        + lines
        + [
            sems((count, fsdp)),
            sems((count, ctx, fsdp, 2)),
            sems((count, ctx, fsdp, 2)),
            sems((count, 2, ctx)),
            sems((count, 2, ctx)),
        ]
        + extra,
        compiler_params=pltpu.CompilerParams(
            collective_id=4 if chain else 2,
            has_side_effects=True,
            vmem_limit_bytes=58 * 1024 * 1024,
        ),
    )(*shards, *chain, *flat)


def heads_kernel(group_size, qkv_ref, out_ref, *outs):
    width = outs[0].shape[1]
    for source, target in ((qkv_ref, outs[0]), (out_ref, outs[3])):
        for block in range(width // 128):
            pair, rest = divmod(2 * block, 2 * group_size)
            g, j = divmod(rest, group_size)
            start = (pair * group_size + j) * 128
            left = source[:, start : start + 128]
            right = source[:, start + 128 : start + 256]
            if g:
                left = pltpu.roll(left, HD, 1)
            else:
                right = pltpu.roll(right, HD, 1)
            lane = lax.broadcasted_iota(jnp.int32, left.shape, 1)
            target[:, block * 128 : (block + 1) * 128] = jnp.where(lane < HD, left, right)
    kv_width = outs[1].shape[1]
    outs[1][...] = qkv_ref[:, width : width + kv_width]
    outs[2][...] = qkv_ref[:, width + kv_width :]


def plain_grads(group_size, qkv, out, kv_width):
    rows, width = out.shape
    vmem = pl.BlockSpec(memory_space=pltpu.VMEM)
    return pl.pallas_call(
        partial(heads_kernel, group_size),
        out_shape=[
            jax.ShapeDtypeStruct((rows, w), out.dtype) for w in (width, kv_width, kv_width, width)
        ],
        in_specs=[vmem] * 2,
        out_specs=[vmem] * 4,
        cost_estimate=pl.CostEstimate(flops=0, bytes_accessed=4 << 20, transcendentals=0),
    )(qkv, out)


def place_kernel(group, count, *refs):
    parts, outs = refs[:count], refs[count:]
    span = sum(v.shape[3] for v in parts)
    for i, out in enumerate(outs):
        for f in range(group):
            start = f * span
            for v in parts:
                width = v.shape[3]
                out[:, start : start + width] = v[f, i].astype(out.dtype)
                start += width


def place_units(parts):
    group, arrays, rows, _ = parts[0].shape
    cols = group * sum(v.shape[3] for v in parts)
    vmem = pl.BlockSpec(memory_space=pltpu.VMEM)
    return pl.pallas_call(
        partial(place_kernel, group, len(parts)),
        out_shape=[jax.ShapeDtypeStruct((rows, cols), jnp.float32)] * arrays,
        in_specs=[vmem] * len(parts),
        out_specs=[vmem] * arrays,
        compiler_params=pltpu.CompilerParams(vmem_limit_bytes=24 * 1024 * 1024),
        cost_estimate=pl.CostEstimate(
            flops=0, bytes_accessed=6 * rows * cols * arrays, transcendentals=0
        ),
    )(*parts)


def local(
    inputs,
    lengths,
    cotangent,
    norm1_gain,
    w_query,
    w_key,
    w_value,
    w_out,
    norm2_gain,
    w_gate,
    w_up,
    w_down,
):
    seq_count, local_rows, model_width = inputs.shape
    tokens = seq_count * local_rows
    half = tokens // 2
    fsdp = lax.axis_size("fsdp")
    ctx = lax.axis_size("ctx")
    shard = w_query.shape[0]
    query_width = w_query.shape[1]
    kv_width = w_key.shape[1]
    kv_end = query_width + 2 * kv_width
    pairs = kv_width // (2 * HD)
    group_size = query_width // kv_width
    group = min(fsdp, 4)
    far = fsdp // group
    own = w_gate.shape[1] // group
    first_units = own * FIRST_EIGHTHS // 8
    widths = (first_units, own - first_units)
    me_c = lax.axis_index("ctx")
    me_t = lax.axis_index("tp")
    low = jnp.bfloat16
    wide = jnp.float32

    def swap(v):
        return lax.ppermute(v, "tp", [(0, 1), (1, 0)])

    inside = shard % 128 == 0
    dims = (fsdp, ctx, shard)
    back_dims = (ctx, fsdp, shard)

    def by_ctx(v):
        if inside:
            return v
        rows = v.shape[0]
        return v.reshape(rows, fsdp, ctx, shard).swapaxes(1, 2).reshape(rows, model_width)

    def by_fsdp(v):
        if inside:
            return v
        rows = v.shape[0]
        return v.reshape(rows, ctx, fsdp, shard).swapaxes(1, 2).reshape(rows, model_width)

    def pair_heads(v):
        rows = v.shape[0]
        return (
            v.reshape(rows, pairs, 2, group_size, HD).swapaxes(2, 3).reshape(rows, query_width)
        )

    x = by_ctx(inputs.reshape(tokens, model_width))
    cot = by_ctx(cotangent.reshape(tokens, model_width))
    positions = me_c * local_rows + jnp.arange(local_rows, dtype=jnp.int32)
    cosines, sines = rope_tables(positions, HD)
    cosines, sines = jnp.tile(cosines, (1, 2)), jnp.tile(sines, (1, 2))

    gains = jnp.pad(jnp.stack([norm1_gain, norm2_gain]).astype(wide), ((0, 14), (0, 0)))
    lined, held = start_exchange(
        fsdp,
        ctx,
        group,
        [
            jnp.concatenate([pair_heads(w_query), w_key, w_value], 1),
            gains,
            pair_heads(w_out),
        ],
        [w_gate, w_up, w_down],
        widths,
    )
    far_groups = [[h * group + g for h in range(far)] for g in range(group)]
    near_groups = [[h * group + g for g in range(group)] for h in range(far)]

    def whole_width(v):
        if far > 1:
            v = lax.all_gather(v, "fsdp", axis=0, tiled=False, axis_index_groups=far_groups)
        return lax.all_gather(v, "ctx", axis=0, tiled=False).reshape(model_width, -1)

    first_full = whole_width(held[0])
    qkv_full, gain_rows = spread_weights(fsdp, ctx, group, lined[:2])
    gain_rows = gain_rows.reshape(ctx * fsdp, 16, shard)
    gain_one = gain_rows[:, 0].reshape(1, model_width)
    gain_two = gain_rows[:, 1].reshape(1, model_width)

    (ff_grad,) = by_rows(
        partial(cot_kernel, dims, local_rows),
        128,
        [(lengths, "smem"), (cot, "rows")],
        [((tokens, model_width), low)],
    )
    first_normed, query, kv_own = by_rows(
        partial(qkv_kernel, dims),
        128,
        [
            (x, "rows"),
            (qkv_full, "whole"),
            (gain_one, "whole"),
            (cosines, "cycle"),
            (sines, "cycle"),
        ],
        [
            ((tokens, model_width), low),
            ((tokens, query_width), low),
            ((tokens, 2 * kv_width), low),
        ],
        flops=2 * tokens * model_width * kv_end,
    )
    out_full, kv_all, ff_grad_all = spread_weights(
        fsdp, ctx, group, lined[2:], (kv_own, ff_grad)
    )
    late_held, kv_all = lax.optimization_barrier((held[1], kv_all))
    late_full = whole_width(late_held)
    attended, lse = attend(lengths, query, kv_all)
    attn_part = jnp.einsum(
        "tj,dj->td", attended, out_full, preferred_element_type=wide
    ).astype(low)
    middle, second_normed = by_rows(
        partial(middle_kernel, dims),
        128,
        [(x, "rows"), (attn_part, "rows"), (swap(attn_part), "rows"), (gain_two, "whole")],
        [((tokens, model_width), wide), ((tokens, model_width), low)],
    )
    normed_all = gather_tokens(group, fsdp, second_normed)

    def unit_term(left, right):
        return jnp.einsum("td,tf->df", left, right, preferred_element_type=wide).astype(low)

    def own_units(term):
        width = term.shape[1]
        own = lax.psum_scatter(
            term.reshape(ctx, fsdp, shard, width), "ctx", scatter_dimension=0, tiled=False
        )
        if far > 1:
            own = lax.psum_scatter(
                own.reshape(far, group, shard, width),
                "fsdp",
                scatter_dimension=0,
                tiled=False,
                axis_index_groups=far_groups,
            )
        return own

    def return_units(both, down):
        units = down.shape[-1]
        pieces = jnp.concatenate([both[..., :units], both[..., units:], down], 1)
        back = lax.all_to_all(
            pieces.reshape(group * 3 * shard, units),
            "fsdp",
            0,
            0,
            tiled=True,
            axis_index_groups=near_groups if far > 1 else None,
        )
        return back.reshape(group, 3, shard, units)

    many = group * tokens
    first_hidden, first_grads, second_part, ff_part = by_rows(
        swiglu_first_kernel,
        256,
        [(normed_all, "rows"), (ff_grad_all, "rows"), (first_full, "whole")],
        [
            ((many, first_units), low),
            ((many, 2 * first_units), low),
            ((many, model_width), low),
            ((many, model_width), low),
        ],
        flops=12 * many * model_width * first_units,
        limit=56,
    )
    first_both = unit_term(normed_all, first_grads)
    second_part, ff_part, _ = lax.optimization_barrier((second_part, ff_part, first_both))
    hidden, both_grad, ff_sums, second_grad, first_down = swiglu(
        fsdp,
        group,
        normed_all,
        ff_grad_all,
        late_full,
        second_part,
        ff_part,
        first_hidden,
    )
    first_own = (own_units(first_both), own_units(first_down))
    second_grad = second_grad.reshape(tokens, model_width)

    middle_grad, attn_grad, gain_two_term = by_rows(
        partial(middle_back_kernel, dims, local_rows),
        128,
        [
            (lengths, "smem"),
            (cot, "rows"),
            (middle, "rows"),
            (second_grad, "rows"),
            (gain_two, "whole"),
        ],
        [((tokens, model_width), wide), ((tokens, model_width), low), ((1, model_width), wide)],
    )
    attended_grad = jnp.dot(attn_grad, out_full, preferred_element_type=wide).astype(low)
    query_grad, kv_parts, ff_branch = attend_back(
        fsdp,
        group,
        lengths,
        query,
        attended_grad,
        lse,
        cosines,
        sines,
        kv_all,
        ff_sums.reshape(group, half, model_width),
    )
    query_grad, late_rows, late_hidden = lax.optimization_barrier(
        (query_grad, ff_grad_all, hidden)
    )
    late_down = unit_term(late_rows, late_hidden)
    late_down_own = own_units(late_down)
    kv_parts, _ = lax.optimization_barrier((kv_parts, late_down))
    out_term = jnp.einsum("td,tj->dj", attn_grad, attended, preferred_element_type=wide)
    w_out_grad, kv_grad, late_both = sum_weights(
        fsdp,
        ctx,
        [out_term.astype(low)],
        (kv_parts, cosines, sines),
        ((normed_all, both_grad),),
    )
    late_both_own = own_units(late_both)
    (output,) = by_rows(
        partial(output_kernel, back_dims, local_rows),
        128,
        [(lengths, "smem"), (middle, "rows"), (ff_branch.reshape(tokens, model_width), "rows")],
        [((tokens, model_width), low)],
    )
    qkv_grad = jnp.concatenate([query_grad, kv_grad], -1)
    qkv_term = jnp.einsum("td,tj->dj", first_normed, qkv_grad, preferred_element_type=wide)
    first_part = jnp.einsum(
        "tj,dj->td", qkv_grad, qkv_full, preferred_element_type=wide
    ).astype(low)
    input_grad, gain_one_term = by_rows(
        partial(input_back_kernel, dims),
        128,
        [
            (x, "rows"),
            (first_part, "rows"),
            (swap(first_part), "rows"),
            (middle_grad, "rows"),
            (gain_one, "whole"),
        ],
        [((tokens, model_width), low), ((1, model_width), wide)],
    )
    gain_terms = jnp.stack(
        [gain_one_term.reshape(-1, shard), gain_two_term.reshape(-1, shard)], 1
    )
    gain_terms = jnp.pad(gain_terms, ((0, 0), (0, 14), (0, 0))).reshape(-1, shard)
    first_back = return_units(*first_own)
    qkv_term, first_back, _ = lax.optimization_barrier(
        (qkv_term.astype(low), first_back, late_both)
    )
    qkv_own, gain_own = sum_weights(fsdp, ctx, [qkv_term, gain_terms])
    w_query_grad, w_key_grad, w_value_grad, w_out_grad = plain_grads(
        group_size, qkv_own, w_out_grad, kv_width
    )
    late_both_own, late_down_own, qkv_own = lax.optimization_barrier(
        (late_both_own, late_down_own, qkv_own)
    )
    late_back = return_units(late_both_own, late_down_own)
    w_gate_grad, w_up_grad, w_down_grad = place_units([first_back, late_back])
    return (
        by_fsdp(output).reshape(inputs.shape),
        by_fsdp(input_grad).reshape(inputs.shape),
        gain_own[0],
        w_query_grad,
        w_key_grad,
        w_value_grad,
        w_out_grad,
        gain_own[1],
        w_gate_grad,
        w_up_grad,
        w_down_grad,
    )


def solution(mesh):
    placed = (
        P("fsdp", "ctx", None),
        P("fsdp"),
        P("fsdp", "ctx", None),
        P(("fsdp", "ctx")),
        P(("fsdp", "ctx"), "tp"),
        P(("fsdp", "ctx"), "tp"),
        P(("fsdp", "ctx"), "tp"),
        P(("fsdp", "ctx"), "tp"),
        P(("fsdp", "ctx")),
        P(("fsdp", "ctx"), "tp"),
        P(("fsdp", "ctx"), "tp"),
        P(("fsdp", "ctx"), "tp"),
    )
    return jax.shard_map(
        local,
        mesh=mesh,
        in_specs=placed,
        out_specs=(
            P("fsdp", "ctx", None),
            P("fsdp", "ctx", None),
            P(("fsdp", "ctx")),
            P(("fsdp", "ctx"), "tp"),
            P(("fsdp", "ctx"), "tp"),
            P(("fsdp", "ctx"), "tp"),
            P(("fsdp", "ctx"), "tp"),
            P(("fsdp", "ctx")),
            P(("fsdp", "ctx"), "tp"),
            P(("fsdp", "ctx"), "tp"),
            P(("fsdp", "ctx"), "tp"),
        ),
        check_vma=False,
    )
```
